32 devices in a mesh: struct: 4 (over y, core), edge: 8 (over z, x).
Axes of the slice: x: 2, y: 2, z: 4, core: 2. Of those that a mesh axis runs over, the one named last changes fastest.
Arguments:
- positions: float32 [3, 4, 512], P(None, 'struct', 'edge'), may hold values from 0 to 3
- species: int32 [4, 512], P('struct', 'edge'), may hold values from 0 to 1
- struct_id: int32 [4, 512], P('struct', 'edge'), may hold values from 0 to 7, as said below
- atom_mask: int32 [4, 512], P('struct', 'edge'), may hold values 0 or 1
- senders: int32 [4, 16384], P('struct', 'edge'), may hold values from 0 to 511, as said below
- receivers: int32 [4, 16384], P('struct', 'edge'), may hold values from 0 to 511, as said below
- edge_mask: int32 [4, 16384], P('struct', 'edge'), may hold values 0 or 1
- energy_cot: float32 [4, 8], P('struct'), may hold values from -6 to 6
- embedding: float32 [2, 4], replicated, may hold values from -4 to 4
- channel_in: float32 [2, 4, 12], replicated, may hold values from -3 to 3
- channel_mix: float32 [2, 12, 12], replicated, may hold values from -1.75 to 1.75
- hidden_weight: float32 [2, 432, 24], replicated, may hold values from -0.3125 to 0.3125
- hidden_bias: float32 [2, 24], replicated, may hold values from -3 to 3
- inner_weight: float32 [2, 24, 16], replicated, may hold values from -1.25 to 1.25
- inner_bias: float32 [2, 16], replicated, may hold values from -3 to 3
- energy_weight: float32 [2, 16], replicated, may hold values from -1.5 to 1.5
- message_weight: float32 [432, 12], replicated, may hold values from -0.3125 to 0.3125
Outputs:
- energies: float32 [4, 8], P('struct')
- position_grad: float32 [3, 4, 512], P(None, 'struct', 'edge')
- embedding_grad: float32 [2, 4], replicated
- channel_in_grad: float32 [2, 4, 12], replicated
- channel_mix_grad: float32 [2, 12, 12], replicated
- hidden_weight_grad: float32 [2, 432, 24], replicated
- hidden_bias_grad: float32 [2, 24], replicated
- inner_weight_grad: float32 [2, 24, 16], replicated
- inner_bias_grad: float32 [2, 16], replicated
- energy_weight_grad: float32 [2, 16], replicated
- message_weight_grad: float32 [432, 12], replicated
The draws below stay inside these ranges and needn't reach their ends.
Inputs may be any that keep to these rules, and one draw needn't show every extreme that they name: struct_id never falls along a group; each structure holds 1 to 256 atoms, and one structure of every group holds exactly 256. `senders`: indices into the atoms of the edge's own group; the sender lies in the same structure as the receiver. `receivers`: indices into the atoms of the edge's own group.
All inputs are finite; a program needn't handle non-finite values. No bound on the sum of `atom_mask` or of `edge_mask` on one device may be relied on, other than what follows from the above.
Results may differ from the reference program's by a relative error of at most 0.0003.
Values sent between devices are 32-bit elements; how exact they have to be, the bound alone decides.
A program may use at most 128 MiB of HBM per device.

```python
import jax
import jax.numpy as jnp
from jax import lax

SPECIES = 2
EMBED_WIDTH = 4
CHANNELS = 12
RADIALS = 6
COMPONENTS = 20
HIDDEN_ONE = 24
HIDDEN_TWO = 16
STRUCTS = 8
FEATURES = 432
GROUP_ATOMS = 512
GROUP_EDGES = 16384
GROUPS = 4
MOST_ATOMS = 256


def structure_lengths(key):

    def one_group(group_key):
        perm_key, move_key, big_key = jax.random.split(group_key, 3)
        others = STRUCTS - 1
        remaining = GROUP_ATOMS - MOST_ATOMS
        ranks = jax.random.permutation(perm_key, others)
        lengths = remaining // others + (ranks < remaining % others).astype(jnp.int32)
        couples = others // 2
        if couples > 0:
            left_side = lengths[0:2 * couples:2]
            right_side = lengths[1:2 * couples:2]
            ceiling = jnp.minimum(left_side - 1, MOST_ATOMS - right_side)
            moved = jax.random.randint(move_key, (couples,), 0, ceiling + 1)
            lengths = lengths.at[0:2 * couples:2].add(-moved).at[1:2 * couples:2].add(moved)
        slots = jnp.arange(STRUCTS, dtype=jnp.int32)
        biggest = jax.random.randint(big_key, (), 0, STRUCTS)
        source = jnp.clip(slots - (slots > biggest).astype(jnp.int32), 0, others - 1)
        return jnp.where(slots == biggest, MOST_ATOMS, jnp.take(lengths, source)).astype(jnp.int32)
    return jax.vmap(one_group)(jax.random.split(key, GROUPS))


def structure_layout(key):
    lengths = structure_lengths(key)
    endings = jnp.cumsum(lengths, axis=1)
    beginnings = endings - lengths
    atom_index = jnp.arange(GROUP_ATOMS, dtype=jnp.int32)
    labels = jnp.sum((atom_index[None, :, None] >= endings[:, None, :]).astype(jnp.int32), axis=2)
    return (lengths, beginnings, labels)


def edge_layout(key):
    lengths, beginnings, labels = structure_layout(key)
    recv_key = jax.random.fold_in(key, 101)
    send_key = jax.random.fold_in(key, 202)
    receiving = jax.random.randint(recv_key, (GROUPS, GROUP_EDGES), 0, GROUP_ATOMS)
    owner_struct = jnp.take_along_axis(labels, receiving, axis=1)
    extent = jnp.take_along_axis(lengths, owner_struct, axis=1)
    beginning = jnp.take_along_axis(beginnings, owner_struct, axis=1)
    stride = jax.random.randint(send_key, (GROUPS, GROUP_EDGES), 0, jnp.maximum(extent - 1, 1))
    sending = beginning + (receiving - beginning + 1 + stride) % extent
    return (sending.astype(jnp.int32), receiving.astype(jnp.int32))


def draw_struct_id(key, part):
    labels = structure_layout(key)[2]
    return labels


def draw_senders(key, part):
    sending = edge_layout(key)[0]
    return sending


def draw_receivers(key, part):
    receiving = edge_layout(key)[1]
    return receiving


def plant(values, rng, smallest, largest):
    longest = values.shape.index(max(values.shape))
    spots = []
    for shift in (0, 1):
        where = [jax.random.randint(jax.random.fold_in(rng, axis), (), 0, length) for axis, length in enumerate(values.shape)]
        where[longest] = (where[longest] + shift) % values.shape[longest]
        spots.append(tuple(where))
    return values.at[spots[0]].set(smallest).at[spots[1]].set(largest)


def level_of(stream_key, dims, cuts, least, top_value):
    gain = 1.0
    for dim, shards_of in cuts:
        draws = jax.random.uniform(jax.random.fold_in(jax.random.fold_in(stream_key, 6), dim), (shards_of,), jnp.float32, least / len(cuts), top_value / len(cuts))
        gain = gain * jnp.repeat(jnp.exp(draws), dims[dim] // shards_of).reshape((-1,) + (1,) * (len(dims) - 1 - dim))
    return gain


def bell_draw(rng, shape, scale, limit, cuts=(), kind=jnp.bfloat16):
    values = jax.random.normal(rng, shape, jnp.float32) * scale
    if len(cuts) > 0:
        values = level_of(rng, shape, cuts, -0.22, 0.18) * values
    return jnp.clip(values, min=-limit, max=limit).astype(kind)


def setup_inputs(seed: int = 0) -> dict:
    key_list = jax.random.split(jax.random.key(seed), 18)
    return {
        "positions": jnp.clip(3.0 * jax.random.uniform(key_list[0], (3, GROUPS, GROUP_ATOMS), jnp.float32) ** level_of(key_list[0], (3, GROUPS, GROUP_ATOMS), ((1, 4), (2, 8)), -0.2, 0.2), 0.0, 3.0),
        "species": plant(jax.random.randint(key_list[1], (GROUPS, GROUP_ATOMS), 0, SPECIES), jax.random.fold_in(key_list[1], 1), 0, SPECIES - 1).astype(jnp.int32),
        "struct_id": draw_struct_id(jax.random.fold_in(key_list[17], 71), 0),
        "atom_mask": plant((jax.random.randint(key_list[3], (GROUPS, GROUP_ATOMS), 0, 8) < 7).astype(jnp.int32), jax.random.fold_in(key_list[3], 1), 0, 1),
        "senders": draw_senders(jax.random.fold_in(key_list[17], 71), 0),
        "receivers": draw_receivers(jax.random.fold_in(key_list[17], 71), 0),
        "edge_mask": plant((jax.random.randint(key_list[6], (GROUPS, GROUP_EDGES), 0, 4) < 3).astype(jnp.int32), jax.random.fold_in(key_list[6], 1), 0, 1),
        "energy_cot": bell_draw(key_list[7], (GROUPS, STRUCTS), 1.0, 6.0, ((0, 4),), jnp.float32),
        "embedding": bell_draw(key_list[8], (SPECIES, EMBED_WIDTH), 1.0, 4.0, (), jnp.float32),
        "channel_in": bell_draw(key_list[9], (2, EMBED_WIDTH, CHANNELS), EMBED_WIDTH ** -0.5, 3.0, (), jnp.float32),
        "channel_mix": bell_draw(key_list[10], (2, CHANNELS, CHANNELS), CHANNELS ** -0.5, 1.75, (), jnp.float32),
        "hidden_weight": bell_draw(key_list[11], (2, FEATURES, HIDDEN_ONE), FEATURES ** -0.5, 0.3125, (), jnp.float32),
        "hidden_bias": bell_draw(key_list[12], (2, HIDDEN_ONE), 0.5, 3.0, (), jnp.float32),
        "inner_weight": bell_draw(key_list[13], (2, HIDDEN_ONE, HIDDEN_TWO), HIDDEN_ONE ** -0.5, 1.25, (), jnp.float32),
        "inner_bias": bell_draw(key_list[14], (2, HIDDEN_TWO), 0.5, 3.0, (), jnp.float32),
        "energy_weight": bell_draw(key_list[15], (2, HIDDEN_TWO), HIDDEN_TWO ** -0.5, 1.5, (), jnp.float32),
        "message_weight": bell_draw(key_list[16], (FEATURES, CHANNELS), FEATURES ** -0.5, 0.3125, (), jnp.float32),
    }


cutoff_radius = 6.0
variance_eps = 1e-05
pair_slots = [4, 5, 6, 5, 7, 8, 6, 8, 9]
triple_slots = [10, 11, 12, 11, 13, 14, 12, 14, 15, 11, 13, 14, 13, 16, 17, 14, 17, 18, 12, 14, 15, 14, 17, 18, 15, 18, 19]

def matmul(left, right):
    return jnp.dot(left, right, precision=lax.Precision.HIGHEST, preferred_element_type=jnp.float32)

def edge_basis(pos_send, pos_recv):
    vector = pos_recv - pos_send
    distance = jnp.sqrt(lax.optimization_barrier(jnp.sum(vector * vector, axis=0)) + 1.0)
    unit_x = vector[0] / distance
    unit_y = vector[1] / distance
    unit_z = vector[2] / distance
    scaled = distance / cutoff_radius
    envelope = (1.0 - scaled * scaled) * (1.0 - scaled * scaled)
    orders = jnp.arange(1, RADIALS + 1).astype(jnp.float32)[:, None]
    radial = jnp.sqrt(2.0 / cutoff_radius) * jnp.sin(orders * jnp.pi * scaled[None, :]) / distance[None, :] * envelope[None, :]
    constant = jnp.ones_like(unit_x)
    angular = jnp.stack([constant, unit_x, unit_y, unit_z, unit_x * unit_x, unit_x * unit_y, unit_x * unit_z, unit_y * unit_y, unit_y * unit_z, unit_z * unit_z, unit_x * unit_x * unit_x, unit_x * unit_x * unit_y, unit_x * unit_x * unit_z, unit_x * unit_y * unit_y, unit_x * unit_y * unit_z, unit_x * unit_z * unit_z, unit_y * unit_y * unit_y, unit_y * unit_y * unit_z, unit_y * unit_z * unit_z, unit_z * unit_z * unit_z], axis=0)
    product = radial[:, None, :] * angular[None, :, :]
    return product.reshape(RADIALS * COMPONENTS, -1).T

def outer_rows(weights, basis):
    return (weights[:, :, None] * basis[:, None, :]).reshape(basis.shape[0], -1)

def atom_features(abasis, mixing):
    atoms = abasis.shape[0]
    blocks = abasis.reshape(atoms, CHANNELS, RADIALS, COMPONENTS)
    scalar = blocks[..., 0]
    vector = blocks[..., 1:4]
    matrix = jnp.take(blocks, jnp.array(pair_slots, dtype=jnp.int32), axis=3).reshape(atoms, CHANNELS, RADIALS, 3, 3)
    cubic = jnp.take(blocks, jnp.array(triple_slots, dtype=jnp.int32), axis=3).reshape(atoms, CHANNELS, RADIALS, 3, 3, 3)
    first = lax.optimization_barrier(jnp.sum(vector * vector, axis=-1))
    second = lax.optimization_barrier(jnp.sum(matrix * matrix, axis=(-2, -1)))
    third = lax.optimization_barrier(jnp.sum(cubic * cubic, axis=(-3, -2, -1)))
    fourth = lax.optimization_barrier(jnp.sum(vector[..., :, None] * matrix * vector[..., None, :], axis=(-2, -1)))
    fifth = lax.optimization_barrier(jnp.sum(vector[..., :, None, None] * cubic * matrix[..., None, :, :], axis=(-3, -2, -1)))
    invariant = jnp.stack([scalar, first, second, third, fourth, fifth], axis=-1)
    mixed = jnp.einsum('acnp,cd->adnp', invariant, mixing, precision=lax.Precision.HIGHEST)
    return mixed.reshape(atoms, -1)

def readout(feats, total, squares, count, weight_a, bias_a, weight_b, bias_b, weight_c):
    mean = total / count
    spread = squares / count - mean * mean
    normed = (feats - mean[None, :]) * lax.rsqrt(spread[None, :] + variance_eps)
    hidden = jax.nn.silu(matmul(normed, weight_a) + bias_a[None, :])
    inner = jax.nn.silu(matmul(hidden, weight_b) + bias_b[None, :])
    return (matmul(inner, weight_c[:, None])[:, 0], normed)

def reference(positions, species, struct_id, atom_mask, senders, receivers, edge_mask, energy_cot, embedding, channel_in, channel_mix, hidden_weight, hidden_bias, inner_weight, inner_bias, energy_weight, message_weight):
    groups = species.shape[0]
    group = species.shape[1]
    atoms = groups * group
    offsets = (jnp.arange(groups, dtype=jnp.int32) * group)[:, None]
    sender_rows = (senders + offsets).reshape(-1)
    receiver_rows = (receivers + offsets).reshape(-1)
    live_edges = edge_mask.reshape(-1).astype(jnp.float32)
    live_atoms = atom_mask.reshape(-1).astype(jnp.float32)
    kinds = (species.reshape(-1)[:, None] == jnp.arange(SPECIES, dtype=jnp.int32)[None, :]).astype(jnp.float32)
    send_kind = kinds[sender_rows]
    structure_rows = (struct_id + (jnp.arange(groups, dtype=jnp.int32) * STRUCTS)[:, None]).reshape(-1)
    count = jnp.maximum(jnp.sum(live_atoms), 1.0)

    def layer_sum(weights, basis):
        weighted = outer_rows(weights * live_edges[:, None], basis)
        return jax.ops.segment_sum(weighted, receiver_rows, num_segments=atoms)

    def statistics(feats):
        return (lax.optimization_barrier(jnp.sum(live_atoms[:, None] * feats, axis=0)), lax.optimization_barrier(jnp.sum(live_atoms[:, None] * feats * feats, axis=0)))

    def forward(coords, embed_table, chan_table, mix_table, weight_a, bias_a, weight_b, bias_b, weight_c, message_table):
        flat = coords.reshape(3, atoms)
        basis = edge_basis(flat[:, sender_rows], flat[:, receiver_rows])
        weights_zero = matmul(send_kind, matmul(embed_table, chan_table[0]))
        feats_zero = atom_features(layer_sum(weights_zero, basis), mix_table[0])
        total_zero, squares_zero = statistics(feats_zero)
        energy_zero, normed_zero = readout(feats_zero, total_zero, squares_zero, count, weight_a[0], bias_a[0], weight_b[0], bias_b[0], weight_c[0])
        message = matmul(normed_zero, message_table)
        weights_one = matmul(send_kind, matmul(embed_table, chan_table[1])) + message[sender_rows]
        feats_one = atom_features(layer_sum(weights_one, basis), mix_table[1])
        total_one, squares_one = statistics(feats_one)
        energy_one, normed_one = readout(feats_one, total_one, squares_one, count, weight_a[1], bias_a[1], weight_b[1], bias_b[1], weight_c[1])
        atom_energy = live_atoms * (energy_zero + energy_one)
        return jax.ops.segment_sum(atom_energy, structure_rows, num_segments=groups * STRUCTS).reshape(groups, STRUCTS)
    energies, pullback = jax.vjp(forward, positions, embedding, channel_in, channel_mix, hidden_weight, hidden_bias, inner_weight, inner_bias, energy_weight, message_weight)
    grads = pullback(energy_cot)
    return (energies, grads[0], grads[1], grads[2], grads[3], grads[4], grads[5], grads[6], grads[7], grads[8], grads[9])
```

```python
import functools
import math

import jax
import jax.numpy as jnp
import numpy as np
from jax import lax
from jax.experimental import pallas as pl
from jax.experimental.pallas import tpu as pltpu
from jax.sharding import PartitionSpec as P

CHANNELS = 12
PADDED = 16
RADIALS = 6
PAIRS = 3
STRUCTS = 8
HIDDEN = 24
INNER = 16
FEATURES = 432
HEAD_ROWS = 40
FEATURE_ROWS = 256
ONES_ROW = 216
BLOCK = 64

cutoff_radius = 6.0
variance_eps = 1e-05
center = 1.5

MESH = pl.DeviceIdType.MESH
F32 = jnp.float32
I32 = jnp.int32
NN = ((1,), (0,))
NT = ((1,), (1,))
TN = ((0,), (0,))

MONOMIALS = sorted(
    [(a, b, c) for a in range(4) for b in range(4) for c in range(4) if a + b + c <= 3],
    key=lambda m: (sum(m), -m[0], -m[1], -m[2]),
)
PLACE = {m: i for i, m in enumerate(MONOMIALS)}
COUNTS = [1, 4, 10, 20]
OFFSETS = [0, 1, 5, 15]
SHELLS = 35


def fitted(function, low, high, degree):
    series = np.polynomial.chebyshev.Chebyshev.interpolate(
        lambda w: function(0.5 * (high - low) * w + 0.5 * (high + low)), degree
    )
    return [float(v) for v in series.convert(kind=np.polynomial.Polynomial).coef]


LOW, HIGH = 0.9, 28.1
ANGLE = math.pi / cutoff_radius
SINE = fitted(lambda u: np.sin(ANGLE * np.sqrt(u)) / np.sqrt(u), LOW, HIGH, 9)
COSINE = fitted(lambda u: np.cos(ANGLE * np.sqrt(u)), LOW, HIGH, 9)
NORM = math.sqrt(2.0 / cutoff_radius)


def mm(left, right, kind=NN):
    return lax.dot_general(
        left, right, (kind, ((), ())), precision=lax.Precision.HIGHEST, preferred_element_type=F32
    )


def iota(shape, dim):
    return lax.broadcasted_iota(I32, shape, dim)


def horner(coefficients, w):
    total = jnp.full_like(w, coefficients[-1])
    for value in coefficients[-2::-1]:
        total = total * w + value
    return total


def shifted(terms, order, x, y, z):
    current = terms
    for axis, value in enumerate((x, y, z)):
        two, three = 2.0 * value, 3.0 * value
        square = value * value
        three_square, cube = 3.0 * square, square * value
        factors = [None, [value], [square, two], [cube, three_square, three]]
        fresh = {}
        for m in MONOMIALS[: COUNTS[order]]:
            if axis == 2 and sum(m) != order:
                continue
            power = m[axis]
            total = current[m]
            for lower in range(power):
                source = m[:axis] + (lower,) + m[axis + 1 :]
                total = total + factors[power][lower] * current[source]
            fresh[m] = total
        current = fresh
    return current


def invariants(terms, x, y, z):
    by_order = []
    for order in range(4):
        own = {m: terms[OFFSETS[order] + i] for i, m in enumerate(MONOMIALS[: COUNTS[order]])}
        by_order.append(shifted(own, order, x, y, z) if order else own)
    scalar = by_order[0][(0, 0, 0)]
    vx, vy, vz = by_order[1][(1, 0, 0)], by_order[1][(0, 1, 0)], by_order[1][(0, 0, 1)]
    m = by_order[2]
    xx, xy, xz = m[(2, 0, 0)], m[(1, 1, 0)], m[(1, 0, 1)]
    yy, yz, zz = m[(0, 2, 0)], m[(0, 1, 1)], m[(0, 0, 2)]
    q = by_order[3]
    xxx, yyy, zzz = q[(3, 0, 0)], q[(0, 3, 0)], q[(0, 0, 3)]
    xxy, xxz, xyy = q[(2, 1, 0)], q[(2, 0, 1)], q[(1, 2, 0)]
    xyz, xzz, yyz, yzz = q[(1, 1, 1)], q[(1, 0, 2)], q[(0, 2, 1)], q[(0, 1, 2)]
    first = vx * vx + vy * vy + vz * vz
    second = xx * xx + yy * yy + zz * zz + 2.0 * (xy * xy + xz * xz + yz * yz)
    third = (
        xxx * xxx
        + yyy * yyy
        + zzz * zzz
        + 3.0 * (xxy * xxy + xxz * xxz + xyy * xyy + xzz * xzz + yyz * yyz + yzz * yzz)
        + 6.0 * (xyz * xyz)
    )
    fourth = (
        vx * (xx * vx + xy * vy + xz * vz)
        + vy * (xy * vx + yy * vy + yz * vz)
        + vz * (xz * vx + yz * vy + zz * vz)
    )
    xy2, xz2, yz2 = 2.0 * xy, 2.0 * xz, 2.0 * yz
    fifth = (
        vx * (xxx * xx + xyy * yy + xzz * zz + xxy * xy2 + xxz * xz2 + xyz * yz2)
        + vy * (xxy * xx + yyy * yy + yzz * zz + xyy * xy2 + xyz * xz2 + yyz * yz2)
        + vz * (xxz * xx + yyz * yy + zzz * zz + xyz * xy2 + xzz * xz2 + yzz * yz2)
    )
    return (scalar, first, second, third, fourth, fifth)


def silu_pair(v):
    gate = 1.0 / (1.0 + jnp.exp(-v))
    return v * gate, gate * (1.0 + v * (1.0 - gate))


class Geometry:
    def __init__(self, columns, own, lane_low):
        dx = own[2:3] + columns[:, 2:3]
        dy = own[3:4] + columns[:, 3:4]
        dz = own[4:5] + columns[:, 4:5]
        self.u = dx * dx + dy * dy + dz * dz + 1.0
        w = (self.u - 0.5 * (LOW + HIGH)) * (2.0 / (HIGH - LOW))
        self.sine = horner(SINE, w)
        self.cosine = horner(COSINE, w)
        self.inverse = lax.rsqrt(self.u)
        self.reach = 1.0 - self.u * (1.0 / (cutoff_radius * cutoff_radius))
        self.lane_low = lane_low

    def sines(self):
        step = 2.0 * (2.0 * self.cosine * self.cosine - 1.0)
        before = jnp.where(self.lane_low, -self.sine, 0.0)
        now = jnp.where(self.lane_low, self.sine, 2.0 * self.cosine * self.sine)
        return self.series(step, before, now)

    def cosines(self):
        double = 2.0 * self.cosine * self.cosine - 1.0
        before = jnp.where(self.lane_low, self.cosine, 1.0)
        now = jnp.where(self.lane_low, self.cosine, double)
        return self.series(2.0 * double, before, now)

    def series(self, step, before, now):
        out = [now]
        for _ in range(PAIRS - 1):
            before, now = now, step * now - before
            out.append(now)
        return out


def body(lanes, structs, *refs):
    (
        positions,
        species,
        struct_id,
        atom_mask,
        senders,
        receivers,
        edge_mask,
        energy_cot,
        embedding,
        channel_in,
        channel_mix,
        hidden_weight,
        hidden_bias,
        inner_weight,
        inner_bias,
        energy_weight,
        message_weight,
        energies_out,
        position_out,
        embedding_out,
        channel_in_out,
        channel_mix_out,
        hidden_weight_out,
        hidden_bias_out,
        inner_weight_out,
        inner_bias_out,
        energy_weight_out,
        message_weight_out,
        pack,
        pack_all,
        send_all,
        masked_recv,
        recv_all,
        counts,
        pair_weight,
        columns,
        sender_rows,
        radial,
        inverse,
        planes,
        weights,
        products,
        sums,
        dsums,
        dplanes,
        dproducts,
        invariant,
        dinvariant,
        feats,
        normed,
        select,
        head,
        head_t,
        stat_own,
        stat_all,
        message_own,
        message_all,
        dmessage_own,
        dmessage_all,
        force_own,
        force_all,
        final_own,
        final_all,
        early_own,
        early_all,
        early_sum,
        late_own,
        late_all,
        late_sum,
        send_sem,
        recv_sem,
    ) = refs
    devices = lanes * structs
    edge_count = senders.shape[1]
    group = pair_weight.shape[0]
    tiles = group // 128
    strips = [slice(k, k + 512) for k in range(0, group, 512)]
    row = lax.axis_index("struct")
    col = lax.axis_index("edge")
    me = row * lanes + col

    def everyone(action):
        def one(k, carry):
            target = lax.rem(me + k, devices)
            action((target // lanes, lax.rem(target, lanes)), target)
            return carry

        if devices <= 32:
            for k in range(1, devices):
                one(k, 0)
        else:
            lax.fori_loop(1, devices, one, 0)

    def members(action):
        def one(k, carry):
            target = lax.rem(col + k, lanes)
            action((row, target), target)
            return carry

        if lanes <= 8:
            for k in range(1, lanes):
                one(k, 0)
        else:
            lax.fori_loop(1, lanes, one, 0)

    def push(phase, source, target, device):
        pltpu.make_async_remote_copy(
            src_ref=source,
            dst_ref=target,
            send_sem=send_sem.at[phase],
            recv_sem=recv_sem.at[phase],
            device_id=device,
            device_id_type=MESH,
        ).start()

    def await_bytes(buffer, count, sem):
        if count:
            view = buffer.at[pl.ds(0, count)]
            pltpu.make_async_copy(view, view, sem).wait()

    barrier = pltpu.get_barrier_semaphore()
    everyone(
        lambda device, _: pl.semaphore_signal(
            barrier, inc=1, device_id=device, device_id_type=MESH
        )
    )

    pack[...] = jnp.ones_like(pack)
    masked_recv[...] = jnp.where(edge_mask[...] > 0, receivers[...], -1)
    kind = species[...]
    for half in (0, BLOCK):
        spot = pl.ds(half, BLOCK)
        pack[0:1, spot] = (kind == 0).astype(F32)
        pack[1:2, spot] = (kind == 1).astype(F32)
        for axis in range(3):
            pack[2 + axis : 3 + axis, spot] = center - positions[axis]
        pack[6:7, spot] = atom_mask[...].astype(F32)
        pack[7:8, spot] = struct_id[...].astype(F32)
    pl.semaphore_wait(barrier, devices - 1)

    members(lambda device, _: push(0, pack, pack_all.at[col], device))
    members(lambda device, _: push(1, senders, send_all.at[col], device))
    members(lambda device, _: push(2, masked_recv, recv_all.at[col], device))
    pack_all[col] = pack[...]
    send_all[col] = senders[...]
    recv_all[col] = masked_recv[...]

    lane = iota((8, 128), 1)
    low_row = lane[0:1] < BLOCK
    low = lane < BLOCK
    row8 = iota((8, 128), 0)
    own = pack[...] * jnp.where((row8 >= 2) & (row8 <= 4), -1.0, 1.0)
    live = own[6:7]
    half_pick = ((iota((2, 128), 1) >= BLOCK).astype(I32) == iota((2, 128), 0)).astype(F32)
    half_sum = ((row8 == 0) & low | (row8 == 1) & ~low).astype(F32)
    half_sum_late = ((row8 == 2) & low | (row8 == 3) & ~low).astype(F32)

    for parity in range(2):
        k = iota((FEATURE_ROWS, FEATURES), 0)
        pair = (k >= 72).astype(I32) + (k >= 144).astype(I32)
        rest = k - 72 * pair
        kind_of = (rest * 5462) >> 16
        channel = rest - 12 * kind_of
        place = channel * 36 + (2 * pair + parity) * 6 + kind_of
        hit = (place == iota((FEATURE_ROWS, FEATURES), 1)) & (k < ONES_ROW)
        select[parity] = hit.astype(F32)
    bias_spot = (iota((2, FEATURE_ROWS), 1) == ONES_ROW) & (
        iota((2, FEATURE_ROWS), 0) == 0
    )
    bias_cols, inner_cols, energy_cols = [], [], []
    head[...] = jnp.zeros_like(head)
    for layer in range(2):
        for parity in range(2):
            base = HEAD_ROWS * parity
            block = mm(hidden_weight[layer], select[parity], NT)
            if parity == 0:
                spot = bias_spot.astype(F32)
                if layer == 1:
                    spot = (
                        (iota((2, FEATURE_ROWS), 1) == ONES_ROW)
                        & (iota((2, FEATURE_ROWS), 0) == 1)
                    ).astype(F32)
                block = block + mm(hidden_bias[...], spot, TN)
            head[layer, base : base + HIDDEN, :] = block
            if layer == 0:
                head[0, base + HIDDEN : base + HIDDEN + CHANNELS, :] = mm(
                    message_weight[...], select[parity], NT
                )
        head_t[layer] = jnp.transpose(head[layer])
        pick = (iota((2, 128), 0) == layer).astype(F32)
        inner_cols.append(mm(inner_bias[...], pick, TN))
        energy_cols.append(mm(energy_weight[...], pick, TN))

    mix_pd = (iota((72, CHANNELS), 0) - 12 * ((iota((72, CHANNELS), 0) * 5462) >> 16)) == iota(
        (72, CHANNELS), 1
    )
    mix_pd = mix_pd.astype(F32)
    mix_pc = ((iota((96, CHANNELS), 0) & 15) == iota((96, CHANNELS), 1)).astype(F32)
    same = ((iota((96, 72), 0) >> 4) == ((iota((96, 72), 1) * 5462) >> 16)).astype(F32)
    same_t = ((iota((72, 96), 1) >> 4) == ((iota((72, 96), 0) * 5462) >> 16)).astype(F32)
    mixers, mixers_t = [], []
    for layer in range(2):
        table = channel_mix[:, layer, :]
        spread_c = mm(mix_pc, table)
        mixers_t.append(mm(spread_c, mix_pd, NT) * same)
        spread_d = mm(mix_pd, table, NT)
        mixers.append(mm(spread_d, mix_pc, NT) * same_t)

    struct_rows = own[7:8].astype(I32)
    member = (struct_rows == iota((STRUCTS, 128), 0)).astype(F32)
    atom_cot = mm(energy_cot[...], member) * live
    seat = ((iota((128, 128), 0) - 96) == struct_rows).astype(F32)

    await_bytes(pack_all, lanes - 1, recv_sem.at[0])
    for q in range(tiles):
        sender_rows[:, 128 * q : 128 * (q + 1)] = jnp.where(low, pack_all[2 * q], pack_all[2 * q + 1])
    columns[...] = jnp.transpose(sender_rows[...])

    def geometry(start):
        cols = columns[pl.ds(start, BLOCK), :]
        return Geometry(cols, own, low_row)

    def radial_block(i, carry):
        start = pl.multiple_of(i * BLOCK, BLOCK)
        geo = geometry(start)
        envelope = geo.reach * geo.reach * NORM
        for pair, value in enumerate(geo.sines()):
            radial[pair, pl.ds(start, BLOCK), :] = value * envelope
        inverse[pl.ds(start, BLOCK), :] = geo.inverse
        return carry

    lax.fori_loop(0, group // BLOCK, radial_block, 0)

    def monomial_rows(rows):
        x, y, z = rows[2:3], rows[3:4], rows[4:5]
        table = {(0, 0, 0): None}
        for m in MONOMIALS[1:]:
            axis = next(i for i in range(3) if m[i])
            lower = m[:axis] + (m[axis] - 1,) + m[axis + 1 :]
            factor = (x, y, z)[axis]
            table[m] = factor if table[lower] is None else table[lower] * factor
        return table

    def spread(layer):
        def one(q, carry):
            spot = pl.ds(pl.multiple_of(q * 128, 128), 128)
            table = monomial_rows(sender_rows[:, spot])
            h = weights[layer, :, spot]
            for i, m in enumerate(MONOMIALS):
                products[layer, PADDED * i : PADDED * (i + 1), spot] = (
                    h if table[m] is None else h * table[m]
                )
            return carry

        lax.fori_loop(0, tiles, one, 0)

    weights[...] = jnp.zeros_like(weights)
    for layer in range(2):
        embedded = mm(embedding[...], sender_rows[0:2, :], TN)
        weights[layer, 0:CHANNELS, :] = mm(channel_in[layer], embedded, TN)
    spread(0)

    await_bytes(send_all, lanes - 1, recv_sem.at[1])
    await_bytes(recv_all, lanes - 1, recv_sem.at[2])
    counts[...] = jnp.zeros_like(counts)
    chunk = min(512, edge_count)
    per_slot = edge_count // chunk
    wide = counts.shape[1]

    def count_block(i, carry):
        slot = i // per_slot
        spot = pl.ds(pl.multiple_of(lax.rem(i, per_slot) * chunk, chunk), chunk)
        send = send_all[slot, :, spot]
        local = recv_all[slot, :, spot] - col * BLOCK
        inside = (local >= 0) & (local < BLOCK)
        key = jnp.where(inside, (send >> 8) * BLOCK + local, -1)
        sender_hot = (iota((256, chunk), 0) == (send & 255)).astype(F32).astype(jnp.bfloat16)
        pair_hot = (iota((wide, chunk), 0) == key).astype(F32).astype(jnp.bfloat16)
        counts[...] += lax.dot_general(
            sender_hot, pair_hot, (NT, ((), ())), preferred_element_type=F32
        )
        return carry

    lax.fori_loop(0, lanes * per_slot, count_block, 0)
    low_tall = iota((256, 128), 1) < BLOCK
    for block in range(group // 256):
        piece = counts[:, 128 * (block // 2) : 128 * (block // 2 + 1)]
        turned = pltpu.roll(piece, BLOCK, 1)
        both = jnp.where(low_tall, piece, turned) if block % 2 == 0 else jnp.where(low_tall, turned, piece)
        pair_weight[256 * block : 256 * (block + 1), :] = both

    def plane_block(i, carry):
        spot = pl.ds(pl.multiple_of(i * BLOCK, BLOCK), BLOCK)
        weight = pair_weight[spot, :]
        step = inverse[spot, :]
        for pair in range(PAIRS):
            value = radial[pair, spot, :] * weight
            for order in range(4):
                planes[order, spot, 128 * pair : 128 * (pair + 1)] = value
                value = value * step
        return carry

    lax.fori_loop(0, group // BLOCK, plane_block, 0)

    xi, yi, zi = (jnp.broadcast_to(own[r : r + 1], (8, 128)) for r in (2, 3, 4))

    def chunk_spots(i):
        pair, tile = i // 2, lax.rem(i, 2)
        return pair, pl.multiple_of(tile * 8, 8), pl.ds(pl.multiple_of(pair * 128, 128), 128)

    def forward(layer):
        for order in range(4):
            rows = PADDED * COUNTS[order]
            start = PADDED * OFFSETS[order]
            sums[layer, start : start + rows, :] = mm(products[layer, 0:rows, :], planes[order])

        def one(i, carry):
            pair, tile, spot = chunk_spots(i)
            terms = [sums[layer, pl.ds(PADDED * m + tile, 8), spot] for m in range(SHELLS)]
            for p, value in enumerate(invariants(terms, xi, yi, zi)):
                invariant[layer, pair, pl.ds(PADDED * p + tile, 8), :] = value
            return carry

        lax.fori_loop(0, 2 * PAIRS, one, 0)
        for pair in range(PAIRS):
            feats[layer, 72 * pair : 72 * (pair + 1), :] = mm(mixers[layer], invariant[layer, pair])

    def send_stats(phase, index, first, second, extra=None):
        both = mm(first[0], first[1], NT) + mm(second[0], second[1], NT)
        stat_own[index, 0:4, :] = both[0:4, 0:128]
        tail = both[0:4, 128:256]
        if extra is not None:
            tail = tail + extra
        stat_own[index, 4:8, :] = tail
        everyone(
            lambda device, _: push(phase, stat_own.at[index], stat_all.at[index, me], device)
        )
        stat_all[index, me] = stat_own[index]

    def get_stats(phase, index):
        await_bytes(stat_all.at[index], devices - 1, recv_sem.at[phase])
        total = stat_all[index, 0]
        for k in range(1, devices):
            total = total + stat_all[index, k]
        return jnp.concatenate([total[0:4], total[4:8]], axis=1)

    ones_rows = iota((FEATURE_ROWS - ONES_ROW, 128), 0) == 0
    for layer in range(2):
        feats[layer, ONES_ROW:FEATURE_ROWS, :] = ones_rows.astype(F32)
        normed[layer, ONES_ROW:FEATURE_ROWS, :] = ones_rows.astype(F32)

    def send_moments(layer, phase):
        values = feats[layer]
        send_stats(phase, layer, (half_sum * live, values), (half_sum_late * live, values * values))

    def normalise(layer, phase):
        both = get_stats(phase, layer)
        count = jnp.maximum(both[0:1, ONES_ROW : ONES_ROW + 1], 1.0)
        mean = both[0:2] / count
        spread_of = both[2:4] / count - mean * mean
        scale = lax.rsqrt(spread_of + variance_eps)
        mean_wide = mm(mean, half_pick, TN)
        scale_wide = mm(scale, half_pick, TN)
        normed[layer, 0:ONES_ROW, :] = (feats[layer, 0:ONES_ROW, :] - mean_wide[0:ONES_ROW]) * scale_wide[
            0:ONES_ROW
        ]
        joined = mm(head[layer], normed[layer])
        chosen = jnp.where(low_row, joined[0:HEAD_ROWS], joined[HEAD_ROWS:])
        return chosen + pltpu.roll(chosen, BLOCK, 1), scale_wide, count

    def run_head(layer, pre):
        hidden, hidden_slope = silu_pair(pre[0:HIDDEN])
        inner_pre = mm(inner_weight[layer], hidden) + inner_cols[layer]
        inner, inner_slope = silu_pair(inner_pre)
        energy = jnp.sum(energy_cols[layer] * inner, axis=0, keepdims=True)
        dinner = energy_cols[layer] * atom_cot * inner_slope
        dhidden = mm(inner_weight[layer], dinner, TN) * hidden_slope
        left = jnp.concatenate([dinner, atom_cot * inner], axis=0)
        blank = jnp.zeros((128 - 32 - 32 * layer, 128), F32)
        right = [hidden, (iota((8, 128), 0) == 0).astype(F32), blank]
        if layer == 1:
            right = [jnp.zeros((32, 128), F32)] + right
        small = mm(jnp.where(low_row, left, 0.0), jnp.concatenate(right, axis=0), NT)
        return energy, dhidden, small

    def halves(value):
        return jnp.where(low_row, value, 0.0), jnp.where(low_row, 0.0, value)

    forward(0)
    send_moments(0, 3)
    pre_zero, scale_zero, count = None, None, None
    pre_zero, scale_zero, count = normalise(0, 3)
    message = pre_zero[HIDDEN:HEAD_ROWS]
    message_own[...] = jnp.where(low, message[0:8], message[8:16])
    members(lambda device, _: push(4, message_own, message_all.at[col], device))
    message_all[col] = message_own[...]
    energy_zero, dhidden_zero, small_zero = run_head(0, pre_zero)
    await_bytes(message_all, lanes - 1, recv_sem.at[4])
    for q in range(tiles):
        even, odd = message_all[2 * q], message_all[2 * q + 1]
        spot = slice(128 * q, 128 * (q + 1))
        weights[1, 0:8, spot] += jnp.where(low, even, pltpu.roll(odd, BLOCK, 1))
        weights[1, 8:16, spot] += jnp.where(low, pltpu.roll(even, BLOCK, 1), odd)

    spread(1)
    forward(1)
    send_moments(1, 5)
    pre_one, scale_one, _ = normalise(1, 5)
    energy_one, dhidden_one, small_one = run_head(1, pre_one)
    d_low, d_high = halves(dhidden_one)
    gap = jnp.zeros((HEAD_ROWS - HIDDEN, 128), F32)
    dhead_one = jnp.concatenate([d_low, gap, d_high, gap], axis=0)
    dnormed_one = mm(head_t[1], dhead_one)
    energy_row = jnp.where(low_row, live * (energy_zero + energy_one), 0.0)
    energy_tail = mm(
        jnp.where(iota((8, 128), 0) == 0, energy_row, 0.0), seat, NT
    )[0:4]
    send_stats(
        6,
        2,
        (half_sum, dnormed_one),
        (half_sum_late, dnormed_one * normed[1]),
        energy_tail,
    )

    d_low, d_high = halves(dhidden_zero)
    dhead_zero = jnp.concatenate([d_low, d_high], axis=0)
    d_low, d_high = halves(dhidden_one)
    dhead_both = [dhead_zero, jnp.concatenate([d_low, d_high], axis=0)]
    for layer in range(2):
        block = mm(dhead_both[layer], normed[layer], NT)
        for r in range(6):
            for half in range(2):
                early_own[12 * layer + 2 * r + half] = block[
                    8 * r : 8 * (r + 1), 128 * half : 128 * (half + 1)
                ]
    small = small_zero + small_one
    for r in range(4):
        early_own[24 + r] = small[8 * r : 8 * (r + 1)]
    early = early_own.shape[0]
    late = late_own.shape[0]
    late_base = devices - late

    def scatter_tiles(phase, source, target, count_of, base):
        for t in range(count_of):

            @pl.when(me != base + t)
            def _():
                there = base + t
                push(phase, source.at[t], target.at[me], (there // lanes, there % lanes))

            @pl.when(me == base + t)
            def _():
                target[me] = source[t]

    def share_tiles(phase, parts, result, count_of, base):
        @pl.when((me >= base) & (me < base + count_of))
        def _():
            await_bytes(parts, devices - 1, recv_sem.at[phase])
            total = parts[0]
            for k in range(1, devices):
                total = total + parts[k]
            result[me - base] = total
            everyone(
                lambda device, _: push(phase + 1, result.at[me - base], result.at[me - base], device)
            )

    def mine(base, count_of):
        return (me >= base) & (me < base + count_of)

    def gather_tiles(phase, result, count_of, base):
        @pl.when(mine(base, count_of))
        def _():
            await_bytes(result, count_of - 1, recv_sem.at[phase + 1])

        @pl.when(jnp.logical_not(mine(base, count_of)))
        def _():
            await_bytes(result, count_of, recv_sem.at[phase + 1])

    def drain_tiles(phase, parts, result, count_of, base):
        @pl.when(mine(base, count_of))
        def _():
            await_bytes(result, count_of - 1, send_sem.at[phase])
            await_bytes(parts, devices - 1, send_sem.at[phase + 1])

        @pl.when(jnp.logical_not(mine(base, count_of)))
        def _():
            await_bytes(result, count_of, send_sem.at[phase])

    def feature_back(layer, phase, index, dnormed, scale_wide):
        both = get_stats(phase, index)
        first = mm(both[0:2] / count, half_pick, TN)
        second = mm(both[2:4] / count, half_pick, TN)
        dfeats = scale_wide * (dnormed - live * (first + second * normed[layer]))
        products_of = jnp.zeros((96, 72), F32)
        for pair in range(PAIRS):
            piece = dfeats[72 * pair : 72 * (pair + 1)]
            dinvariant[pair] = mm(mixers_t[layer], piece)
            products_of = products_of + mm(invariant[layer, pair], piece, NT)
        return products_of * same, both

    def shell_back(layer):
        def one(i, carry):
            pair, tile, spot = chunk_spots(i)
            terms = [sums[layer, pl.ds(PADDED * m + tile, 8), spot] for m in range(SHELLS)]
            cots = tuple(dinvariant[pair, pl.ds(PADDED * p + tile, 8), :] for p in range(6))
            _, pull = jax.vjp(invariants, terms, xi, yi, zi)
            dterms, dx, dy, dz = pull(cots)
            for m in range(SHELLS):
                dsums[layer, pl.ds(PADDED * m + tile, 8), spot] = dterms[m]
            return (carry[0] + dx, carry[1] + dy, carry[2] + dz)

        blank = jnp.zeros((8, 128), F32)
        return lax.fori_loop(0, 2 * PAIRS, one, (blank, blank, blank))

    def product_back(layer):
        for order in (3, 2, 1, 0):
            rows = PADDED * COUNTS[order]
            start = PADDED * OFFSETS[order]
            for spot in strips:
                block = mm(dsums[layer, start : start + rows, :], planes[order, spot, :], NT)
                if order == 3:
                    dproducts[:, spot] = block
                else:
                    dproducts[0:rows, spot] += block

    def weight_back():
        out = []
        for q in range(tiles):
            spot = slice(128 * q, 128 * (q + 1))
            table = monomial_rows(sender_rows[:, spot])
            total = dproducts[0:PADDED, spot]
            for i, m in enumerate(MONOMIALS[1:], 1):
                total = total + table[m] * dproducts[PADDED * i : PADDED * (i + 1), spot]
            out.append(total)
        return out

    def coordinate_back(layer):
        out = []
        for q in range(tiles):
            spot = slice(128 * q, 128 * (q + 1))
            table = monomial_rows(sender_rows[:, spot])
            h = weights[layer, :, spot]
            parts = []
            for axis in range(3):
                total = None
                for i, m in enumerate(MONOMIALS):
                    if not m[axis]:
                        continue
                    lower = table[m[:axis] + (m[axis] - 1,) + m[axis + 1 :]]
                    term = dproducts[PADDED * i : PADDED * (i + 1), spot]
                    if lower is not None:
                        term = (float(m[axis]) * lower) * term
                    total = term if total is None else total + term
                parts.append(jnp.sum(h * total, axis=0, keepdims=True))
            out.append(parts)
        return out

    def plane_back(layer, first):
        for order in range(4):
            rows = PADDED * COUNTS[order]
            start = PADDED * OFFSETS[order]
            for spot in strips:
                block = mm(products[layer, 0:rows, spot], dsums[layer, start : start + rows, :], TN)
                if first:
                    dplanes[order, spot, :] = block
                else:
                    dplanes[order, spot, :] += block

    mix_one, both_back = feature_back(1, 6, 2, dnormed_one, scale_one)
    scatter_tiles(11, early_own, early_all, early, 0)
    group_energy = stat_all[2, row * lanes, 4:5, 96 : 96 + STRUCTS]
    for k in range(1, lanes):
        group_energy = group_energy + stat_all[2, row * lanes + k, 4:5, 96 : 96 + STRUCTS]
    energies_out[...] = group_energy
    moved_one = shell_back(1)
    product_back(1)
    dweights_one = weight_back()
    for q in range(tiles):
        top, bottom = dweights_one[q][0:8], dweights_one[q][8:16]
        dmessage_own[2 * q] = jnp.where(low, top, pltpu.roll(bottom, BLOCK, 1))
        dmessage_own[2 * q + 1] = jnp.where(low, pltpu.roll(top, BLOCK, 1), bottom)
    members(
        lambda device, target: push(7, dmessage_own.at[target], dmessage_all.at[col], device)
    )
    dmessage_all[col] = dmessage_own[col]
    kinds_of = sender_rows[...]
    dtable_one = jnp.zeros((PADDED, 8), F32)
    for q in range(tiles):
        dtable_one = dtable_one + mm(dweights_one[q], kinds_of[:, 128 * q : 128 * (q + 1)], NT)
    slopes_one = coordinate_back(1)
    share_tiles(11, early_all, early_sum, early, 0)
    await_bytes(dmessage_all, lanes - 1, recv_sem.at[7])
    arrived = dmessage_all[0]
    for k in range(1, lanes):
        arrived = arrived + dmessage_all[k]
    turned = pltpu.roll(arrived, BLOCK, 1)
    dmessage = jnp.concatenate([jnp.where(low, arrived, turned), jnp.where(low, turned, arrived)], axis=0)

    h_low, h_high = halves(dhidden_zero)
    m_low, m_high = halves(dmessage)
    dnormed_zero = mm(head_t[0], jnp.concatenate([h_low, m_low, h_high, m_high], axis=0))
    send_stats(
        8, 3, (half_sum, dnormed_zero), (half_sum_late, dnormed_zero * normed[0])
    )
    dmessage_weight = mm(jnp.concatenate([m_low, m_high], axis=0), normed[0], NT)
    for r in range(4):
        for half in range(2):
            late_own[2 * r + half] = dmessage_weight[
                8 * r : 8 * (r + 1), 128 * half : 128 * (half + 1)
            ]
    plane_back(1, True)
    mix_zero, _ = feature_back(0, 8, 3, dnormed_zero, scale_zero)
    scatter_tiles(13, late_own, late_all, late, late_base)
    moved_zero = shell_back(0)
    product_back(0)
    dweights_zero = weight_back()
    dtable_zero = jnp.zeros((PADDED, 8), F32)
    for q in range(tiles):
        dtable_zero = dtable_zero + mm(dweights_zero[q], kinds_of[:, 128 * q : 128 * (q + 1)], NT)
    slopes_zero = coordinate_back(0)

    fold_c = (iota((PADDED, 96), 0) == (iota((PADDED, 96), 1) & 15)).astype(F32)
    d_of = iota((72, 128), 0) - 12 * ((iota((72, 128), 0) * 5462) >> 16)
    seat_mix = [(iota((72, 128), 1) == d_of + 12 * layer).astype(F32) for layer in range(2)]
    seat_kind = [
        ((iota((8, 128), 1) == row8 + 24 + 2 * layer) & (row8 < 2)).astype(F32)
        for layer in range(2)
    ]
    final = mm(mm(fold_c, mix_zero), seat_mix[0]) + mm(mm(fold_c, mix_one), seat_mix[1])
    final = final + mm(dtable_zero, seat_kind[0]) + mm(dtable_one, seat_kind[1])
    final_own[...] = final[0:8] + pltpu.roll(final[8:16], 32, 1)
    everyone(lambda device, _: push(10, final_own, final_all.at[me], device))
    final_all[me] = final_own[...]
    share_tiles(13, late_all, late_sum, late, late_base)

    plane_back(0, False)
    turn = ANGLE * (2.0 * PAIRS - 5.0 + (iota((1, 128), 1) >= BLOCK).astype(F32))

    def slope_block(i, carry):
        start = pl.multiple_of(i * BLOCK, BLOCK)
        spot = pl.ds(start, BLOCK)
        geo = geometry(start)
        step = geo.inverse
        square = step * step
        envelope = geo.reach * geo.reach * NORM
        slope = geo.reach * (-2.0 * NORM / (cutoff_radius * cutoff_radius))
        total = None
        for pair, (sine, cosine) in enumerate(zip(geo.sines(), geo.cosines())):
            d0, d1, d2, d3 = (
                dplanes[order, spot, 128 * pair : 128 * (pair + 1)] for order in range(4)
            )
            plain = d0 + step * (d1 + step * (d2 + step * d3))
            sloped = step * (0.5 * d1 + step * (d2 + 1.5 * step * d3))
            rate = (turn + 2.0 * ANGLE * pair) * cosine - sine
            change = (0.5 * square) * rate * envelope + sine * slope
            term = plain * change - sloped * (sine * envelope) * square
            total = term if total is None else total + term
        radial[0, spot, :] = total * pair_weight[spot, :]
        return carry

    lax.fori_loop(0, group // BLOCK, slope_block, 0)
    pull_of = radial[0]
    to_own = mm(sender_rows[...], pull_of)
    to_sender = mm(own, pull_of, NT)
    force_own[...] = jnp.zeros_like(force_own)
    for q in range(tiles):
        spot = slice(128 * q, 128 * (q + 1))
        weight_row = to_sender[5:6, spot]
        for axis in range(3):
            value = -2.0 * (to_sender[2 + axis : 3 + axis, spot] + sender_rows[2 + axis : 3 + axis, spot] * weight_row)
            value = value - slopes_zero[q][axis] - slopes_one[q][axis]
            force_own[2 * q, axis : axis + 1, :] = value
            force_own[2 * q + 1, axis : axis + 1, :] = pltpu.roll(value, BLOCK, 1)
    members(lambda device, target: push(9, force_own.at[target], force_all.at[col], device))
    force_all[col] = force_own[col]
    own_force = []
    for axis in range(3):
        pairwise = 2.0 * (to_own[2 + axis : 3 + axis] + own[2 + axis : 3 + axis] * to_own[5:6])
        moved = jnp.sum(moved_zero[axis] + moved_one[axis], axis=0, keepdims=True)
        both = pairwise + moved
        own_force.append(both + pltpu.roll(both, BLOCK, 1))

    gather_tiles(11, early_sum, early, 0)
    pick_ones = ((iota((8, FEATURE_ROWS), 0) == 0) & (iota((8, FEATURE_ROWS), 1) == ONES_ROW)).astype(F32)
    for layer in range(2):
        total = None
        for parity in range(2):
            rows = []
            for r in range(3):
                at = 12 * layer + 6 * parity + 2 * r
                rows.append(jnp.concatenate([early_sum[at], early_sum[at + 1]], axis=1))
            block = jnp.concatenate(rows, axis=0)
            if parity == 0:
                hidden_bias_out[layer : layer + 1, :] = mm(pick_ones, block, NT)[0:1]
            part = mm(block, select[parity])
            total = part if total is None else total + part
        hidden_weight_out[layer] = total
    small_sum = jnp.concatenate([early_sum[24 + r] for r in range(4)], axis=0)
    for layer in range(2):
        inner_weight_out[layer] = small_sum[0:INNER, 32 * layer : 32 * layer + HIDDEN]
        pick = ((row8 == 0) & (lane == 32 * layer + HIDDEN)).astype(F32)
        flat = mm(pick, small_sum, NT)
        inner_bias_out[layer : layer + 1, :] = flat[0:1, 0:INNER]
        energy_weight_out[layer : layer + 1, :] = flat[0:1, INNER : 2 * INNER]
    gather_tiles(13, late_sum, late, late_base)
    total = None
    for parity in range(2):
        rows = [
            jnp.concatenate([late_sum[4 * parity + 2 * r], late_sum[4 * parity + 2 * r + 1]], axis=1)
            for r in range(2)
        ]
        part = mm(jnp.concatenate(rows, axis=0), select[parity])
        total = part if total is None else total + part
    message_weight_out[...] = total[0:CHANNELS]

    await_bytes(final_all, devices - 1, recv_sem.at[10])
    final = final_all[0]
    for k in range(1, devices):
        final = final + final_all[k]
    final = jnp.concatenate([final, pltpu.roll(final, 96, 1)], axis=0)
    dembedding = None
    for layer in range(2):
        channel_mix_out[:, layer, :] = final[0:CHANNELS, 12 * layer : 12 * (layer + 1)]
        dtable = final[0:CHANNELS, 24 + 2 * layer : 26 + 2 * layer]
        channel_in_out[layer] = lax.dot_general(
            embedding[...],
            dtable,
            (((0,), (1,)), ((), ())),
            precision=lax.Precision.HIGHEST,
            preferred_element_type=F32,
        )
        part = lax.dot_general(
            dtable,
            channel_in[layer],
            (((0,), (1,)), ((), ())),
            precision=lax.Precision.HIGHEST,
            preferred_element_type=F32,
        )
        dembedding = part if dembedding is None else dembedding + part
    embedding_out[...] = dembedding

    await_bytes(force_all, lanes - 1, recv_sem.at[9])
    force = force_all[0]
    for k in range(1, lanes):
        force = force + force_all[k]
    for axis in range(3):
        position_out[axis] = (force[axis : axis + 1] + own_force[axis])[:, 0:BLOCK]

    await_bytes(pack_all, lanes - 1, send_sem.at[0])
    await_bytes(send_all, lanes - 1, send_sem.at[1])
    await_bytes(recv_all, lanes - 1, send_sem.at[2])
    await_bytes(stat_all.at[0], devices - 1, send_sem.at[3])
    await_bytes(message_all, lanes - 1, send_sem.at[4])
    await_bytes(stat_all.at[1], devices - 1, send_sem.at[5])
    await_bytes(stat_all.at[2], devices - 1, send_sem.at[6])
    await_bytes(dmessage_all, lanes - 1, send_sem.at[7])
    await_bytes(stat_all.at[3], devices - 1, send_sem.at[8])
    await_bytes(force_all, lanes - 1, send_sem.at[9])
    await_bytes(final_all, devices - 1, send_sem.at[10])
    drain_tiles(11, early_all, early_sum, early, 0)
    drain_tiles(13, late_all, late_sum, late, late_base)


def solution(mesh):
    lanes = mesh.shape["edge"]
    structs = mesh.shape["struct"]
    devices = lanes * structs

    def step(
        positions,
        species,
        struct_id,
        atom_mask,
        senders,
        receivers,
        edge_mask,
        energy_cot,
        embedding,
        channel_in,
        channel_mix,
        hidden_weight,
        hidden_bias,
        inner_weight,
        inner_bias,
        energy_weight,
        message_weight,
    ):
        owned = positions.shape[2]
        group = owned * lanes
        edges = senders.shape[1]
        early, late = 28, 8
        vmem = pltpu.VMEM
        shapes = [
            (1, STRUCTS),
            (3, 1, owned),
            embedding.shape,
            channel_in.shape,
            (CHANNELS, 2, CHANNELS),
            (2, HIDDEN, FEATURES),
            hidden_bias.shape,
            (2, INNER, HIDDEN),
            inner_bias.shape,
            energy_weight.shape,
            (CHANNELS, FEATURES),
        ]
        scratch = [
            vmem((8, 128), F32),
            vmem((lanes, 8, 128), F32),
            vmem((lanes, 1, edges), I32),
            vmem((1, edges), I32),
            vmem((lanes, 1, edges), I32),
            vmem((256, BLOCK * (group // 256)), F32),
            vmem((group, 128), F32),
            vmem((group, 8), F32),
            vmem((8, group), F32),
            vmem((PAIRS, group, 128), F32),
            vmem((group, 128), F32),
            vmem((4, group, 128 * PAIRS), F32),
            vmem((2, PADDED, group), F32),
            vmem((2, PADDED * 20, group), F32),
            vmem((2, PADDED * SHELLS, 128 * PAIRS), F32),
            vmem((2, PADDED * SHELLS, 128 * PAIRS), F32),
            vmem((4, group, 128 * PAIRS), F32),
            vmem((PADDED * 20, group), F32),
            vmem((2, PAIRS, 96, 128), F32),
            vmem((PAIRS, 96, 128), F32),
            vmem((2, FEATURE_ROWS, 128), F32),
            vmem((2, FEATURE_ROWS, 128), F32),
            vmem((2, FEATURE_ROWS, FEATURES), F32),
            vmem((2, 2 * HEAD_ROWS, FEATURE_ROWS), F32),
            vmem((2, FEATURE_ROWS, 2 * HEAD_ROWS), F32),
            vmem((4, 8, 128), F32),
            vmem((4, devices, 8, 128), F32),
            vmem((8, 128), F32),
            vmem((lanes, 8, 128), F32),
            vmem((lanes, 8, 128), F32),
            vmem((lanes, 8, 128), F32),
            vmem((lanes, 8, 128), F32),
            vmem((lanes, 8, 128), F32),
            vmem((8, 128), F32),
            vmem((devices, 8, 128), F32),
            vmem((early, 8, 128), F32),
            vmem((devices, 8, 128), F32),
            vmem((early, 8, 128), F32),
            vmem((late, 8, 128), F32),
            vmem((devices, 8, 128), F32),
            vmem((late, 8, 128), F32),
            pltpu.SemaphoreType.DMA((16,)),
            pltpu.SemaphoreType.DMA((16,)),
        ]
        outs = pl.pallas_call(
            functools.partial(body, lanes, structs),
            out_shape=[jax.ShapeDtypeStruct(s, F32) for s in shapes],
            in_specs=[pl.BlockSpec(memory_space=vmem)] * 17,
            out_specs=[pl.BlockSpec(memory_space=vmem)] * 11,
            scratch_shapes=scratch,
            compiler_params=pltpu.CompilerParams(
                collective_id=0, has_side_effects=True, vmem_limit_bytes=60 * 1024 * 1024
            ),
        )(
            positions,
            species,
            struct_id,
            atom_mask,
            senders,
            receivers,
            edge_mask,
            energy_cot,
            embedding,
            channel_in,
            jnp.transpose(channel_mix, (1, 0, 2)),
            jnp.transpose(hidden_weight, (0, 2, 1)),
            hidden_bias,
            jnp.transpose(inner_weight, (0, 2, 1)),
            inner_bias,
            energy_weight,
            jnp.transpose(message_weight),
        )
        outs = list(outs)
        outs[4] = jnp.transpose(outs[4], (1, 0, 2))
        outs[5] = jnp.transpose(outs[5], (0, 2, 1))
        outs[7] = jnp.transpose(outs[7], (0, 2, 1))
        outs[10] = jnp.transpose(outs[10])
        return tuple(outs)

    tiled = P("struct", "edge")
    return jax.shard_map(
        step,
        mesh=mesh,
        in_specs=(
            P(None, "struct", "edge"),
            tiled,
            tiled,
            tiled,
            tiled,
            tiled,
            tiled,
            P("struct", None),
        )
        + (P(),) * 9,
        out_specs=(P("struct", None), P(None, "struct", "edge")) + (P(),) * 9,
        check_vma=False,
    )
```

```python
import functools
import math

import jax
import jax.numpy as jnp
import numpy as np
from jax import lax
from jax.experimental import pallas as pl
from jax.experimental.pallas import tpu as pltpu
from jax.sharding import PartitionSpec as P

CHANNELS = 12
PADDED = 16
RADIALS = 6
PAIRS = 3
STRUCTS = 8
HIDDEN = 24
INNER = 16
FEATURES = 432
HEAD_ROWS = 40
FEATURE_ROWS = 256
ONES_ROW = 216
BLOCK = 64

cutoff_radius = 6.0
variance_eps = 1e-05
center = 1.5

MESH = pl.DeviceIdType.MESH
F32 = jnp.float32
BF16 = jnp.bfloat16
I32 = jnp.int32
NN = ((1,), (0,))
NT = ((1,), (1,))
TN = ((0,), (0,))

MONOMIALS = sorted(
    [(a, b, c) for a in range(4) for b in range(4) for c in range(4) if a + b + c <= 3],
    key=lambda m: (sum(m), -m[0], -m[1], -m[2]),
)
PLACE = {m: i for i, m in enumerate(MONOMIALS)}
COUNTS = [1, 4, 10, 20]
OFFSETS = [0, 1, 5, 15]
SHELLS = 35
KIND_ROWS = [8, 8, 24, 40]
RADIX = 4096.0


def fitted(function, low, high, degree):
    series = np.polynomial.chebyshev.Chebyshev.interpolate(
        lambda w: function(0.5 * (high - low) * w + 0.5 * (high + low)), degree
    )
    return [float(v) for v in series.convert(kind=np.polynomial.Polynomial).coef]


LOW, HIGH = 0.9, 28.1
ANGLE = math.pi / cutoff_radius
SINE = fitted(lambda u: np.sin(ANGLE * np.sqrt(u)) / np.sqrt(u), LOW, HIGH, 9)
COSINE = fitted(lambda u: np.cos(ANGLE * np.sqrt(u)), LOW, HIGH, 9)
NORM = math.sqrt(2.0 / cutoff_radius)


def mm(left, right, kind=NN, precision=lax.Precision.HIGHEST):
    return lax.dot_general(
        left, right, (kind, ((), ())), precision=precision, preferred_element_type=F32
    )


def once(left, right, kind=NN):
    return lax.dot_general(left, right, (kind, ((), ())), preferred_element_type=F32)


def parts(value):
    high = value.astype(BF16)
    rest = value - high.astype(F32)
    middle = rest.astype(BF16)
    return high, middle, (rest - middle.astype(F32)).astype(BF16)


def loop(count, action, carry):
    if count <= 8:
        for i in range(count):
            carry = action(i, carry)
        return carry
    return lax.fori_loop(0, count, action, carry)


def aligned(value, size):
    return value if isinstance(value, int) else pl.multiple_of(value, size)


def iota(shape, dim):
    return lax.broadcasted_iota(I32, shape, dim)


def horner(coefficients, w):
    total = jnp.full_like(w, coefficients[-1])
    for value in coefficients[-2::-1]:
        total = total * w + value
    return total


def shifted(terms, order, x, y, z):
    current = terms
    for axis, value in enumerate((x, y, z)):
        two, three = 2.0 * value, 3.0 * value
        square = value * value
        three_square, cube = 3.0 * square, square * value
        factors = [None, [value], [square, two], [cube, three_square, three]]
        fresh = {}
        for m in MONOMIALS[: COUNTS[order]]:
            if axis == 2 and sum(m) != order:
                continue
            power = m[axis]
            total = current[m]
            for lower in range(power):
                source = m[:axis] + (lower,) + m[axis + 1 :]
                total = total + factors[power][lower] * current[source]
            fresh[m] = total
        current = fresh
    return current


def invariants(terms, x, y, z):
    by_order = []
    for order in range(4):
        own = {m: terms[OFFSETS[order] + i] for i, m in enumerate(MONOMIALS[: COUNTS[order]])}
        by_order.append(shifted(own, order, x, y, z) if order else own)
    scalar = by_order[0][(0, 0, 0)]
    vx, vy, vz = by_order[1][(1, 0, 0)], by_order[1][(0, 1, 0)], by_order[1][(0, 0, 1)]
    m = by_order[2]
    xx, xy, xz = m[(2, 0, 0)], m[(1, 1, 0)], m[(1, 0, 1)]
    yy, yz, zz = m[(0, 2, 0)], m[(0, 1, 1)], m[(0, 0, 2)]
    q = by_order[3]
    xxx, yyy, zzz = q[(3, 0, 0)], q[(0, 3, 0)], q[(0, 0, 3)]
    xxy, xxz, xyy = q[(2, 1, 0)], q[(2, 0, 1)], q[(1, 2, 0)]
    xyz, xzz, yyz, yzz = q[(1, 1, 1)], q[(1, 0, 2)], q[(0, 2, 1)], q[(0, 1, 2)]
    first = vx * vx + vy * vy + vz * vz
    second = xx * xx + yy * yy + zz * zz + 2.0 * (xy * xy + xz * xz + yz * yz)
    third = (
        xxx * xxx
        + yyy * yyy
        + zzz * zzz
        + 3.0 * (xxy * xxy + xxz * xxz + xyy * xyy + xzz * xzz + yyz * yyz + yzz * yzz)
        + 6.0 * (xyz * xyz)
    )
    fourth = (
        vx * (xx * vx + xy * vy + xz * vz)
        + vy * (xy * vx + yy * vy + yz * vz)
        + vz * (xz * vx + yz * vy + zz * vz)
    )
    xy2, xz2, yz2 = 2.0 * xy, 2.0 * xz, 2.0 * yz
    fifth = (
        vx * (xxx * xx + xyy * yy + xzz * zz + xxy * xy2 + xxz * xz2 + xyz * yz2)
        + vy * (xxy * xx + yyy * yy + yzz * zz + xyy * xy2 + xyz * xz2 + yyz * yz2)
        + vz * (xxz * xx + yyz * yy + zzz * zz + xyz * xy2 + xzz * xz2 + yzz * yz2)
    )
    return (scalar, first, second, third, fourth, fifth)


def silu_pair(v):
    gate = 1.0 / (1.0 + jnp.exp(-v))
    return v * gate, gate * (1.0 + v * (1.0 - gate))


class Geometry:
    def __init__(self, columns, own, lane_low):
        dx = own[2:3] + columns[:, 2:3]
        dy = own[3:4] + columns[:, 3:4]
        dz = own[4:5] + columns[:, 4:5]
        self.u = dx * dx + dy * dy + dz * dz + 1.0
        w = (self.u - 0.5 * (LOW + HIGH)) * (2.0 / (HIGH - LOW))
        self.sine = horner(SINE, w)
        self.cosine = horner(COSINE, w)
        self.inverse = lax.rsqrt(self.u)
        self.reach = 1.0 - self.u * (1.0 / (cutoff_radius * cutoff_radius))
        self.lane_low = lane_low

    def sines(self):
        step = 2.0 * (2.0 * self.cosine * self.cosine - 1.0)
        before = jnp.where(self.lane_low, -self.sine, 0.0)
        now = jnp.where(self.lane_low, self.sine, 2.0 * self.cosine * self.sine)
        return self.series(step, before, now)

    def cosines(self):
        double = 2.0 * self.cosine * self.cosine - 1.0
        before = jnp.where(self.lane_low, self.cosine, 1.0)
        now = jnp.where(self.lane_low, self.cosine, double)
        return self.series(2.0 * double, before, now)

    def series(self, step, before, now):
        out = [now]
        for _ in range(PAIRS - 1):
            before, now = now, step * now - before
            out.append(now)
        return out


def body(lanes, structs, *refs):
    (
        positions,
        species,
        struct_id,
        atom_mask,
        senders,
        receivers,
        edge_mask,
        energy_cot,
        embedding,
        channel_in,
        channel_mix,
        hidden_weight,
        hidden_bias,
        inner_weight,
        inner_bias,
        energy_weight,
        message_weight,
        energies_out,
        position_out,
        embedding_out,
        channel_in_out,
        channel_mix_out,
        hidden_weight_out,
        hidden_bias_out,
        inner_weight_out,
        inner_bias_out,
        energy_weight_out,
        message_weight_out,
        pack,
        pack_all,
        send_all,
        masked_recv,
        recv_all,
        counts,
        pair_weight,
        columns,
        sender_rows,
        radial,
        inverse,
        planes,
        slopes,
        pulls,
        weights,
        products,
        sums,
        dsums,
        kind_products,
        kind_stack,
        kind_sums,
        dkind_sums,
        dkind_products,
        dproducts,
        invariant,
        dinvariant,
        feats,
        normed,
        select,
        head,
        head_t,
        stat_own,
        stat_all,
        message_own,
        message_all,
        dmessage_own,
        dmessage_all,
        force_own,
        force_all,
        final_own,
        final_all,
        early_own,
        early_all,
        early_sum,
        late_own,
        late_all,
        late_sum,
        send_sem,
        recv_sem,
    ) = refs
    devices = lanes * structs
    edge_count = senders.shape[1]
    group = pair_weight.shape[0]
    tiles = group // 128
    strips = [slice(k, k + 512) for k in range(0, group, 512)]
    row = lax.axis_index("struct")
    col = lax.axis_index("edge")
    me = row * lanes + col

    def everyone(action):
        def one(k, carry):
            target = lax.rem(me + k, devices)
            action((target // lanes, lax.rem(target, lanes)), target)
            return carry

        if devices <= 32:
            for k in range(1, devices):
                one(k, 0)
        else:
            lax.fori_loop(1, devices, one, 0)

    def members(action):
        def one(k, carry):
            target = lax.rem(col + k, lanes)
            action((row, target), target)
            return carry

        if lanes <= 8:
            for k in range(1, lanes):
                one(k, 0)
        else:
            lax.fori_loop(1, lanes, one, 0)

    def push(phase, source, target, device):
        pltpu.make_async_remote_copy(
            src_ref=source,
            dst_ref=target,
            send_sem=send_sem.at[phase],
            recv_sem=recv_sem.at[phase],
            device_id=device,
            device_id_type=MESH,
        ).start()

    def await_bytes(buffer, count, sem):
        if count:
            view = buffer.at[pl.ds(0, count)]
            pltpu.make_async_copy(view, view, sem).wait()

    barrier = pltpu.get_barrier_semaphore()
    everyone(
        lambda device, _: pl.semaphore_signal(
            barrier, inc=1, device_id=device, device_id_type=MESH
        )
    )

    pack[...] = jnp.ones_like(pack)
    masked_recv[...] = jnp.where(edge_mask[...] > 0, receivers[...], -1)
    kind = species[...]
    for half in (0, BLOCK):
        spot = pl.ds(half, BLOCK)
        pack[0:1, spot] = (kind == 0).astype(F32)
        pack[1:2, spot] = (kind == 1).astype(F32)
        for axis in range(3):
            pack[2 + axis : 3 + axis, spot] = center - positions[axis]
        pack[6:7, spot] = atom_mask[...].astype(F32)
        pack[7:8, spot] = struct_id[...].astype(F32)
    pl.semaphore_wait(barrier, devices - 1)

    members(lambda device, _: push(0, pack, pack_all.at[col], device))
    members(lambda device, _: push(1, senders, send_all.at[col], device))
    members(lambda device, _: push(2, masked_recv, recv_all.at[col], device))
    pack_all[col] = pack[...]
    send_all[col] = senders[...]
    recv_all[col] = masked_recv[...]

    lane = iota((8, 128), 1)
    low_row = lane[0:1] < BLOCK
    low = lane < BLOCK
    row8 = iota((8, 128), 0)
    own = pack[...] * jnp.where((row8 >= 2) & (row8 <= 4), -1.0, 1.0)
    live = own[6:7]
    half_pick = ((iota((2, 128), 1) >= BLOCK).astype(I32) == iota((2, 128), 0)).astype(F32)
    half_sum = ((row8 == 0) & low | (row8 == 1) & ~low).astype(F32)
    half_sum_late = ((row8 == 2) & low | (row8 == 3) & ~low).astype(F32)

    mix_pd = (iota((72, CHANNELS), 0) - 12 * ((iota((72, CHANNELS), 0) * 5462) >> 16)) == iota(
        (72, CHANNELS), 1
    )
    mix_pd = mix_pd.astype(F32)
    mix_pc = ((iota((96, CHANNELS), 0) & 15) == iota((96, CHANNELS), 1)).astype(F32)
    same = ((iota((96, 72), 0) >> 4) == ((iota((96, 72), 1) * 5462) >> 16)).astype(F32)
    same_t = ((iota((72, 96), 1) >> 4) == ((iota((72, 96), 0) * 5462) >> 16)).astype(F32)
    mixers, mixers_t = [], []
    for layer in range(2):
        table = channel_mix[:, layer, :]
        spread_c = mm(mix_pc, table)
        mixers_t.append(mm(spread_c, mix_pd, NT) * same)
        spread_d = mm(mix_pd, table, NT)
        mixers.append(mm(spread_d, mix_pc, NT) * same_t)

    struct_rows = own[7:8].astype(I32)
    member = (struct_rows == iota((STRUCTS, 128), 0)).astype(F32)
    atom_cot = mm(energy_cot[...], member) * live
    seat = ((iota((128, 128), 0) - 96) == struct_rows).astype(F32)

    await_bytes(pack_all, lanes - 1, recv_sem.at[0])
    for q in range(tiles):
        sender_rows[:, 128 * q : 128 * (q + 1)] = jnp.where(low, pack_all[2 * q], pack_all[2 * q + 1])
    columns[...] = jnp.transpose(sender_rows[...])

    def geometry(start):
        cols = columns[pl.ds(start, BLOCK), :]
        return Geometry(cols, own, low_row)

    def radial_block(i, carry):
        start = aligned(i * BLOCK, BLOCK)
        geo = geometry(start)
        envelope = geo.reach * geo.reach * NORM
        for pair, value in enumerate(geo.sines()):
            radial[pair, pl.ds(start, BLOCK), :] = value * envelope
        inverse[pl.ds(start, BLOCK), :] = geo.inverse
        return carry

    loop(group // BLOCK, radial_block, 0)

    def monomial_rows(rows):
        x, y, z = rows[2:3], rows[3:4], rows[4:5]
        table = {(0, 0, 0): None}
        for m in MONOMIALS[1:]:
            axis = next(i for i in range(3) if m[i])
            lower = m[:axis] + (m[axis] - 1,) + m[axis + 1 :]
            factor = (x, y, z)[axis]
            table[m] = factor if table[lower] is None else table[lower] * factor
        return table

    def spread():
        def one(q, carry):
            spot = pl.ds(aligned(q * 128, 128), 128)
            table = monomial_rows(sender_rows[:, spot])
            h = weights[:, spot]
            for i, m in enumerate(MONOMIALS):
                products[PADDED * i : PADDED * (i + 1), spot] = h if table[m] is None else h * table[m]
            return carry

        loop(tiles, one, 0)

    dkind_sums[...] = jnp.zeros_like(dkind_sums)

    def kind_spread(q, carry):
        spot = pl.ds(aligned(q * 128, 128), 128)
        table = monomial_rows(sender_rows[:, spot])
        kinds = sender_rows[0:2, spot]
        for i, m in enumerate(MONOMIALS):
            kind_products[2 * i : 2 * i + 2, spot] = kinds if table[m] is None else kinds * table[m]
        return carry

    loop(tiles, kind_spread, 0)
    columns_of = []
    for kind_of in range(2):
        embedded = mm(embedding[...], (iota((2, 128), 0) == kind_of).astype(F32), TN)
        padded = jnp.concatenate(
            [mm(channel_in[0], embedded, TN), jnp.zeros((PADDED - CHANNELS, 128), F32)], axis=0
        )
        columns_of.append([padded[0:8], padded[8:16]])

    await_bytes(send_all, lanes - 1, recv_sem.at[1])
    await_bytes(recv_all, lanes - 1, recv_sem.at[2])
    counts[...] = jnp.zeros_like(counts)
    chunk = min(2048, edge_count)
    per_slot = edge_count // chunk
    wide = counts.shape[2]

    def count_block(i, carry):
        slot = i // per_slot
        spot = pl.ds(aligned((i % per_slot) * chunk, chunk), chunk)
        send = send_all[slot, :, spot]
        local = recv_all[slot, :, spot] - col * BLOCK
        inside = (local >= 0) & (local < BLOCK)
        key = jnp.where(inside, (send >> 8) * BLOCK + local, -1)
        step = jnp.where((send & 128) > 0, RADIX, 1.0)
        sender_hot = jnp.where(iota((128, chunk), 0) == (send & 127), step, 0.0).astype(BF16)
        pair_hot = jnp.where(iota((wide, chunk), 0) == key, 1.0, 0.0).astype(BF16)
        found = once(sender_hot, pair_hot, NT)
        upper = jnp.floor(found * (1.0 / RADIX))
        counts[0] += found - RADIX * upper
        counts[1] += upper
        return carry

    loop(lanes * per_slot, count_block, 0)
    low_tall = iota((128, 128), 1) < BLOCK
    for block in range(group // 128):
        turn_of = block // 2
        piece = counts[block % 2, :, 128 * (turn_of // 2) : 128 * (turn_of // 2 + 1)]
        turned = pltpu.roll(piece, BLOCK, 1)
        first_half, second_half = (piece, turned) if turn_of % 2 == 0 else (turned, piece)
        pair_weight[128 * block : 128 * (block + 1), :] = jnp.where(
            low_tall, first_half, second_half
        )

    def plane_block(i, carry):
        spot = pl.ds(aligned(i * BLOCK, BLOCK), BLOCK)
        weight = pair_weight[spot, :]
        step = inverse[spot, :]
        for pair in range(PAIRS):
            value = radial[pair, spot, :] * weight
            for order in range(4):
                planes[order, spot, 128 * pair : 128 * (pair + 1)] = value
                value = value * step
        return carry

    loop(group // BLOCK, plane_block, 0)

    xi, yi, zi = (jnp.broadcast_to(own[r : r + 1], (8, 128)) for r in (2, 3, 4))

    def chunk_spots(i):
        pair, tile = i // 2, i % 2
        return pair, tile, slice(128 * pair, 128 * (pair + 1))

    def kind_terms(pair):
        spot = slice(128 * pair, 128 * (pair + 1))
        out = []
        for order in range(4):
            for m in range(COUNTS[order]):
                out.append(
                    [
                        jnp.broadcast_to(kind_sums[order, 2 * m + k : 2 * m + k + 1, spot], (8, 128))
                        for k in range(2)
                    ]
                )
        return out

    def mix_invariants(layer):
        for pair in range(PAIRS):
            feats[layer, 72 * pair : 72 * (pair + 1), :] = mm(mixers[layer], invariant[layer, pair])

    def forward_kinds():
        for order in range(4):
            rows = KIND_ROWS[order]
            kind_sums[order, 0:rows, :] = mm(kind_products[0:rows, :], planes[order])
        for pair in range(PAIRS):
            both = kind_terms(pair)
            for tile in range(2):
                terms = [columns_of[0][tile] * a + columns_of[1][tile] * b for a, b in both]
                for p, value in enumerate(invariants(terms, xi, yi, zi)):
                    start = PADDED * p + 8 * tile
                    invariant[0, pair, start : start + 8, :] = value
        mix_invariants(0)

    def forward():
        for order in range(4):
            rows = PADDED * COUNTS[order]
            start = PADDED * OFFSETS[order]
            sums[start : start + rows, :] = mm(products[0:rows, :], planes[order])
        for i in range(2 * PAIRS):
            pair, tile, spot = chunk_spots(i)
            terms = [sums[PADDED * m + 8 * tile : PADDED * m + 8 * tile + 8, spot] for m in range(SHELLS)]
            for p, value in enumerate(invariants(terms, xi, yi, zi)):
                start = PADDED * p + 8 * tile
                invariant[1, pair, start : start + 8, :] = value
        mix_invariants(1)

    def send_stats(phase, index, first, second, extra=None):
        both = mm(first[0], first[1], NT) + mm(second[0], second[1], NT)
        stat_own[index, 0:4, :] = both[0:4, 0:128]
        tail = both[0:4, 128:256]
        if extra is not None:
            tail = tail + extra
        stat_own[index, 4:8, :] = tail
        everyone(
            lambda device, _: push(phase, stat_own.at[index], stat_all.at[index, me], device)
        )
        stat_all[index, me] = stat_own[index]

    def get_stats(phase, index):
        await_bytes(stat_all.at[index], devices - 1, recv_sem.at[phase])
        total = stat_all[index, 0]
        for k in range(1, devices):
            total = total + stat_all[index, k]
        return jnp.concatenate([total[0:4], total[4:8]], axis=1)

    ones_rows = iota((FEATURE_ROWS - ONES_ROW, 128), 0) == 0
    for layer in range(2):
        feats[layer, ONES_ROW:FEATURE_ROWS, :] = ones_rows.astype(F32)
        normed[layer, ONES_ROW:FEATURE_ROWS, :] = ones_rows.astype(F32)

    def send_moments(layer, phase):
        values = feats[layer]
        send_stats(phase, layer, (half_sum * live, values), (half_sum_late * live, values * values))

    def normalise(layer, phase):
        both = get_stats(phase, layer)
        count = jnp.maximum(both[0:1, ONES_ROW : ONES_ROW + 1], 1.0)
        mean = both[0:2] / count
        spread_of = both[2:4] / count - mean * mean
        scale = lax.rsqrt(spread_of + variance_eps)
        mean_wide = mm(mean, half_pick, TN)
        scale_wide = mm(scale, half_pick, TN)
        normed[layer, 0:ONES_ROW, :] = (feats[layer, 0:ONES_ROW, :] - mean_wide[0:ONES_ROW]) * scale_wide[
            0:ONES_ROW
        ]
        joined = mm(head[layer], normed[layer])
        chosen = jnp.where(low_row, joined[0:HEAD_ROWS], joined[HEAD_ROWS:])
        return chosen + pltpu.roll(chosen, BLOCK, 1), scale_wide, count

    def run_head(layer, pre):
        hidden, hidden_slope = silu_pair(pre[0:HIDDEN])
        inner_pre = mm(inner_weight[layer], hidden) + inner_cols[layer]
        inner, inner_slope = silu_pair(inner_pre)
        energy = jnp.sum(energy_cols[layer] * inner, axis=0, keepdims=True)
        dinner = energy_cols[layer] * atom_cot * inner_slope
        dhidden = mm(inner_weight[layer], dinner, TN) * hidden_slope
        left = jnp.concatenate([dinner, atom_cot * inner], axis=0)
        blank = jnp.zeros((128 - 32 - 32 * layer, 128), F32)
        right = [hidden, (iota((8, 128), 0) == 0).astype(F32), blank]
        if layer == 1:
            right = [jnp.zeros((32, 128), F32)] + right
        small = mm(jnp.where(low_row, left, 0.0), jnp.concatenate(right, axis=0), NT)
        return energy, dhidden, small

    def halves(value):
        return jnp.where(low_row, value, 0.0), jnp.where(low_row, 0.0, value)

    forward_kinds()
    send_moments(0, 3)
    pre_zero, scale_zero, count = None, None, None
    for parity in range(2):
        k = iota((FEATURE_ROWS, FEATURES), 0)
        pair = (k >= 72).astype(I32) + (k >= 144).astype(I32)
        rest = k - 72 * pair
        kind_of = (rest * 5462) >> 16
        channel = rest - 12 * kind_of
        place = channel * 36 + (2 * pair + parity) * 6 + kind_of
        hit = (place == iota((FEATURE_ROWS, FEATURES), 1)) & (k < ONES_ROW)
        select[parity] = hit.astype(F32)
    bias_spot = (iota((2, FEATURE_ROWS), 1) == ONES_ROW) & (
        iota((2, FEATURE_ROWS), 0) == 0
    )
    bias_cols, inner_cols, energy_cols = [], [], []
    head[...] = jnp.zeros_like(head)
    for layer in range(2):
        for parity in range(2):
            base = HEAD_ROWS * parity
            block = mm(hidden_weight[layer], select[parity], NT)
            if parity == 0:
                spot = bias_spot.astype(F32)
                if layer == 1:
                    spot = (
                        (iota((2, FEATURE_ROWS), 1) == ONES_ROW)
                        & (iota((2, FEATURE_ROWS), 0) == 1)
                    ).astype(F32)
                block = block + mm(hidden_bias[...], spot, TN)
            head[layer, base : base + HIDDEN, :] = block
            if layer == 0:
                head[0, base + HIDDEN : base + HIDDEN + CHANNELS, :] = mm(
                    message_weight[...], select[parity], NT
                )
        head_t[layer] = jnp.transpose(head[layer])
        pick = (iota((2, 128), 0) == layer).astype(F32)
        inner_cols.append(mm(inner_bias[...], pick, TN))
        energy_cols.append(mm(energy_weight[...], pick, TN))

    turn = ANGLE * (1.0 + (iota((1, 128), 1) >= BLOCK).astype(F32))

    def slope_block(i, carry):
        start = aligned(i * BLOCK, BLOCK)
        spot = pl.ds(start, BLOCK)
        geo = geometry(start)
        step = geo.inverse
        square = step * step
        envelope = geo.reach * geo.reach * NORM
        slope = geo.reach * (-2.0 * NORM / (cutoff_radius * cutoff_radius))
        weight = pair_weight[spot, :]
        for pair, (sine, cosine) in enumerate(zip(geo.sines(), geo.cosines())):
            at = slice(128 * pair, 128 * (pair + 1))
            rate = (turn + 2.0 * ANGLE * pair) * cosine - sine
            value = weight * ((0.5 * square) * rate * envelope + sine * slope)
            slopes[0, spot, at] = value
            for order in range(1, 4):
                value = value * step - (0.5 * square) * planes[order, spot, at]
                slopes[order, spot, at] = value
        return carry

    loop(group // BLOCK, slope_block, 0)
    for q in strips:
        first, second, third = (v.astype(F32) for v in parts(kind_products[:, q]))
        stack = jnp.concatenate([first, first, second, first, third, second], axis=0)
        kind_stack[:, q] = stack.astype(BF16)

    pre_zero, scale_zero, count = normalise(0, 3)
    message = pre_zero[HIDDEN:HEAD_ROWS]
    message_own[...] = jnp.where(low, message[0:8], message[8:16])
    members(lambda device, _: push(4, message_own, message_all.at[col], device))
    message_all[col] = message_own[...]
    energy_zero, dhidden_zero, small_zero = run_head(0, pre_zero)
    weights[...] = jnp.zeros_like(weights)
    embedded = mm(embedding[...], sender_rows[0:2, :], TN)
    weights[0:CHANNELS, :] = mm(channel_in[1], embedded, TN)
    await_bytes(message_all, lanes - 1, recv_sem.at[4])
    for q in range(tiles):
        even, odd = message_all[2 * q], message_all[2 * q + 1]
        spot = slice(128 * q, 128 * (q + 1))
        weights[0:8, spot] += jnp.where(low, even, pltpu.roll(odd, BLOCK, 1))
        weights[8:16, spot] += jnp.where(low, pltpu.roll(even, BLOCK, 1), odd)

    spread()
    forward()
    send_moments(1, 5)
    pre_one, scale_one, _ = normalise(1, 5)
    energy_one, dhidden_one, small_one = run_head(1, pre_one)
    d_low, d_high = halves(dhidden_one)
    gap = jnp.zeros((HEAD_ROWS - HIDDEN, 128), F32)
    dhead_one = jnp.concatenate([d_low, gap, d_high, gap], axis=0)
    dnormed_one = mm(head_t[1], dhead_one)
    energy_row = jnp.where(low_row, live * (energy_zero + energy_one), 0.0)
    energy_tail = mm(
        jnp.where(iota((8, 128), 0) == 0, energy_row, 0.0), seat, NT
    )[0:4]
    send_stats(
        6,
        2,
        (half_sum, dnormed_one),
        (half_sum_late, dnormed_one * normed[1]),
        energy_tail,
    )

    d_low, d_high = halves(dhidden_zero)
    dhead_zero = jnp.concatenate([d_low, d_high], axis=0)
    d_low, d_high = halves(dhidden_one)
    dhead_both = [dhead_zero, jnp.concatenate([d_low, d_high], axis=0)]
    for layer in range(2):
        block = mm(dhead_both[layer], normed[layer], NT)
        for r in range(6):
            for half in range(2):
                early_own[12 * layer + 2 * r + half] = block[
                    8 * r : 8 * (r + 1), 128 * half : 128 * (half + 1)
                ]
    small = small_zero + small_one
    for r in range(4):
        early_own[24 + r] = small[8 * r : 8 * (r + 1)]
    early = early_own.shape[0]
    late = late_own.shape[0]
    late_base = devices - late

    def scatter_tiles(phase, source, target, count_of, base):
        for t in range(count_of):

            @pl.when(me != base + t)
            def _():
                there = base + t
                push(phase, source.at[t], target.at[me], (there // lanes, there % lanes))

            @pl.when(me == base + t)
            def _():
                target[me] = source[t]

    def share_tiles(phase, parts, result, count_of, base):
        @pl.when((me >= base) & (me < base + count_of))
        def _():
            await_bytes(parts, devices - 1, recv_sem.at[phase])
            total = parts[0]
            for k in range(1, devices):
                total = total + parts[k]
            result[me - base] = total
            everyone(
                lambda device, _: push(phase + 1, result.at[me - base], result.at[me - base], device)
            )

    def mine(base, count_of):
        return (me >= base) & (me < base + count_of)

    def gather_tiles(phase, result, count_of, base):
        @pl.when(mine(base, count_of))
        def _():
            await_bytes(result, count_of - 1, recv_sem.at[phase + 1])

        @pl.when(jnp.logical_not(mine(base, count_of)))
        def _():
            await_bytes(result, count_of, recv_sem.at[phase + 1])

    def drain_tiles(phase, parts, result, count_of, base):
        @pl.when(mine(base, count_of))
        def _():
            await_bytes(result, count_of - 1, send_sem.at[phase])
            await_bytes(parts, devices - 1, send_sem.at[phase + 1])

        @pl.when(jnp.logical_not(mine(base, count_of)))
        def _():
            await_bytes(result, count_of, send_sem.at[phase])

    def feature_back(layer, phase, index, dnormed, scale_wide):
        both = get_stats(phase, index)
        first = mm(both[0:2] / count, half_pick, TN)
        second = mm(both[2:4] / count, half_pick, TN)
        dfeats = scale_wide * (dnormed - live * (first + second * normed[layer]))
        products_of = jnp.zeros((96, 72), F32)
        for pair in range(PAIRS):
            piece = dfeats[72 * pair : 72 * (pair + 1)]
            dinvariant[pair] = mm(mixers_t[layer], piece)
            products_of = products_of + mm(invariant[layer, pair], piece, NT)
        return products_of * same, both

    blank = jnp.zeros((8, 128), F32)

    def shell_back():
        moved = (blank, blank, blank)
        for i in range(2 * PAIRS):
            pair, tile, spot = chunk_spots(i)
            terms = [sums[PADDED * m + 8 * tile : PADDED * m + 8 * tile + 8, spot] for m in range(SHELLS)]
            cots = tuple(dinvariant[pair, PADDED * p + 8 * tile : PADDED * p + 8 * tile + 8, :] for p in range(6))
            _, pull = jax.vjp(invariants, terms, xi, yi, zi)
            dterms, *shift = pull(cots)
            for m in range(SHELLS):
                dsums[PADDED * m + 8 * tile : PADDED * m + 8 * tile + 8, spot] = dterms[m]
            moved = tuple(a + b for a, b in zip(moved, shift))
        return moved

    def shell_back_kinds():
        moved = (blank, blank, blank)
        dtable = [[blank, blank], [blank, blank]]
        for pair in range(PAIRS):
            both = kind_terms(pair)
            folded = [[None, None] for _ in range(SHELLS)]
            for tile in range(2):
                terms = [columns_of[0][tile] * a + columns_of[1][tile] * b for a, b in both]
                cots = tuple(dinvariant[pair, PADDED * p + 8 * tile : PADDED * p + 8 * tile + 8, :] for p in range(6))
                _, pull = jax.vjp(invariants, terms, xi, yi, zi)
                dterms, *shift = pull(cots)
                moved = tuple(a + b for a, b in zip(moved, shift))
                for m in range(SHELLS):
                    for k in range(2):
                        dtable[k][tile] = dtable[k][tile] + dterms[m] * both[m][k]
                        value = columns_of[k][tile] * dterms[m]
                        folded[m][k] = value if tile == 0 else folded[m][k] + value
            for order in range(4):
                for m in range(COUNTS[order]):
                    for k in range(2):
                        dkind_sums[order, 2 * m + k : 2 * m + k + 1, 128 * pair : 128 * (pair + 1)] = jnp.sum(
                            folded[OFFSETS[order] + m][k], axis=0, keepdims=True
                        )
        return moved, [jnp.concatenate(halves_of, axis=0) for halves_of in dtable]

    def product_back():
        for order in (3, 2, 1, 0):
            rows = PADDED * COUNTS[order]
            start = PADDED * OFFSETS[order]
            for spot in strips:
                block = mm(
                    dsums[start : start + rows, :], planes[order, spot, :], NT, lax.Precision.HIGH
                )
                if order == 3:
                    dproducts[:, spot] = block
                else:
                    dproducts[0:rows, spot] += block

    def product_back_kinds():
        for order in (3, 2, 1, 0):
            rows = KIND_ROWS[order]
            for spot in strips:
                block = mm(
                    dkind_sums[order, 0:rows, :], planes[order, spot, :], NT, lax.Precision.HIGH
                )
                if order == 3:
                    dkind_products[:, spot] = block
                else:
                    dkind_products[0:rows, spot] += block

    def weight_back():
        out = []
        for q in range(tiles):
            spot = slice(128 * q, 128 * (q + 1))
            table = monomial_rows(sender_rows[:, spot])
            total = dproducts[0:PADDED, spot]
            for i, m in enumerate(MONOMIALS[1:], 1):
                total = total + table[m] * dproducts[PADDED * i : PADDED * (i + 1), spot]
            out.append(total)
        return out

    def axis_slope(table, axis, value_of):
        total = None
        for i, m in enumerate(MONOMIALS):
            if not m[axis]:
                continue
            lower = table[m[:axis] + (m[axis] - 1,) + m[axis + 1 :]]
            term = value_of(i)
            if lower is not None:
                term = (float(m[axis]) * lower) * term
            total = term if total is None else total + term
        return total

    def coordinate_back():
        out = []
        for q in range(tiles):
            spot = slice(128 * q, 128 * (q + 1))
            table = monomial_rows(sender_rows[:, spot])
            h = weights[:, spot]
            out.append(
                [
                    jnp.sum(
                        h * axis_slope(table, axis, lambda i: dproducts[PADDED * i : PADDED * (i + 1), spot]),
                        axis=0,
                        keepdims=True,
                    )
                    for axis in range(3)
                ]
            )
        return out

    def coordinate_back_kinds():
        out = []
        for q in range(tiles):
            spot = slice(128 * q, 128 * (q + 1))
            table = monomial_rows(sender_rows[:, spot])
            kinds = sender_rows[0:2, spot]
            rows = [
                jnp.sum(kinds * dkind_products[2 * i : 2 * i + 2, spot], axis=0, keepdims=True)
                for i in range(len(MONOMIALS))
            ]
            out.append([axis_slope(table, axis, lambda i: rows[i]) for axis in range(3)])
        return out

    def radial_pull(block, order, spot):
        total = None
        for pair in range(PAIRS):
            at = slice(128 * pair, 128 * (pair + 1))
            term = block[:, at] * slopes[order, spot, at]
            total = term if total is None else total + term
        return total

    def plane_back():
        for order in range(4):
            rows = PADDED * COUNTS[order]
            start = PADDED * OFFSETS[order]
            for spot in strips:
                block = mm(products[0:rows, spot], dsums[start : start + rows, :], TN)
                term = radial_pull(block, order, spot)
                if order == 0:
                    pulls[spot, :] = term
                else:
                    pulls[spot, :] += term

    def plane_back_kinds():
        for order in range(4):
            first, second, third = parts(dkind_sums[order])
            right = jnp.concatenate(
                [v.astype(F32) for v in (first, second, first, third, first, second)], axis=0
            ).astype(BF16)
            for spot in strips:
                block = once(kind_stack[:, spot], right, TN)
                pulls[spot, :] += radial_pull(block, order, spot)

    mix_one, both_back = feature_back(1, 6, 2, dnormed_one, scale_one)
    scatter_tiles(11, early_own, early_all, early, 0)
    group_energy = stat_all[2, row * lanes, 4:5, 96 : 96 + STRUCTS]
    for k in range(1, lanes):
        group_energy = group_energy + stat_all[2, row * lanes + k, 4:5, 96 : 96 + STRUCTS]
    energies_out[...] = group_energy
    moved_one = shell_back()
    product_back()
    dweights_one = weight_back()
    for q in range(tiles):
        top, bottom = dweights_one[q][0:8], dweights_one[q][8:16]
        dmessage_own[2 * q] = jnp.where(low, top, pltpu.roll(bottom, BLOCK, 1))
        dmessage_own[2 * q + 1] = jnp.where(low, pltpu.roll(top, BLOCK, 1), bottom)
    members(
        lambda device, target: push(7, dmessage_own.at[target], dmessage_all.at[col], device)
    )
    dmessage_all[col] = dmessage_own[col]
    kinds_of = sender_rows[...]
    dtable_one = jnp.zeros((PADDED, 8), F32)
    for q in range(tiles):
        dtable_one = dtable_one + mm(dweights_one[q], kinds_of[:, 128 * q : 128 * (q + 1)], NT)
    slopes_one = coordinate_back()
    await_bytes(dmessage_all, lanes - 1, recv_sem.at[7])
    arrived = dmessage_all[0]
    for k in range(1, lanes):
        arrived = arrived + dmessage_all[k]
    turned = pltpu.roll(arrived, BLOCK, 1)
    dmessage = jnp.concatenate([jnp.where(low, arrived, turned), jnp.where(low, turned, arrived)], axis=0)

    h_low, h_high = halves(dhidden_zero)
    m_low, m_high = halves(dmessage)
    dnormed_zero = mm(head_t[0], jnp.concatenate([h_low, m_low, h_high, m_high], axis=0))
    send_stats(
        8, 3, (half_sum, dnormed_zero), (half_sum_late, dnormed_zero * normed[0])
    )
    share_tiles(11, early_all, early_sum, early, 0)
    dmessage_weight = mm(jnp.concatenate([m_low, m_high], axis=0), normed[0], NT)
    for r in range(4):
        for half in range(2):
            late_own[2 * r + half] = dmessage_weight[
                8 * r : 8 * (r + 1), 128 * half : 128 * (half + 1)
            ]
    scatter_tiles(13, late_own, late_all, late, late_base)
    plane_back()
    mix_zero, _ = feature_back(0, 8, 3, dnormed_zero, scale_zero)
    share_tiles(13, late_all, late_sum, late, late_base)

    moved_zero, dtables = shell_back_kinds()
    fold_c = (iota((PADDED, 96), 0) == (iota((PADDED, 96), 1) & 15)).astype(F32)
    d_of = iota((72, 128), 0) - 12 * ((iota((72, 128), 0) * 5462) >> 16)
    seat_mix = [(iota((72, 128), 1) == d_of + 12 * layer).astype(F32) for layer in range(2)]
    seat_kind = [
        ((iota((8, 128), 1) == row8 + 24 + 2 * layer) & (row8 < 2)).astype(F32)
        for layer in range(2)
    ]
    final = mm(mm(fold_c, mix_zero), seat_mix[0]) + mm(mm(fold_c, mix_one), seat_mix[1])
    final = final + mm(dtable_one, seat_kind[1])
    for k in range(2):
        total = jnp.sum(dtables[k], axis=1, keepdims=True)
        final = final + jnp.where(iota((PADDED, 128), 1) == 24 + k, total, 0.0)
    final_own[...] = final[0:8] + pltpu.roll(final[8:16], 32, 1)
    everyone(lambda device, _: push(10, final_own, final_all.at[me], device))
    final_all[me] = final_own[...]
    plane_back_kinds()
    product_back_kinds()
    slopes_zero = coordinate_back_kinds()
    pull_of = pulls[...]
    to_own = mm(sender_rows[...], pull_of)
    to_sender = mm(own, pull_of, NT)
    force_own[...] = jnp.zeros_like(force_own)
    for q in range(tiles):
        spot = slice(128 * q, 128 * (q + 1))
        weight_row = to_sender[5:6, spot]
        for axis in range(3):
            value = -2.0 * (to_sender[2 + axis : 3 + axis, spot] + sender_rows[2 + axis : 3 + axis, spot] * weight_row)
            value = value - slopes_zero[q][axis] - slopes_one[q][axis]
            force_own[2 * q, axis : axis + 1, :] = value
            force_own[2 * q + 1, axis : axis + 1, :] = pltpu.roll(value, BLOCK, 1)
    members(lambda device, target: push(9, force_own.at[target], force_all.at[col], device))
    force_all[col] = force_own[col]
    own_force = []
    for axis in range(3):
        pairwise = 2.0 * (to_own[2 + axis : 3 + axis] + own[2 + axis : 3 + axis] * to_own[5:6])
        moved = jnp.sum(moved_zero[axis] + moved_one[axis], axis=0, keepdims=True)
        both = pairwise + moved
        own_force.append(both + pltpu.roll(both, BLOCK, 1))

    gather_tiles(11, early_sum, early, 0)
    pick_ones = ((iota((8, FEATURE_ROWS), 0) == 0) & (iota((8, FEATURE_ROWS), 1) == ONES_ROW)).astype(F32)
    for layer in range(2):
        total = None
        for parity in range(2):
            rows = []
            for r in range(3):
                at = 12 * layer + 6 * parity + 2 * r
                rows.append(jnp.concatenate([early_sum[at], early_sum[at + 1]], axis=1))
            block = jnp.concatenate(rows, axis=0)
            if parity == 0:
                hidden_bias_out[layer : layer + 1, :] = mm(pick_ones, block, NT)[0:1]
            part = mm(block, select[parity])
            total = part if total is None else total + part
        hidden_weight_out[layer] = total
    small_sum = jnp.concatenate([early_sum[24 + r] for r in range(4)], axis=0)
    for layer in range(2):
        inner_weight_out[layer] = small_sum[0:INNER, 32 * layer : 32 * layer + HIDDEN]
        pick = ((row8 == 0) & (lane == 32 * layer + HIDDEN)).astype(F32)
        flat = mm(pick, small_sum, NT)
        inner_bias_out[layer : layer + 1, :] = flat[0:1, 0:INNER]
        energy_weight_out[layer : layer + 1, :] = flat[0:1, INNER : 2 * INNER]
    gather_tiles(13, late_sum, late, late_base)
    total = None
    for parity in range(2):
        rows = [
            jnp.concatenate([late_sum[4 * parity + 2 * r], late_sum[4 * parity + 2 * r + 1]], axis=1)
            for r in range(2)
        ]
        part = mm(jnp.concatenate(rows, axis=0), select[parity])
        total = part if total is None else total + part
    message_weight_out[...] = total[0:CHANNELS]

    await_bytes(final_all, devices - 1, recv_sem.at[10])
    final = final_all[0]
    for k in range(1, devices):
        final = final + final_all[k]
    final = jnp.concatenate([final, pltpu.roll(final, 96, 1)], axis=0)
    dembedding = None
    for layer in range(2):
        channel_mix_out[:, layer, :] = final[0:CHANNELS, 12 * layer : 12 * (layer + 1)]
        dtable = final[0:CHANNELS, 24 + 2 * layer : 26 + 2 * layer]
        channel_in_out[layer] = lax.dot_general(
            embedding[...],
            dtable,
            (((0,), (1,)), ((), ())),
            precision=lax.Precision.HIGHEST,
            preferred_element_type=F32,
        )
        part = lax.dot_general(
            dtable,
            channel_in[layer],
            (((0,), (1,)), ((), ())),
            precision=lax.Precision.HIGHEST,
            preferred_element_type=F32,
        )
        dembedding = part if dembedding is None else dembedding + part
    embedding_out[...] = dembedding

    await_bytes(force_all, lanes - 1, recv_sem.at[9])
    force = force_all[0]
    for k in range(1, lanes):
        force = force + force_all[k]
    for axis in range(3):
        position_out[axis] = (force[axis : axis + 1] + own_force[axis])[:, 0:BLOCK]

    await_bytes(pack_all, lanes - 1, send_sem.at[0])
    await_bytes(send_all, lanes - 1, send_sem.at[1])
    await_bytes(recv_all, lanes - 1, send_sem.at[2])
    await_bytes(stat_all.at[0], devices - 1, send_sem.at[3])
    await_bytes(message_all, lanes - 1, send_sem.at[4])
    await_bytes(stat_all.at[1], devices - 1, send_sem.at[5])
    await_bytes(stat_all.at[2], devices - 1, send_sem.at[6])
    await_bytes(dmessage_all, lanes - 1, send_sem.at[7])
    await_bytes(stat_all.at[3], devices - 1, send_sem.at[8])
    await_bytes(force_all, lanes - 1, send_sem.at[9])
    await_bytes(final_all, devices - 1, send_sem.at[10])
    drain_tiles(11, early_all, early_sum, early, 0)
    drain_tiles(13, late_all, late_sum, late, late_base)


def hand_over(*refs):
    for source, target in zip(refs[:11], refs[11:]):
        target[...] = source[...]


def solution(mesh):
    lanes = mesh.shape["edge"]
    structs = mesh.shape["struct"]
    devices = lanes * structs

    def step(
        positions,
        species,
        struct_id,
        atom_mask,
        senders,
        receivers,
        edge_mask,
        energy_cot,
        embedding,
        channel_in,
        channel_mix,
        hidden_weight,
        hidden_bias,
        inner_weight,
        inner_bias,
        energy_weight,
        message_weight,
    ):
        owned = positions.shape[2]
        group = owned * lanes
        edges = senders.shape[1]
        early, late = 28, 8
        vmem = pltpu.VMEM
        shapes = [
            (1, STRUCTS),
            (3, 1, owned),
            embedding.shape,
            channel_in.shape,
            (CHANNELS, 2, CHANNELS),
            (2, HIDDEN, FEATURES),
            hidden_bias.shape,
            (2, INNER, HIDDEN),
            inner_bias.shape,
            energy_weight.shape,
            (CHANNELS, FEATURES),
        ]
        scratch = [
            vmem((8, 128), F32),
            vmem((lanes, 8, 128), F32),
            vmem((lanes, 1, edges), I32),
            vmem((1, edges), I32),
            vmem((lanes, 1, edges), I32),
            vmem((2, 128, BLOCK * (group // 256)), F32),
            vmem((group, 128), F32),
            vmem((group, 8), F32),
            vmem((8, group), F32),
            vmem((PAIRS, group, 128), F32),
            vmem((group, 128), F32),
            vmem((4, group, 128 * PAIRS), F32),
            vmem((4, group, 128 * PAIRS), F32),
            vmem((group, 128), F32),
            vmem((PADDED, group), F32),
            vmem((PADDED * 20, group), F32),
            vmem((PADDED * SHELLS, 128 * PAIRS), F32),
            vmem((PADDED * SHELLS, 128 * PAIRS), F32),
            vmem((40, group), F32),
            vmem((240, group), BF16),
            vmem((4, 40, 128 * PAIRS), F32),
            vmem((4, 40, 128 * PAIRS), F32),
            vmem((40, group), F32),
            vmem((PADDED * 20, group), F32),
            vmem((2, PAIRS, 96, 128), F32),
            vmem((PAIRS, 96, 128), F32),
            vmem((2, FEATURE_ROWS, 128), F32),
            vmem((2, FEATURE_ROWS, 128), F32),
            vmem((2, FEATURE_ROWS, FEATURES), F32),
            vmem((2, 2 * HEAD_ROWS, FEATURE_ROWS), F32),
            vmem((2, FEATURE_ROWS, 2 * HEAD_ROWS), F32),
            vmem((4, 8, 128), F32),
            vmem((4, devices, 8, 128), F32),
            vmem((8, 128), F32),
            vmem((lanes, 8, 128), F32),
            vmem((lanes, 8, 128), F32),
            vmem((lanes, 8, 128), F32),
            vmem((lanes, 8, 128), F32),
            vmem((lanes, 8, 128), F32),
            vmem((8, 128), F32),
            vmem((devices, 8, 128), F32),
            vmem((early, 8, 128), F32),
            vmem((devices, 8, 128), F32),
            vmem((early, 8, 128), F32),
            vmem((late, 8, 128), F32),
            vmem((devices, 8, 128), F32),
            vmem((late, 8, 128), F32),
            pltpu.SemaphoreType.DMA((16,)),
            pltpu.SemaphoreType.DMA((16,)),
        ]
        outs = pl.pallas_call(
            functools.partial(body, lanes, structs),
            out_shape=[jax.ShapeDtypeStruct(s, F32) for s in shapes],
            in_specs=[pl.BlockSpec(memory_space=vmem)] * 17,
            out_specs=[pl.BlockSpec(memory_space=vmem)] * 11,
            scratch_shapes=scratch,
            compiler_params=pltpu.CompilerParams(
                collective_id=0, has_side_effects=True, vmem_limit_bytes=60 * 1024 * 1024
            ),
        )(
            positions,
            species,
            struct_id,
            atom_mask,
            senders,
            receivers,
            edge_mask,
            energy_cot,
            embedding,
            channel_in,
            jnp.transpose(channel_mix, (1, 0, 2)),
            jnp.transpose(hidden_weight, (0, 2, 1)),
            hidden_bias,
            jnp.transpose(inner_weight, (0, 2, 1)),
            inner_bias,
            energy_weight,
            jnp.transpose(message_weight),
        )
        outs = pl.pallas_call(
            hand_over,
            out_shape=[jax.ShapeDtypeStruct(s, F32) for s in shapes],
            in_specs=[pl.BlockSpec(memory_space=vmem)] * 11,
            out_specs=[pl.BlockSpec(memory_space=vmem)] * 11,
        )(*outs)
        outs = list(outs)
        outs[4] = jnp.transpose(outs[4], (1, 0, 2))
        outs[5] = jnp.transpose(outs[5], (0, 2, 1))
        outs[7] = jnp.transpose(outs[7], (0, 2, 1))
        outs[10] = jnp.transpose(outs[10])
        return tuple(outs)

    tiled = P("struct", "edge")
    return jax.shard_map(
        step,
        mesh=mesh,
        in_specs=(
            P(None, "struct", "edge"),
            tiled,
            tiled,
            tiled,
            tiled,
            tiled,
            tiled,
            P("struct", None),
        )
        + (P(),) * 9,
        out_specs=(P("struct", None), P(None, "struct", "edge")) + (P(),) * 9,
        check_vma=False,
    )
```

```python
import functools
import math

import jax
import jax.numpy as jnp
import numpy as np
from jax import lax
from jax.experimental import pallas as pl
from jax.experimental.pallas import tpu as pltpu
from jax.sharding import PartitionSpec as P

CHANNELS = 12
PADDED = 16
RADIALS = 6
PAIRS = 3
STRUCTS = 8
HIDDEN = 24
INNER = 16
FEATURES = 432
HEAD_ROWS = 40
FEATURE_ROWS = 256
ONES_ROW = 216
BLOCK = 64

cutoff_radius = 6.0
variance_eps = 1e-05
center = 1.5

MESH = pl.DeviceIdType.MESH
F32 = jnp.float32
BF16 = jnp.bfloat16
I32 = jnp.int32
NN = ((1,), (0,))
NT = ((1,), (1,))
TN = ((0,), (0,))

MONOMIALS = sorted(
    [(a, b, c) for a in range(4) for b in range(4) for c in range(4) if a + b + c <= 3],
    key=lambda m: (sum(m), -m[0], -m[1], -m[2]),
)
PLACE = {m: i for i, m in enumerate(MONOMIALS)}
COUNTS = [1, 4, 10, 20]
OFFSETS = [0, 1, 5, 15]
SHELLS = 35
DEGREE_ROWS = [0, 16, 56, 128, 248]
ROW_OF = [
    DEGREE_ROWS[sum(m)] + CHANNELS * (i - (0, 1, 4, 10)[sum(m)]) for i, m in enumerate(MONOMIALS)
]
PRODUCT_ROWS = 256
LANE_TILES = [(3, 0), (3, 1), (3, 2), (2, 2), (2, 0), (2, 1), (1, 0), (1, 1), (1, 2), (0, 2), (0, 0), (0, 1)]
GROUPS = [(3, 0, 4), (2, 4, 6), (1, 6, 10), (0, 10, 12)]
PLANE_LANES = 128 * len(LANE_TILES)


def tile_of(order, pair):
    at = LANE_TILES.index((order, pair))
    return slice(128 * at, 128 * (at + 1))


RADIX = 4096.0


def fitted(function, low, high, degree):
    series = np.polynomial.chebyshev.Chebyshev.interpolate(
        lambda w: function(0.5 * (high - low) * w + 0.5 * (high + low)), degree
    )
    return [float(v) for v in series.convert(kind=np.polynomial.Polynomial).coef]


LOW, HIGH = 0.9, 28.1
ANGLE = math.pi / cutoff_radius
SINE = fitted(lambda u: np.sin(ANGLE * np.sqrt(u)) / np.sqrt(u), LOW, HIGH, 9)
COSINE = fitted(lambda u: np.cos(ANGLE * np.sqrt(u)), LOW, HIGH, 9)
NORM = math.sqrt(2.0 / cutoff_radius)


def mm(left, right, kind=NN, precision=lax.Precision.HIGHEST):
    return lax.dot_general(
        left, right, (kind, ((), ())), precision=precision, preferred_element_type=F32
    )


def once(left, right, kind=NN):
    return lax.dot_general(left, right, (kind, ((), ())), preferred_element_type=F32)


def parts(value):
    high = value.astype(BF16).astype(F32)
    rest = value - high
    middle = rest.astype(BF16).astype(F32)
    return high, middle, rest - middle


def stack_left(value):
    high, middle, tail = parts(value)
    return jnp.concatenate([high, high, middle, high, tail, middle], axis=0).astype(BF16)


def stack_right(value):
    high, middle, tail = parts(value)
    return jnp.concatenate([high, middle, high, tail, high, middle], axis=0).astype(BF16)


def stacked(left, right):
    return once(left, stack_right(right), TN)


def three_rows(value):
    return jnp.concatenate(parts(value), axis=0).astype(BF16)


def exact(left, right, kind=NN):
    rows = left.shape[0]
    out = once(three_rows(left), right, kind)
    return out[0:rows] + (out[rows : 2 * rows] + out[2 * rows :])


def loop(count, action, carry):
    if count <= 8:
        for i in range(count):
            carry = action(i, carry)
        return carry
    return lax.fori_loop(0, count, action, carry)


def aligned(value, size):
    return value if isinstance(value, int) else pl.multiple_of(value, size)


def iota(shape, dim):
    return lax.broadcasted_iota(I32, shape, dim)


def horner(coefficients, w):
    total = jnp.full_like(w, coefficients[-1])
    for value in coefficients[-2::-1]:
        total = total * w + value
    return total


def shifted(terms, order, x, y, z):
    current = terms
    for axis, value in enumerate((x, y, z)):
        two, three = 2.0 * value, 3.0 * value
        square = value * value
        three_square, cube = 3.0 * square, square * value
        factors = [None, [value], [square, two], [cube, three_square, three]]
        fresh = {}
        for m in MONOMIALS[: COUNTS[order]]:
            if axis == 2 and sum(m) != order:
                continue
            power = m[axis]
            total = current[m]
            for lower in range(power):
                source = m[:axis] + (lower,) + m[axis + 1 :]
                total = total + factors[power][lower] * current[source]
            fresh[m] = total
        current = fresh
    return current


def invariants(terms, x, y, z):
    by_order = []
    for order in range(4):
        own = {m: terms[OFFSETS[order] + i] for i, m in enumerate(MONOMIALS[: COUNTS[order]])}
        by_order.append(shifted(own, order, x, y, z) if order else own)
    scalar = by_order[0][(0, 0, 0)]
    vx, vy, vz = by_order[1][(1, 0, 0)], by_order[1][(0, 1, 0)], by_order[1][(0, 0, 1)]
    m = by_order[2]
    xx, xy, xz = m[(2, 0, 0)], m[(1, 1, 0)], m[(1, 0, 1)]
    yy, yz, zz = m[(0, 2, 0)], m[(0, 1, 1)], m[(0, 0, 2)]
    q = by_order[3]
    xxx, yyy, zzz = q[(3, 0, 0)], q[(0, 3, 0)], q[(0, 0, 3)]
    xxy, xxz, xyy = q[(2, 1, 0)], q[(2, 0, 1)], q[(1, 2, 0)]
    xyz, xzz, yyz, yzz = q[(1, 1, 1)], q[(1, 0, 2)], q[(0, 2, 1)], q[(0, 1, 2)]
    first = vx * vx + vy * vy + vz * vz
    second = xx * xx + yy * yy + zz * zz + 2.0 * (xy * xy + xz * xz + yz * yz)
    third = (
        xxx * xxx
        + yyy * yyy
        + zzz * zzz
        + 3.0 * (xxy * xxy + xxz * xxz + xyy * xyy + xzz * xzz + yyz * yyz + yzz * yzz)
        + 6.0 * (xyz * xyz)
    )
    fourth = (
        vx * (xx * vx + xy * vy + xz * vz)
        + vy * (xy * vx + yy * vy + yz * vz)
        + vz * (xz * vx + yz * vy + zz * vz)
    )
    xy2, xz2, yz2 = 2.0 * xy, 2.0 * xz, 2.0 * yz
    fifth = (
        vx * (xxx * xx + xyy * yy + xzz * zz + xxy * xy2 + xxz * xz2 + xyz * yz2)
        + vy * (xxy * xx + yyy * yy + yzz * zz + xyy * xy2 + xyz * xz2 + yyz * yz2)
        + vz * (xxz * xx + yyz * yy + zzz * zz + xyz * xy2 + xzz * xz2 + yzz * yz2)
    )
    return (scalar, first, second, third, fourth, fifth)


def silu_pair(v):
    gate = 1.0 / (1.0 + jnp.exp(-v))
    return v * gate, gate * (1.0 + v * (1.0 - gate))


class Geometry:
    def __init__(self, columns, own, lane_low):
        dx = own[2:3] + columns[:, 2:3]
        dy = own[3:4] + columns[:, 3:4]
        dz = own[4:5] + columns[:, 4:5]
        self.u = dx * dx + dy * dy + dz * dz + 1.0
        w = (self.u - 0.5 * (LOW + HIGH)) * (2.0 / (HIGH - LOW))
        self.sine = horner(SINE, w)
        self.cosine = horner(COSINE, w)
        self.inverse = lax.rsqrt(self.u)
        self.reach = 1.0 - self.u * (1.0 / (cutoff_radius * cutoff_radius))
        self.lane_low = lane_low

    def sines(self):
        step = 2.0 * (2.0 * self.cosine * self.cosine - 1.0)
        before = jnp.where(self.lane_low, -self.sine, 0.0)
        now = jnp.where(self.lane_low, self.sine, 2.0 * self.cosine * self.sine)
        return self.series(step, before, now)

    def cosines(self):
        double = 2.0 * self.cosine * self.cosine - 1.0
        before = jnp.where(self.lane_low, self.cosine, 1.0)
        now = jnp.where(self.lane_low, self.cosine, double)
        return self.series(2.0 * double, before, now)

    def series(self, step, before, now):
        out = [now]
        for _ in range(PAIRS - 1):
            before, now = now, step * now - before
            out.append(now)
        return out


def body(lanes, structs, *refs):
    sources, held, refs = refs[:17], refs[-17:], refs[17:-17]
    (
        positions,
        species,
        struct_id,
        atom_mask,
        senders,
        receivers,
        edge_mask,
        energy_cot,
        embedding,
        channel_in,
        channel_mix,
        hidden_weight,
        hidden_bias,
        inner_weight,
        inner_bias,
        energy_weight,
        message_weight,
    ) = held
    (
        energies_out,
        position_out,
        embedding_out,
        channel_in_out,
        channel_mix_out,
        hidden_weight_out,
        hidden_bias_out,
        inner_weight_out,
        inner_bias_out,
        energy_weight_out,
        message_weight_out,
        pack,
        pack_all,
        send_all,
        masked_recv,
        recv_all,
        counts,
        pair_weight,
        columns,
        sender_rows,
        radial,
        inverse,
        planes_high,
        planes_low,
        slopes,
        pulls,
        weights,
        products,
        product_three,
        product_two,
        sums,
        dsums,
        kind_products,
        kind_three,
        kind_stack,
        kind_sums,
        dkind_sums,
        dkind_products,
        dproducts,
        invariant,
        dinvariant,
        feats,
        normed,
        select,
        head,
        head_rows,
        head_stack,
        message_stack,
        inner_forward,
        inner_back,
        mix_stack,
        mix_back,
        stat_own,
        stat_all,
        message_own,
        message_all,
        dmessage_own,
        dmessage_all,
        force_own,
        force_all,
        final_own,
        final_all,
        tiles_a,
        tiles_a_all,
        tiles_a_sum,
        tiles_b,
        tiles_b_all,
        tiles_b_sum,
        tiles_c,
        tiles_c_all,
        tiles_c_sum,
        send_sem,
        recv_sem,
        input_sem,
    ) = refs
    devices = lanes * structs
    edge_count = senders.shape[1]
    inputs = [
        pltpu.make_async_copy(source, target, input_sem.at[i])
        for i, (source, target) in enumerate(zip(sources, held))
    ]
    for one_input in inputs:
        one_input.start()
    group = pair_weight.shape[0]
    tiles = group // 128
    strips = [slice(k, k + 512) for k in range(0, group, 512)]
    row = lax.axis_index("struct")
    col = lax.axis_index("edge")
    me = row * lanes + col

    def everyone(action):
        def one(k, carry):
            target = lax.rem(me + k, devices)
            action((target // lanes, lax.rem(target, lanes)), target)
            return carry

        if devices <= 32:
            for k in range(1, devices):
                one(k, 0)
        else:
            lax.fori_loop(1, devices, one, 0)

    def members(action):
        def one(k, carry):
            target = lax.rem(col + k, lanes)
            action((row, target), target)
            return carry

        if lanes <= 8:
            for k in range(1, lanes):
                one(k, 0)
        else:
            lax.fori_loop(1, lanes, one, 0)

    def push(phase, source, target, device):
        pltpu.make_async_remote_copy(
            src_ref=source,
            dst_ref=target,
            send_sem=send_sem.at[phase],
            recv_sem=recv_sem.at[phase],
            device_id=device,
            device_id_type=MESH,
        ).start()

    def await_bytes(buffer, count, sem):
        if count:
            view = buffer.at[pl.ds(0, count)]
            pltpu.make_async_copy(view, view, sem).wait()

    barrier = pltpu.get_barrier_semaphore()
    everyone(
        lambda device, _: pl.semaphore_signal(
            barrier, inc=1, device_id=device, device_id_type=MESH
        )
    )

    for one_input in inputs[:7]:
        one_input.wait()
    pack[...] = jnp.ones_like(pack)
    masked_recv[...] = jnp.where(edge_mask[...] > 0, receivers[...], -1)
    kind = species[...]
    for half in (0, BLOCK):
        spot = pl.ds(half, BLOCK)
        pack[0:1, spot] = (kind == 0).astype(F32)
        pack[1:2, spot] = (kind == 1).astype(F32)
        for axis in range(3):
            pack[2 + axis : 3 + axis, spot] = center - positions[axis]
        pack[6:7, spot] = atom_mask[...].astype(F32)
        pack[7:8, spot] = struct_id[...].astype(F32)
    pl.semaphore_wait(barrier, devices - 1)

    members(lambda device, _: push(0, pack, pack_all.at[col], device))
    members(lambda device, _: push(1, senders, send_all.at[col], device))
    members(lambda device, _: push(2, masked_recv, recv_all.at[col], device))
    pack_all[col] = pack[...]
    send_all[col] = senders[...]
    recv_all[col] = masked_recv[...]

    for one_input in inputs[7:]:
        one_input.wait()
    lane = iota((8, 128), 1)
    low_row = lane[0:1] < BLOCK
    low = lane < BLOCK
    row8 = iota((8, 128), 0)
    own = pack[...] * jnp.where((row8 >= 2) & (row8 <= 4), -1.0, 1.0)
    live = own[6:7]
    first_rows = iota((16, 128), 0)
    lane_half = (iota((16, 128), 1) >= BLOCK).astype(I32)
    half_sum = (first_rows == lane_half).astype(F32)
    wide_lane = iota((8, 512), 1)
    spot_of = 2 * (wide_lane >> 7) + ((wide_lane & 127) >= BLOCK).astype(I32)
    half_pick = (iota((8, 512), 0) == spot_of).astype(F32)
    half_pick = jnp.concatenate([half_pick] * 3 + [jnp.zeros((8, 512), F32)], axis=0).astype(BF16)

    mix_pd = (iota((72, CHANNELS), 0) - 12 * ((iota((72, CHANNELS), 0) * 5462) >> 16)) == iota(
        (72, CHANNELS), 1
    )
    mix_pd = mix_pd.astype(F32)
    mix_pc = ((iota((96, CHANNELS), 0) & 15) == iota((96, CHANNELS), 1)).astype(F32)
    same = ((iota((96, 72), 0) >> 4) == ((iota((96, 72), 1) * 5462) >> 16)).astype(F32)
    same_t = ((iota((72, 96), 1) >> 4) == ((iota((72, 96), 0) * 5462) >> 16)).astype(F32)
    for layer in range(2):
        table = channel_mix[:, layer, :]
        spread_c = mm(mix_pc, table)
        mix_back[layer] = stack_left(mm(mm(mix_pd, table, NT), mix_pc, NT) * same_t)
        mix_stack[layer] = stack_left(mm(spread_c, mix_pd, NT) * same)

    struct_rows = own[7:8].astype(I32)
    member = (struct_rows == iota((STRUCTS, 128), 0)).astype(F32)
    atom_cot = mm(energy_cot[...], member) * live
    counts[...] = jnp.zeros_like(counts)
    chunk = min(2048, edge_count)
    per_slot = edge_count // chunk
    wide = counts.shape[2]

    def count_edges(send, recv):
        local = recv - col * BLOCK
        inside = (local >= 0) & (local < BLOCK)
        key = jnp.where(inside, (send >> 8) * BLOCK + local, -1)
        step = jnp.where((send & 128) > 0, RADIX, 1.0)
        sender_hot = jnp.where(iota((128, chunk), 0) == (send & 127), step, 0.0).astype(BF16)
        pair_hot = jnp.where(iota((wide, chunk), 0) == key, 1.0, 0.0).astype(BF16)
        found = once(sender_hot, pair_hot, NT)
        upper = jnp.floor(found * (1.0 / RADIX))
        counts[0] += found - RADIX * upper
        counts[1] += upper

    def count_slot(slot, carry):
        for k in range(per_slot):
            spot = slice(k * chunk, (k + 1) * chunk)
            count_edges(send_all[slot, :, spot], recv_all[slot, :, spot])
        return carry

    count_slot(col, 0)

    await_bytes(pack_all, lanes - 1, recv_sem.at[0])
    for q in range(tiles):
        sender_rows[:, 128 * q : 128 * (q + 1)] = jnp.where(low, pack_all[2 * q], pack_all[2 * q + 1])
    columns[...] = jnp.transpose(sender_rows[...])

    def geometry(start):
        cols = columns[pl.ds(start, BLOCK), :]
        return Geometry(cols, own, low_row)

    def radial_block(i, carry):
        start = aligned(i * BLOCK, BLOCK)
        geo = geometry(start)
        envelope = geo.reach * geo.reach * NORM
        for pair, value in enumerate(geo.sines()):
            radial[pair, pl.ds(start, BLOCK), :] = value * envelope
        inverse[pl.ds(start, BLOCK), :] = geo.inverse
        return carry

    loop(group // BLOCK, radial_block, 0)

    def monomial_rows(rows):
        x, y, z = rows[2:3], rows[3:4], rows[4:5]
        table = {(0, 0, 0): None}
        for m in MONOMIALS[1:]:
            axis = next(i for i in range(3) if m[i])
            lower = m[:axis] + (m[axis] - 1,) + m[axis + 1 :]
            factor = (x, y, z)[axis]
            table[m] = factor if table[lower] is None else table[lower] * factor
        return table

    def spread():
        def one(q, carry):
            spot = pl.ds(aligned(q * 128, 128), 128)
            table = monomial_rows(sender_rows[:, spot])
            h = weights[0:CHANNELS, spot]
            for i, m in enumerate(MONOMIALS):
                products[ROW_OF[i] : ROW_OF[i] + CHANNELS, spot] = h if table[m] is None else h * table[m]
            return carry

        loop(tiles, one, 0)
        for q in strips:
            split = parts(products[:, q])
            three, two = [], []
            for start, end in zip(DEGREE_ROWS, DEGREE_ROWS[1:]):
                three += [v[start:end] for v in split]
                two += [v[start:end] for v in split[:2]]
            three.append(jnp.zeros((8, three[0].shape[1]), F32))
            product_three[:, q] = jnp.concatenate(three, axis=0).astype(BF16)
            product_two[:, q] = jnp.concatenate(two, axis=0).astype(BF16)

    dkind_sums[...] = jnp.zeros_like(dkind_sums)
    dsums[...] = jnp.zeros_like(dsums)
    products[...] = jnp.zeros_like(products)

    def kind_spread(q, carry):
        spot = pl.ds(aligned(q * 128, 128), 128)
        table = monomial_rows(sender_rows[:, spot])
        kinds = sender_rows[0:2, spot]
        for i, m in enumerate(MONOMIALS):
            kind_products[2 * i : 2 * i + 2, spot] = kinds if table[m] is None else kinds * table[m]
        return carry

    loop(tiles, kind_spread, 0)
    for q in strips:
        kind_parts = jnp.concatenate(parts(kind_products[:, q]), axis=0)
        blank_rows = jnp.zeros((8, kind_parts.shape[1]), F32)
        kind_three[:, q] = jnp.concatenate([kind_parts, blank_rows], axis=0).astype(BF16)
    columns_of = []
    for kind_of in range(2):
        embedded = mm(embedding[...], (iota((2, 128), 0) == kind_of).astype(F32), TN)
        padded = jnp.concatenate(
            [mm(channel_in[0], embedded, TN), jnp.zeros((PADDED - CHANNELS, 128), F32)], axis=0
        )
        columns_of.append([padded[0:8], padded[8:16]])

    await_bytes(send_all, lanes - 1, recv_sem.at[1])
    await_bytes(recv_all, lanes - 1, recv_sem.at[2])
    if devices <= 32:
        for k in range(1, lanes):
            count_slot(lax.rem(col + k, lanes), 0)
    else:
        lax.fori_loop(1, lanes, lambda k, carry: count_slot(lax.rem(col + k, lanes), carry), 0)
    low_tall = iota((128, 128), 1) < BLOCK
    for block in range(group // 128):
        turn_of = block // 2
        piece = counts[block % 2, :, 128 * (turn_of // 2) : 128 * (turn_of // 2 + 1)]
        turned = pltpu.roll(piece, BLOCK, 1)
        first_half, second_half = (piece, turned) if turn_of % 2 == 0 else (turned, piece)
        pair_weight[128 * block : 128 * (block + 1), :] = jnp.where(
            low_tall, first_half, second_half
        )

    def plane_block(i, carry):
        spot = pl.ds(aligned(i * BLOCK, BLOCK), BLOCK)
        weight = pair_weight[spot, :]
        step = inverse[spot, :]
        for pair in range(PAIRS):
            value = radial[pair, spot, :] * weight
            for order in range(4):
                high = value.astype(BF16)
                planes_high[spot, tile_of(order, pair)] = high
                planes_low[spot, tile_of(order, pair)] = (value - high.astype(F32)).astype(BF16)
                value = value * step
        return carry

    loop(group // BLOCK, plane_block, 0)

    xi, yi, zi = (jnp.broadcast_to(own[r : r + 1], (8, 128)) for r in (2, 3, 4))

    def chunk_spots(i):
        pair, tile = i // 2, i % 2
        return pair, tile, slice(128 * pair, 128 * (pair + 1))

    def kind_terms(pair):
        out = []
        for order in range(4):
            spot = tile_of(order, pair)
            for m in range(COUNTS[order]):
                out.append(
                    [
                        jnp.broadcast_to(kind_sums[2 * m + k : 2 * m + k + 1, spot], (8, 128))
                        for k in range(2)
                    ]
                )
        return out

    def shell_terms(pair, tile):
        out = []
        for order in range(4):
            spot = tile_of(order, pair)
            for m in range(COUNTS[order]):
                start = ROW_OF[m] + 8 * tile
                out.append(sums[start : start + 8, spot])
        return out

    def live_rows(value, tile):
        return value if tile == 0 else jnp.where(row8 < CHANNELS - 8, value, 0.0)

    def mix_invariants(layer):
        mixed = stacked(mix_stack[layer], invariant[layer])
        for pair in range(PAIRS):
            feats[layer, 72 * pair : 72 * (pair + 1), :] = mixed[:, 128 * pair : 128 * (pair + 1)]

    def forward_kinds():
        by_high = once(kind_three[...], planes_high[...])
        by_low = once(kind_three[0:80, :], planes_low[...])
        kind_sums[...] = by_high[0:40] + ((by_high[40:80] + by_low[0:40]) + (by_high[80:120] + by_low[40:80]))
        for pair in range(PAIRS):
            both = kind_terms(pair)
            for tile in range(2):
                terms = [columns_of[0][tile] * a + columns_of[1][tile] * b for a, b in both]
                for p, value in enumerate(invariants(terms, xi, yi, zi)):
                    start = PADDED * p + 8 * tile
                    invariant[0, start : start + 8, 128 * pair : 128 * (pair + 1)] = value
        mix_invariants(0)

    def forward():
        for order, first, last in GROUPS:
            spot = slice(128 * first, 128 * last)
            end = DEGREE_ROWS[order + 1]
            by_high = once(product_three[0 : -(-3 * end // 16) * 16, :], planes_high[:, spot])
            by_low = once(product_two[0 : 2 * end, :], planes_low[:, spot])
            for start, stop in zip(DEGREE_ROWS[: order + 1], DEGREE_ROWS[1:]):
                size = stop - start
                h, l = 3 * start, 2 * start
                sums[start:stop, spot] = by_high[h : h + size] + (
                    (by_high[h + size : h + 2 * size] + by_low[l : l + size])
                    + (by_high[h + 2 * size : h + 3 * size] + by_low[l + size : l + 2 * size])
                )
        for i in range(2 * PAIRS):
            pair, tile, spot = chunk_spots(i)
            terms = shell_terms(pair, tile)
            for p, value in enumerate(invariants(terms, xi, yi, zi)):
                start = PADDED * p + 8 * tile
                invariant[1, start : start + 8, spot] = live_rows(value, tile)
        mix_invariants(1)

    def send_stats(phase, index, select_rows, first, second, extra=None):
        values = jnp.concatenate([first, second], axis=0)
        wide_values = jnp.concatenate(parts(values), axis=1).astype(BF16)
        rows = jnp.concatenate([select_rows] * 3, axis=1).astype(BF16)
        both = once(rows, wide_values, NT)
        for k in range(4):
            stat_own[index, 2 * k : 2 * k + 2, :] = both[0:2, 128 * k : 128 * (k + 1)]
        if extra is not None:
            stat_own[index, 2:3, 96 : 96 + STRUCTS] = extra
        everyone(
            lambda device, _: push(phase, stat_own.at[index], stat_all.at[index, me], device)
        )
        stat_all[index, me] = stat_own[index]

    def get_stats(phase, index):
        await_bytes(stat_all.at[index], devices - 1, recv_sem.at[phase])
        sums_of = [stat_all[index, k] for k in range(8)]
        for k in range(8, devices):
            sums_of[k % 8] = sums_of[k % 8] + stat_all[index, k]
        while len(sums_of) > 1:
            sums_of = [a + b for a, b in zip(sums_of[::2], sums_of[1::2])]
        return sums_of[0]

    def widen(rows):
        return once(
            jnp.concatenate([three_rows(rows), jnp.zeros((8, 128), BF16)], axis=0), half_pick, TN
        )

    rest_rows = ONES_ROW - 128

    def tall(wide, start):
        return jnp.concatenate(
            [wide[:, start : start + 128], wide[0:rest_rows, start + 128 : start + 256]], axis=0
        )

    ones_rows = iota((FEATURE_ROWS - ONES_ROW, 128), 0) == 0
    for layer in range(2):
        feats[layer, ONES_ROW:FEATURE_ROWS, :] = ones_rows.astype(F32)
        normed[layer, ONES_ROW:FEATURE_ROWS, :] = ones_rows.astype(F32)

    def send_moments(layer, phase):
        values = feats[layer]
        send_stats(phase, layer, half_sum * live, values, values * values)

    def normalise(layer, phase):
        total = get_stats(phase, layer)
        inverse_count = 1.0 / jnp.maximum(total[2:3, ONES_ROW - 128 : ONES_ROW - 127], 1.0)
        scaled = total * inverse_count
        means = pltpu.roll(scaled, 4, 0)
        scales = lax.rsqrt(scaled - means * means + variance_eps)
        wide = widen(jnp.where(row8 < 4, scaled, scales))
        scale = tall(wide, 256)
        normed[layer, 0:ONES_ROW, :] = (feats[layer, 0:ONES_ROW, :] - tall(wide, 0)) * scale
        rows = 2 * HEAD_ROWS
        high, middle, tail = (v.astype(BF16) for v in parts(normed[layer]))
        by_high = once(head_rows[layer], high)
        by_middle = once(head_rows[layer, 0 : 2 * rows, :], middle)
        by_tail = once(head_rows[layer, 0:rows, :], tail)
        joined = by_high[0:rows] + (
            (by_high[rows : 2 * rows] + by_middle[0:rows])
            + (by_high[2 * rows :] + by_middle[rows:] + by_tail)
        )
        chosen = jnp.where(low_row, joined[0:HEAD_ROWS], joined[HEAD_ROWS:])
        return chosen + pltpu.roll(chosen, BLOCK, 1), scale, inverse_count

    def run_head(layer, pre):
        hidden, hidden_slope = silu_pair(pre[0:HIDDEN])
        inner, inner_slope = silu_pair(stacked(inner_forward[layer], hidden) + inner_cols[layer])
        dinner = energy_cols[layer] * atom_cot * inner_slope
        dhidden = stacked(inner_back[layer], dinner) * hidden_slope
        return hidden, inner, dinner, dhidden

    def small_grad(layer, hidden, inner, dinner):
        left = jnp.concatenate([dinner, atom_cot * inner], axis=0)
        blank = jnp.zeros((128 - 32 - 32 * layer, 128), F32)
        right = [hidden, (iota((8, 128), 0) == 0).astype(F32), blank]
        if layer == 1:
            right = [jnp.zeros((32, 128), F32)] + right
        return mm(jnp.where(low_row, left, 0.0), jnp.concatenate(right, axis=0), NT)

    def halves(value):
        return jnp.where(low_row, value, 0.0), jnp.where(low_row, 0.0, value)

    def scatter_tiles(phase, source, target, base):
        for t in range(source.shape[0]):

            @pl.when(me != base + t)
            def _():
                there = base + t
                push(phase, source.at[t], target.at[me], (there // lanes, there % lanes))

            @pl.when(me == base + t)
            def _():
                target[me] = source[t]

    def mine(base, result):
        return (me >= base) & (me < base + result.shape[0])

    def share_tiles(phase, parts_of, result, base):
        @pl.when(mine(base, result))
        def _():
            await_bytes(parts_of, devices - 1, recv_sem.at[phase])
            total = parts_of[0]
            for k in range(1, devices):
                total = total + parts_of[k]
            result[me - base] = total
            everyone(
                lambda device, _: push(phase + 1, result.at[me - base], result.at[me - base], device)
            )

    def gather_tiles(phase, result, base):
        count_of = result.shape[0]

        @pl.when(mine(base, result))
        def _():
            await_bytes(result, count_of - 1, recv_sem.at[phase + 1])

        @pl.when(jnp.logical_not(mine(base, result)))
        def _():
            await_bytes(result, count_of, recv_sem.at[phase + 1])

    def drain_tiles(phase, parts_of, result, base):
        count_of = result.shape[0]

        @pl.when(mine(base, result))
        def _():
            await_bytes(result, count_of - 1, send_sem.at[phase])
            await_bytes(parts_of, devices - 1, send_sem.at[phase + 1])

        @pl.when(jnp.logical_not(mine(base, result)))
        def _():
            await_bytes(result, count_of, send_sem.at[phase])

    base_a, base_b, base_c = 0, tiles_a.shape[0], devices - tiles_c.shape[0]

    forward_kinds()
    send_moments(0, 3)
    for parity in range(2):
        k = iota((FEATURE_ROWS, FEATURES), 0)
        pair = (k >= 72).astype(I32) + (k >= 144).astype(I32)
        rest = k - 72 * pair
        kind_of = (rest * 5462) >> 16
        channel = rest - 12 * kind_of
        place = channel * 36 + (2 * pair + parity) * 6 + kind_of
        hit = (place == iota((FEATURE_ROWS, FEATURES), 1)) & (k < ONES_ROW)
        select[parity] = hit.astype(F32).astype(BF16)
    inner_cols, energy_cols = [], []
    head[...] = jnp.zeros_like(head)
    for layer in range(2):
        for parity in range(2):
            base = HEAD_ROWS * parity
            block = exact(hidden_weight[layer], select[parity], NT)
            if parity == 0:
                spot = (iota((2, FEATURE_ROWS), 1) == ONES_ROW) & (
                    iota((2, FEATURE_ROWS), 0) == layer
                )
                block = block + mm(hidden_bias[...], spot.astype(F32), TN)
            head[layer, base : base + HIDDEN, :] = block
            if layer == 0:
                message_rows = jnp.concatenate(
                    [message_weight[...], jnp.zeros((PADDED - CHANNELS, FEATURES), F32)], axis=0
                )
                head[0, base + HIDDEN : base + HEAD_ROWS, :] = exact(message_rows, select[parity], NT)
        whole = head[layer]
        head_rows[layer] = three_rows(whole)
        head_stack[layer] = stack_left(whole)
        if layer == 0:
            message_stack[...] = stack_left(
                jnp.concatenate([whole[HIDDEN:HEAD_ROWS], whole[HEAD_ROWS + HIDDEN :]], axis=0)
            )
        inner_back[layer] = stack_left(inner_weight[layer])
        inner_forward[layer] = stack_left(jnp.transpose(inner_weight[layer]))
        pick = (iota((2, 128), 0) == layer).astype(F32)
        inner_cols.append(mm(inner_bias[...], pick, TN))
        energy_cols.append(mm(energy_weight[...], pick, TN))

    pre_zero, scale_zero, inverse_count = normalise(0, 3)
    message = pre_zero[HIDDEN:HEAD_ROWS]
    message_own[...] = jnp.where(low, message[0:8], message[8:16])
    members(lambda device, _: push(4, message_own, message_all.at[col], device))
    message_all[col] = message_own[...]
    hidden_zero, inner_zero, dinner_zero, dhidden_zero = run_head(0, pre_zero)
    d_low, d_high = halves(dhidden_zero)
    gap = jnp.zeros((HEAD_ROWS - HIDDEN, 128), F32)
    dnormed_head = stacked(head_stack[0], jnp.concatenate([d_low, gap, d_high, gap], axis=0))

    def pack_head(target, layer, d_low, d_high):
        block = mm(jnp.concatenate([d_low, d_high], axis=0), normed[layer], NT)
        for r in range(6):
            for half in range(2):
                target[2 * r + half] = block[8 * r : 8 * (r + 1), 128 * half : 128 * (half + 1)]

    pack_head(tiles_a, 0, d_low, d_high)
    scatter_tiles(11, tiles_a, tiles_a_all, 0)
    weights[...] = jnp.zeros_like(weights)
    embedded = mm(embedding[...], sender_rows[0:2, :], TN)
    weights[0:CHANNELS, :] = mm(channel_in[1], embedded, TN)
    await_bytes(message_all, lanes - 1, recv_sem.at[4])
    for q in range(tiles):
        even, odd = message_all[2 * q], message_all[2 * q + 1]
        spot = slice(128 * q, 128 * (q + 1))
        weights[0:8, spot] += jnp.where(low, even, pltpu.roll(odd, BLOCK, 1))
        weights[8:16, spot] += jnp.where(low, pltpu.roll(even, BLOCK, 1), odd)

    spread()
    forward()
    send_moments(1, 5)
    turn = ANGLE * (1.0 + (iota((1, 128), 1) >= BLOCK).astype(F32))

    def slope_block(i, carry):
        start = aligned(i * BLOCK, BLOCK)
        spot = pl.ds(start, BLOCK)
        geo = geometry(start)
        step = geo.inverse
        square = step * step
        envelope = geo.reach * geo.reach * NORM
        slope = geo.reach * (-2.0 * NORM / (cutoff_radius * cutoff_radius))
        weight = pair_weight[spot, :]
        for pair, (sine, cosine) in enumerate(zip(geo.sines(), geo.cosines())):
            rate = (turn + 2.0 * ANGLE * pair) * cosine - sine
            value = weight * ((0.5 * square) * rate * envelope + sine * slope)
            plane = weight * (sine * envelope)
            slopes[spot, tile_of(0, pair)] = value
            for order in range(1, 4):
                plane = plane * step
                value = value * step - (0.5 * square) * plane
                slopes[spot, tile_of(order, pair)] = value
        return carry

    loop(group // BLOCK, slope_block, 0)
    for q in strips:
        kind_stack[:, q] = stack_left(kind_products[:, q])

    share_tiles(11, tiles_a_all, tiles_a_sum, base_a)
    pre_one, scale_one, _ = normalise(1, 5)
    hidden_one, inner_one, dinner_one, dhidden_one = run_head(1, pre_one)
    d_low, d_high = halves(dhidden_one)
    dnormed_one = stacked(head_stack[1], jnp.concatenate([d_low, gap, d_high, gap], axis=0))
    send_stats(6, 2, half_sum, dnormed_one, dnormed_one * normed[1])

    pack_head(tiles_b, 1, d_low, d_high)
    small = small_grad(0, hidden_zero, inner_zero, dinner_zero)
    small = small + small_grad(1, hidden_one, inner_one, dinner_one)
    for r in range(2):
        tiles_b[12 + r] = small[8 * r : 8 * (r + 1)] + pltpu.roll(small[16 + 8 * r : 24 + 8 * r], 64, 1)
    atom_energy = jnp.sum(energy_cols[0] * inner_zero + energy_cols[1] * inner_one, axis=0, keepdims=True)
    atom_energy = jnp.where(low_row, live * atom_energy, 0.0)
    energy_rows = mm(jnp.broadcast_to(atom_energy, (8, 128)), member, NT)[0:1]
    def feature_back(layer, phase, index, dnormed, scale):
        total = get_stats(phase, index)
        wide = widen(total * inverse_count)
        dfeats = scale * (
            dnormed[0:ONES_ROW] - live * (tall(wide, 0) + tall(wide, 256) * normed[layer, 0:ONES_ROW, :])
        )
        dmixed = jnp.concatenate([dfeats[72 * pair : 72 * (pair + 1)] for pair in range(PAIRS)], axis=1)
        dinvariant[...] = stacked(mix_back[layer], dmixed)
        return dmixed

    def mix_grad(layer, dmixed):
        return mm(invariant[layer], dmixed, NT) * same

    blank = jnp.zeros((8, 128), F32)

    def shell_back():
        moved = (blank, blank, blank)
        for i in range(2 * PAIRS):
            pair, tile, spot = chunk_spots(i)
            terms = shell_terms(pair, tile)
            cots = tuple(dinvariant[PADDED * p + 8 * tile : PADDED * p + 8 * tile + 8, 128 * pair : 128 * (pair + 1)] for p in range(6))
            _, pull = jax.vjp(invariants, terms, xi, yi, zi)
            dterms, *shift = pull(cots)
            for order in range(4):
                for m in range(COUNTS[order]):
                    value = dterms[OFFSETS[order] + m]
                    start = ROW_OF[m] + 8 * tile
                    if tile == 0:
                        dsums[start : start + 8, tile_of(order, pair)] = value
                    else:
                        dsums[start : start + CHANNELS - 8, tile_of(order, pair)] = value[0 : CHANNELS - 8]
            moved = tuple(a + live_rows(b, tile) for a, b in zip(moved, shift))
        return moved

    def shell_back_kinds():
        moved = (blank, blank, blank)
        dtable = [[blank, blank], [blank, blank]]
        for pair in range(PAIRS):
            both = kind_terms(pair)
            folded = [[None, None] for _ in range(SHELLS)]
            for tile in range(2):
                terms = [columns_of[0][tile] * a + columns_of[1][tile] * b for a, b in both]
                cots = tuple(dinvariant[PADDED * p + 8 * tile : PADDED * p + 8 * tile + 8, 128 * pair : 128 * (pair + 1)] for p in range(6))
                _, pull = jax.vjp(invariants, terms, xi, yi, zi)
                dterms, *shift = pull(cots)
                moved = tuple(a + b for a, b in zip(moved, shift))
                for m in range(SHELLS):
                    for k in range(2):
                        dtable[k][tile] = dtable[k][tile] + dterms[m] * both[m][k]
                        value = columns_of[k][tile] * dterms[m]
                        folded[m][k] = value if tile == 0 else folded[m][k] + value
            for order in range(4):
                for m in range(COUNTS[order]):
                    for k in range(2):
                        dkind_sums[2 * m + k : 2 * m + k + 1, tile_of(order, pair)] = jnp.sum(
                            folded[OFFSETS[order] + m][k], axis=0, keepdims=True
                        )
        return moved, [jnp.concatenate(halves_of, axis=0) for halves_of in dtable]

    def product_back():
        for order, first, last in GROUPS:
            lane_spot = slice(128 * first, 128 * last)
            end = DEGREE_ROWS[order + 1]
            high, low_part, _ = parts(dsums[0:end, lane_spot])
            left = jnp.concatenate([high, low_part], axis=0).astype(BF16)
            for spot in strips:
                by_high = once(left, planes_high[spot, lane_spot], NT)
                block = by_high[0:end] + (by_high[end:] + once(left[0:end], planes_low[spot, lane_spot], NT))
                if order == 3:
                    dproducts[0:end, spot] = block
                else:
                    dproducts[0:end, spot] += block

    def product_back_kinds():
        high, low_part, _ = parts(dkind_sums[...])
        left = jnp.concatenate([high, low_part], axis=0).astype(BF16)
        for spot in strips:
            by_high = once(left, planes_high[spot, :], NT)
            dkind_products[:, spot] = by_high[0:40] + (by_high[40:] + once(left, planes_low[spot, :], NT)[0:40])

    def weight_back():
        out = []
        for q in range(tiles):
            spot = slice(128 * q, 128 * (q + 1))
            table = monomial_rows(sender_rows[:, spot])
            both = []
            for tile in range(2):
                total = None
                for i, m in enumerate(MONOMIALS):
                    term = dproducts[ROW_OF[i] + 8 * tile : ROW_OF[i] + 8 * tile + 8, spot]
                    term = term if table[m] is None else term * table[m]
                    total = term if total is None else total + term
                both.append(live_rows(total, tile))
            out.append(jnp.concatenate(both, axis=0))
        return out

    def axis_slope(table, axis, value_of):
        total = None
        for i, m in enumerate(MONOMIALS):
            if not m[axis]:
                continue
            lower = table[m[:axis] + (m[axis] - 1,) + m[axis + 1 :]]
            term = value_of(i)
            if lower is not None:
                term = (float(m[axis]) * lower) * term
            total = term if total is None else total + term
        return total

    def coordinate_back():
        out = []
        for q in range(tiles):
            spot = slice(128 * q, 128 * (q + 1))
            table = monomial_rows(sender_rows[:, spot])
            sides = []
            for axis in range(3):
                total = None
                for tile in range(2):
                    slope = axis_slope(
                        table, axis, lambda i: dproducts[ROW_OF[i] + 8 * tile : ROW_OF[i] + 8 * tile + 8, spot]
                    )
                    term = weights[8 * tile : 8 * tile + 8, spot] * live_rows(slope, tile)
                    total = term if total is None else total + term
                sides.append(jnp.sum(total, axis=0, keepdims=True))
            out.append(sides)
        return out

    def coordinate_back_kinds():
        out = []
        for q in range(tiles):
            spot = slice(128 * q, 128 * (q + 1))
            table = monomial_rows(sender_rows[:, spot])
            kinds = sender_rows[0:2, spot]
            rows = [
                jnp.sum(kinds * dkind_products[2 * i : 2 * i + 2, spot], axis=0, keepdims=True)
                for i in range(len(MONOMIALS))
            ]
            out.append([axis_slope(table, axis, lambda i: rows[i]) for axis in range(3)])
        return out

    def radial_pull(block, first, last, spot):
        total = None
        for at in range(first, last):
            term = block[:, 128 * (at - first) : 128 * (at - first + 1)] * slopes[spot, 128 * at : 128 * (at + 1)]
            total = term if total is None else total + term
        return total

    def plane_back():
        for order, first, last in GROUPS:
            end = DEGREE_ROWS[order + 1]
            for spot in strips:
                block = mm(products[0:end, spot], dsums[0:end, 128 * first : 128 * last], TN)
                term = radial_pull(block, first, last, spot)
                if order == 3:
                    pulls[spot, :] = term
                else:
                    pulls[spot, :] += term

    def plane_back_kinds():
        right = stack_right(dkind_sums[...])
        for order, first, last in GROUPS:
            for spot in strips:
                block = once(kind_stack[:, spot], right[:, 128 * first : 128 * last], TN)
                pulls[spot, :] += radial_pull(block, first, last, spot)

    dmixed_one = feature_back(1, 6, 2, dnormed_one, scale_one)
    moved_one = shell_back()
    product_back()
    dweights_one = weight_back()
    for q in range(tiles):
        top, bottom = dweights_one[q][0:8], dweights_one[q][8:16]
        dmessage_own[2 * q] = jnp.where(low, top, pltpu.roll(bottom, BLOCK, 1))
        dmessage_own[2 * q + 1] = jnp.where(low, pltpu.roll(top, BLOCK, 1), bottom)
    members(
        lambda device, target: push(7, dmessage_own.at[target], dmessage_all.at[col], device)
    )
    dmessage_all[col] = dmessage_own[col]
    kinds_of = sender_rows[...]
    dtable_one = jnp.zeros((PADDED, 8), F32)
    for q in range(tiles):
        dtable_one = dtable_one + mm(dweights_one[q], kinds_of[:, 128 * q : 128 * (q + 1)], NT)
    slopes_one = coordinate_back()
    mix_one = mix_grad(1, dmixed_one)
    scatter_tiles(13, tiles_b, tiles_b_all, base_b)
    await_bytes(dmessage_all, lanes - 1, recv_sem.at[7])
    arrived = dmessage_all[0]
    for k in range(1, lanes):
        arrived = arrived + dmessage_all[k]
    turned = pltpu.roll(arrived, BLOCK, 1)
    dmessage = jnp.concatenate([jnp.where(low, arrived, turned), jnp.where(low, turned, arrived)], axis=0)

    m_low, m_high = halves(dmessage)
    dmessage_both = jnp.concatenate([m_low, m_high], axis=0)
    dnormed_zero = dnormed_head + stacked(message_stack[...], dmessage_both)
    send_stats(8, 3, half_sum, dnormed_zero, dnormed_zero * normed[0], energy_rows)
    dmessage_weight = mm(dmessage_both, normed[0], NT)
    for r in range(4):
        for half in range(2):
            tiles_c[2 * r + half] = dmessage_weight[
                8 * r : 8 * (r + 1), 128 * half : 128 * (half + 1)
            ]
    scatter_tiles(15, tiles_c, tiles_c_all, base_c)
    fold_c = (iota((PADDED, 96), 0) == (iota((PADDED, 96), 1) & 15)).astype(F32)
    d_of = iota((72, 128), 0) - 12 * ((iota((72, 128), 0) * 5462) >> 16)
    seat_mix = [(iota((72, 128), 1) == d_of + 12 * layer).astype(F32) for layer in range(2)]
    seat_kind = ((lane == row8 + 26) & (row8 < 2)).astype(F32)
    final_one = mm(mm(fold_c, mix_one), seat_mix[1]) + mm(dtable_one, seat_kind)
    plane_back()
    share_tiles(13, tiles_b_all, tiles_b_sum, base_b)
    dmixed_zero = feature_back(0, 8, 3, dnormed_zero, scale_zero)
    share_tiles(15, tiles_c_all, tiles_c_sum, base_c)
    moved_zero, dtables = shell_back_kinds()
    mix_zero = mix_grad(0, dmixed_zero)
    final = mm(mm(fold_c, mix_zero), seat_mix[0]) + final_one
    for k in range(2):
        total = jnp.sum(dtables[k], axis=1, keepdims=True)
        final = final + jnp.where(iota((PADDED, 128), 1) == 24 + k, total, 0.0)
    folded = final[0:8] + pltpu.roll(pltpu.roll(final[0:8], 4, 0), 32, 1) + pltpu.roll(final[8:16], 64, 1)
    final_own[...] = folded[0:4]
    everyone(lambda device, _: push(10, final_own, final_all.at[me], device))
    final_all[me] = final_own[...]
    plane_back_kinds()
    product_back_kinds()
    slopes_zero = coordinate_back_kinds()
    pull_of = pulls[...]
    to_own = mm(sender_rows[...], pull_of)
    to_sender = mm(own, pull_of, NT)
    force_own[...] = jnp.zeros_like(force_own)
    for q in range(tiles):
        spot = slice(128 * q, 128 * (q + 1))
        weight_row = to_sender[5:6, spot]
        for axis in range(3):
            value = -2.0 * (to_sender[2 + axis : 3 + axis, spot] + sender_rows[2 + axis : 3 + axis, spot] * weight_row)
            value = value - slopes_zero[q][axis] - slopes_one[q][axis]
            force_own[2 * q, axis : axis + 1, :] = value
            force_own[2 * q + 1, axis : axis + 1, :] = pltpu.roll(value, BLOCK, 1)
    members(lambda device, target: push(9, force_own.at[target], force_all.at[col], device))
    force_all[col] = force_own[col]
    own_force = []
    for axis in range(3):
        pairwise = 2.0 * (to_own[2 + axis : 3 + axis] + own[2 + axis : 3 + axis] * to_own[5:6])
        moved = jnp.sum(moved_zero[axis] + moved_one[axis], axis=0, keepdims=True)
        both = pairwise + moved
        own_force.append(both + pltpu.roll(both, BLOCK, 1))

    group_energy = stat_all[3, row * lanes, 2:3, 96 : 96 + STRUCTS]
    for k in range(1, lanes):
        group_energy = group_energy + stat_all[3, row * lanes + k, 2:3, 96 : 96 + STRUCTS]
    energies_out[...] = group_energy

    gather_tiles(11, tiles_a_sum, base_a)
    gather_tiles(13, tiles_b_sum, base_b)
    pick_ones = ((iota((8, FEATURE_ROWS), 0) == 0) & (iota((8, FEATURE_ROWS), 1) == ONES_ROW)).astype(F32)
    for layer in range(2):
        total = None
        for parity in range(2):
            rows = []
            for r in range(3):
                at = 6 * parity + 2 * r
                summed = (tiles_a_sum, tiles_b_sum)[layer]
                rows.append(jnp.concatenate([summed[at], summed[at + 1]], axis=1))
            block = jnp.concatenate(rows, axis=0)
            if parity == 0:
                hidden_bias_out[layer : layer + 1, :] = mm(pick_ones, block, NT)[0:1]
            part = exact(block, select[parity])
            total = part if total is None else total + part
        hidden_weight_out[layer] = total
    small_sum = jnp.concatenate([tiles_b_sum[12 + r] for r in range(2)], axis=0)
    for layer in range(2):
        inner_weight_out[layer] = small_sum[0:INNER, 32 * layer : 32 * layer + HIDDEN]
        pick = ((row8 == 0) & (lane == 32 * layer + HIDDEN)).astype(F32)
        inner_bias_out[layer : layer + 1, :] = mm(pick, small_sum, NT)[0:1]
        pick = ((row8 == 0) & (lane == 64 + 32 * layer + HIDDEN)).astype(F32)
        energy_weight_out[layer : layer + 1, :] = mm(pick, small_sum, NT)[0:1]
    gather_tiles(15, tiles_c_sum, base_c)
    total = None
    for parity in range(2):
        rows = [
            jnp.concatenate(
                [tiles_c_sum[4 * parity + 2 * r], tiles_c_sum[4 * parity + 2 * r + 1]], axis=1
            )
            for r in range(2)
        ]
        part = exact(jnp.concatenate(rows, axis=0), select[parity])
        total = part if total is None else total + part
    message_weight_out[...] = total[0:CHANNELS]

    await_bytes(final_all, devices - 1, recv_sem.at[10])
    final = final_all[0]
    for k in range(1, devices):
        final = final + final_all[k]
    final = jnp.concatenate([final, jnp.zeros((4, 128), F32)], axis=0)
    upper = jnp.where(row8 < 4, final, pltpu.roll(pltpu.roll(final, 4, 0), 96, 1))
    final = jnp.concatenate([upper, pltpu.roll(final, 64, 1)], axis=0)
    dembedding = None
    for layer in range(2):
        channel_mix_out[:, layer, :] = final[0:CHANNELS, 12 * layer : 12 * (layer + 1)]
        dtable = final[0:CHANNELS, 24 + 2 * layer : 26 + 2 * layer]
        channel_in_out[layer] = lax.dot_general(
            embedding[...],
            dtable,
            (((0,), (1,)), ((), ())),
            precision=lax.Precision.HIGHEST,
            preferred_element_type=F32,
        )
        part = lax.dot_general(
            dtable,
            channel_in[layer],
            (((0,), (1,)), ((), ())),
            precision=lax.Precision.HIGHEST,
            preferred_element_type=F32,
        )
        dembedding = part if dembedding is None else dembedding + part
    embedding_out[...] = dembedding

    await_bytes(force_all, lanes - 1, recv_sem.at[9])
    force = force_all[0]
    for k in range(1, lanes):
        force = force + force_all[k]
    for axis in range(3):
        position_out[axis] = (force[axis : axis + 1] + own_force[axis])[:, 0:BLOCK]

    await_bytes(pack_all, lanes - 1, send_sem.at[0])
    await_bytes(send_all, lanes - 1, send_sem.at[1])
    await_bytes(recv_all, lanes - 1, send_sem.at[2])
    await_bytes(stat_all.at[0], devices - 1, send_sem.at[3])
    await_bytes(message_all, lanes - 1, send_sem.at[4])
    await_bytes(stat_all.at[1], devices - 1, send_sem.at[5])
    await_bytes(stat_all.at[2], devices - 1, send_sem.at[6])
    await_bytes(dmessage_all, lanes - 1, send_sem.at[7])
    await_bytes(stat_all.at[3], devices - 1, send_sem.at[8])
    await_bytes(force_all, lanes - 1, send_sem.at[9])
    await_bytes(final_all, devices - 1, send_sem.at[10])
    drain_tiles(11, tiles_a_all, tiles_a_sum, base_a)
    drain_tiles(13, tiles_b_all, tiles_b_sum, base_b)
    drain_tiles(15, tiles_c_all, tiles_c_sum, base_c)


def hand_over(*refs):
    for source, target in zip(refs[:11], refs[11:]):
        target[...] = source[...]


def solution(mesh):
    lanes = mesh.shape["edge"]
    structs = mesh.shape["struct"]
    devices = lanes * structs

    def step(
        positions,
        species,
        struct_id,
        atom_mask,
        senders,
        receivers,
        edge_mask,
        energy_cot,
        embedding,
        channel_in,
        channel_mix,
        hidden_weight,
        hidden_bias,
        inner_weight,
        inner_bias,
        energy_weight,
        message_weight,
    ):
        owned = positions.shape[2]
        group = owned * lanes
        edges = senders.shape[1]
        inputs = [
            positions,
            species,
            struct_id,
            atom_mask,
            senders,
            receivers,
            edge_mask,
            energy_cot,
            embedding,
            channel_in,
            jnp.transpose(channel_mix, (1, 0, 2)),
            jnp.transpose(hidden_weight, (0, 2, 1)),
            hidden_bias,
            jnp.transpose(inner_weight, (0, 2, 1)),
            inner_bias,
            energy_weight,
            jnp.transpose(message_weight),
        ]
        vmem = pltpu.VMEM
        shapes = [
            (1, STRUCTS),
            (3, 1, owned),
            embedding.shape,
            channel_in.shape,
            (CHANNELS, 2, CHANNELS),
            (2, HIDDEN, FEATURES),
            hidden_bias.shape,
            (2, INNER, HIDDEN),
            inner_bias.shape,
            energy_weight.shape,
            (CHANNELS, FEATURES),
        ]
        scratch = [
            vmem((8, 128), F32),
            vmem((lanes, 8, 128), F32),
            vmem((lanes, 1, edges), I32),
            vmem((1, edges), I32),
            vmem((lanes, 1, edges), I32),
            vmem((2, 128, BLOCK * (group // 256)), F32),
            vmem((group, 128), F32),
            vmem((group, 8), F32),
            vmem((8, group), F32),
            vmem((PAIRS, group, 128), F32),
            vmem((group, 128), F32),
            vmem((group, PLANE_LANES), BF16),
            vmem((group, PLANE_LANES), BF16),
            vmem((group, PLANE_LANES), F32),
            vmem((group, 128), F32),
            vmem((PADDED, group), F32),
            vmem((PRODUCT_ROWS, group), F32),
            vmem((752, group), BF16),
            vmem((496, group), BF16),
            vmem((PRODUCT_ROWS, PLANE_LANES), F32),
            vmem((PRODUCT_ROWS, PLANE_LANES), F32),
            vmem((40, group), F32),
            vmem((128, group), BF16),
            vmem((240, group), BF16),
            vmem((40, PLANE_LANES), F32),
            vmem((40, PLANE_LANES), F32),
            vmem((40, group), F32),
            vmem((PRODUCT_ROWS, group), F32),
            vmem((2, 96, 128 * PAIRS), F32),
            vmem((96, 128 * PAIRS), F32),
            vmem((2, FEATURE_ROWS, 128), F32),
            vmem((2, FEATURE_ROWS, 128), F32),
            vmem((2, FEATURE_ROWS, FEATURES), BF16),
            vmem((2, 2 * HEAD_ROWS, FEATURE_ROWS), F32),
            vmem((2, 6 * HEAD_ROWS, FEATURE_ROWS), BF16),
            vmem((2, 12 * HEAD_ROWS, FEATURE_ROWS), BF16),
            vmem((12 * PADDED, FEATURE_ROWS), BF16),
            vmem((2, 6 * HIDDEN, INNER), BF16),
            vmem((2, 6 * INNER, HIDDEN), BF16),
            vmem((2, 6 * 96, 72), BF16),
            vmem((2, 6 * 72, 96), BF16),
            vmem((4, 8, 128), F32),
            vmem((4, devices, 8, 128), F32),
            vmem((8, 128), F32),
            vmem((lanes, 8, 128), F32),
            vmem((lanes, 8, 128), F32),
            vmem((lanes, 8, 128), F32),
            vmem((lanes, 8, 128), F32),
            vmem((lanes, 8, 128), F32),
            vmem((4, 128), F32),
            vmem((devices, 4, 128), F32),
            vmem((12, 8, 128), F32),
            vmem((devices, 8, 128), F32),
            vmem((12, 8, 128), F32),
            vmem((14, 8, 128), F32),
            vmem((devices, 8, 128), F32),
            vmem((14, 8, 128), F32),
            vmem((8, 8, 128), F32),
            vmem((devices, 8, 128), F32),
            vmem((8, 8, 128), F32),
            pltpu.SemaphoreType.DMA((20,)),
            pltpu.SemaphoreType.DMA((20,)),
            pltpu.SemaphoreType.DMA((17,)),
        ] + [vmem(v.shape, v.dtype) for v in inputs]
        outs = pl.pallas_call(
            functools.partial(body, lanes, structs),
            out_shape=[vmem(s, F32) for s in shapes],
            in_specs=[pl.BlockSpec(memory_space=pl.ANY)] * 17,
            out_specs=[pl.BlockSpec(memory_space=vmem)] * 11,
            scratch_shapes=scratch,
            compiler_params=pltpu.CompilerParams(
                collective_id=0, has_side_effects=True, vmem_limit_bytes=60 * 1024 * 1024
            ),
        )(*inputs)
        outs = pl.pallas_call(
            hand_over,
            out_shape=[jax.ShapeDtypeStruct(s, F32) for s in shapes],
            in_specs=[pl.BlockSpec(memory_space=vmem)] * 11,
            out_specs=[pl.BlockSpec(memory_space=vmem)] * 11,
        )(*(pltpu.with_memory_space_constraint(v, pltpu.VMEM) for v in outs))
        outs = list(outs)
        outs[4] = jnp.transpose(outs[4], (1, 0, 2))
        outs[5] = jnp.transpose(outs[5], (0, 2, 1))
        outs[7] = jnp.transpose(outs[7], (0, 2, 1))
        outs[10] = jnp.transpose(outs[10])
        return tuple(outs)

    tiled = P("struct", "edge")
    return jax.shard_map(
        step,
        mesh=mesh,
        in_specs=(
            P(None, "struct", "edge"),
            tiled,
            tiled,
            tiled,
            tiled,
            tiled,
            tiled,
            P("struct", None),
        )
        + (P(),) * 9,
        out_specs=(P("struct", None), P(None, "struct", "edge")) + (P(),) * 9,
        check_vma=False,
    )
```

```python
import functools
import math

import jax
import jax.numpy as jnp
import numpy as np
from jax import lax
from jax.experimental import pallas as pl
from jax.experimental.pallas import tpu as pltpu
from jax.sharding import PartitionSpec as P

CHANNELS = 12
PADDED = 16
RADIALS = 6
PAIRS = 3
STRUCTS = 8
HIDDEN = 24
INNER = 16
FEATURES = 432
HEAD_ROWS = 40
FEATURE_ROWS = 256
ONES_ROW = 216
BLOCK = 64

cutoff_radius = 6.0
variance_eps = 1e-05
center = 1.5

MESH = pl.DeviceIdType.MESH
F32 = jnp.float32
BF16 = jnp.bfloat16
I32 = jnp.int32
NN = ((1,), (0,))
NT = ((1,), (1,))
TN = ((0,), (0,))

MONOMIALS = sorted(
    [(a, b, c) for a in range(4) for b in range(4) for c in range(4) if a + b + c <= 3],
    key=lambda m: (sum(m), -m[0], -m[1], -m[2]),
)
PLACE = {m: i for i, m in enumerate(MONOMIALS)}
COUNTS = [1, 4, 10, 20]
OFFSETS = [0, 1, 5, 15]
SHELLS = 35
DEGREE_ROWS = [0, 16, 56, 128, 248]
DEGREE_COUNTS = [1, 3, 6, 10]


def row_of(place, tile):
    degree = sum(MONOMIALS[place])
    within = place - sum(DEGREE_COUNTS[:degree])
    return DEGREE_ROWS[degree] + (8 * DEGREE_COUNTS[degree] + 4 * within if tile else 8 * within)


PRODUCT_ROWS = 256
LANE_TILES = [(3, 0), (3, 1), (3, 2), (2, 2), (2, 0), (2, 1), (1, 0), (1, 1), (1, 2), (0, 2), (0, 0), (0, 1)]
GROUPS = [(3, 0, 4), (2, 4, 6), (1, 6, 10), (0, 10, 12)]
PLANE_LANES = 128 * len(LANE_TILES)


def tile_of(order, pair):
    at = LANE_TILES.index((order, pair))
    return slice(128 * at, 128 * (at + 1))


RADIX = 4096.0
SEND_STEP = 27


def fitted(function, low, high, degree):
    series = np.polynomial.chebyshev.Chebyshev.interpolate(
        lambda w: function(0.5 * (high - low) * w + 0.5 * (high + low)), degree
    )
    return [float(v) for v in series.convert(kind=np.polynomial.Polynomial).coef]


LOW, HIGH = 0.9, 28.1
ANGLE = math.pi / cutoff_radius
SINE = fitted(lambda u: np.sin(ANGLE * np.sqrt(u)) / np.sqrt(u), LOW, HIGH, 6)
COSINE = fitted(lambda u: np.cos(ANGLE * np.sqrt(u)), LOW, HIGH, 6)
NORM = math.sqrt(2.0 / cutoff_radius)


def mm(left, right, kind=NN, precision=lax.Precision.HIGHEST):
    return lax.dot_general(
        left, right, (kind, ((), ())), precision=precision, preferred_element_type=F32
    )


def once(left, right, kind=NN):
    return lax.dot_general(left, right, (kind, ((), ())), preferred_element_type=F32)


def parts(value):
    high = value.astype(BF16).astype(F32)
    rest = value - high
    middle = rest.astype(BF16).astype(F32)
    return high, middle, rest - middle


def stack_left(value):
    high, middle, tail = parts(value)
    return jnp.concatenate([high, high, middle, high, tail, middle], axis=0).astype(BF16)


def stack_right(value):
    high, middle, tail = parts(value)
    return jnp.concatenate([high, middle, high, tail, high, middle], axis=0).astype(BF16)


def stacked(left, right):
    return once(left, stack_right(right), TN)


def three_rows(value):
    return jnp.concatenate(parts(value), axis=0).astype(BF16)


def exact(left, right, kind=NN):
    rows = left.shape[0]
    out = once(three_rows(left), right, kind)
    return out[0:rows] + (out[rows : 2 * rows] + out[2 * rows :])


def loop(count, action, carry):
    if count <= 8:
        for i in range(count):
            carry = action(i, carry)
        return carry
    return lax.fori_loop(0, count, action, carry)


def aligned(value, size):
    return value if isinstance(value, int) else pl.multiple_of(value, size)


def iota(shape, dim):
    return lax.broadcasted_iota(I32, shape, dim)


def horner(coefficients, w):
    total = jnp.full_like(w, coefficients[-1])
    for value in coefficients[-2::-1]:
        total = total * w + value
    return total


def shifted(terms, order, x, y, z):
    current = terms
    for axis, value in enumerate((x, y, z)):
        two, three = 2.0 * value, 3.0 * value
        square = value * value
        three_square, cube = 3.0 * square, square * value
        factors = [None, [value], [square, two], [cube, three_square, three]]
        fresh = {}
        for m in MONOMIALS[: COUNTS[order]]:
            if axis == 2 and sum(m) != order:
                continue
            power = m[axis]
            total = current[m]
            for lower in range(power):
                source = m[:axis] + (lower,) + m[axis + 1 :]
                total = total + factors[power][lower] * current[source]
            fresh[m] = total
        current = fresh
    return current


def all_shifted(terms, x, y, z):
    out = []
    for order in range(4):
        own = {m: terms[OFFSETS[order] + i] for i, m in enumerate(MONOMIALS[: COUNTS[order]])}
        moved = shifted(own, order, x, y, z) if order else own
        out += [moved[m] for m in MONOMIALS if sum(m) == order]
    return out


def contracted(components):
    by_order = [{}, {}, {}, {}]
    for m, value in zip(MONOMIALS, components):
        by_order[sum(m)][m] = value
    scalar = by_order[0][(0, 0, 0)]
    vx, vy, vz = by_order[1][(1, 0, 0)], by_order[1][(0, 1, 0)], by_order[1][(0, 0, 1)]
    m = by_order[2]
    xx, xy, xz = m[(2, 0, 0)], m[(1, 1, 0)], m[(1, 0, 1)]
    yy, yz, zz = m[(0, 2, 0)], m[(0, 1, 1)], m[(0, 0, 2)]
    q = by_order[3]
    xxx, yyy, zzz = q[(3, 0, 0)], q[(0, 3, 0)], q[(0, 0, 3)]
    xxy, xxz, xyy = q[(2, 1, 0)], q[(2, 0, 1)], q[(1, 2, 0)]
    xyz, xzz, yyz, yzz = q[(1, 1, 1)], q[(1, 0, 2)], q[(0, 2, 1)], q[(0, 1, 2)]
    first = vx * vx + vy * vy + vz * vz
    second = xx * xx + yy * yy + zz * zz + 2.0 * (xy * xy + xz * xz + yz * yz)
    third = (
        xxx * xxx
        + yyy * yyy
        + zzz * zzz
        + 3.0 * (xxy * xxy + xxz * xxz + xyy * xyy + xzz * xzz + yyz * yyz + yzz * yzz)
        + 6.0 * (xyz * xyz)
    )
    fourth = (
        vx * (xx * vx + xy * vy + xz * vz)
        + vy * (xy * vx + yy * vy + yz * vz)
        + vz * (xz * vx + yz * vy + zz * vz)
    )
    xy2, xz2, yz2 = 2.0 * xy, 2.0 * xz, 2.0 * yz
    fifth = (
        vx * (xxx * xx + xyy * yy + xzz * zz + xxy * xy2 + xxz * xz2 + xyz * yz2)
        + vy * (xxy * xx + yyy * yy + yzz * zz + xyy * xy2 + xyz * xz2 + yyz * yz2)
        + vz * (xxz * xx + yyz * yy + zzz * zz + xyz * xy2 + xzz * xz2 + yzz * yz2)
    )
    return (scalar, first, second, third, fourth, fifth)


def invariants(terms, x, y, z):
    return contracted(all_shifted(terms, x, y, z))


def row_sums(values, row8):
    def fold(a, b, size):
        if b is None:
            return a + pltpu.roll(a, 8 - size, 0)
        first = (row8 & size) == 0
        if size == 4:
            return jnp.where(first, a, b) + pltpu.roll(jnp.where(first, b, a), 4, 0)
        return jnp.where(first, a + pltpu.roll(a, 8 - size, 0), b + pltpu.roll(b, size, 0))

    values = list(values) + [None] * (8 - len(values))
    for size in (4, 2, 1):
        values = [fold(values[i], values[i + size], size) for i in range(size)]
    return values[0]


def silu_pair(v):
    gate = 1.0 / (1.0 + jnp.exp(-v))
    return v * gate, gate * (1.0 + v * (1.0 - gate))


class Geometry:
    def __init__(self, columns, own, lane_low):
        dx = own[2:3] + columns[:, 2:3]
        dy = own[3:4] + columns[:, 3:4]
        dz = own[4:5] + columns[:, 4:5]
        self.u = dx * dx + dy * dy + dz * dz + 1.0
        w = (self.u - 0.5 * (LOW + HIGH)) * (2.0 / (HIGH - LOW))
        self.sine = horner(SINE, w)
        self.cosine = horner(COSINE, w)
        self.inverse = lax.rsqrt(self.u)
        self.reach = 1.0 - self.u * (1.0 / (cutoff_radius * cutoff_radius))
        self.lane_low = lane_low

    def sines(self):
        step = 2.0 * (2.0 * self.cosine * self.cosine - 1.0)
        before = jnp.where(self.lane_low, -self.sine, 0.0)
        now = jnp.where(self.lane_low, self.sine, 2.0 * self.cosine * self.sine)
        return self.series(step, before, now)

    def cosines(self):
        double = 2.0 * self.cosine * self.cosine - 1.0
        before = jnp.where(self.lane_low, self.cosine, 1.0)
        now = jnp.where(self.lane_low, self.cosine, double)
        return self.series(2.0 * double, before, now)

    def series(self, step, before, now):
        out = [now]
        for _ in range(PAIRS - 1):
            before, now = now, step * now - before
            out.append(now)
        return out


def body(lanes, structs, *refs):
    sources, held, refs = refs[:17], refs[-17:], refs[17:-17]
    (
        positions,
        species,
        struct_id,
        atom_mask,
        senders,
        receivers,
        edge_mask,
        energy_cot,
        embedding,
        channel_in,
        channel_mix,
        hidden_weight,
        hidden_bias,
        inner_weight,
        inner_bias,
        energy_weight,
        message_weight,
    ) = held
    (
        energies_out,
        position_out,
        embedding_out,
        channel_in_out,
        channel_mix_out,
        hidden_weight_out,
        hidden_bias_out,
        inner_weight_out,
        inner_bias_out,
        energy_weight_out,
        message_weight_out,
        pack,
        pack_all,
        send_all,
        masked_recv,
        recv_all,
        counts,
        pair_weight,
        columns,
        sender_rows,
        radial,
        inverse,
        planes_high,
        planes_low,
        slopes,
        pulls,
        weights,
        products,
        product_three,
        product_two,
        sums,
        dsums,
        kind_products,
        kind_three,
        kind_stack,
        kind_sums,
        kind_shells,
        kind_moved,
        dkind_sums,
        dkind_products,
        dproducts,
        invariant,
        dinvariant,
        feats,
        normed,
        select,
        head,
        head_rows,
        head_stack,
        message_stack,
        inner_forward,
        inner_back,
        mix_stack,
        mix_back,
        stat_own,
        stat_all,
        message_own,
        message_all,
        dmessage_own,
        dmessage_all,
        force_own,
        force_all,
        final_own,
        final_all,
        tiles_a,
        tiles_a_all,
        tiles_a_sum,
        tiles_b,
        tiles_b_all,
        tiles_b_sum,
        tiles_c,
        tiles_c_all,
        tiles_c_sum,
        send_sem,
        recv_sem,
        input_sem,
    ) = refs
    devices = lanes * structs
    edge_count = senders.shape[1]
    inputs = [
        pltpu.make_async_copy(source, target, input_sem.at[i])
        for i, (source, target) in enumerate(zip(sources, held))
    ]
    group = pair_weight.shape[0]
    tiles = group // 128
    strips = [slice(k, k + 512) for k in range(0, group, 512)]
    row = lax.axis_index("struct")
    col = lax.axis_index("edge")
    me = row * lanes + col

    def everyone(action):
        def one(k, carry):
            target = lax.rem(me + k, devices)
            action((target // lanes, lax.rem(target, lanes)), target)
            return carry

        if devices <= 32:
            for k in range(1, devices):
                one(SEND_STEP * k % devices, 0)
        else:
            lax.fori_loop(1, devices, one, 0)

    def members(action):
        def one(k, carry):
            target = lax.rem(col + k, lanes)
            action((row, target), target)
            return carry

        if lanes <= 8:
            for k in range(1, lanes):
                one(k, 0)
        else:
            lax.fori_loop(1, lanes, one, 0)

    def push(phase, source, target, device):
        pltpu.make_async_remote_copy(
            src_ref=source,
            dst_ref=target,
            send_sem=send_sem.at[phase],
            recv_sem=recv_sem.at[phase],
            device_id=device,
            device_id_type=MESH,
        ).start()

    def await_bytes(buffer, count, sem):
        if count:
            view = buffer.at[pl.ds(0, count)]
            pltpu.make_async_copy(view, view, sem).wait()

    for one_input in inputs[:7]:
        one_input.start()
    barrier = pltpu.get_barrier_semaphore()
    def enter(device, _):
        pl.semaphore_signal(barrier, inc=1, device_id=device, device_id_type=MESH)

    everyone(enter)

    for one_input in inputs[7:]:
        one_input.start()
    for one_input in inputs[:7]:
        one_input.wait()
    pack[...] = jnp.ones_like(pack)
    masked_recv[...] = jnp.where(edge_mask[...] > 0, receivers[...], -1)
    kind = species[...]
    for half in (0, BLOCK):
        spot = pl.ds(half, BLOCK)
        pack[0:1, spot] = (kind == 0).astype(F32)
        pack[1:2, spot] = (kind == 1).astype(F32)
        for axis in range(3):
            pack[2 + axis : 3 + axis, spot] = center - positions[axis]
        pack[6:7, spot] = atom_mask[...].astype(F32)
        pack[7:8, spot] = struct_id[...].astype(F32)
    pl.semaphore_wait(barrier, devices - 1)

    members(lambda device, _: push(0, pack, pack_all.at[col], device))
    members(lambda device, _: push(1, senders, send_all.at[col], device))
    members(lambda device, _: push(2, masked_recv, recv_all.at[col], device))
    pack_all[col] = pack[...]
    send_all[col] = senders[...]
    recv_all[col] = masked_recv[...]

    for one_input in inputs[7:]:
        one_input.wait()
    lane = iota((8, 128), 1)
    low_row = lane[0:1] < BLOCK
    low = lane < BLOCK
    row8 = iota((8, 128), 0)
    own = pack[...] * jnp.where((row8 >= 2) & (row8 <= 4), -1.0, 1.0)
    live = own[6:7]
    first_rows = iota((16, 128), 0)
    lane_half = (iota((16, 128), 1) >= BLOCK).astype(I32)
    half_sum = (first_rows == lane_half).astype(F32)
    wide_lane = iota((8, 512), 1)
    spot_of = 2 * (wide_lane >> 7) + ((wide_lane & 127) >= BLOCK).astype(I32)
    half_pick = (iota((8, 512), 0) == spot_of).astype(F32)
    half_pick = jnp.concatenate([half_pick] * 3 + [jnp.zeros((8, 512), F32)], axis=0).astype(BF16)

    mix_pd = (iota((72, CHANNELS), 0) - 12 * ((iota((72, CHANNELS), 0) * 5462) >> 16)) == iota(
        (72, CHANNELS), 1
    )
    mix_pd = mix_pd.astype(F32)
    mix_pc = ((iota((96, CHANNELS), 0) & 15) == iota((96, CHANNELS), 1)).astype(F32)
    same = ((iota((96, 72), 0) >> 4) == ((iota((96, 72), 1) * 5462) >> 16)).astype(F32)
    same_t = ((iota((72, 96), 1) >> 4) == ((iota((72, 96), 0) * 5462) >> 16)).astype(F32)
    for layer in range(2):
        table = channel_mix[:, layer, :]
        spread_c = mm(mix_pc, table)
        mix_back[layer] = stack_left(mm(mm(mix_pd, table, NT), mix_pc, NT) * same_t)
        mix_stack[layer] = stack_left(mm(spread_c, mix_pd, NT) * same)

    struct_rows = own[7:8].astype(I32)
    member = (struct_rows == iota((STRUCTS, 128), 0)).astype(F32)
    atom_cot = mm(energy_cot[...], member) * live
    counts[...] = jnp.zeros_like(counts)
    chunk = min(2048, edge_count)
    per_slot = edge_count // chunk
    wide = counts.shape[2]

    hot_rows = iota((128, chunk), 0).astype(F32).astype(BF16)
    none = jnp.zeros((), BF16)

    def count_edges(send, recv):
        local = recv - col * BLOCK
        inside = (local >= 0) & (local < BLOCK)
        key = jnp.where(inside, (send >> 8) * BLOCK + local, -1)
        step = jnp.where((send & 128) > 0, RADIX, 1.0).astype(BF16)
        sender_hot = jnp.where(hot_rows == (send & 127).astype(F32).astype(BF16), step, none)
        pair_hot = []
        for first in range(0, wide, 128):
            local_key = jnp.where((key >= first) & (key < first + 128), key - first, -1)
            hit = hot_rows == local_key.astype(F32).astype(BF16)
            pair_hot.append(jnp.where(hit, jnp.ones((), BF16), none))
        pair_hot = jnp.concatenate(pair_hot, axis=0)
        found = once(sender_hot, pair_hot, NT)
        upper = jnp.floor(found * (1.0 / RADIX))
        counts[0] += found - RADIX * upper
        counts[1] += upper

    def count_slot(slot, carry):
        for k in range(per_slot):
            spot = slice(k * chunk, (k + 1) * chunk)
            count_edges(send_all[slot, :, spot], recv_all[slot, :, spot])
        return carry

    count_slot(col, 0)

    for blank_ref in (dkind_sums, dsums, products):
        blank_ref[...] = jnp.zeros_like(blank_ref)
    await_bytes(pack_all, lanes - 1, recv_sem.at[0])
    for q in range(tiles):
        sender_rows[:, 128 * q : 128 * (q + 1)] = jnp.where(low, pack_all[2 * q], pack_all[2 * q + 1])
    columns[...] = jnp.transpose(sender_rows[...])

    def geometry(start):
        cols = columns[pl.ds(start, BLOCK), :]
        return Geometry(cols, own, low_row)

    def radial_block(i, carry):
        start = aligned(i * BLOCK, BLOCK)
        geo = geometry(start)
        envelope = geo.reach * geo.reach * NORM
        for pair, value in enumerate(geo.sines()):
            radial[pair, pl.ds(start, BLOCK), :] = value * envelope
        inverse[pl.ds(start, BLOCK), :] = geo.inverse
        return carry

    loop(group // BLOCK, radial_block, 0)

    def monomial_rows(rows):
        x, y, z = rows[2:3], rows[3:4], rows[4:5]
        table = {(0, 0, 0): None}
        for m in MONOMIALS[1:]:
            axis = next(i for i in range(3) if m[i])
            lower = m[:axis] + (m[axis] - 1,) + m[axis + 1 :]
            factor = (x, y, z)[axis]
            table[m] = factor if table[lower] is None else table[lower] * factor
        return table

    def spread():
        def one(q, carry):
            spot = pl.ds(aligned(q * 128, 128), 128)
            table = monomial_rows(sender_rows[:, spot])
            h = weights[0:CHANNELS, spot]
            for i, m in enumerate(MONOMIALS):
                value = h if table[m] is None else h * table[m]
                products[row_of(i, 0) : row_of(i, 0) + 8, spot] = value[0:8]
                products[row_of(i, 1) : row_of(i, 1) + 4, spot] = value[8:12]
            return carry

        loop(tiles, one, 0)
        for q in strips:
            split = parts(products[:, q])
            three, two = [], []
            for start, end in zip(DEGREE_ROWS, DEGREE_ROWS[1:]):
                three += [v[start:end] for v in split]
                two += [v[start:end] for v in split[:2]]
            three.append(jnp.zeros((8, three[0].shape[1]), F32))
            product_three[:, q] = jnp.concatenate(three, axis=0).astype(BF16)
            product_two[:, q] = jnp.concatenate(two, axis=0).astype(BF16)


    def kind_spread(q, carry):
        spot = pl.ds(aligned(q * 128, 128), 128)
        table = monomial_rows(sender_rows[:, spot])
        kinds = sender_rows[0:2, spot]
        for i, m in enumerate(MONOMIALS):
            kind_products[2 * i : 2 * i + 2, spot] = kinds if table[m] is None else kinds * table[m]
        return carry

    loop(tiles, kind_spread, 0)
    for q in strips:
        kind_parts = jnp.concatenate(parts(kind_products[:, q]), axis=0)
        blank_rows = jnp.zeros((8, kind_parts.shape[1]), F32)
        kind_three[:, q] = jnp.concatenate([kind_parts, blank_rows], axis=0).astype(BF16)
    columns_of = []
    for kind_of in range(2):
        embedded = mm(embedding[...], (iota((2, 128), 0) == kind_of).astype(F32), TN)
        padded = jnp.concatenate(
            [mm(channel_in[0], embedded, TN), jnp.zeros((PADDED - CHANNELS, 128), F32)], axis=0
        )
        columns_of.append([padded[0:8], padded[8:16]])

    await_bytes(send_all, lanes - 1, recv_sem.at[1])
    await_bytes(recv_all, lanes - 1, recv_sem.at[2])
    if devices <= 32:
        for k in range(1, lanes):
            count_slot(lax.rem(col + k, lanes), 0)
    else:
        lax.fori_loop(1, lanes, lambda k, carry: count_slot(lax.rem(col + k, lanes), carry), 0)
    low_tall = iota((128, 128), 1) < BLOCK
    for block in range(group // 128):
        turn_of = block // 2
        piece = counts[block % 2, :, 128 * (turn_of // 2) : 128 * (turn_of // 2 + 1)]
        turned = pltpu.roll(piece, BLOCK, 1)
        first_half, second_half = (piece, turned) if turn_of % 2 == 0 else (turned, piece)
        pair_weight[128 * block : 128 * (block + 1), :] = jnp.where(
            low_tall, first_half, second_half
        )

    def plane_block(i, carry):
        spot = pl.ds(aligned(i * BLOCK, BLOCK), BLOCK)
        weight = pair_weight[spot, :]
        step = inverse[spot, :]
        for pair in range(PAIRS):
            value = radial[pair, spot, :] * weight
            for order in range(4):
                high = value.astype(BF16)
                planes_high[spot, tile_of(order, pair)] = high
                planes_low[spot, tile_of(order, pair)] = (value - high.astype(F32)).astype(BF16)
                value = value * step
        return carry

    loop(group // BLOCK, plane_block, 0)

    xi, yi, zi = (jnp.broadcast_to(own[r : r + 1], (8, 128)) for r in (2, 3, 4))

    def chunk_spots(i):
        pair, tile = i // 2, i % 2
        return pair, tile, slice(128 * pair, 128 * (pair + 1))

    def kind_component(place, pair):
        return [
            jnp.broadcast_to(kind_moved[place, 2 * pair + k : 2 * pair + k + 1, :], (8, 128))
            for k in range(2)
        ]

    def kind_expand(both, tile):
        return [columns_of[0][tile] * a + columns_of[1][tile] * b for a, b in both]

    def shell_terms(pair, tile):
        out = []
        for order in range(4):
            spot = tile_of(order, pair)
            for m in range(COUNTS[order]):
                start = row_of(m, tile)
                out.append(sums[start : start + 8, spot])
        return out

    def live_rows(value, tile):
        return value if tile == 0 else jnp.where(row8 < CHANNELS - 8, value, 0.0)

    def mix_invariants(layer):
        mixed = stacked(mix_stack[layer], invariant[layer])
        for pair in range(PAIRS):
            feats[layer, 72 * pair : 72 * (pair + 1), :] = mixed[:, 128 * pair : 128 * (pair + 1)]

    def forward_kinds():
        by_high = once(kind_three[...], planes_high[...])
        by_low = once(kind_three[0:80, :], planes_low[...])
        kind_sums[...] = by_high[0:40] + ((by_high[40:80] + by_low[0:40]) + (by_high[80:120] + by_low[40:80]))
        for order in range(4):
            for m in range(COUNTS[order]):
                pieces = [kind_sums[2 * m : 2 * m + 2, tile_of(order, pair)] for pair in range(PAIRS)]
                kind_shells[OFFSETS[order] + m] = jnp.concatenate(
                    pieces + [jnp.zeros((2, 128), F32)], axis=0
                )
        moved = all_shifted([kind_shells[m] for m in range(SHELLS)], xi, yi, zi)
        for place, value in enumerate(moved):
            kind_moved[place] = value
        for pair in range(PAIRS):
            both = [kind_component(place, pair) for place in range(20)]
            for tile in range(2):
                for p, value in enumerate(contracted(kind_expand(both, tile))):
                    start = PADDED * p + 8 * tile
                    invariant[0, start : start + 8, 128 * pair : 128 * (pair + 1)] = value
        mix_invariants(0)

    def forward():
        for order, first, last in GROUPS:
            spot = slice(128 * first, 128 * last)
            end = DEGREE_ROWS[order + 1]
            by_high = once(product_three[0 : -(-3 * end // 16) * 16, :], planes_high[:, spot])
            by_low = once(product_two[0 : 2 * end, :], planes_low[:, spot])
            for start, stop in zip(DEGREE_ROWS[: order + 1], DEGREE_ROWS[1:]):
                size = stop - start
                h, l = 3 * start, 2 * start
                sums[start:stop, spot] = by_high[h : h + size] + (
                    (by_high[h + size : h + 2 * size] + by_low[l : l + size])
                    + (by_high[h + 2 * size : h + 3 * size] + by_low[l + size : l + 2 * size])
                )
        for i in range(2 * PAIRS):
            pair, tile, spot = chunk_spots(i)
            terms = shell_terms(pair, tile)
            for p, value in enumerate(invariants(terms, xi, yi, zi)):
                start = PADDED * p + 8 * tile
                invariant[1, start : start + 8, spot] = live_rows(value, tile)
        mix_invariants(1)

    def send_stats(phase, index, select_rows, first, second, extra=None):
        values = jnp.concatenate([first, second], axis=0)
        wide_values = jnp.concatenate(parts(values), axis=1).astype(BF16)
        rows = jnp.concatenate([select_rows] * 3, axis=1).astype(BF16)
        both = once(rows, wide_values, NT)
        for k in range(4):
            stat_own[index, 2 * k : 2 * k + 2, :] = both[0:2, 128 * k : 128 * (k + 1)]
        if extra is not None:
            stat_own[index, 2:3, 96 : 96 + STRUCTS] = extra
        everyone(
            lambda device, _: push(phase, stat_own.at[index], stat_all.at[index, me], device)
        )
        stat_all[index, me] = stat_own[index]

    def get_stats(phase, index):
        await_bytes(stat_all.at[index], devices - 1, recv_sem.at[phase])
        sums_of = [stat_all[index, k] for k in range(8)]
        for k in range(8, devices):
            sums_of[k % 8] = sums_of[k % 8] + stat_all[index, k]
        while len(sums_of) > 1:
            sums_of = [a + b for a, b in zip(sums_of[::2], sums_of[1::2])]
        return sums_of[0]

    def widen(rows):
        return once(
            jnp.concatenate([three_rows(rows), jnp.zeros((8, 128), BF16)], axis=0), half_pick, TN
        )

    rest_rows = ONES_ROW - 128

    def tall(wide, start):
        return jnp.concatenate(
            [wide[:, start : start + 128], wide[0:rest_rows, start + 128 : start + 256]], axis=0
        )

    ones_rows = iota((FEATURE_ROWS - ONES_ROW, 128), 0) == 0
    for layer in range(2):
        feats[layer, ONES_ROW:FEATURE_ROWS, :] = ones_rows.astype(F32)
        normed[layer, ONES_ROW:FEATURE_ROWS, :] = ones_rows.astype(F32)

    def send_moments(layer, phase):
        values = feats[layer]
        send_stats(phase, layer, half_sum * live, values, values * values)

    def normalise(layer, phase):
        total = get_stats(phase, layer)
        inverse_count = 1.0 / jnp.maximum(total[2:3, ONES_ROW - 128 : ONES_ROW - 127], 1.0)
        scaled = total * inverse_count
        means = pltpu.roll(scaled, 4, 0)
        scales = lax.rsqrt(scaled - means * means + variance_eps)
        wide = widen(jnp.where(row8 < 4, scaled, scales))
        scale = tall(wide, 256)
        normed[layer, 0:ONES_ROW, :] = (feats[layer, 0:ONES_ROW, :] - tall(wide, 0)) * scale
        rows = 2 * HEAD_ROWS
        high, middle, tail = (v.astype(BF16) for v in parts(normed[layer]))
        by_high = once(head_rows[layer], high)
        by_middle = once(head_rows[layer, 0 : 2 * rows, :], middle)
        by_tail = once(head_rows[layer, 0:rows, :], tail)
        joined = by_high[0:rows] + (
            (by_high[rows : 2 * rows] + by_middle[0:rows])
            + (by_high[2 * rows :] + by_middle[rows:] + by_tail)
        )
        chosen = jnp.where(low_row, joined[0:HEAD_ROWS], joined[HEAD_ROWS:])
        return chosen + pltpu.roll(chosen, BLOCK, 1), scale, inverse_count

    def run_head(layer, pre):
        hidden, hidden_slope = silu_pair(pre[0:HIDDEN])
        inner, inner_slope = silu_pair(stacked(inner_forward[layer], hidden) + inner_cols[layer])
        dinner = energy_cols[layer] * atom_cot * inner_slope
        dhidden = stacked(inner_back[layer], dinner) * hidden_slope
        return hidden, inner, dinner, dhidden

    def small_grad(layer, hidden, inner, dinner):
        left = jnp.concatenate([dinner, atom_cot * inner], axis=0)
        blank = jnp.zeros((128 - 32 - 32 * layer, 128), F32)
        right = [hidden, (iota((8, 128), 0) == 0).astype(F32), blank]
        if layer == 1:
            right = [jnp.zeros((32, 128), F32)] + right
        return mm(jnp.where(low_row, left, 0.0), jnp.concatenate(right, axis=0), NT)

    def halves(value):
        return jnp.where(low_row, value, 0.0), jnp.where(low_row, 0.0, value)

    def scatter_tiles(phase, source, target, base):
        for t in range(source.shape[0]):

            @pl.when(me != base + t)
            def _():
                there = base + t
                push(phase, source.at[t], target.at[me], (there // lanes, there % lanes))

            @pl.when(me == base + t)
            def _():
                target[me] = source[t]

    def mine(base, result):
        return (me >= base) & (me < base + result.shape[0])

    def share_tiles(phase, parts_of, result, base):
        @pl.when(mine(base, result))
        def _():
            await_bytes(parts_of, devices - 1, recv_sem.at[phase])
            total = parts_of[0]
            for k in range(1, devices):
                total = total + parts_of[k]
            result[me - base] = total
            everyone(
                lambda device, _: push(phase + 1, result.at[me - base], result.at[me - base], device)
            )

    def gather_tiles(phase, result, base):
        count_of = result.shape[0]

        @pl.when(mine(base, result))
        def _():
            await_bytes(result, count_of - 1, recv_sem.at[phase + 1])

        @pl.when(jnp.logical_not(mine(base, result)))
        def _():
            await_bytes(result, count_of, recv_sem.at[phase + 1])

    def drain_tiles(phase, parts_of, result, base):
        count_of = result.shape[0]

        @pl.when(mine(base, result))
        def _():
            await_bytes(result, count_of - 1, send_sem.at[phase])
            await_bytes(parts_of, devices - 1, send_sem.at[phase + 1])

        @pl.when(jnp.logical_not(mine(base, result)))
        def _():
            await_bytes(result, count_of, send_sem.at[phase])

    base_a, base_b, base_c = 0, tiles_a.shape[0], devices - tiles_c.shape[0]

    forward_kinds()
    send_moments(0, 3)
    for parity in range(2):
        k = iota((FEATURE_ROWS, FEATURES), 0)
        pair = (k >= 72).astype(I32) + (k >= 144).astype(I32)
        rest = k - 72 * pair
        kind_of = (rest * 5462) >> 16
        channel = rest - 12 * kind_of
        place = channel * 36 + (2 * pair + parity) * 6 + kind_of
        hit = (place == iota((FEATURE_ROWS, FEATURES), 1)) & (k < ONES_ROW)
        select[parity] = hit.astype(F32).astype(BF16)
    inner_cols, energy_cols = [], []
    head[...] = jnp.zeros_like(head)
    for layer in range(2):
        for parity in range(2):
            base = HEAD_ROWS * parity
            block = exact(hidden_weight[layer], select[parity], NT)
            if parity == 0:
                spot = (iota((2, FEATURE_ROWS), 1) == ONES_ROW) & (
                    iota((2, FEATURE_ROWS), 0) == layer
                )
                block = block + mm(hidden_bias[...], spot.astype(F32), TN)
            head[layer, base : base + HIDDEN, :] = block
            if layer == 0:
                message_rows = jnp.concatenate(
                    [message_weight[...], jnp.zeros((PADDED - CHANNELS, FEATURES), F32)], axis=0
                )
                head[0, base + HIDDEN : base + HEAD_ROWS, :] = exact(message_rows, select[parity], NT)
        whole = head[layer]
        head_rows[layer] = three_rows(whole)
        head_stack[layer] = stack_left(whole)
        if layer == 0:
            message_stack[...] = stack_left(
                jnp.concatenate([whole[HIDDEN:HEAD_ROWS], whole[HEAD_ROWS + HIDDEN :]], axis=0)
            )
        inner_back[layer] = stack_left(inner_weight[layer])
        inner_forward[layer] = stack_left(jnp.transpose(inner_weight[layer]))
        pick = (iota((2, 128), 0) == layer).astype(F32)
        inner_cols.append(mm(inner_bias[...], pick, TN))
        energy_cols.append(mm(energy_weight[...], pick, TN))

    pre_zero, scale_zero, inverse_count = normalise(0, 3)
    message = pre_zero[HIDDEN:HEAD_ROWS]
    message_own[...] = jnp.where(low, message[0:8], message[8:16])
    members(lambda device, _: push(4, message_own, message_all.at[col], device))
    message_all[col] = message_own[...]
    hidden_zero, inner_zero, dinner_zero, dhidden_zero = run_head(0, pre_zero)
    d_low, d_high = halves(dhidden_zero)
    gap = jnp.zeros((HEAD_ROWS - HIDDEN, 128), F32)
    dnormed_head = stacked(head_stack[0], jnp.concatenate([d_low, gap, d_high, gap], axis=0))

    def pack_head(target, layer, d_low, d_high):
        block = mm(jnp.concatenate([d_low, d_high], axis=0), normed[layer], NT)
        for r in range(6):
            for half in range(2):
                target[2 * r + half] = block[8 * r : 8 * (r + 1), 128 * half : 128 * (half + 1)]

    pack_head(tiles_a, 0, d_low, d_high)
    scatter_tiles(11, tiles_a, tiles_a_all, 0)
    weights[...] = jnp.zeros_like(weights)
    embedded = mm(embedding[...], sender_rows[0:2, :], TN)
    weights[0:CHANNELS, :] = mm(channel_in[1], embedded, TN)
    await_bytes(message_all, lanes - 1, recv_sem.at[4])
    for q in range(tiles):
        even, odd = message_all[2 * q], message_all[2 * q + 1]
        spot = slice(128 * q, 128 * (q + 1))
        weights[0:8, spot] += jnp.where(low, even, pltpu.roll(odd, BLOCK, 1))
        weights[8:16, spot] += jnp.where(low, pltpu.roll(even, BLOCK, 1), odd)

    spread()
    forward()
    send_moments(1, 5)
    turn = ANGLE * (1.0 + (iota((1, 128), 1) >= BLOCK).astype(F32))

    def slope_block(i, carry):
        start = aligned(i * BLOCK, BLOCK)
        spot = pl.ds(start, BLOCK)
        geo = geometry(start)
        step = geo.inverse
        square = step * step
        envelope = geo.reach * geo.reach * NORM
        slope = geo.reach * (-2.0 * NORM / (cutoff_radius * cutoff_radius))
        weight = pair_weight[spot, :]
        for pair, (sine, cosine) in enumerate(zip(geo.sines(), geo.cosines())):
            rate = (turn + 2.0 * ANGLE * pair) * cosine - sine
            value = weight * ((0.5 * square) * rate * envelope + sine * slope)
            plane = weight * (sine * envelope)
            slopes[spot, tile_of(0, pair)] = value
            for order in range(1, 4):
                plane = plane * step
                value = value * step - (0.5 * square) * plane
                slopes[spot, tile_of(order, pair)] = value
        return carry

    loop(group // BLOCK, slope_block, 0)
    for q in strips:
        kind_stack[:, q] = stack_left(kind_products[:, q])

    share_tiles(11, tiles_a_all, tiles_a_sum, base_a)
    pre_one, scale_one, _ = normalise(1, 5)
    hidden_one, inner_one, dinner_one, dhidden_one = run_head(1, pre_one)
    d_low, d_high = halves(dhidden_one)
    dnormed_one = stacked(head_stack[1], jnp.concatenate([d_low, gap, d_high, gap], axis=0))
    send_stats(6, 2, half_sum, dnormed_one, dnormed_one * normed[1])

    pack_head(tiles_b, 1, d_low, d_high)
    small = small_grad(0, hidden_zero, inner_zero, dinner_zero)
    small = small + small_grad(1, hidden_one, inner_one, dinner_one)
    for r in range(2):
        tiles_b[12 + r] = small[8 * r : 8 * (r + 1)] + pltpu.roll(small[16 + 8 * r : 24 + 8 * r], 64, 1)
    atom_energy = jnp.sum(energy_cols[0] * inner_zero + energy_cols[1] * inner_one, axis=0, keepdims=True)
    atom_energy = jnp.where(low_row, live * atom_energy, 0.0)
    energy_rows = mm(jnp.broadcast_to(atom_energy, (8, 128)), member, NT)[0:1]
    def feature_back(layer, phase, index, dnormed, scale):
        total = get_stats(phase, index)
        wide = widen(total * inverse_count)
        dfeats = scale * (
            dnormed[0:ONES_ROW] - live * (tall(wide, 0) + tall(wide, 256) * normed[layer, 0:ONES_ROW, :])
        )
        dmixed = jnp.concatenate([dfeats[72 * pair : 72 * (pair + 1)] for pair in range(PAIRS)], axis=1)
        dinvariant[...] = stacked(mix_back[layer], dmixed)
        return dmixed

    def mix_grad(layer, dmixed):
        return mm(invariant[layer], dmixed, NT, lax.Precision.HIGH) * same

    blank = jnp.zeros((8, 128), F32)

    def shell_back():
        moved = (blank, blank, blank)
        for i in range(2 * PAIRS):
            pair, tile, spot = chunk_spots(i)
            terms = shell_terms(pair, tile)
            cots = tuple(dinvariant[PADDED * p + 8 * tile : PADDED * p + 8 * tile + 8, 128 * pair : 128 * (pair + 1)] for p in range(6))
            _, pull = jax.vjp(invariants, terms, xi, yi, zi)
            dterms, *shift = pull(cots)
            for order in range(4):
                for m in range(COUNTS[order]):
                    value = dterms[OFFSETS[order] + m]
                    start = row_of(m, tile)
                    if tile == 0:
                        dsums[start : start + 8, tile_of(order, pair)] = value
                    else:
                        dsums[start : start + CHANNELS - 8, tile_of(order, pair)] = value[0 : CHANNELS - 8]
            moved = tuple(a + live_rows(b, tile) for a, b in zip(moved, shift))
        return moved

    def shell_back_kinds():
        dtable = [[blank, blank], [blank, blank]]
        folded = [[] for _ in range(20)]
        for pair in range(PAIRS):
            both = [kind_component(place, pair) for place in range(20)]
            sides = []
            for tile in range(2):
                cots = tuple(dinvariant[PADDED * p + 8 * tile : PADDED * p + 8 * tile + 8, 128 * pair : 128 * (pair + 1)] for p in range(6))
                _, pull = jax.vjp(contracted, kind_expand(both, tile))
                sides.append(pull(cots)[0])
                for k in range(2):
                    for place in range(20):
                        dtable[k][tile] = dtable[k][tile] + sides[tile][place] * both[place][k]
            for place in range(20):
                for k in range(2):
                    folded[place].append(
                        columns_of[k][0] * sides[0][place] + columns_of[k][1] * sides[1][place]
                    )
        dmoved = [jnp.where(row8 < 2 * PAIRS, row_sums(v, row8), 0.0) for v in folded]
        _, pull = jax.vjp(all_shifted, [kind_shells[m] for m in range(SHELLS)], xi, yi, zi)
        dterms, *moved = pull(dmoved)
        for order in range(4):
            for m in range(COUNTS[order]):
                value = dterms[OFFSETS[order] + m]
                for pair in range(PAIRS):
                    dkind_sums[2 * m : 2 * m + 2, tile_of(order, pair)] = value[2 * pair : 2 * pair + 2]
        return tuple(moved), [jnp.concatenate(halves_of, axis=0) for halves_of in dtable]

    def product_back():
        for order, first, last in GROUPS:
            lane_spot = slice(128 * first, 128 * last)
            end = DEGREE_ROWS[order + 1]
            high, low_part, _ = parts(dsums[0:end, lane_spot])
            left = jnp.concatenate([high, low_part], axis=0).astype(BF16)
            for spot in strips:
                by_high = once(left, planes_high[spot, lane_spot], NT)
                block = by_high[0:end] + (by_high[end:] + once(left[0:end], planes_low[spot, lane_spot], NT))
                if order == 3:
                    dproducts[0:end, spot] = block
                else:
                    dproducts[0:end, spot] += block

    def product_back_kinds():
        high, low_part, _ = parts(dkind_sums[...])
        left = jnp.concatenate([high, low_part], axis=0).astype(BF16)
        for spot in strips:
            by_high = once(left, planes_high[spot, :], NT)
            dkind_products[:, spot] = by_high[0:40] + (by_high[40:] + once(left, planes_low[spot, :], NT)[0:40])

    def weight_back():
        out = []
        for q in range(tiles):
            spot = slice(128 * q, 128 * (q + 1))
            table = monomial_rows(sender_rows[:, spot])
            both = []
            for tile in range(2):
                total = None
                for i, m in enumerate(MONOMIALS):
                    term = dproducts[row_of(i, tile) : row_of(i, tile) + 8, spot]
                    term = term if table[m] is None else term * table[m]
                    total = term if total is None else total + term
                both.append(live_rows(total, tile))
            out.append(jnp.concatenate(both, axis=0))
        return out

    def axis_slope(table, axis, value_of):
        total = None
        for i, m in enumerate(MONOMIALS):
            if not m[axis]:
                continue
            lower = table[m[:axis] + (m[axis] - 1,) + m[axis + 1 :]]
            term = value_of(i)
            if lower is not None:
                term = (float(m[axis]) * lower) * term
            total = term if total is None else total + term
        return total

    def coordinate_back():
        out = []
        for q in range(tiles):
            spot = slice(128 * q, 128 * (q + 1))
            table = monomial_rows(sender_rows[:, spot])
            sides = []
            for axis in range(3):
                total = None
                for tile in range(2):
                    slope = axis_slope(
                        table, axis, lambda i: dproducts[row_of(i, tile) : row_of(i, tile) + 8, spot]
                    )
                    term = weights[8 * tile : 8 * tile + 8, spot] * live_rows(slope, tile)
                    total = term if total is None else total + term
                sides.append(jnp.sum(total, axis=0, keepdims=True))
            out.append(sides)
        return out

    def coordinate_back_kinds():
        out = []
        for q in range(tiles):
            spot = slice(128 * q, 128 * (q + 1))
            table = monomial_rows(sender_rows[:, spot])
            kinds = sender_rows[0:2, spot]
            rows = [
                jnp.sum(kinds * dkind_products[2 * i : 2 * i + 2, spot], axis=0, keepdims=True)
                for i in range(len(MONOMIALS))
            ]
            out.append([axis_slope(table, axis, lambda i: rows[i]) for axis in range(3)])
        return out

    def radial_pull(block, first, last, spot):
        total = None
        for at in range(first, last):
            term = block[:, 128 * (at - first) : 128 * (at - first + 1)] * slopes[spot, 128 * at : 128 * (at + 1)]
            total = term if total is None else total + term
        return total

    def plane_back():
        for order, first, last in GROUPS:
            end = DEGREE_ROWS[order + 1]
            for spot in strips:
                block = mm(products[0:end, spot], dsums[0:end, 128 * first : 128 * last], TN)
                term = radial_pull(block, first, last, spot)
                if order == 3:
                    pulls[spot, :] = term
                else:
                    pulls[spot, :] += term

    def plane_back_kinds():
        right = stack_right(dkind_sums[...])
        for order, first, last in GROUPS:
            for spot in strips:
                block = once(kind_stack[:, spot], right[:, 128 * first : 128 * last], TN)
                pulls[spot, :] += radial_pull(block, first, last, spot)

    dmixed_one = feature_back(1, 6, 2, dnormed_one, scale_one)
    moved_one = shell_back()
    product_back()
    dweights_one = weight_back()
    for q in range(tiles):
        top, bottom = dweights_one[q][0:8], dweights_one[q][8:16]
        dmessage_own[2 * q] = jnp.where(low, top, pltpu.roll(bottom, BLOCK, 1))
        dmessage_own[2 * q + 1] = jnp.where(low, pltpu.roll(top, BLOCK, 1), bottom)
    members(
        lambda device, target: push(7, dmessage_own.at[target], dmessage_all.at[col], device)
    )
    dmessage_all[col] = dmessage_own[col]
    kinds_of = sender_rows[...]
    dtable_one = jnp.zeros((PADDED, 8), F32)
    for q in range(tiles):
        dtable_one = dtable_one + mm(dweights_one[q], kinds_of[:, 128 * q : 128 * (q + 1)], NT)
    slopes_one = coordinate_back()
    mix_one = mix_grad(1, dmixed_one)
    scatter_tiles(13, tiles_b, tiles_b_all, base_b)
    await_bytes(dmessage_all, lanes - 1, recv_sem.at[7])
    arrived = dmessage_all[0]
    for k in range(1, lanes):
        arrived = arrived + dmessage_all[k]
    turned = pltpu.roll(arrived, BLOCK, 1)
    dmessage = jnp.concatenate([jnp.where(low, arrived, turned), jnp.where(low, turned, arrived)], axis=0)

    m_low, m_high = halves(dmessage)
    dmessage_both = jnp.concatenate([m_low, m_high], axis=0)
    dnormed_zero = dnormed_head + stacked(message_stack[...], dmessage_both)
    send_stats(8, 3, half_sum, dnormed_zero, dnormed_zero * normed[0], energy_rows)
    dmessage_weight = mm(dmessage_both, normed[0], NT)
    for r in range(4):
        for half in range(2):
            tiles_c[2 * r + half] = dmessage_weight[
                8 * r : 8 * (r + 1), 128 * half : 128 * (half + 1)
            ]
    scatter_tiles(15, tiles_c, tiles_c_all, base_c)
    fold_c = (iota((PADDED, 96), 0) == (iota((PADDED, 96), 1) & 15)).astype(F32)
    d_of = iota((72, 128), 0) - 12 * ((iota((72, 128), 0) * 5462) >> 16)
    seat_mix = [(iota((72, 128), 1) == d_of + 12 * layer).astype(BF16) for layer in range(2)]
    seat_kind = ((lane == row8 + 26) & (row8 < 2)).astype(F32)

    def fold_mix(layer, value):
        wide_value = once(fold_c.astype(BF16), jnp.concatenate(parts(exact(value, seat_mix[layer])), axis=1).astype(BF16))
        return wide_value[:, 0:128] + (wide_value[:, 128:256] + wide_value[:, 256:384])

    final_one = fold_mix(1, mix_one) + mm(dtable_one, seat_kind)
    plane_back()
    share_tiles(13, tiles_b_all, tiles_b_sum, base_b)
    dmixed_zero = feature_back(0, 8, 3, dnormed_zero, scale_zero)
    share_tiles(15, tiles_c_all, tiles_c_sum, base_c)
    moved_zero, dtables = shell_back_kinds()
    mix_zero = mix_grad(0, dmixed_zero)
    final = fold_mix(0, mix_zero) + final_one
    for k in range(2):
        total = jnp.sum(dtables[k], axis=1, keepdims=True)
        final = final + jnp.where(iota((PADDED, 128), 1) == 24 + k, total, 0.0)
    folded = final[0:8] + pltpu.roll(pltpu.roll(final[0:8], 4, 0), 32, 1) + pltpu.roll(final[8:16], 64, 1)
    final_own[...] = folded[0:4]
    everyone(lambda device, _: push(10, final_own, final_all.at[me], device))
    final_all[me] = final_own[...]
    plane_back_kinds()
    product_back_kinds()
    slopes_zero = coordinate_back_kinds()
    pull_of = pulls[...]
    to_own = mm(sender_rows[...], pull_of, NN, lax.Precision.HIGH)
    to_sender = mm(own, pull_of, NT, lax.Precision.HIGH)
    force_own[...] = jnp.zeros_like(force_own)
    for q in range(tiles):
        spot = slice(128 * q, 128 * (q + 1))
        weight_row = to_sender[5:6, spot]
        for axis in range(3):
            value = -2.0 * (to_sender[2 + axis : 3 + axis, spot] + sender_rows[2 + axis : 3 + axis, spot] * weight_row)
            value = value - slopes_zero[q][axis] - slopes_one[q][axis]
            force_own[2 * q, axis : axis + 1, :] = value
            force_own[2 * q + 1, axis : axis + 1, :] = pltpu.roll(value, BLOCK, 1)
    members(lambda device, target: push(9, force_own.at[target], force_all.at[col], device))
    force_all[col] = force_own[col]
    own_force = []
    for axis in range(3):
        pairwise = 2.0 * (to_own[2 + axis : 3 + axis] + own[2 + axis : 3 + axis] * to_own[5:6])
        moved = jnp.sum(moved_zero[axis] + moved_one[axis], axis=0, keepdims=True)
        both = pairwise + moved
        own_force.append(both + pltpu.roll(both, BLOCK, 1))

    group_energy = stat_all[3, row * lanes, 2:3, 96 : 96 + STRUCTS]
    for k in range(1, lanes):
        group_energy = group_energy + stat_all[3, row * lanes + k, 2:3, 96 : 96 + STRUCTS]
    energies_out[...] = group_energy

    gather_tiles(11, tiles_a_sum, base_a)
    gather_tiles(13, tiles_b_sum, base_b)
    pick_ones = ((iota((8, FEATURE_ROWS), 0) == 0) & (iota((8, FEATURE_ROWS), 1) == ONES_ROW)).astype(F32)
    for layer in range(2):
        total = None
        for parity in range(2):
            rows = []
            for r in range(3):
                at = 6 * parity + 2 * r
                summed = (tiles_a_sum, tiles_b_sum)[layer]
                rows.append(jnp.concatenate([summed[at], summed[at + 1]], axis=1))
            block = jnp.concatenate(rows, axis=0)
            if parity == 0:
                hidden_bias_out[layer : layer + 1, :] = mm(pick_ones, block, NT)[0:1]
            part = exact(block, select[parity])
            total = part if total is None else total + part
        hidden_weight_out[layer] = total
    small_sum = jnp.concatenate([tiles_b_sum[12 + r] for r in range(2)], axis=0)
    for layer in range(2):
        inner_weight_out[layer] = small_sum[0:INNER, 32 * layer : 32 * layer + HIDDEN]
        pick = ((row8 == 0) & (lane == 32 * layer + HIDDEN)).astype(F32)
        inner_bias_out[layer : layer + 1, :] = mm(pick, small_sum, NT)[0:1]
        pick = ((row8 == 0) & (lane == 64 + 32 * layer + HIDDEN)).astype(F32)
        energy_weight_out[layer : layer + 1, :] = mm(pick, small_sum, NT)[0:1]
    gather_tiles(15, tiles_c_sum, base_c)
    total = None
    for parity in range(2):
        rows = [
            jnp.concatenate(
                [tiles_c_sum[4 * parity + 2 * r], tiles_c_sum[4 * parity + 2 * r + 1]], axis=1
            )
            for r in range(2)
        ]
        part = exact(jnp.concatenate(rows, axis=0), select[parity])
        total = part if total is None else total + part
    message_weight_out[...] = total[0:CHANNELS]

    await_bytes(final_all, devices - 1, recv_sem.at[10])
    final = final_all[0]
    for k in range(1, devices):
        final = final + final_all[k]
    final = jnp.concatenate([final, jnp.zeros((4, 128), F32)], axis=0)
    upper = jnp.where(row8 < 4, final, pltpu.roll(pltpu.roll(final, 4, 0), 96, 1))
    final = jnp.concatenate([upper, pltpu.roll(final, 64, 1)], axis=0)
    dembedding = None
    for layer in range(2):
        channel_mix_out[:, layer, :] = final[0:CHANNELS, 12 * layer : 12 * (layer + 1)]
        dtable = final[0:CHANNELS, 24 + 2 * layer : 26 + 2 * layer]
        channel_in_out[layer] = lax.dot_general(
            embedding[...],
            dtable,
            (((0,), (1,)), ((), ())),
            precision=lax.Precision.HIGHEST,
            preferred_element_type=F32,
        )
        part = lax.dot_general(
            dtable,
            channel_in[layer],
            (((0,), (1,)), ((), ())),
            precision=lax.Precision.HIGHEST,
            preferred_element_type=F32,
        )
        dembedding = part if dembedding is None else dembedding + part
    embedding_out[...] = dembedding

    await_bytes(force_all, lanes - 1, recv_sem.at[9])
    force = force_all[0]
    for k in range(1, lanes):
        force = force + force_all[k]
    for axis in range(3):
        position_out[axis] = (force[axis : axis + 1] + own_force[axis])[:, 0:BLOCK]

    await_bytes(pack_all, lanes - 1, send_sem.at[0])
    await_bytes(send_all, lanes - 1, send_sem.at[1])
    await_bytes(recv_all, lanes - 1, send_sem.at[2])
    await_bytes(stat_all.at[0], devices - 1, send_sem.at[3])
    await_bytes(message_all, lanes - 1, send_sem.at[4])
    await_bytes(stat_all.at[1], devices - 1, send_sem.at[5])
    await_bytes(stat_all.at[2], devices - 1, send_sem.at[6])
    await_bytes(dmessage_all, lanes - 1, send_sem.at[7])
    await_bytes(stat_all.at[3], devices - 1, send_sem.at[8])
    await_bytes(force_all, lanes - 1, send_sem.at[9])
    await_bytes(final_all, devices - 1, send_sem.at[10])
    drain_tiles(11, tiles_a_all, tiles_a_sum, base_a)
    drain_tiles(13, tiles_b_all, tiles_b_sum, base_b)
    drain_tiles(15, tiles_c_all, tiles_c_sum, base_c)


def hand_over(*refs):
    for source, target in zip(refs[:11], refs[11:]):
        target[...] = source[...]


def solution(mesh):
    lanes = mesh.shape["edge"]
    structs = mesh.shape["struct"]
    devices = lanes * structs

    def step(
        positions,
        species,
        struct_id,
        atom_mask,
        senders,
        receivers,
        edge_mask,
        energy_cot,
        embedding,
        channel_in,
        channel_mix,
        hidden_weight,
        hidden_bias,
        inner_weight,
        inner_bias,
        energy_weight,
        message_weight,
    ):
        owned = positions.shape[2]
        group = owned * lanes
        edges = senders.shape[1]
        inputs = [
            positions,
            species,
            struct_id,
            atom_mask,
            senders,
            receivers,
            edge_mask,
            energy_cot,
            embedding,
            channel_in,
            jnp.transpose(channel_mix, (1, 0, 2)),
            jnp.transpose(hidden_weight, (0, 2, 1)),
            hidden_bias,
            jnp.transpose(inner_weight, (0, 2, 1)),
            inner_bias,
            energy_weight,
            jnp.transpose(message_weight),
        ]
        vmem = pltpu.VMEM
        shapes = [
            (1, STRUCTS),
            (3, 1, owned),
            embedding.shape,
            channel_in.shape,
            (CHANNELS, 2, CHANNELS),
            (2, HIDDEN, FEATURES),
            hidden_bias.shape,
            (2, INNER, HIDDEN),
            inner_bias.shape,
            energy_weight.shape,
            (CHANNELS, FEATURES),
        ]
        scratch = [
            vmem((8, 128), F32),
            vmem((lanes, 8, 128), F32),
            vmem((lanes, 1, edges), I32),
            vmem((1, edges), I32),
            vmem((lanes, 1, edges), I32),
            vmem((2, 128, BLOCK * (group // 256)), F32),
            vmem((group, 128), F32),
            vmem((group, 8), F32),
            vmem((8, group), F32),
            vmem((PAIRS, group, 128), F32),
            vmem((group, 128), F32),
            vmem((group, PLANE_LANES), BF16),
            vmem((group, PLANE_LANES), BF16),
            vmem((group, PLANE_LANES), F32),
            vmem((group, 128), F32),
            vmem((PADDED, group), F32),
            vmem((PRODUCT_ROWS, group), F32),
            vmem((752, group), BF16),
            vmem((496, group), BF16),
            vmem((PRODUCT_ROWS, PLANE_LANES), F32),
            vmem((PRODUCT_ROWS, PLANE_LANES), F32),
            vmem((40, group), F32),
            vmem((128, group), BF16),
            vmem((240, group), BF16),
            vmem((40, PLANE_LANES), F32),
            vmem((SHELLS, 8, 128), F32),
            vmem((20, 8, 128), F32),
            vmem((40, PLANE_LANES), F32),
            vmem((40, group), F32),
            vmem((PRODUCT_ROWS, group), F32),
            vmem((2, 96, 128 * PAIRS), F32),
            vmem((96, 128 * PAIRS), F32),
            vmem((2, FEATURE_ROWS, 128), F32),
            vmem((2, FEATURE_ROWS, 128), F32),
            vmem((2, FEATURE_ROWS, FEATURES), BF16),
            vmem((2, 2 * HEAD_ROWS, FEATURE_ROWS), F32),
            vmem((2, 6 * HEAD_ROWS, FEATURE_ROWS), BF16),
            vmem((2, 12 * HEAD_ROWS, FEATURE_ROWS), BF16),
            vmem((12 * PADDED, FEATURE_ROWS), BF16),
            vmem((2, 6 * HIDDEN, INNER), BF16),
            vmem((2, 6 * INNER, HIDDEN), BF16),
            vmem((2, 6 * 96, 72), BF16),
            vmem((2, 6 * 72, 96), BF16),
            vmem((4, 8, 128), F32),
            vmem((4, devices, 8, 128), F32),
            vmem((8, 128), F32),
            vmem((lanes, 8, 128), F32),
            vmem((lanes, 8, 128), F32),
            vmem((lanes, 8, 128), F32),
            vmem((lanes, 8, 128), F32),
            vmem((lanes, 8, 128), F32),
            vmem((4, 128), F32),
            vmem((devices, 4, 128), F32),
            vmem((12, 8, 128), F32),
            vmem((devices, 8, 128), F32),
            vmem((12, 8, 128), F32),
            vmem((14, 8, 128), F32),
            vmem((devices, 8, 128), F32),
            vmem((14, 8, 128), F32),
            vmem((8, 8, 128), F32),
            vmem((devices, 8, 128), F32),
            vmem((8, 8, 128), F32),
            pltpu.SemaphoreType.DMA((20,)),
            pltpu.SemaphoreType.DMA((20,)),
            pltpu.SemaphoreType.DMA((17,)),
        ] + [vmem(v.shape, v.dtype) for v in inputs]
        outs = pl.pallas_call(
            functools.partial(body, lanes, structs),
            out_shape=[vmem(s, F32) for s in shapes],
            in_specs=[pl.BlockSpec(memory_space=pl.ANY)] * 17,
            out_specs=[pl.BlockSpec(memory_space=vmem)] * 11,
            scratch_shapes=scratch,
            compiler_params=pltpu.CompilerParams(
                collective_id=0, has_side_effects=True, vmem_limit_bytes=60 * 1024 * 1024
            ),
        )(*inputs)
        outs = pl.pallas_call(
            hand_over,
            out_shape=[jax.ShapeDtypeStruct(s, F32) for s in shapes],
            in_specs=[pl.BlockSpec(memory_space=vmem)] * 11,
            out_specs=[pl.BlockSpec(memory_space=vmem)] * 11,
        )(*(pltpu.with_memory_space_constraint(v, pltpu.VMEM) for v in outs))
        outs = list(outs)
        outs[4] = jnp.transpose(outs[4], (1, 0, 2))
        outs[5] = jnp.transpose(outs[5], (0, 2, 1))
        outs[7] = jnp.transpose(outs[7], (0, 2, 1))
        outs[10] = jnp.transpose(outs[10])
        return tuple(outs)

    tiled = P("struct", "edge")
    return jax.shard_map(
        step,
        mesh=mesh,
        in_specs=(
            P(None, "struct", "edge"),
            tiled,
            tiled,
            tiled,
            tiled,
            tiled,
            tiled,
            P("struct", None),
        )
        + (P(),) * 9,
        out_specs=(P("struct", None), P(None, "struct", "edge")) + (P(),) * 9,
        check_vma=False,
    )
```

```python
import functools
import math

import jax
import jax.numpy as jnp
import numpy as np
from jax import lax
from jax.experimental import pallas as pl
from jax.experimental.pallas import tpu as pltpu
from jax.sharding import PartitionSpec as P

CHANNELS = 12
PADDED = 16
RADIALS = 6
PAIRS = 3
STRUCTS = 8
HIDDEN = 24
INNER = 16
FEATURES = 432
HEAD_ROWS = 40
FEATURE_ROWS = 256
ONES_ROW = 216
BLOCK = 64

cutoff_radius = 6.0
variance_eps = 1e-05
center = 1.5

MESH = pl.DeviceIdType.MESH
F32 = jnp.float32
BF16 = jnp.bfloat16
I32 = jnp.int32
NN = ((1,), (0,))
NT = ((1,), (1,))
TN = ((0,), (0,))

MONOMIALS = sorted(
    [(a, b, c) for a in range(4) for b in range(4) for c in range(4) if a + b + c <= 3],
    key=lambda m: (sum(m), -m[0], -m[1], -m[2]),
)
PLACE = {m: i for i, m in enumerate(MONOMIALS)}
COUNTS = [1, 4, 10, 20]
OFFSETS = [0, 1, 5, 15]
SHELLS = 35
DEGREE_ROWS = [0, 16, 56, 128, 248]
DEGREE_COUNTS = [1, 3, 6, 10]


def row_of(place, tile):
    degree = sum(MONOMIALS[place])
    within = place - sum(DEGREE_COUNTS[:degree])
    return DEGREE_ROWS[degree] + (8 * DEGREE_COUNTS[degree] + 4 * within if tile else 8 * within)


PRODUCT_ROWS = 256
LANE_TILES = [(3, 0), (3, 1), (3, 2), (2, 2), (2, 0), (2, 1), (1, 0), (1, 1), (1, 2), (0, 2), (0, 0), (0, 1)]
GROUPS = [(3, 0, 4), (2, 4, 6), (1, 6, 10), (0, 10, 12)]
PLANE_LANES = 128 * len(LANE_TILES)


def tile_of(order, pair):
    at = LANE_TILES.index((order, pair))
    return slice(128 * at, 128 * (at + 1))


RADIX = 4096.0


def fitted(function, low, high, degree):
    series = np.polynomial.chebyshev.Chebyshev.interpolate(
        lambda w: function(0.5 * (high - low) * w + 0.5 * (high + low)), degree
    )
    return [float(v) for v in series.convert(kind=np.polynomial.Polynomial).coef]


LOW, HIGH = 0.9, 28.1
ANGLE = math.pi / cutoff_radius
SINE = fitted(lambda u: np.sin(ANGLE * np.sqrt(u)) / np.sqrt(u), LOW, HIGH, 6)
COSINE = fitted(lambda u: np.cos(ANGLE * np.sqrt(u)), LOW, HIGH, 6)
NORM = math.sqrt(2.0 / cutoff_radius)


def mm(left, right, kind=NN, precision=lax.Precision.HIGHEST):
    return lax.dot_general(
        left, right, (kind, ((), ())), precision=precision, preferred_element_type=F32
    )


def once(left, right, kind=NN):
    return lax.dot_general(left, right, (kind, ((), ())), preferred_element_type=F32)


def parts(value):
    high = value.astype(BF16).astype(F32)
    rest = value - high
    middle = rest.astype(BF16).astype(F32)
    return high, middle, rest - middle


def stack_left(value):
    high, middle, tail = parts(value)
    stack = jnp.concatenate([high, high, middle, high, tail, middle], axis=0)
    return jnp.transpose(stack).astype(BF16)


def stack_right(value):
    high, middle, tail = parts(value)
    return jnp.concatenate([high, middle, high, tail, high, middle], axis=0).astype(BF16)


def stacked(left, right):
    return once(left, stack_right(right))


def three_rows(value):
    return jnp.concatenate(parts(value), axis=0).astype(BF16)


def exact(left, right, kind=NN):
    rows = left.shape[0]
    out = once(three_rows(left), right, kind)
    return out[0:rows] + (out[rows : 2 * rows] + out[2 * rows :])


def loop(count, action, carry):
    if count <= 8:
        for i in range(count):
            carry = action(i, carry)
        return carry
    return lax.fori_loop(0, count, action, carry)


def aligned(value, size):
    return value if isinstance(value, int) else pl.multiple_of(value, size)


def iota(shape, dim):
    return lax.broadcasted_iota(I32, shape, dim)


def horner(coefficients, w):
    total = jnp.full_like(w, coefficients[-1])
    for value in coefficients[-2::-1]:
        total = total * w + value
    return total


def shifted(terms, order, x, y, z):
    current = terms
    for axis, value in enumerate((x, y, z)):
        two, three = 2.0 * value, 3.0 * value
        square = value * value
        three_square, cube = 3.0 * square, square * value
        factors = [None, [value], [square, two], [cube, three_square, three]]
        fresh = {}
        for m in MONOMIALS[: COUNTS[order]]:
            if axis == 2 and sum(m) != order:
                continue
            power = m[axis]
            total = current[m]
            for lower in range(power):
                source = m[:axis] + (lower,) + m[axis + 1 :]
                total = total + factors[power][lower] * current[source]
            fresh[m] = total
        current = fresh
    return current


def all_shifted(terms, x, y, z):
    out = []
    for order in range(4):
        own = {m: terms[OFFSETS[order] + i] for i, m in enumerate(MONOMIALS[: COUNTS[order]])}
        moved = shifted(own, order, x, y, z) if order else own
        out += [moved[m] for m in MONOMIALS if sum(m) == order]
    return out


def contracted(components):
    by_order = [{}, {}, {}, {}]
    for m, value in zip(MONOMIALS, components):
        by_order[sum(m)][m] = value
    scalar = by_order[0][(0, 0, 0)]
    vx, vy, vz = by_order[1][(1, 0, 0)], by_order[1][(0, 1, 0)], by_order[1][(0, 0, 1)]
    m = by_order[2]
    xx, xy, xz = m[(2, 0, 0)], m[(1, 1, 0)], m[(1, 0, 1)]
    yy, yz, zz = m[(0, 2, 0)], m[(0, 1, 1)], m[(0, 0, 2)]
    q = by_order[3]
    xxx, yyy, zzz = q[(3, 0, 0)], q[(0, 3, 0)], q[(0, 0, 3)]
    xxy, xxz, xyy = q[(2, 1, 0)], q[(2, 0, 1)], q[(1, 2, 0)]
    xyz, xzz, yyz, yzz = q[(1, 1, 1)], q[(1, 0, 2)], q[(0, 2, 1)], q[(0, 1, 2)]
    first = vx * vx + vy * vy + vz * vz
    second = xx * xx + yy * yy + zz * zz + 2.0 * (xy * xy + xz * xz + yz * yz)
    third = (
        xxx * xxx
        + yyy * yyy
        + zzz * zzz
        + 3.0 * (xxy * xxy + xxz * xxz + xyy * xyy + xzz * xzz + yyz * yyz + yzz * yzz)
        + 6.0 * (xyz * xyz)
    )
    fourth = (
        vx * (xx * vx + xy * vy + xz * vz)
        + vy * (xy * vx + yy * vy + yz * vz)
        + vz * (xz * vx + yz * vy + zz * vz)
    )
    xy2, xz2, yz2 = 2.0 * xy, 2.0 * xz, 2.0 * yz
    fifth = (
        vx * (xxx * xx + xyy * yy + xzz * zz + xxy * xy2 + xxz * xz2 + xyz * yz2)
        + vy * (xxy * xx + yyy * yy + yzz * zz + xyy * xy2 + xyz * xz2 + yyz * yz2)
        + vz * (xxz * xx + yyz * yy + zzz * zz + xyz * xy2 + xzz * xz2 + yzz * yz2)
    )
    return (scalar, first, second, third, fourth, fifth)


def invariants(terms, x, y, z):
    return contracted(all_shifted(terms, x, y, z))


def row_sums(values, row8):
    def fold(a, b, size):
        if b is None:
            return a + pltpu.roll(a, 8 - size, 0)
        first = (row8 & size) == 0
        if size == 4:
            return jnp.where(first, a, b) + pltpu.roll(jnp.where(first, b, a), 4, 0)
        return jnp.where(first, a + pltpu.roll(a, 8 - size, 0), b + pltpu.roll(b, size, 0))

    values = list(values) + [None] * (8 - len(values))
    for size in (4, 2, 1):
        values = [fold(values[i], values[i + size], size) for i in range(size)]
    return values[0]


def silu_pair(v):
    gate = 1.0 / (1.0 + jnp.exp(-v))
    return v * gate, gate * (1.0 + v * (1.0 - gate))


class Geometry:
    def __init__(self, columns, own, lane_low):
        dx = own[2:3] + columns[:, 2:3]
        dy = own[3:4] + columns[:, 3:4]
        dz = own[4:5] + columns[:, 4:5]
        self.u = dx * dx + dy * dy + dz * dz + 1.0
        w = (self.u - 0.5 * (LOW + HIGH)) * (2.0 / (HIGH - LOW))
        self.sine = horner(SINE, w)
        self.cosine = horner(COSINE, w)
        self.inverse = lax.rsqrt(self.u)
        self.reach = 1.0 - self.u * (1.0 / (cutoff_radius * cutoff_radius))
        self.lane_low = lane_low

    def sines(self):
        step = 2.0 * (2.0 * self.cosine * self.cosine - 1.0)
        before = jnp.where(self.lane_low, -self.sine, 0.0)
        now = jnp.where(self.lane_low, self.sine, 2.0 * self.cosine * self.sine)
        return self.series(step, before, now)

    def cosines(self):
        double = 2.0 * self.cosine * self.cosine - 1.0
        before = jnp.where(self.lane_low, self.cosine, 1.0)
        now = jnp.where(self.lane_low, self.cosine, double)
        return self.series(2.0 * double, before, now)

    def series(self, step, before, now):
        out = [now]
        for _ in range(PAIRS - 1):
            before, now = now, step * now - before
            out.append(now)
        return out


def body(lanes, structs, *refs):
    sources, held, refs = refs[:17], refs[-17:], refs[17:-17]
    (
        positions,
        species,
        struct_id,
        atom_mask,
        senders,
        receivers,
        edge_mask,
        energy_cot,
        embedding,
        channel_in,
        channel_mix,
        hidden_weight,
        hidden_bias,
        inner_weight,
        inner_bias,
        energy_weight,
        message_weight,
    ) = held
    (
        energies_out,
        position_out,
        embedding_out,
        channel_in_out,
        channel_mix_out,
        hidden_weight_out,
        hidden_bias_out,
        inner_weight_out,
        inner_bias_out,
        energy_weight_out,
        message_weight_out,
        pack,
        pack_all,
        send_all,
        masked_recv,
        recv_all,
        counts,
        pair_weight,
        columns,
        sender_rows,
        radial,
        inverse,
        planes_high,
        planes_low,
        turned_high,
        turned_low,
        slopes,
        pulls,
        weights,
        products,
        product_three,
        product_two,
        sums,
        dsums,
        kind_products,
        kind_three,
        kind_stack,
        kind_sums,
        kind_shells,
        kind_moved,
        dkind_sums,
        dkind_products,
        dproducts,
        invariant,
        dinvariant,
        feats,
        normed,
        select,
        head,
        head_rows,
        head_stack,
        message_stack,
        inner_forward,
        inner_back,
        mix_stack,
        mix_back,
        stat_own,
        stat_all,
        message_own,
        message_all,
        dmessage_own,
        dmessage_all,
        force_own,
        force_all,
        final_own,
        final_all,
        tiles_a,
        tiles_a_all,
        tiles_a_sum,
        tiles_b,
        tiles_b_all,
        tiles_b_sum,
        tiles_c,
        tiles_c_all,
        tiles_c_sum,
        send_sem,
        recv_sem,
        input_sem,
    ) = refs
    devices = lanes * structs
    edge_count = senders.shape[1]
    inputs = [
        pltpu.make_async_copy(source, target, input_sem.at[i])
        for i, (source, target) in enumerate(zip(sources, held))
    ]
    group = pair_weight.shape[0]
    tiles = group // 128
    strips = [slice(k, k + 512) for k in range(0, group, 512)]
    row = lax.axis_index("struct")
    col = lax.axis_index("edge")
    me = row * lanes + col

    def everyone(action):
        def one(k, carry):
            target = lax.rem(me + k, devices)
            action((target // lanes, lax.rem(target, lanes)), target)
            return carry

        if (structs, lanes) == (4, 8):
            for k in range(devices - 1, 0, -1):
                at, there = row ^ (k % structs), col ^ (k // structs)
                action((at, there), at * lanes + there)
        else:
            lax.fori_loop(1, devices, one, 0)

    def members(action):
        def one(k, carry):
            target = lax.rem(col + k, lanes)
            action((row, target), target)
            return carry

        if lanes <= 8:
            for k in range(1, lanes):
                one(k, 0)
        else:
            lax.fori_loop(1, lanes, one, 0)

    def push(phase, source, target, device):
        pltpu.make_async_remote_copy(
            src_ref=source,
            dst_ref=target,
            send_sem=send_sem.at[phase],
            recv_sem=recv_sem.at[phase],
            device_id=device,
            device_id_type=MESH,
        ).start()

    def await_bytes(buffer, count, sem):
        if count:
            view = buffer.at[pl.ds(0, count)]
            pltpu.make_async_copy(view, view, sem).wait()

    for one_input in inputs[:7]:
        one_input.start()
    barrier = pltpu.get_barrier_semaphore()
    def enter(device, _):
        pl.semaphore_signal(barrier, inc=1, device_id=device, device_id_type=MESH)

    everyone(enter)
    for one_input in inputs[7:]:
        one_input.start()
    for one_input in inputs[:7]:
        one_input.wait()
    pack[...] = jnp.ones_like(pack)
    masked_recv[...] = jnp.where(edge_mask[...] > 0, receivers[...], -1)
    kind = species[...]
    for half in (0, BLOCK):
        spot = pl.ds(half, BLOCK)
        pack[0:1, spot] = (kind == 0).astype(F32)
        pack[1:2, spot] = (kind == 1).astype(F32)
        for axis in range(3):
            pack[2 + axis : 3 + axis, spot] = center - positions[axis]
        pack[6:7, spot] = atom_mask[...].astype(F32)
        pack[7:8, spot] = struct_id[...].astype(F32)
    pl.semaphore_wait(barrier, devices - 1)

    members(lambda device, _: push(0, pack, pack_all.at[col], device))
    members(lambda device, _: push(1, senders, send_all.at[col], device))
    members(lambda device, _: push(2, masked_recv, recv_all.at[col], device))
    pack_all[col] = pack[...]
    send_all[col] = senders[...]
    recv_all[col] = masked_recv[...]

    for one_input in inputs[7:]:
        one_input.wait()
    lane = iota((8, 128), 1)
    low_row = lane[0:1] < BLOCK
    low = lane < BLOCK
    row8 = iota((8, 128), 0)
    own = pack[...] * jnp.where((row8 >= 2) & (row8 <= 4), -1.0, 1.0)
    live = own[6:7]
    first_rows = iota((16, 128), 0)
    lane_half = (iota((16, 128), 1) >= BLOCK).astype(I32)
    half_sum = (first_rows == lane_half).astype(F32)
    wide_lane = iota((8, 512), 1)
    spot_of = 2 * (wide_lane >> 7) + ((wide_lane & 127) >= BLOCK).astype(I32)
    half_pick = (iota((8, 512), 0) == spot_of).astype(F32)
    half_pick = jnp.concatenate([half_pick] * 3 + [jnp.zeros((8, 512), F32)], axis=0).astype(BF16)

    mix_pd = (iota((72, CHANNELS), 0) - 12 * ((iota((72, CHANNELS), 0) * 5462) >> 16)) == iota(
        (72, CHANNELS), 1
    )
    mix_pd = mix_pd.astype(F32)
    mix_pc = ((iota((96, CHANNELS), 0) & 15) == iota((96, CHANNELS), 1)).astype(F32)
    same = ((iota((96, 72), 0) >> 4) == ((iota((96, 72), 1) * 5462) >> 16)).astype(F32)
    same_t = ((iota((72, 96), 1) >> 4) == ((iota((72, 96), 0) * 5462) >> 16)).astype(F32)
    for layer in range(2):
        table = channel_mix[:, layer, :]
        spread_c = mm(mix_pc, table)
        mix_back[layer] = stack_left(mm(mm(mix_pd, table, NT), mix_pc, NT) * same_t)
        mix_stack[layer] = stack_left(mm(spread_c, mix_pd, NT) * same)

    struct_rows = own[7:8].astype(I32)
    member = (struct_rows == iota((STRUCTS, 128), 0)).astype(F32)
    atom_cot = mm(energy_cot[...], member) * live
    counts[...] = jnp.zeros_like(counts)
    chunk = min(2048, edge_count)
    per_slot = edge_count // chunk
    wide = counts.shape[2]

    hot_rows = iota((128, chunk), 0).astype(F32).astype(BF16)
    none = jnp.zeros((), BF16)

    def count_edges(send, recv):
        local = recv - col * BLOCK
        inside = (local >= 0) & (local < BLOCK)
        key = jnp.where(inside, (send >> 8) * BLOCK + local, -1)
        step = jnp.where((send & 128) > 0, RADIX, 1.0).astype(BF16)
        sender_hot = jnp.where(hot_rows == (send & 127).astype(F32).astype(BF16), step, none)
        pair_hot = []
        for first in range(0, wide, 128):
            local_key = jnp.where((key >= first) & (key < first + 128), key - first, -1)
            hit = hot_rows == local_key.astype(F32).astype(BF16)
            pair_hot.append(jnp.where(hit, jnp.ones((), BF16), none))
        pair_hot = jnp.concatenate(pair_hot, axis=0)
        found = once(sender_hot, pair_hot, NT)
        upper = jnp.floor(found * (1.0 / RADIX))
        counts[0] += found - RADIX * upper
        counts[1] += upper

    def count_slot(slot, carry):
        for k in range(per_slot):
            spot = slice(k * chunk, (k + 1) * chunk)
            count_edges(send_all[slot, :, spot], recv_all[slot, :, spot])
        return carry

    count_slot(col, 0)

    for blank_ref in (dkind_sums, dsums, products, invariant.at[1]):
        blank_ref[...] = jnp.zeros(blank_ref.shape, F32)
    await_bytes(pack_all, lanes - 1, recv_sem.at[0])
    for q in range(tiles):
        sender_rows[:, 128 * q : 128 * (q + 1)] = jnp.where(low, pack_all[2 * q], pack_all[2 * q + 1])
    columns[...] = jnp.transpose(sender_rows[...])

    def geometry(start):
        cols = columns[pl.ds(start, BLOCK), :]
        return Geometry(cols, own, low_row)

    def radial_block(i, carry):
        start = aligned(i * BLOCK, BLOCK)
        geo = geometry(start)
        envelope = geo.reach * geo.reach * NORM
        for pair, value in enumerate(geo.sines()):
            radial[pair, pl.ds(start, BLOCK), :] = value * envelope
        inverse[pl.ds(start, BLOCK), :] = geo.inverse
        return carry

    loop(group // BLOCK, radial_block, 0)

    def monomial_rows(rows):
        x, y, z = rows[2:3], rows[3:4], rows[4:5]
        table = {(0, 0, 0): None}
        for m in MONOMIALS[1:]:
            axis = next(i for i in range(3) if m[i])
            lower = m[:axis] + (m[axis] - 1,) + m[axis + 1 :]
            factor = (x, y, z)[axis]
            table[m] = factor if table[lower] is None else table[lower] * factor
        return table

    def spread():
        def one(q, carry):
            spot = pl.ds(aligned(q * 128, 128), 128)
            table = monomial_rows(sender_rows[:, spot])
            h = weights[0:CHANNELS, spot]
            for i, m in enumerate(MONOMIALS):
                value = h if table[m] is None else h * table[m]
                products[row_of(i, 0) : row_of(i, 0) + 8, spot] = value[0:8]
                products[row_of(i, 1) : row_of(i, 1) + 4, spot] = value[8:12]
            return carry

        loop(tiles, one, 0)
        for q in strips:
            split = parts(products[:, q])
            three, two = [], []
            for start, end in zip(DEGREE_ROWS, DEGREE_ROWS[1:]):
                three += [v[start:end] for v in split]
                two += [v[start:end] for v in split[:2]]
            three.append(jnp.zeros((8, three[0].shape[1]), F32))
            product_three[:, q] = jnp.concatenate(three, axis=0).astype(BF16)
            product_two[:, q] = jnp.concatenate(two, axis=0).astype(BF16)


    def kind_spread(q, carry):
        spot = pl.ds(aligned(q * 128, 128), 128)
        table = monomial_rows(sender_rows[:, spot])
        kinds = sender_rows[0:2, spot]
        for i, m in enumerate(MONOMIALS):
            kind_products[2 * i : 2 * i + 2, spot] = kinds if table[m] is None else kinds * table[m]
        return carry

    loop(tiles, kind_spread, 0)
    for q in strips:
        kind_parts = jnp.concatenate(parts(kind_products[:, q]), axis=0)
        blank_rows = jnp.zeros((8, kind_parts.shape[1]), F32)
        kind_three[:, q] = jnp.concatenate([kind_parts, blank_rows], axis=0).astype(BF16)
    columns_of = []
    for kind_of in range(2):
        embedded = mm(embedding[...], (iota((2, 128), 0) == kind_of).astype(F32), TN)
        padded = jnp.concatenate(
            [mm(channel_in[0], embedded, TN), jnp.zeros((PADDED - CHANNELS, 128), F32)], axis=0
        )
        columns_of.append([padded[0:8], padded[8:16]])

    await_bytes(send_all, lanes - 1, recv_sem.at[1])
    await_bytes(recv_all, lanes - 1, recv_sem.at[2])
    if devices <= 32:
        for k in range(1, lanes):
            count_slot(lax.rem(col + k, lanes), 0)
    else:
        lax.fori_loop(1, lanes, lambda k, carry: count_slot(lax.rem(col + k, lanes), carry), 0)
    low_tall = iota((128, 128), 1) < BLOCK
    for block in range(group // 128):
        turn_of = block // 2
        piece = counts[block % 2, :, 128 * (turn_of // 2) : 128 * (turn_of // 2 + 1)]
        turned = pltpu.roll(piece, BLOCK, 1)
        first_half, second_half = (piece, turned) if turn_of % 2 == 0 else (turned, piece)
        pair_weight[128 * block : 128 * (block + 1), :] = jnp.where(
            low_tall, first_half, second_half
        )

    def plane_block(i, carry):
        spot = pl.ds(aligned(i * BLOCK, BLOCK), BLOCK)
        weight = pair_weight[spot, :]
        step = inverse[spot, :]
        for pair in range(PAIRS):
            value = radial[pair, spot, :] * weight
            for order in range(4):
                high = value.astype(BF16)
                planes_high[spot, tile_of(order, pair)] = high
                planes_low[spot, tile_of(order, pair)] = (value - high.astype(F32)).astype(BF16)
                value = value * step
        return carry

    loop(group // BLOCK, plane_block, 0)

    xi, yi, zi = (jnp.broadcast_to(own[r : r + 1], (8, 128)) for r in (2, 3, 4))

    def chunk_spots(i):
        pair, tile = i // 2, i % 2
        return pair, tile, slice(128 * pair, 128 * (pair + 1))

    def kind_component(place, pair):
        return [
            jnp.broadcast_to(kind_moved[place, 2 * pair + k : 2 * pair + k + 1, :], (8, 128))
            for k in range(2)
        ]

    def kind_expand(both, tile):
        return [columns_of[0][tile] * a + columns_of[1][tile] * b for a, b in both]

    units = [(0, pair, None) for pair in range(PAIRS)]
    units += [(1, pair, pair + 1 if pair + 1 < PAIRS else None) for pair in range(0, PAIRS, 2)]

    def joined_rows(ref, start, spot, other):
        value = ref[start : start + 8, spot]
        return value if other is None else jnp.where(row8 < 4, value, ref[start - 4 : start + 4, other])

    def shell_terms(tile, pair, second):
        out = []
        for order in range(4):
            spot = tile_of(order, pair)
            other = None if second is None else tile_of(order, second)
            for m in range(COUNTS[order]):
                out.append(joined_rows(sums, row_of(m, tile), spot, other))
        return out

    def store_rows(ref, start, tile, spot, other, value):
        if tile == 0:
            ref[start : start + 8, spot] = value
        else:
            ref[start : start + 4, spot] = value[0:4]
            if other is not None:
                ref[start : start + 4, other] = value[4:8]

    def pair_lanes(pair):
        return None if pair is None else slice(128 * pair, 128 * (pair + 1))

    def live_rows(value, tile):
        return value if tile == 0 else jnp.where(row8 < CHANNELS - 8, value, 0.0)

    def mix_invariants(layer):
        mixed = stacked(mix_stack[layer], invariant[layer])
        for pair in range(PAIRS):
            feats[layer, 72 * pair : 72 * (pair + 1), :] = mixed[:, 128 * pair : 128 * (pair + 1)]

    def forward_kinds():
        by_high = once(kind_three[...], planes_high[...])
        by_low = once(kind_three[0:80, :], planes_low[...])
        kind_sums[...] = by_high[0:40] + ((by_high[40:80] + by_low[0:40]) + (by_high[80:120] + by_low[40:80]))
        for order in range(4):
            for m in range(COUNTS[order]):
                pieces = [kind_sums[2 * m : 2 * m + 2, tile_of(order, pair)] for pair in range(PAIRS)]
                kind_shells[OFFSETS[order] + m] = jnp.concatenate(
                    pieces + [jnp.zeros((2, 128), F32)], axis=0
                )
        moved = all_shifted([kind_shells[m] for m in range(SHELLS)], xi, yi, zi)
        for place, value in enumerate(moved):
            kind_moved[place] = value
        for pair in range(PAIRS):
            both = [kind_component(place, pair) for place in range(20)]
            for tile in range(2):
                for p, value in enumerate(contracted(kind_expand(both, tile))):
                    start = PADDED * p + 8 * tile
                    invariant[0, start : start + 8, 128 * pair : 128 * (pair + 1)] = value
        mix_invariants(0)

    def forward():
        for order, first, last in GROUPS:
            spot = slice(128 * first, 128 * last)
            end = DEGREE_ROWS[order + 1]
            by_high = once(product_three[0 : -(-3 * end // 16) * 16, :], planes_high[:, spot])
            by_low = once(product_two[0 : 2 * end, :], planes_low[:, spot])
            for start, stop in zip(DEGREE_ROWS[: order + 1], DEGREE_ROWS[1:]):
                size = stop - start
                h, l = 3 * start, 2 * start
                sums[start:stop, spot] = by_high[h : h + size] + (
                    (by_high[h + size : h + 2 * size] + by_low[l : l + size])
                    + (by_high[h + 2 * size : h + 3 * size] + by_low[l + size : l + 2 * size])
                )
        for tile, pair, second in units:
            for p, value in enumerate(invariants(shell_terms(tile, pair, second), xi, yi, zi)):
                store_rows(
                    invariant.at[1], PADDED * p + 8 * tile, tile, pair_lanes(pair), pair_lanes(second), value
                )
        mix_invariants(1)

    def send_stats(phase, index, select_rows, first, second, extra=None):
        values = jnp.concatenate([first, second], axis=0)
        wide_values = jnp.concatenate(parts(values), axis=1).astype(BF16)
        rows = jnp.concatenate([select_rows] * 3, axis=1).astype(BF16)
        both = once(rows, wide_values, NT)
        for k in range(4):
            stat_own[index, 2 * k : 2 * k + 2, :] = both[0:2, 128 * k : 128 * (k + 1)]
        if extra is not None:
            stat_own[index, 2:3, 96 : 96 + STRUCTS] = extra
        everyone(
            lambda device, _: push(phase, stat_own.at[index], stat_all.at[index, me], device)
        )
        stat_all[index, me] = stat_own[index]

    def get_stats(phase, index):
        await_bytes(stat_all.at[index], devices - 1, recv_sem.at[phase])
        sums_of = [stat_all[index, k] for k in range(8)]
        for k in range(8, devices):
            sums_of[k % 8] = sums_of[k % 8] + stat_all[index, k]
        while len(sums_of) > 1:
            sums_of = [a + b for a, b in zip(sums_of[::2], sums_of[1::2])]
        return sums_of[0]

    def widen(rows):
        return once(
            jnp.concatenate([three_rows(rows), jnp.zeros((8, 128), BF16)], axis=0), half_pick, TN
        )

    rest_rows = ONES_ROW - 128

    def tall(wide, start):
        return jnp.concatenate(
            [wide[:, start : start + 128], wide[0:rest_rows, start + 128 : start + 256]], axis=0
        )

    ones_rows = iota((FEATURE_ROWS - ONES_ROW, 128), 0) == 0
    for layer in range(2):
        feats[layer, ONES_ROW:FEATURE_ROWS, :] = ones_rows.astype(F32)
        normed[layer, ONES_ROW:FEATURE_ROWS, :] = ones_rows.astype(F32)

    def send_moments(layer, phase):
        values = feats[layer]
        send_stats(phase, layer, half_sum * live, values, values * values)

    def normalise(layer, phase):
        total = get_stats(phase, layer)
        inverse_count = 1.0 / jnp.maximum(total[2:3, ONES_ROW - 128 : ONES_ROW - 127], 1.0)
        scaled = total * inverse_count
        means = pltpu.roll(scaled, 4, 0)
        scales = lax.rsqrt(scaled - means * means + variance_eps)
        wide = widen(jnp.where(row8 < 4, scaled, scales))
        scale = tall(wide, 256)
        normed[layer, 0:ONES_ROW, :] = (feats[layer, 0:ONES_ROW, :] - tall(wide, 0)) * scale
        rows = 2 * HEAD_ROWS
        high, middle, tail = (v.astype(BF16) for v in parts(normed[layer]))
        by_high = once(head_rows[layer], high)
        by_middle = once(head_rows[layer, 0 : 2 * rows, :], middle)
        by_tail = once(head_rows[layer, 0:rows, :], tail)
        joined = by_high[0:rows] + (
            (by_high[rows : 2 * rows] + by_middle[0:rows])
            + (by_high[2 * rows :] + by_middle[rows:] + by_tail)
        )
        chosen = jnp.where(low_row, joined[0:HEAD_ROWS], joined[HEAD_ROWS:])
        return chosen + pltpu.roll(chosen, BLOCK, 1), scale, inverse_count

    def run_head(layer, pre):
        hidden, hidden_slope = silu_pair(pre[0:HIDDEN])
        inner, inner_slope = silu_pair(stacked(inner_forward[layer], hidden) + inner_cols[layer])
        dinner = energy_cols[layer] * atom_cot * inner_slope
        dhidden = stacked(inner_back[layer], dinner) * hidden_slope
        return hidden, inner, dinner, dhidden

    def small_grad(layer, hidden, inner, dinner):
        left = jnp.concatenate([dinner, atom_cot * inner], axis=0)
        blank = jnp.zeros((128 - 32 - 32 * layer, 128), F32)
        right = [hidden, (iota((8, 128), 0) == 0).astype(F32), blank]
        if layer == 1:
            right = [jnp.zeros((32, 128), F32)] + right
        return mm(jnp.where(low_row, left, 0.0), jnp.concatenate(right, axis=0), NT)

    def halves(value):
        return jnp.where(low_row, value, 0.0), jnp.where(low_row, 0.0, value)

    def scatter_tiles(phase, source, target, base):
        for t in range(source.shape[0]):

            @pl.when(me != base + t)
            def _():
                there = base + t
                push(phase, source.at[t], target.at[me], (there // lanes, there % lanes))

            @pl.when(me == base + t)
            def _():
                target[me] = source[t]

    def mine(base, result):
        return (me >= base) & (me < base + result.shape[0])

    def share_tiles(phase, parts_of, result, base):
        @pl.when(mine(base, result))
        def _():
            await_bytes(parts_of, devices - 1, recv_sem.at[phase])
            total = parts_of[0]
            for k in range(1, devices):
                total = total + parts_of[k]
            result[me - base] = total
            everyone(
                lambda device, _: push(phase + 1, result.at[me - base], result.at[me - base], device)
            )

    def gather_tiles(phase, result, base):
        count_of = result.shape[0]

        @pl.when(mine(base, result))
        def _():
            await_bytes(result, count_of - 1, recv_sem.at[phase + 1])

        @pl.when(jnp.logical_not(mine(base, result)))
        def _():
            await_bytes(result, count_of, recv_sem.at[phase + 1])

    def drain_tiles(phase, parts_of, result, base):
        count_of = result.shape[0]

        @pl.when(mine(base, result))
        def _():
            await_bytes(result, count_of - 1, send_sem.at[phase])
            await_bytes(parts_of, devices - 1, send_sem.at[phase + 1])

        @pl.when(jnp.logical_not(mine(base, result)))
        def _():
            await_bytes(result, count_of, send_sem.at[phase])

    base_a, base_b, base_c = 0, tiles_a.shape[0], devices - tiles_c.shape[0]

    forward_kinds()
    send_moments(0, 3)
    for parity in range(2):
        k = iota((FEATURE_ROWS, FEATURES), 0)
        pair = (k >= 72).astype(I32) + (k >= 144).astype(I32)
        rest = k - 72 * pair
        kind_of = (rest * 5462) >> 16
        channel = rest - 12 * kind_of
        place = channel * 36 + (2 * pair + parity) * 6 + kind_of
        hit = (place == iota((FEATURE_ROWS, FEATURES), 1)) & (k < ONES_ROW)
        select[parity] = hit.astype(F32).astype(BF16)
    inner_cols, energy_cols = [], []
    head[...] = jnp.zeros_like(head)
    for layer in range(2):
        for parity in range(2):
            base = HEAD_ROWS * parity
            block = exact(hidden_weight[layer], select[parity], NT)
            if parity == 0:
                spot = (iota((2, FEATURE_ROWS), 1) == ONES_ROW) & (
                    iota((2, FEATURE_ROWS), 0) == layer
                )
                block = block + mm(hidden_bias[...], spot.astype(F32), TN)
            head[layer, base : base + HIDDEN, :] = block
            if layer == 0:
                message_rows = jnp.concatenate(
                    [message_weight[...], jnp.zeros((PADDED - CHANNELS, FEATURES), F32)], axis=0
                )
                head[0, base + HIDDEN : base + HEAD_ROWS, :] = exact(message_rows, select[parity], NT)
        whole = head[layer]
        head_rows[layer] = three_rows(whole)
        head_stack[layer] = stack_left(whole)
        if layer == 0:
            message_stack[...] = stack_left(
                jnp.concatenate([whole[HIDDEN:HEAD_ROWS], whole[HEAD_ROWS + HIDDEN :]], axis=0)
            )
        inner_back[layer] = stack_left(inner_weight[layer])
        inner_forward[layer] = stack_left(jnp.transpose(inner_weight[layer]))
        pick = (iota((2, 128), 0) == layer).astype(F32)
        inner_cols.append(mm(inner_bias[...], pick, TN))
        energy_cols.append(mm(energy_weight[...], pick, TN))

    if group <= 512:
        turned_high[...] = jnp.transpose(planes_high[...])
        turned_low[...] = jnp.transpose(planes_low[...])

    def against(left, lane_spot, spot, low_part):
        if group <= 512:
            return once(left, (turned_low if low_part else turned_high)[lane_spot, spot])
        return once(left, (planes_low if low_part else planes_high)[spot, lane_spot], NT)

    pre_zero, scale_zero, inverse_count = normalise(0, 3)
    message = pre_zero[HIDDEN:HEAD_ROWS]
    message_own[...] = jnp.where(low, message[0:8], message[8:16])
    members(lambda device, _: push(4, message_own, message_all.at[col], device))
    message_all[col] = message_own[...]
    hidden_zero, inner_zero, dinner_zero, dhidden_zero = run_head(0, pre_zero)
    d_low, d_high = halves(dhidden_zero)
    gap = jnp.zeros((HEAD_ROWS - HIDDEN, 128), F32)
    dnormed_head = stacked(head_stack[0], jnp.concatenate([d_low, gap, d_high, gap], axis=0))

    def pack_head(target, layer, d_low, d_high):
        block = mm(jnp.concatenate([d_low, d_high], axis=0), normed[layer], NT)
        for r in range(6):
            for half in range(2):
                target[2 * r + half] = block[8 * r : 8 * (r + 1), 128 * half : 128 * (half + 1)]

    pack_head(tiles_a, 0, d_low, d_high)
    scatter_tiles(11, tiles_a, tiles_a_all, 0)
    weights[...] = jnp.zeros_like(weights)
    embedded = mm(embedding[...], sender_rows[0:2, :], TN)
    weights[0:CHANNELS, :] = mm(channel_in[1], embedded, TN)
    await_bytes(message_all, lanes - 1, recv_sem.at[4])
    for q in range(tiles):
        even, odd = message_all[2 * q], message_all[2 * q + 1]
        spot = slice(128 * q, 128 * (q + 1))
        weights[0:8, spot] += jnp.where(low, even, pltpu.roll(odd, BLOCK, 1))
        weights[8:16, spot] += jnp.where(low, pltpu.roll(even, BLOCK, 1), odd)

    spread()
    forward()
    send_moments(1, 5)
    turn = ANGLE * (1.0 + (iota((1, 128), 1) >= BLOCK).astype(F32))

    def slope_block(i, carry):
        start = aligned(i * BLOCK, BLOCK)
        spot = pl.ds(start, BLOCK)
        geo = geometry(start)
        step = geo.inverse
        square = step * step
        envelope = geo.reach * geo.reach * NORM
        slope = geo.reach * (-2.0 * NORM / (cutoff_radius * cutoff_radius))
        weight = pair_weight[spot, :]
        for pair, (sine, cosine) in enumerate(zip(geo.sines(), geo.cosines())):
            rate = (turn + 2.0 * ANGLE * pair) * cosine - sine
            value = weight * ((0.5 * square) * rate * envelope + sine * slope)
            plane = weight * (sine * envelope)
            slopes[spot, tile_of(0, pair)] = value
            for order in range(1, 4):
                plane = plane * step
                value = value * step - (0.5 * square) * plane
                slopes[spot, tile_of(order, pair)] = value
        return carry

    loop(group // BLOCK, slope_block, 0)
    for q in strips:
        kind_stack[q, :] = stack_left(kind_products[:, q])

    share_tiles(11, tiles_a_all, tiles_a_sum, base_a)
    pre_one, scale_one, _ = normalise(1, 5)
    hidden_one, inner_one, dinner_one, dhidden_one = run_head(1, pre_one)
    d_low, d_high = halves(dhidden_one)
    dnormed_one = stacked(head_stack[1], jnp.concatenate([d_low, gap, d_high, gap], axis=0))
    send_stats(6, 2, half_sum, dnormed_one, dnormed_one * normed[1])

    pack_head(tiles_b, 1, d_low, d_high)
    small = small_grad(0, hidden_zero, inner_zero, dinner_zero)
    small = small + small_grad(1, hidden_one, inner_one, dinner_one)
    for r in range(2):
        tiles_b[12 + r] = small[8 * r : 8 * (r + 1)] + pltpu.roll(small[16 + 8 * r : 24 + 8 * r], 64, 1)
    atom_energy = jnp.sum(energy_cols[0] * inner_zero + energy_cols[1] * inner_one, axis=0, keepdims=True)
    atom_energy = jnp.where(low_row, live * atom_energy, 0.0)
    energy_rows = mm(jnp.broadcast_to(atom_energy, (8, 128)), member, NT)[0:1]
    def feature_back(layer, total, dnormed, scale):
        wide = widen(total * inverse_count)
        dfeats = scale * (
            dnormed[0:ONES_ROW] - live * (tall(wide, 0) + tall(wide, 256) * normed[layer, 0:ONES_ROW, :])
        )
        dmixed = jnp.concatenate([dfeats[72 * pair : 72 * (pair + 1)] for pair in range(PAIRS)], axis=1)
        dinvariant[...] = stacked(mix_back[layer], dmixed)
        return dmixed

    def mix_grad(layer, dmixed):
        return mm(invariant[layer], dmixed, NT, lax.Precision.HIGH) * same

    blank = jnp.zeros((8, 128), F32)

    def shell_back(some_units, moved):
        for tile, pair, second in some_units:
            cots = tuple(
                joined_rows(dinvariant, PADDED * p + 8 * tile, pair_lanes(pair), pair_lanes(second))
                for p in range(6)
            )
            _, pull = jax.vjp(invariants, shell_terms(tile, pair, second), xi, yi, zi)
            dterms, *shift = pull(cots)
            for order in range(4):
                spot = tile_of(order, pair)
                other = None if second is None else tile_of(order, second)
                for m in range(COUNTS[order]):
                    store_rows(dsums, row_of(m, tile), tile, spot, other, dterms[OFFSETS[order] + m])
            if tile == 1 and second is None:
                shift = [jnp.where(row8 < 4, v, 0.0) for v in shift]
            moved = tuple(a + b for a, b in zip(moved, shift))
        return moved

    def shell_back_kinds():
        dtable = [[blank, blank], [blank, blank]]
        folded = [[] for _ in range(20)]
        for pair in range(PAIRS):
            both = [kind_component(place, pair) for place in range(20)]
            sides = []
            for tile in range(2):
                cots = tuple(dinvariant[PADDED * p + 8 * tile : PADDED * p + 8 * tile + 8, 128 * pair : 128 * (pair + 1)] for p in range(6))
                _, pull = jax.vjp(contracted, kind_expand(both, tile))
                sides.append(pull(cots)[0])
                for k in range(2):
                    for place in range(20):
                        dtable[k][tile] = dtable[k][tile] + sides[tile][place] * both[place][k]
            for place in range(20):
                for k in range(2):
                    folded[place].append(
                        columns_of[k][0] * sides[0][place] + columns_of[k][1] * sides[1][place]
                    )
        dmoved = [jnp.where(row8 < 2 * PAIRS, row_sums(v, row8), 0.0) for v in folded]
        _, pull = jax.vjp(all_shifted, [kind_shells[m] for m in range(SHELLS)], xi, yi, zi)
        dterms, *moved = pull(dmoved)
        for order in range(4):
            for m in range(COUNTS[order]):
                value = dterms[OFFSETS[order] + m]
                for pair in range(PAIRS):
                    dkind_sums[2 * m : 2 * m + 2, tile_of(order, pair)] = value[2 * pair : 2 * pair + 2]
        return tuple(moved), [jnp.concatenate(halves_of, axis=0) for halves_of in dtable]

    def product_back(groups, done):
        for order, first, last in groups:
            lane_spot = slice(128 * first, 128 * last)
            end = DEGREE_ROWS[order + 1]
            high, low_part, _ = parts(dsums[0:end, lane_spot])
            left = jnp.concatenate([high, low_part], axis=0).astype(BF16)
            for spot in strips:
                by_high = against(left, lane_spot, spot, False)
                block = by_high[0:end] + (by_high[end:] + against(left[0:end], lane_spot, spot, True))
                shared = min(done, end)
                if shared:
                    dproducts[0:shared, spot] += block[0:shared]
                if end > done:
                    dproducts[done:end, spot] = block[done:end]
            done = max(done, end)

    def product_back_kinds():
        high, low_part, _ = parts(dkind_sums[...])
        left = jnp.concatenate([high, low_part], axis=0).astype(BF16)
        for spot in strips:
            whole = slice(0, PLANE_LANES)
            by_high = against(left, whole, spot, False)
            dkind_products[:, spot] = by_high[0:40] + (by_high[40:] + against(left, whole, spot, True)[0:40])

    def weight_back():
        out = []
        for q in range(tiles):
            spot = slice(128 * q, 128 * (q + 1))
            table = monomial_rows(sender_rows[:, spot])
            both = []
            for tile in range(2):
                total = None
                for i, m in enumerate(MONOMIALS):
                    term = dproducts[row_of(i, tile) : row_of(i, tile) + 8, spot]
                    term = term if table[m] is None else term * table[m]
                    total = term if total is None else total + term
                both.append(live_rows(total, tile))
            out.append(jnp.concatenate(both, axis=0))
        return out

    def axis_slope(table, axis, value_of):
        total = None
        for i, m in enumerate(MONOMIALS):
            if not m[axis]:
                continue
            lower = table[m[:axis] + (m[axis] - 1,) + m[axis + 1 :]]
            term = value_of(i)
            if lower is not None:
                term = (float(m[axis]) * lower) * term
            total = term if total is None else total + term
        return total

    def coordinate_back():
        out = []
        for q in range(tiles):
            spot = slice(128 * q, 128 * (q + 1))
            table = monomial_rows(sender_rows[:, spot])
            sides = []
            for axis in range(3):
                total = None
                for tile in range(2):
                    slope = axis_slope(
                        table, axis, lambda i: dproducts[row_of(i, tile) : row_of(i, tile) + 8, spot]
                    )
                    term = weights[8 * tile : 8 * tile + 8, spot] * live_rows(slope, tile)
                    total = term if total is None else total + term
                sides.append(jnp.sum(total, axis=0, keepdims=True))
            out.append(sides)
        return out

    def coordinate_back_kinds():
        out = []
        for q in range(tiles):
            spot = slice(128 * q, 128 * (q + 1))
            table = monomial_rows(sender_rows[:, spot])
            kinds = sender_rows[0:2, spot]
            rows = [
                jnp.sum(kinds * dkind_products[2 * i : 2 * i + 2, spot], axis=0, keepdims=True)
                for i in range(len(MONOMIALS))
            ]
            out.append([axis_slope(table, axis, lambda i: rows[i]) for axis in range(3)])
        return out

    def radial_pull(block, first, last, spot):
        total = None
        for at in range(first, last):
            term = block[:, 128 * (at - first) : 128 * (at - first + 1)] * slopes[spot, 128 * at : 128 * (at + 1)]
            total = term if total is None else total + term
        return total

    def plane_back():
        for order, first, last in GROUPS:
            end = DEGREE_ROWS[order + 1]
            for spot in strips:
                block = mm(products[0:end, spot], dsums[0:end, 128 * first : 128 * last], TN)
                term = radial_pull(block, first, last, spot)
                if order == 3:
                    pulls[spot, :] = term
                else:
                    pulls[spot, :] += term

    def plane_back_kinds():
        right = stack_right(dkind_sums[...])
        for order, first, last in GROUPS:
            for spot in strips:
                block = once(kind_stack[spot, :], right[:, 128 * first : 128 * last])
                pulls[spot, :] += radial_pull(block, first, last, spot)

    dmixed_one = feature_back(1, get_stats(6, 2), dnormed_one, scale_one)
    moved_one = shell_back([units[0], units[1], units[3]], (blank, blank, blank))
    product_back([GROUPS[1]], 0)
    moved_one = shell_back([units[2], units[4]], moved_one)
    product_back([GROUPS[0]] + GROUPS[2:], DEGREE_ROWS[3])
    dweights_one = weight_back()
    for q in range(tiles):
        top, bottom = dweights_one[q][0:8], dweights_one[q][8:16]
        dmessage_own[2 * q] = jnp.where(low, top, pltpu.roll(bottom, BLOCK, 1))
        dmessage_own[2 * q + 1] = jnp.where(low, pltpu.roll(top, BLOCK, 1), bottom)
    members(
        lambda device, target: push(7, dmessage_own.at[target], dmessage_all.at[col], device)
    )
    dmessage_all[col] = dmessage_own[col]
    kinds_of = sender_rows[...]
    dtable_one = jnp.zeros((PADDED, 8), F32)
    for q in range(tiles):
        dtable_one = dtable_one + mm(dweights_one[q], kinds_of[:, 128 * q : 128 * (q + 1)], NT)
    slopes_one = coordinate_back()
    mix_one = mix_grad(1, dmixed_one)
    scatter_tiles(13, tiles_b, tiles_b_all, base_b)
    await_bytes(dmessage_all, lanes - 1, recv_sem.at[7])
    arrived = dmessage_all[0]
    for k in range(1, lanes):
        arrived = arrived + dmessage_all[k]
    turned = pltpu.roll(arrived, BLOCK, 1)
    dmessage = jnp.concatenate([jnp.where(low, arrived, turned), jnp.where(low, turned, arrived)], axis=0)

    m_low, m_high = halves(dmessage)
    dmessage_both = jnp.concatenate([m_low, m_high], axis=0)
    dnormed_zero = dnormed_head + stacked(message_stack[...], dmessage_both)
    send_stats(8, 3, half_sum, dnormed_zero, dnormed_zero * normed[0], energy_rows)
    dmessage_weight = mm(dmessage_both, normed[0], NT)
    for r in range(4):
        for half in range(2):
            tiles_c[2 * r + half] = dmessage_weight[
                8 * r : 8 * (r + 1), 128 * half : 128 * (half + 1)
            ]
    scatter_tiles(15, tiles_c, tiles_c_all, base_c)
    fold_c = (iota((PADDED, 96), 0) == (iota((PADDED, 96), 1) & 15)).astype(F32)
    d_of = iota((72, 128), 0) - 12 * ((iota((72, 128), 0) * 5462) >> 16)
    seat_mix = [(iota((72, 128), 1) == d_of + 12 * layer).astype(BF16) for layer in range(2)]
    seat_kind = ((lane == row8 + 26) & (row8 < 2)).astype(F32)

    def fold_mix(layer, value):
        wide_value = once(fold_c.astype(BF16), jnp.concatenate(parts(exact(value, seat_mix[layer])), axis=1).astype(BF16))
        return wide_value[:, 0:128] + (wide_value[:, 128:256] + wide_value[:, 256:384])

    final_one = fold_mix(1, mix_one) + mm(dtable_one, seat_kind)
    plane_back()
    share_tiles(13, tiles_b_all, tiles_b_sum, base_b)
    share_tiles(15, tiles_c_all, tiles_c_sum, base_c)
    total_zero = get_stats(8, 3)
    dmixed_zero = feature_back(0, total_zero, dnormed_zero, scale_zero)
    final = fold_mix(0, mix_grad(0, dmixed_zero)) + final_one
    moved_zero, dtables = shell_back_kinds()
    for k in range(2):
        total = jnp.sum(dtables[k], axis=1, keepdims=True)
        final = final + jnp.where(iota((PADDED, 128), 1) == 24 + k, total, 0.0)
    folded = final[0:8] + pltpu.roll(pltpu.roll(final[0:8], 4, 0), 32, 1) + pltpu.roll(final[8:16], 64, 1)
    final_own[...] = folded[0:4]
    everyone(lambda device, _: push(10, final_own, final_all.at[me], device))
    final_all[me] = final_own[...]
    plane_back_kinds()
    product_back_kinds()
    slopes_zero = coordinate_back_kinds()
    pull_of = pulls[...]
    to_own = mm(sender_rows[...], pull_of, NN, lax.Precision.HIGH)
    to_sender = mm(own, pull_of, NT, lax.Precision.HIGH)
    force_own[...] = jnp.zeros_like(force_own)
    for q in range(tiles):
        spot = slice(128 * q, 128 * (q + 1))
        weight_row = to_sender[5:6, spot]
        for axis in range(3):
            value = -2.0 * (to_sender[2 + axis : 3 + axis, spot] + sender_rows[2 + axis : 3 + axis, spot] * weight_row)
            value = value - slopes_zero[q][axis] - slopes_one[q][axis]
            force_own[2 * q, axis : axis + 1, :] = value
            force_own[2 * q + 1, axis : axis + 1, :] = pltpu.roll(value, BLOCK, 1)
    members(lambda device, target: push(9, force_own.at[target], force_all.at[col], device))
    force_all[col] = force_own[col]
    own_force = []
    for axis in range(3):
        pairwise = 2.0 * (to_own[2 + axis : 3 + axis] + own[2 + axis : 3 + axis] * to_own[5:6])
        moved = jnp.sum(moved_zero[axis] + moved_one[axis], axis=0, keepdims=True)
        both = pairwise + moved
        own_force.append(both + pltpu.roll(both, BLOCK, 1))

    group_energy = stat_all[3, row * lanes, 2:3, 96 : 96 + STRUCTS]
    for k in range(1, lanes):
        group_energy = group_energy + stat_all[3, row * lanes + k, 2:3, 96 : 96 + STRUCTS]
    energies_out[...] = group_energy

    gather_tiles(11, tiles_a_sum, base_a)
    gather_tiles(13, tiles_b_sum, base_b)
    pick_ones = ((iota((8, FEATURE_ROWS), 0) == 0) & (iota((8, FEATURE_ROWS), 1) == ONES_ROW)).astype(F32)
    for layer in range(2):
        total = None
        for parity in range(2):
            rows = []
            for r in range(3):
                at = 6 * parity + 2 * r
                summed = (tiles_a_sum, tiles_b_sum)[layer]
                rows.append(jnp.concatenate([summed[at], summed[at + 1]], axis=1))
            block = jnp.concatenate(rows, axis=0)
            if parity == 0:
                hidden_bias_out[layer : layer + 1, :] = mm(pick_ones, block, NT)[0:1]
            part = exact(block, select[parity])
            total = part if total is None else total + part
        hidden_weight_out[layer] = total
    small_sum = jnp.concatenate([tiles_b_sum[12 + r] for r in range(2)], axis=0)
    for layer in range(2):
        inner_weight_out[layer] = small_sum[0:INNER, 32 * layer : 32 * layer + HIDDEN]
        pick = ((row8 == 0) & (lane == 32 * layer + HIDDEN)).astype(F32)
        inner_bias_out[layer : layer + 1, :] = mm(pick, small_sum, NT)[0:1]
        pick = ((row8 == 0) & (lane == 64 + 32 * layer + HIDDEN)).astype(F32)
        energy_weight_out[layer : layer + 1, :] = mm(pick, small_sum, NT)[0:1]
    gather_tiles(15, tiles_c_sum, base_c)
    total = None
    for parity in range(2):
        rows = [
            jnp.concatenate(
                [tiles_c_sum[4 * parity + 2 * r], tiles_c_sum[4 * parity + 2 * r + 1]], axis=1
            )
            for r in range(2)
        ]
        part = exact(jnp.concatenate(rows, axis=0), select[parity])
        total = part if total is None else total + part
    message_weight_out[...] = total[0:CHANNELS]

    await_bytes(final_all, devices - 1, recv_sem.at[10])
    final = final_all[0]
    for k in range(1, devices):
        final = final + final_all[k]
    final = jnp.concatenate([final, jnp.zeros((4, 128), F32)], axis=0)
    upper = jnp.where(row8 < 4, final, pltpu.roll(pltpu.roll(final, 4, 0), 96, 1))
    final = jnp.concatenate([upper, pltpu.roll(final, 64, 1)], axis=0)
    dembedding = None
    for layer in range(2):
        channel_mix_out[:, layer, :] = final[0:CHANNELS, 12 * layer : 12 * (layer + 1)]
        dtable = final[0:CHANNELS, 24 + 2 * layer : 26 + 2 * layer]
        channel_in_out[layer] = lax.dot_general(
            embedding[...],
            dtable,
            (((0,), (1,)), ((), ())),
            precision=lax.Precision.HIGHEST,
            preferred_element_type=F32,
        )
        part = lax.dot_general(
            dtable,
            channel_in[layer],
            (((0,), (1,)), ((), ())),
            precision=lax.Precision.HIGHEST,
            preferred_element_type=F32,
        )
        dembedding = part if dembedding is None else dembedding + part
    embedding_out[...] = dembedding

    await_bytes(force_all, lanes - 1, recv_sem.at[9])
    force = force_all[0]
    for k in range(1, lanes):
        force = force + force_all[k]
    for axis in range(3):
        position_out[axis] = (force[axis : axis + 1] + own_force[axis])[:, 0:BLOCK]

    await_bytes(pack_all, lanes - 1, send_sem.at[0])
    await_bytes(send_all, lanes - 1, send_sem.at[1])
    await_bytes(recv_all, lanes - 1, send_sem.at[2])
    await_bytes(stat_all.at[0], devices - 1, send_sem.at[3])
    await_bytes(message_all, lanes - 1, send_sem.at[4])
    await_bytes(stat_all.at[1], devices - 1, send_sem.at[5])
    await_bytes(stat_all.at[2], devices - 1, send_sem.at[6])
    await_bytes(dmessage_all, lanes - 1, send_sem.at[7])
    await_bytes(stat_all.at[3], devices - 1, send_sem.at[8])
    await_bytes(force_all, lanes - 1, send_sem.at[9])
    await_bytes(final_all, devices - 1, send_sem.at[10])
    drain_tiles(11, tiles_a_all, tiles_a_sum, base_a)
    drain_tiles(13, tiles_b_all, tiles_b_sum, base_b)
    drain_tiles(15, tiles_c_all, tiles_c_sum, base_c)


def hand_over(*refs):
    for source, target in zip(refs[:11], refs[11:]):
        target[...] = source[...]


def solution(mesh):
    lanes = mesh.shape["edge"]
    structs = mesh.shape["struct"]
    devices = lanes * structs

    def step(
        positions,
        species,
        struct_id,
        atom_mask,
        senders,
        receivers,
        edge_mask,
        energy_cot,
        embedding,
        channel_in,
        channel_mix,
        hidden_weight,
        hidden_bias,
        inner_weight,
        inner_bias,
        energy_weight,
        message_weight,
    ):
        owned = positions.shape[2]
        group = owned * lanes
        edges = senders.shape[1]
        inputs = [
            positions,
            species,
            struct_id,
            atom_mask,
            senders,
            receivers,
            edge_mask,
            energy_cot,
            embedding,
            channel_in,
            jnp.transpose(channel_mix, (1, 0, 2)),
            jnp.transpose(hidden_weight, (0, 2, 1)),
            hidden_bias,
            jnp.transpose(inner_weight, (0, 2, 1)),
            inner_bias,
            energy_weight,
            jnp.transpose(message_weight),
        ]
        vmem = pltpu.VMEM
        shapes = [
            (1, STRUCTS),
            (3, 1, owned),
            embedding.shape,
            channel_in.shape,
            (CHANNELS, 2, CHANNELS),
            (2, HIDDEN, FEATURES),
            hidden_bias.shape,
            (2, INNER, HIDDEN),
            inner_bias.shape,
            energy_weight.shape,
            (CHANNELS, FEATURES),
        ]
        scratch = [
            vmem((8, 128), F32),
            vmem((lanes, 8, 128), F32),
            vmem((lanes, 1, edges), I32),
            vmem((1, edges), I32),
            vmem((lanes, 1, edges), I32),
            vmem((2, 128, BLOCK * (group // 256)), F32),
            vmem((group, 128), F32),
            vmem((group, 8), F32),
            vmem((8, group), F32),
            vmem((PAIRS, group, 128), F32),
            vmem((group, 128), F32),
            vmem((group, PLANE_LANES), BF16),
            vmem((group, PLANE_LANES), BF16),
            vmem((PLANE_LANES, group if group <= 512 else 128), BF16),
            vmem((PLANE_LANES, group if group <= 512 else 128), BF16),
            vmem((group, PLANE_LANES), F32),
            vmem((group, 128), F32),
            vmem((PADDED, group), F32),
            vmem((PRODUCT_ROWS, group), F32),
            vmem((752, group), BF16),
            vmem((496, group), BF16),
            vmem((PRODUCT_ROWS, PLANE_LANES), F32),
            vmem((PRODUCT_ROWS, PLANE_LANES), F32),
            vmem((40, group), F32),
            vmem((128, group), BF16),
            vmem((group, 240), BF16),
            vmem((40, PLANE_LANES), F32),
            vmem((SHELLS, 8, 128), F32),
            vmem((20, 8, 128), F32),
            vmem((40, PLANE_LANES), F32),
            vmem((40, group), F32),
            vmem((PRODUCT_ROWS, group), F32),
            vmem((2, 96, 128 * PAIRS), F32),
            vmem((96, 128 * PAIRS), F32),
            vmem((2, FEATURE_ROWS, 128), F32),
            vmem((2, FEATURE_ROWS, 128), F32),
            vmem((2, FEATURE_ROWS, FEATURES), BF16),
            vmem((2, 2 * HEAD_ROWS, FEATURE_ROWS), F32),
            vmem((2, 6 * HEAD_ROWS, FEATURE_ROWS), BF16),
            vmem((2, FEATURE_ROWS, 12 * HEAD_ROWS), BF16),
            vmem((FEATURE_ROWS, 12 * PADDED), BF16),
            vmem((2, INNER, 6 * HIDDEN), BF16),
            vmem((2, HIDDEN, 6 * INNER), BF16),
            vmem((2, 72, 6 * 96), BF16),
            vmem((2, 96, 6 * 72), BF16),
            vmem((4, 8, 128), F32),
            vmem((4, devices, 8, 128), F32),
            vmem((8, 128), F32),
            vmem((lanes, 8, 128), F32),
            vmem((lanes, 8, 128), F32),
            vmem((lanes, 8, 128), F32),
            vmem((lanes, 8, 128), F32),
            vmem((lanes, 8, 128), F32),
            vmem((4, 128), F32),
            vmem((devices, 4, 128), F32),
            vmem((12, 8, 128), F32),
            vmem((devices, 8, 128), F32),
            vmem((12, 8, 128), F32),
            vmem((14, 8, 128), F32),
            vmem((devices, 8, 128), F32),
            vmem((14, 8, 128), F32),
            vmem((8, 8, 128), F32),
            vmem((devices, 8, 128), F32),
            vmem((8, 8, 128), F32),
            pltpu.SemaphoreType.DMA((20,)),
            pltpu.SemaphoreType.DMA((20,)),
            pltpu.SemaphoreType.DMA((17,)),
        ] + [vmem(v.shape, v.dtype) for v in inputs]
        outs = pl.pallas_call(
            functools.partial(body, lanes, structs),
            out_shape=[vmem(s, F32) for s in shapes],
            in_specs=[pl.BlockSpec(memory_space=pl.ANY)] * 17,
            out_specs=[pl.BlockSpec(memory_space=vmem)] * 11,
            scratch_shapes=scratch,
            compiler_params=pltpu.CompilerParams(
                collective_id=0, has_side_effects=True, vmem_limit_bytes=60 * 1024 * 1024
            ),
        )(*inputs)
        outs = pl.pallas_call(
            hand_over,
            out_shape=[jax.ShapeDtypeStruct(s, F32) for s in shapes],
            in_specs=[pl.BlockSpec(memory_space=vmem)] * 11,
            out_specs=[pl.BlockSpec(memory_space=vmem)] * 11,
        )(*(pltpu.with_memory_space_constraint(v, pltpu.VMEM) for v in outs))
        outs = list(outs)
        outs[4] = jnp.transpose(outs[4], (1, 0, 2))
        outs[5] = jnp.transpose(outs[5], (0, 2, 1))
        outs[7] = jnp.transpose(outs[7], (0, 2, 1))
        outs[10] = jnp.transpose(outs[10])
        return tuple(outs)

    tiled = P("struct", "edge")
    return jax.shard_map(
        step,
        mesh=mesh,
        in_specs=(
            P(None, "struct", "edge"),
            tiled,
            tiled,
            tiled,
            tiled,
            tiled,
            tiled,
            P("struct", None),
        )
        + (P(),) * 9,
        out_specs=(P("struct", None), P(None, "struct", "edge")) + (P(),) * 9,
        check_vma=False,
    )
```

```python
import functools
import math

import jax
import jax.numpy as jnp
import numpy as np
from jax import lax
from jax.experimental import pallas as pl
from jax.experimental.pallas import tpu as pltpu
from jax.sharding import PartitionSpec as P

CHANNELS = 12
PADDED = 16
RADIALS = 6
PAIRS = 3
STRUCTS = 8
HIDDEN = 24
INNER = 16
FEATURES = 432
HEAD_ROWS = 40
FEATURE_ROWS = 256
ONES_ROW = 216
BLOCK = 64

cutoff_radius = 6.0
variance_eps = 1e-05
center = 1.5

MESH = pl.DeviceIdType.MESH
F32 = jnp.float32
BF16 = jnp.bfloat16
I32 = jnp.int32
NN = ((1,), (0,))
NT = ((1,), (1,))
TN = ((0,), (0,))

MONOMIALS = sorted(
    [(a, b, c) for a in range(4) for b in range(4) for c in range(4) if a + b + c <= 3],
    key=lambda m: (sum(m), -m[0], -m[1], -m[2]),
)
PLACE = {m: i for i, m in enumerate(MONOMIALS)}
COUNTS = [1, 4, 10, 20]
OFFSETS = [0, 1, 5, 15]
SHELLS = 35
DEGREE_ROWS = [0, 16, 56, 128, 248]
DEGREE_COUNTS = [1, 3, 6, 10]


def row_of(place, tile):
    degree = sum(MONOMIALS[place])
    within = place - sum(DEGREE_COUNTS[:degree])
    return DEGREE_ROWS[degree] + (8 * DEGREE_COUNTS[degree] + 4 * within if tile else 8 * within)


PRODUCT_ROWS = 256
LANE_TILES = [(3, 0), (3, 1), (3, 2), (2, 2), (2, 0), (2, 1), (1, 0), (1, 1), (1, 2), (0, 2), (0, 0), (0, 1)]
GROUPS = [(3, 0, 4), (2, 4, 6), (1, 6, 10), (0, 10, 12)]
PLANE_LANES = 128 * len(LANE_TILES)


def tile_of(order, pair):
    at = LANE_TILES.index((order, pair))
    return slice(128 * at, 128 * (at + 1))


RADIX = 4096.0


def fitted(function, low, high, degree):
    series = np.polynomial.chebyshev.Chebyshev.interpolate(
        lambda w: function(0.5 * (high - low) * w + 0.5 * (high + low)), degree
    )
    return [float(v) for v in series.convert(kind=np.polynomial.Polynomial).coef]


LOW, HIGH = 0.9, 28.1
ANGLE = math.pi / cutoff_radius
SINE = fitted(lambda u: np.sin(ANGLE * np.sqrt(u)) / np.sqrt(u), LOW, HIGH, 6)
COSINE = fitted(lambda u: np.cos(ANGLE * np.sqrt(u)), LOW, HIGH, 6)
NORM = math.sqrt(2.0 / cutoff_radius)


def mm(left, right, kind=NN, precision=lax.Precision.HIGHEST):
    return lax.dot_general(
        left, right, (kind, ((), ())), precision=precision, preferred_element_type=F32
    )


def once(left, right, kind=NN):
    return lax.dot_general(left, right, (kind, ((), ())), preferred_element_type=F32)


def parts(value):
    high = value.astype(BF16).astype(F32)
    rest = value - high
    middle = rest.astype(BF16).astype(F32)
    return high, middle, rest - middle


def stack_left(value):
    high, middle, tail = parts(value)
    stack = jnp.concatenate([high, high, middle, high, tail, middle], axis=0)
    return jnp.transpose(stack).astype(BF16)


def stack_right(value):
    high, middle, tail = parts(value)
    return jnp.concatenate([high, middle, high, tail, high, middle], axis=0).astype(BF16)


def stacked(left, right):
    return once(left, stack_right(right))


def three_rows(value):
    return jnp.concatenate(parts(value), axis=0).astype(BF16)


def exact(left, right, kind=NN):
    rows = left.shape[0]
    out = once(three_rows(left), right, kind)
    return out[0:rows] + (out[rows : 2 * rows] + out[2 * rows :])


def loop(count, action, carry):
    if count <= 8:
        for i in range(count):
            carry = action(i, carry)
        return carry
    return lax.fori_loop(0, count, action, carry)


def aligned(value, size):
    return value if isinstance(value, int) else pl.multiple_of(value, size)


def iota(shape, dim):
    return lax.broadcasted_iota(I32, shape, dim)


def horner(coefficients, w):
    total = jnp.full_like(w, coefficients[-1])
    for value in coefficients[-2::-1]:
        total = total * w + value
    return total


def shifted(terms, order, x, y, z):
    current = terms
    for axis, value in enumerate((x, y, z)):
        two, three = 2.0 * value, 3.0 * value
        square = value * value
        three_square, cube = 3.0 * square, square * value
        factors = [None, [value], [square, two], [cube, three_square, three]]
        fresh = {}
        for m in MONOMIALS[: COUNTS[order]]:
            if axis == 2 and sum(m) != order:
                continue
            power = m[axis]
            total = current[m]
            for lower in range(power):
                source = m[:axis] + (lower,) + m[axis + 1 :]
                total = total + factors[power][lower] * current[source]
            fresh[m] = total
        current = fresh
    return current


def all_shifted(terms, x, y, z):
    out = []
    for order in range(4):
        own = {m: terms[OFFSETS[order] + i] for i, m in enumerate(MONOMIALS[: COUNTS[order]])}
        moved = shifted(own, order, x, y, z) if order else own
        out += [moved[m] for m in MONOMIALS if sum(m) == order]
    return out


def contracted(components):
    by_order = [{}, {}, {}, {}]
    for m, value in zip(MONOMIALS, components):
        by_order[sum(m)][m] = value
    scalar = by_order[0][(0, 0, 0)]
    vx, vy, vz = by_order[1][(1, 0, 0)], by_order[1][(0, 1, 0)], by_order[1][(0, 0, 1)]
    m = by_order[2]
    xx, xy, xz = m[(2, 0, 0)], m[(1, 1, 0)], m[(1, 0, 1)]
    yy, yz, zz = m[(0, 2, 0)], m[(0, 1, 1)], m[(0, 0, 2)]
    q = by_order[3]
    xxx, yyy, zzz = q[(3, 0, 0)], q[(0, 3, 0)], q[(0, 0, 3)]
    xxy, xxz, xyy = q[(2, 1, 0)], q[(2, 0, 1)], q[(1, 2, 0)]
    xyz, xzz, yyz, yzz = q[(1, 1, 1)], q[(1, 0, 2)], q[(0, 2, 1)], q[(0, 1, 2)]
    first = vx * vx + vy * vy + vz * vz
    second = xx * xx + yy * yy + zz * zz + 2.0 * (xy * xy + xz * xz + yz * yz)
    third = (
        xxx * xxx
        + yyy * yyy
        + zzz * zzz
        + 3.0 * (xxy * xxy + xxz * xxz + xyy * xyy + xzz * xzz + yyz * yyz + yzz * yzz)
        + 6.0 * (xyz * xyz)
    )
    fourth = (
        vx * (xx * vx + xy * vy + xz * vz)
        + vy * (xy * vx + yy * vy + yz * vz)
        + vz * (xz * vx + yz * vy + zz * vz)
    )
    xy2, xz2, yz2 = 2.0 * xy, 2.0 * xz, 2.0 * yz
    fifth = (
        vx * (xxx * xx + xyy * yy + xzz * zz + xxy * xy2 + xxz * xz2 + xyz * yz2)
        + vy * (xxy * xx + yyy * yy + yzz * zz + xyy * xy2 + xyz * xz2 + yyz * yz2)
        + vz * (xxz * xx + yyz * yy + zzz * zz + xyz * xy2 + xzz * xz2 + yzz * yz2)
    )
    return (scalar, first, second, third, fourth, fifth)


def invariants(terms, x, y, z):
    return contracted(all_shifted(terms, x, y, z))


def row_sums(values, row8):
    def fold(a, b, size):
        if b is None:
            return a + pltpu.roll(a, 8 - size, 0)
        first = (row8 & size) == 0
        if size == 4:
            return jnp.where(first, a, b) + pltpu.roll(jnp.where(first, b, a), 4, 0)
        return jnp.where(first, a + pltpu.roll(a, 8 - size, 0), b + pltpu.roll(b, size, 0))

    values = list(values) + [None] * (8 - len(values))
    for size in (4, 2, 1):
        values = [fold(values[i], values[i + size], size) for i in range(size)]
    return values[0]


def silu_pair(v):
    gate = 1.0 / (1.0 + jnp.exp(-v))
    return v * gate, gate * (1.0 + v * (1.0 - gate))


class Geometry:
    def __init__(self, columns, own, lane_low):
        dx = own[2:3] + columns[:, 2:3]
        dy = own[3:4] + columns[:, 3:4]
        dz = own[4:5] + columns[:, 4:5]
        self.u = dx * dx + dy * dy + dz * dz + 1.0
        w = (self.u - 0.5 * (LOW + HIGH)) * (2.0 / (HIGH - LOW))
        self.sine = horner(SINE, w)
        self.cosine = horner(COSINE, w)
        self.inverse = lax.rsqrt(self.u)
        self.reach = 1.0 - self.u * (1.0 / (cutoff_radius * cutoff_radius))
        self.lane_low = lane_low

    def sines(self):
        step = 2.0 * (2.0 * self.cosine * self.cosine - 1.0)
        before = jnp.where(self.lane_low, -self.sine, 0.0)
        now = jnp.where(self.lane_low, self.sine, 2.0 * self.cosine * self.sine)
        return self.series(step, before, now)

    def cosines(self):
        double = 2.0 * self.cosine * self.cosine - 1.0
        before = jnp.where(self.lane_low, self.cosine, 1.0)
        now = jnp.where(self.lane_low, self.cosine, double)
        return self.series(2.0 * double, before, now)

    def series(self, step, before, now):
        out = [now]
        for _ in range(PAIRS - 1):
            before, now = now, step * now - before
            out.append(now)
        return out


def body(lanes, structs, *refs):
    sources, held, refs = refs[:17], refs[-17:], refs[17:-17]
    (
        positions,
        species,
        struct_id,
        atom_mask,
        senders,
        receivers,
        edge_mask,
        energy_cot,
        embedding,
        channel_in,
        channel_mix,
        hidden_weight,
        hidden_bias,
        inner_weight,
        inner_bias,
        energy_weight,
        message_weight,
    ) = held
    (
        energies_out,
        position_out,
        embedding_out,
        channel_in_out,
        channel_mix_out,
        hidden_weight_out,
        hidden_bias_out,
        inner_weight_out,
        inner_bias_out,
        energy_weight_out,
        message_weight_out,
        pack,
        pack_all,
        send_all,
        masked_recv,
        recv_all,
        counts,
        pair_weight,
        columns,
        sender_rows,
        radial,
        inverse,
        planes_high,
        planes_low,
        turned_high,
        turned_low,
        slopes,
        pulls,
        weights,
        products,
        product_three,
        product_two,
        sums,
        dsums,
        kind_products,
        kind_three,
        kind_stack,
        kind_sums,
        kind_shells,
        kind_moved,
        dkind_sums,
        dkind_products,
        dproducts,
        invariant,
        dinvariant,
        feats,
        normed,
        select,
        head,
        head_rows,
        head_stack,
        message_stack,
        inner_forward,
        inner_back,
        mix_stack,
        mix_back,
        stat_own,
        stat_all,
        message_own,
        message_all,
        dmessage_own,
        dmessage_all,
        force_own,
        force_all,
        final_own,
        final_all,
        tiles_a,
        tiles_a_all,
        tiles_a_sum,
        tiles_b,
        tiles_b_all,
        tiles_b_sum,
        tiles_c,
        tiles_c_all,
        tiles_c_sum,
        send_sem,
        recv_sem,
        input_sem,
    ) = refs
    devices = lanes * structs
    edge_count = senders.shape[1]
    inputs = [
        pltpu.make_async_copy(source, target, input_sem.at[i])
        for i, (source, target) in enumerate(zip(sources, held))
    ]
    group = pair_weight.shape[0]
    tiles = group // 128
    strips = [slice(k, k + 512) for k in range(0, group, 512)]
    row = lax.axis_index("struct")
    col = lax.axis_index("edge")
    me = row * lanes + col

    def everyone(action):
        def one(k, carry):
            target = lax.rem(me + k, devices)
            action((target // lanes, lax.rem(target, lanes)), target)
            return carry

        if (structs, lanes) == (4, 8):
            for k in range(devices - 1, 0, -1):
                at, there = row ^ (k % structs), col ^ (k // structs)
                action((at, there), at * lanes + there)
        else:
            lax.fori_loop(1, devices, one, 0)

    def members(action):
        def one(k, carry):
            target = lax.rem(col + k, lanes)
            action((row, target), target)
            return carry

        if lanes <= 8:
            for k in range(lanes - 1, 0, -1):
                action((row, col ^ k), col ^ k)
        else:
            lax.fori_loop(1, lanes, one, 0)

    def push(phase, source, target, device):
        pltpu.make_async_remote_copy(
            src_ref=source,
            dst_ref=target,
            send_sem=send_sem.at[phase],
            recv_sem=recv_sem.at[phase],
            device_id=device,
            device_id_type=MESH,
        ).start()

    def await_bytes(buffer, count, sem):
        if count:
            view = buffer.at[pl.ds(0, count)]
            pltpu.make_async_copy(view, view, sem).wait()

    for one_input in inputs[:7]:
        one_input.start()
    barrier = pltpu.get_barrier_semaphore()
    def enter(device, _):
        pl.semaphore_signal(barrier, inc=1, device_id=device, device_id_type=MESH)

    everyone(enter)
    for one_input in inputs[7:]:
        one_input.start()
    for one_input in inputs[:7]:
        one_input.wait()
    pack[...] = jnp.ones_like(pack)
    masked_recv[...] = jnp.where(edge_mask[...] > 0, receivers[...], -1)
    kind = species[...]
    for half in (0, BLOCK):
        spot = pl.ds(half, BLOCK)
        pack[0:1, spot] = (kind == 0).astype(F32)
        pack[1:2, spot] = (kind == 1).astype(F32)
        for axis in range(3):
            pack[2 + axis : 3 + axis, spot] = center - positions[axis]
        pack[6:7, spot] = atom_mask[...].astype(F32)
        pack[7:8, spot] = struct_id[...].astype(F32)
    pl.semaphore_wait(barrier, devices - 1)

    members(lambda device, _: push(0, pack, pack_all.at[col], device))
    members(lambda device, _: push(1, senders, send_all.at[col], device))
    members(lambda device, _: push(2, masked_recv, recv_all.at[col], device))
    pack_all[col] = pack[...]
    send_all[col] = senders[...]
    recv_all[col] = masked_recv[...]

    for one_input in inputs[7:]:
        one_input.wait()
    lane = iota((8, 128), 1)
    low_row = lane[0:1] < BLOCK
    low = lane < BLOCK
    row8 = iota((8, 128), 0)
    own = pack[...] * jnp.where((row8 >= 2) & (row8 <= 4), -1.0, 1.0)
    live = own[6:7]
    first_rows = iota((16, 128), 0)
    lane_half = (iota((16, 128), 1) >= BLOCK).astype(I32)
    half_sum = (first_rows == lane_half).astype(F32)
    wide_lane = iota((8, 512), 1)
    spot_of = 2 * (wide_lane >> 7) + ((wide_lane & 127) >= BLOCK).astype(I32)
    half_pick = (iota((8, 512), 0) == spot_of).astype(F32)
    half_pick = jnp.concatenate([half_pick] * 3 + [jnp.zeros((8, 512), F32)], axis=0).astype(BF16)

    mix_pd = (iota((72, CHANNELS), 0) - 12 * ((iota((72, CHANNELS), 0) * 5462) >> 16)) == iota(
        (72, CHANNELS), 1
    )
    mix_pd = mix_pd.astype(F32)
    mix_pc = ((iota((96, CHANNELS), 0) & 15) == iota((96, CHANNELS), 1)).astype(F32)
    same = ((iota((96, 72), 0) >> 4) == ((iota((96, 72), 1) * 5462) >> 16)).astype(F32)
    same_t = ((iota((72, 96), 1) >> 4) == ((iota((72, 96), 0) * 5462) >> 16)).astype(F32)
    for layer in range(2):
        table = channel_mix[:, layer, :]
        spread_c = mm(mix_pc, table)
        mix_back[layer] = stack_left(mm(mm(mix_pd, table, NT), mix_pc, NT) * same_t)
        mix_stack[layer] = stack_left(mm(spread_c, mix_pd, NT) * same)

    struct_rows = own[7:8].astype(I32)
    member = (struct_rows == iota((STRUCTS, 128), 0)).astype(F32)
    atom_cot = mm(energy_cot[...], member) * live
    counts[...] = jnp.zeros_like(counts)
    chunk = min(2048, edge_count)
    per_slot = edge_count // chunk
    wide = counts.shape[2]

    hot_rows = iota((128, chunk), 0).astype(F32).astype(BF16)
    none = jnp.zeros((), BF16)

    def count_edges(send, recv):
        local = recv - col * BLOCK
        inside = (local >= 0) & (local < BLOCK)
        key = jnp.where(inside, (send >> 8) * BLOCK + local, -1)
        step = jnp.where((send & 128) > 0, RADIX, 1.0).astype(BF16)
        sender_hot = jnp.where(hot_rows == (send & 127).astype(F32).astype(BF16), step, none)
        pair_hot = []
        for first in range(0, wide, 128):
            local_key = jnp.where((key >= first) & (key < first + 128), key - first, -1)
            hit = hot_rows == local_key.astype(F32).astype(BF16)
            pair_hot.append(jnp.where(hit, jnp.ones((), BF16), none))
        pair_hot = jnp.concatenate(pair_hot, axis=0)
        found = once(sender_hot, pair_hot, NT)
        upper = jnp.floor(found * (1.0 / RADIX))
        counts[0] += found - RADIX * upper
        counts[1] += upper

    def count_slot(slot, carry):
        for k in range(per_slot):
            spot = slice(k * chunk, (k + 1) * chunk)
            count_edges(send_all[slot, :, spot], recv_all[slot, :, spot])
        return carry

    count_slot(col, 0)

    for blank_ref in (dkind_sums, dsums, products, invariant.at[1]):
        blank_ref[...] = jnp.zeros(blank_ref.shape, F32)
    await_bytes(pack_all, lanes - 1, recv_sem.at[0])
    for q in range(tiles):
        sender_rows[:, 128 * q : 128 * (q + 1)] = jnp.where(low, pack_all[2 * q], pack_all[2 * q + 1])
    columns[...] = jnp.transpose(sender_rows[...])

    def geometry(start):
        cols = columns[pl.ds(start, BLOCK), :]
        return Geometry(cols, own, low_row)

    def radial_block(i, carry):
        start = aligned(i * BLOCK, BLOCK)
        geo = geometry(start)
        envelope = geo.reach * geo.reach * NORM
        for pair, value in enumerate(geo.sines()):
            radial[pair, pl.ds(start, BLOCK), :] = value * envelope
        inverse[pl.ds(start, BLOCK), :] = geo.inverse
        return carry

    loop(group // BLOCK, radial_block, 0)

    def monomial_rows(rows):
        x, y, z = rows[2:3], rows[3:4], rows[4:5]
        table = {(0, 0, 0): None}
        for m in MONOMIALS[1:]:
            axis = next(i for i in range(3) if m[i])
            lower = m[:axis] + (m[axis] - 1,) + m[axis + 1 :]
            factor = (x, y, z)[axis]
            table[m] = factor if table[lower] is None else table[lower] * factor
        return table

    def spread():
        def one(q, carry):
            spot = pl.ds(aligned(q * 128, 128), 128)
            table = monomial_rows(sender_rows[:, spot])
            h = weights[0:CHANNELS, spot]
            for i, m in enumerate(MONOMIALS):
                value = h if table[m] is None else h * table[m]
                products[row_of(i, 0) : row_of(i, 0) + 8, spot] = value[0:8]
                products[row_of(i, 1) : row_of(i, 1) + 4, spot] = value[8:12]
            return carry

        loop(tiles, one, 0)
        for q in strips:
            split = parts(products[:, q])
            three, two = [], []
            for start, end in zip(DEGREE_ROWS, DEGREE_ROWS[1:]):
                three += [v[start:end] for v in split]
                two += [v[start:end] for v in split[:2]]
            three.append(jnp.zeros((8, three[0].shape[1]), F32))
            product_three[:, q] = jnp.concatenate(three, axis=0).astype(BF16)
            product_two[:, q] = jnp.concatenate(two, axis=0).astype(BF16)


    def kind_spread(q, carry):
        spot = pl.ds(aligned(q * 128, 128), 128)
        table = monomial_rows(sender_rows[:, spot])
        kinds = sender_rows[0:2, spot]
        for i, m in enumerate(MONOMIALS):
            kind_products[2 * i : 2 * i + 2, spot] = kinds if table[m] is None else kinds * table[m]
        return carry

    loop(tiles, kind_spread, 0)
    for q in strips:
        kind_parts = jnp.concatenate(parts(kind_products[:, q]), axis=0)
        blank_rows = jnp.zeros((8, kind_parts.shape[1]), F32)
        kind_three[:, q] = jnp.concatenate([kind_parts, blank_rows], axis=0).astype(BF16)
    columns_of = []
    for kind_of in range(2):
        embedded = mm(embedding[...], (iota((2, 128), 0) == kind_of).astype(F32), TN)
        padded = jnp.concatenate(
            [mm(channel_in[0], embedded, TN), jnp.zeros((PADDED - CHANNELS, 128), F32)], axis=0
        )
        columns_of.append([padded[0:8], padded[8:16]])

    await_bytes(send_all, lanes - 1, recv_sem.at[1])
    await_bytes(recv_all, lanes - 1, recv_sem.at[2])
    if devices <= 32:
        for k in range(1, lanes):
            count_slot(lax.rem(col + k, lanes), 0)
    else:
        lax.fori_loop(1, lanes, lambda k, carry: count_slot(lax.rem(col + k, lanes), carry), 0)
    low_tall = iota((128, 128), 1) < BLOCK
    for block in range(group // 128):
        turn_of = block // 2
        piece = counts[block % 2, :, 128 * (turn_of // 2) : 128 * (turn_of // 2 + 1)]
        turned = pltpu.roll(piece, BLOCK, 1)
        first_half, second_half = (piece, turned) if turn_of % 2 == 0 else (turned, piece)
        pair_weight[128 * block : 128 * (block + 1), :] = jnp.where(
            low_tall, first_half, second_half
        )

    def plane_block(i, carry):
        spot = pl.ds(aligned(i * BLOCK, BLOCK), BLOCK)
        weight = pair_weight[spot, :]
        step = inverse[spot, :]
        for pair in range(PAIRS):
            value = radial[pair, spot, :] * weight
            for order in range(4):
                high = value.astype(BF16)
                planes_high[spot, tile_of(order, pair)] = high
                planes_low[spot, tile_of(order, pair)] = (value - high.astype(F32)).astype(BF16)
                value = value * step
        return carry

    loop(group // BLOCK, plane_block, 0)

    xi, yi, zi = (jnp.broadcast_to(own[r : r + 1], (8, 128)) for r in (2, 3, 4))

    def chunk_spots(i):
        pair, tile = i // 2, i % 2
        return pair, tile, slice(128 * pair, 128 * (pair + 1))

    def kind_component(place, pair):
        return [
            jnp.broadcast_to(kind_moved[place, 2 * pair + k : 2 * pair + k + 1, :], (8, 128))
            for k in range(2)
        ]

    def kind_expand(both, tile):
        return [columns_of[0][tile] * a + columns_of[1][tile] * b for a, b in both]

    units = [(0, pair, None) for pair in range(PAIRS)]
    units += [(1, pair, pair + 1 if pair + 1 < PAIRS else None) for pair in range(0, PAIRS, 2)]

    def joined_rows(ref, start, spot, other):
        value = ref[start : start + 8, spot]
        return value if other is None else jnp.where(row8 < 4, value, ref[start - 4 : start + 4, other])

    def shell_terms(tile, pair, second):
        out = []
        for order in range(4):
            spot = tile_of(order, pair)
            other = None if second is None else tile_of(order, second)
            for m in range(COUNTS[order]):
                out.append(joined_rows(sums, row_of(m, tile), spot, other))
        return out

    def store_rows(ref, start, tile, spot, other, value):
        if tile == 0:
            ref[start : start + 8, spot] = value
        else:
            ref[start : start + 4, spot] = value[0:4]
            if other is not None:
                ref[start : start + 4, other] = value[4:8]

    def pair_lanes(pair):
        return None if pair is None else slice(128 * pair, 128 * (pair + 1))

    def live_rows(value, tile):
        return value if tile == 0 else jnp.where(row8 < CHANNELS - 8, value, 0.0)

    def mix_invariants(layer):
        mixed = stacked(mix_stack[layer], invariant[layer])
        for pair in range(PAIRS):
            feats[layer, 72 * pair : 72 * (pair + 1), :] = mixed[:, 128 * pair : 128 * (pair + 1)]

    def forward_kinds():
        by_high = once(kind_three[...], planes_high[...])
        by_low = once(kind_three[0:80, :], planes_low[...])
        kind_sums[...] = by_high[0:40] + ((by_high[40:80] + by_low[0:40]) + (by_high[80:120] + by_low[40:80]))
        for order in range(4):
            for m in range(COUNTS[order]):
                pieces = [kind_sums[2 * m : 2 * m + 2, tile_of(order, pair)] for pair in range(PAIRS)]
                kind_shells[OFFSETS[order] + m] = jnp.concatenate(
                    pieces + [jnp.zeros((2, 128), F32)], axis=0
                )
        moved = all_shifted([kind_shells[m] for m in range(SHELLS)], xi, yi, zi)
        for place, value in enumerate(moved):
            kind_moved[place] = value
        for pair in range(PAIRS):
            both = [kind_component(place, pair) for place in range(20)]
            for tile in range(2):
                for p, value in enumerate(contracted(kind_expand(both, tile))):
                    start = PADDED * p + 8 * tile
                    invariant[0, start : start + 8, 128 * pair : 128 * (pair + 1)] = value
        mix_invariants(0)

    def forward():
        for order, first, last in GROUPS:
            spot = slice(128 * first, 128 * last)
            end = DEGREE_ROWS[order + 1]
            by_high = once(product_three[0 : -(-3 * end // 16) * 16, :], planes_high[:, spot])
            by_low = once(product_two[0 : 2 * end, :], planes_low[:, spot])
            for start, stop in zip(DEGREE_ROWS[: order + 1], DEGREE_ROWS[1:]):
                size = stop - start
                h, l = 3 * start, 2 * start
                sums[start:stop, spot] = by_high[h : h + size] + (
                    (by_high[h + size : h + 2 * size] + by_low[l : l + size])
                    + (by_high[h + 2 * size : h + 3 * size] + by_low[l + size : l + 2 * size])
                )
        for tile, pair, second in units:
            for p, value in enumerate(invariants(shell_terms(tile, pair, second), xi, yi, zi)):
                store_rows(
                    invariant.at[1], PADDED * p + 8 * tile, tile, pair_lanes(pair), pair_lanes(second), value
                )
        mix_invariants(1)

    def send_stats(phase, index, select_rows, first, second, extra=None):
        values = jnp.concatenate([first, second], axis=0)
        wide_values = jnp.concatenate(parts(values), axis=1).astype(BF16)
        rows = jnp.concatenate([select_rows] * 3, axis=1).astype(BF16)
        both = once(rows, wide_values, NT)
        for k in range(4):
            stat_own[index, 2 * k : 2 * k + 2, :] = both[0:2, 128 * k : 128 * (k + 1)]
        if extra is not None:
            stat_own[index, 2:3, 96 : 96 + STRUCTS] = extra
        everyone(
            lambda device, _: push(phase, stat_own.at[index], stat_all.at[index, me], device)
        )
        stat_all[index, me] = stat_own[index]

    def get_stats(phase, index):
        await_bytes(stat_all.at[index], devices - 1, recv_sem.at[phase])
        sums_of = [stat_all[index, k] for k in range(8)]
        for k in range(8, devices):
            sums_of[k % 8] = sums_of[k % 8] + stat_all[index, k]
        while len(sums_of) > 1:
            sums_of = [a + b for a, b in zip(sums_of[::2], sums_of[1::2])]
        return sums_of[0]

    def widen(rows):
        return once(
            jnp.concatenate([three_rows(rows), jnp.zeros((8, 128), BF16)], axis=0), half_pick, TN
        )

    rest_rows = ONES_ROW - 128

    def tall(wide, start):
        return jnp.concatenate(
            [wide[:, start : start + 128], wide[0:rest_rows, start + 128 : start + 256]], axis=0
        )

    ones_rows = iota((FEATURE_ROWS - ONES_ROW, 128), 0) == 0
    for layer in range(2):
        feats[layer, ONES_ROW:FEATURE_ROWS, :] = ones_rows.astype(F32)
        normed[layer, ONES_ROW:FEATURE_ROWS, :] = ones_rows.astype(F32)

    def send_moments(layer, phase):
        values = feats[layer]
        send_stats(phase, layer, half_sum * live, values, values * values)

    def normalise(layer, phase):
        total = get_stats(phase, layer)
        inverse_count = 1.0 / jnp.maximum(total[2:3, ONES_ROW - 128 : ONES_ROW - 127], 1.0)
        scaled = total * inverse_count
        means = pltpu.roll(scaled, 4, 0)
        scales = lax.rsqrt(scaled - means * means + variance_eps)
        wide = widen(jnp.where(row8 < 4, scaled, scales))
        scale = tall(wide, 256)
        normed[layer, 0:ONES_ROW, :] = (feats[layer, 0:ONES_ROW, :] - tall(wide, 0)) * scale
        rows = 2 * HEAD_ROWS
        high, middle, tail = (v.astype(BF16) for v in parts(normed[layer]))
        by_high = once(head_rows[layer], high)
        by_middle = once(head_rows[layer, 0 : 2 * rows, :], middle)
        by_tail = once(head_rows[layer, 0:rows, :], tail)
        joined = by_high[0:rows] + (
            (by_high[rows : 2 * rows] + by_middle[0:rows])
            + (by_high[2 * rows :] + by_middle[rows:] + by_tail)
        )
        chosen = jnp.where(low_row, joined[0:HEAD_ROWS], joined[HEAD_ROWS:])
        return chosen + pltpu.roll(chosen, BLOCK, 1), scale, inverse_count

    def run_head(layer, pre):
        hidden, hidden_slope = silu_pair(pre[0:HIDDEN])
        inner, inner_slope = silu_pair(stacked(inner_forward[layer], hidden) + inner_cols[layer])
        dinner = energy_cols[layer] * atom_cot * inner_slope
        dhidden = stacked(inner_back[layer], dinner) * hidden_slope
        return hidden, inner, dinner, dhidden

    def small_grad(layer, hidden, inner, dinner):
        left = jnp.concatenate([dinner, atom_cot * inner], axis=0)
        blank = jnp.zeros((128 - 32 - 32 * layer, 128), F32)
        right = [hidden, (iota((8, 128), 0) == 0).astype(F32), blank]
        if layer == 1:
            right = [jnp.zeros((32, 128), F32)] + right
        return mm(jnp.where(low_row, left, 0.0), jnp.concatenate(right, axis=0), NT)

    def halves(value):
        return jnp.where(low_row, value, 0.0), jnp.where(low_row, 0.0, value)

    def scatter_tiles(phase, source, target, base):
        for k in range(source.shape[0]):
            t = lax.rem(me + k, source.shape[0])

            @pl.when(me != base + t)
            def _():
                there = base + t
                push(phase, source.at[t], target.at[me], (there // lanes, lax.rem(there, lanes)))

            @pl.when(me == base + t)
            def _():
                target[me] = source[t]

    def mine(base, result):
        return (me >= base) & (me < base + result.shape[0])

    def share_tiles(phase, parts_of, result, base):
        @pl.when(mine(base, result))
        def _():
            await_bytes(parts_of, devices - 1, recv_sem.at[phase])
            total = parts_of[0]
            for k in range(1, devices):
                total = total + parts_of[k]
            result[me - base] = total
            everyone(
                lambda device, _: push(phase + 1, result.at[me - base], result.at[me - base], device)
            )

    def gather_tiles(phase, result, base):
        count_of = result.shape[0]

        @pl.when(mine(base, result))
        def _():
            await_bytes(result, count_of - 1, recv_sem.at[phase + 1])

        @pl.when(jnp.logical_not(mine(base, result)))
        def _():
            await_bytes(result, count_of, recv_sem.at[phase + 1])

    def drain_tiles(phase, parts_of, result, base):
        count_of = result.shape[0]

        @pl.when(mine(base, result))
        def _():
            await_bytes(result, count_of - 1, send_sem.at[phase])
            await_bytes(parts_of, devices - 1, send_sem.at[phase + 1])

        @pl.when(jnp.logical_not(mine(base, result)))
        def _():
            await_bytes(result, count_of, send_sem.at[phase])

    base_a, base_b, base_c = 0, tiles_a.shape[0], devices - tiles_c.shape[0]

    forward_kinds()
    send_moments(0, 3)
    for parity in range(2):
        k = iota((FEATURE_ROWS, FEATURES), 0)
        pair = (k >= 72).astype(I32) + (k >= 144).astype(I32)
        rest = k - 72 * pair
        kind_of = (rest * 5462) >> 16
        channel = rest - 12 * kind_of
        place = channel * 36 + (2 * pair + parity) * 6 + kind_of
        hit = (place == iota((FEATURE_ROWS, FEATURES), 1)) & (k < ONES_ROW)
        select[parity] = hit.astype(F32).astype(BF16)
    inner_cols, energy_cols = [], []
    head[...] = jnp.zeros_like(head)
    for layer in range(2):
        for parity in range(2):
            base = HEAD_ROWS * parity
            block = exact(hidden_weight[layer], select[parity], NT)
            if parity == 0:
                spot = (iota((2, FEATURE_ROWS), 1) == ONES_ROW) & (
                    iota((2, FEATURE_ROWS), 0) == layer
                )
                block = block + mm(hidden_bias[...], spot.astype(F32), TN)
            head[layer, base : base + HIDDEN, :] = block
            if layer == 0:
                message_rows = jnp.concatenate(
                    [message_weight[...], jnp.zeros((PADDED - CHANNELS, FEATURES), F32)], axis=0
                )
                head[0, base + HIDDEN : base + HEAD_ROWS, :] = exact(message_rows, select[parity], NT)
        whole = head[layer]
        head_rows[layer] = three_rows(whole)
        head_stack[layer] = stack_left(whole)
        if layer == 0:
            message_stack[...] = stack_left(
                jnp.concatenate([whole[HIDDEN:HEAD_ROWS], whole[HEAD_ROWS + HIDDEN :]], axis=0)
            )
        inner_back[layer] = stack_left(inner_weight[layer])
        inner_forward[layer] = stack_left(jnp.transpose(inner_weight[layer]))
        pick = (iota((2, 128), 0) == layer).astype(F32)
        inner_cols.append(mm(inner_bias[...], pick, TN))
        energy_cols.append(mm(energy_weight[...], pick, TN))

    if group <= 512:
        turned_high[...] = jnp.transpose(planes_high[...])
        turned_low[...] = jnp.transpose(planes_low[...])

    def against(left, lane_spot, spot, low_part):
        if group <= 512:
            return once(left, (turned_low if low_part else turned_high)[lane_spot, spot])
        return once(left, (planes_low if low_part else planes_high)[spot, lane_spot], NT)

    pre_zero, scale_zero, inverse_count = normalise(0, 3)
    message = pre_zero[HIDDEN:HEAD_ROWS]
    message_own[...] = jnp.where(low, message[0:8], message[8:16])
    members(lambda device, _: push(4, message_own, message_all.at[col], device))
    message_all[col] = message_own[...]
    hidden_zero, inner_zero, dinner_zero, dhidden_zero = run_head(0, pre_zero)
    d_low, d_high = halves(dhidden_zero)
    gap = jnp.zeros((HEAD_ROWS - HIDDEN, 128), F32)
    dnormed_head = stacked(head_stack[0], jnp.concatenate([d_low, gap, d_high, gap], axis=0))

    def pack_head(target, layer, d_low, d_high):
        block = mm(jnp.concatenate([d_low, d_high], axis=0), normed[layer], NT)
        for r in range(6):
            for half in range(2):
                target[2 * r + half] = block[8 * r : 8 * (r + 1), 128 * half : 128 * (half + 1)]

    pack_head(tiles_a, 0, d_low, d_high)
    scatter_tiles(11, tiles_a, tiles_a_all, 0)
    weights[...] = jnp.zeros_like(weights)
    embedded = mm(embedding[...], sender_rows[0:2, :], TN)
    weights[0:CHANNELS, :] = mm(channel_in[1], embedded, TN)
    await_bytes(message_all, lanes - 1, recv_sem.at[4])
    for q in range(tiles):
        even, odd = message_all[2 * q], message_all[2 * q + 1]
        spot = slice(128 * q, 128 * (q + 1))
        weights[0:8, spot] += jnp.where(low, even, pltpu.roll(odd, BLOCK, 1))
        weights[8:16, spot] += jnp.where(low, pltpu.roll(even, BLOCK, 1), odd)

    spread()
    forward()
    send_moments(1, 5)
    turn = ANGLE * (1.0 + (iota((1, 128), 1) >= BLOCK).astype(F32))

    def slope_block(i, carry):
        start = aligned(i * BLOCK, BLOCK)
        spot = pl.ds(start, BLOCK)
        geo = geometry(start)
        step = geo.inverse
        square = step * step
        envelope = geo.reach * geo.reach * NORM
        slope = geo.reach * (-2.0 * NORM / (cutoff_radius * cutoff_radius))
        weight = pair_weight[spot, :]
        for pair, (sine, cosine) in enumerate(zip(geo.sines(), geo.cosines())):
            rate = (turn + 2.0 * ANGLE * pair) * cosine - sine
            value = weight * ((0.5 * square) * rate * envelope + sine * slope)
            plane = weight * (sine * envelope)
            slopes[spot, tile_of(0, pair)] = value
            for order in range(1, 4):
                plane = plane * step
                value = value * step - (0.5 * square) * plane
                slopes[spot, tile_of(order, pair)] = value
        return carry

    loop(group // BLOCK, slope_block, 0)
    for q in strips:
        kind_stack[q, :] = stack_left(kind_products[:, q])

    share_tiles(11, tiles_a_all, tiles_a_sum, base_a)
    pre_one, scale_one, _ = normalise(1, 5)
    hidden_one, inner_one, dinner_one, dhidden_one = run_head(1, pre_one)
    d_low, d_high = halves(dhidden_one)
    dnormed_one = stacked(head_stack[1], jnp.concatenate([d_low, gap, d_high, gap], axis=0))
    send_stats(6, 2, half_sum, dnormed_one, dnormed_one * normed[1])

    pack_head(tiles_b, 1, d_low, d_high)
    small = small_grad(0, hidden_zero, inner_zero, dinner_zero)
    small = small + small_grad(1, hidden_one, inner_one, dinner_one)
    for r in range(2):
        tiles_b[12 + r] = small[8 * r : 8 * (r + 1)] + pltpu.roll(small[16 + 8 * r : 24 + 8 * r], 64, 1)
    atom_energy = jnp.sum(energy_cols[0] * inner_zero + energy_cols[1] * inner_one, axis=0, keepdims=True)
    atom_energy = jnp.where(low_row, live * atom_energy, 0.0)
    energy_rows = mm(jnp.broadcast_to(atom_energy, (8, 128)), member, NT)[0:1]
    def feature_back(layer, total, dnormed, scale):
        wide = widen(total * inverse_count)
        dfeats = scale * (
            dnormed[0:ONES_ROW] - live * (tall(wide, 0) + tall(wide, 256) * normed[layer, 0:ONES_ROW, :])
        )
        dmixed = jnp.concatenate([dfeats[72 * pair : 72 * (pair + 1)] for pair in range(PAIRS)], axis=1)
        dinvariant[...] = stacked(mix_back[layer], dmixed)
        return dmixed

    def mix_grad(layer, dmixed):
        return mm(invariant[layer], dmixed, NT, lax.Precision.HIGH) * same

    blank = jnp.zeros((8, 128), F32)

    def shell_back(some_units, moved):
        for tile, pair, second in some_units:
            cots = tuple(
                joined_rows(dinvariant, PADDED * p + 8 * tile, pair_lanes(pair), pair_lanes(second))
                for p in range(6)
            )
            _, pull = jax.vjp(invariants, shell_terms(tile, pair, second), xi, yi, zi)
            dterms, *shift = pull(cots)
            for order in range(4):
                spot = tile_of(order, pair)
                other = None if second is None else tile_of(order, second)
                for m in range(COUNTS[order]):
                    store_rows(dsums, row_of(m, tile), tile, spot, other, dterms[OFFSETS[order] + m])
            if tile == 1 and second is None:
                shift = [jnp.where(row8 < 4, v, 0.0) for v in shift]
            moved = tuple(a + b for a, b in zip(moved, shift))
        return moved

    def shell_back_kinds():
        dtable = [[blank, blank], [blank, blank]]
        folded = [[] for _ in range(20)]
        for pair in range(PAIRS):
            both = [kind_component(place, pair) for place in range(20)]
            sides = []
            for tile in range(2):
                cots = tuple(dinvariant[PADDED * p + 8 * tile : PADDED * p + 8 * tile + 8, 128 * pair : 128 * (pair + 1)] for p in range(6))
                _, pull = jax.vjp(contracted, kind_expand(both, tile))
                sides.append(pull(cots)[0])
                for k in range(2):
                    for place in range(20):
                        dtable[k][tile] = dtable[k][tile] + sides[tile][place] * both[place][k]
            for place in range(20):
                for k in range(2):
                    folded[place].append(
                        columns_of[k][0] * sides[0][place] + columns_of[k][1] * sides[1][place]
                    )
        dmoved = [jnp.where(row8 < 2 * PAIRS, row_sums(v, row8), 0.0) for v in folded]
        _, pull = jax.vjp(all_shifted, [kind_shells[m] for m in range(SHELLS)], xi, yi, zi)
        dterms, *moved = pull(dmoved)
        for order in range(4):
            for m in range(COUNTS[order]):
                value = dterms[OFFSETS[order] + m]
                for pair in range(PAIRS):
                    dkind_sums[2 * m : 2 * m + 2, tile_of(order, pair)] = value[2 * pair : 2 * pair + 2]
        return tuple(moved), [jnp.concatenate(halves_of, axis=0) for halves_of in dtable]

    def product_back(groups, done):
        for order, first, last in groups:
            lane_spot = slice(128 * first, 128 * last)
            end = DEGREE_ROWS[order + 1]
            high, low_part, _ = parts(dsums[0:end, lane_spot])
            left = jnp.concatenate([high, low_part], axis=0).astype(BF16)
            for spot in strips:
                by_high = against(left, lane_spot, spot, False)
                block = by_high[0:end] + (by_high[end:] + against(left[0:end], lane_spot, spot, True))
                shared = min(done, end)
                if shared:
                    dproducts[0:shared, spot] += block[0:shared]
                if end > done:
                    dproducts[done:end, spot] = block[done:end]
            done = max(done, end)

    def product_back_kinds():
        high, low_part, _ = parts(dkind_sums[...])
        left = jnp.concatenate([high, low_part], axis=0).astype(BF16)
        for spot in strips:
            whole = slice(0, PLANE_LANES)
            by_high = against(left, whole, spot, False)
            dkind_products[:, spot] = by_high[0:40] + (by_high[40:] + against(left, whole, spot, True)[0:40])

    def weight_back():
        out = []
        for q in range(tiles):
            spot = slice(128 * q, 128 * (q + 1))
            table = monomial_rows(sender_rows[:, spot])
            both = []
            for tile in range(2):
                total = None
                for i, m in enumerate(MONOMIALS):
                    term = dproducts[row_of(i, tile) : row_of(i, tile) + 8, spot]
                    term = term if table[m] is None else term * table[m]
                    total = term if total is None else total + term
                both.append(live_rows(total, tile))
            out.append(jnp.concatenate(both, axis=0))
        return out

    def axis_slope(table, axis, value_of):
        total = None
        for i, m in enumerate(MONOMIALS):
            if not m[axis]:
                continue
            lower = table[m[:axis] + (m[axis] - 1,) + m[axis + 1 :]]
            term = value_of(i)
            if lower is not None:
                term = (float(m[axis]) * lower) * term
            total = term if total is None else total + term
        return total

    def coordinate_back():
        out = []
        for q in range(tiles):
            spot = slice(128 * q, 128 * (q + 1))
            table = monomial_rows(sender_rows[:, spot])
            sides = []
            for axis in range(3):
                total = None
                for tile in range(2):
                    slope = axis_slope(
                        table, axis, lambda i: dproducts[row_of(i, tile) : row_of(i, tile) + 8, spot]
                    )
                    term = weights[8 * tile : 8 * tile + 8, spot] * live_rows(slope, tile)
                    total = term if total is None else total + term
                sides.append(jnp.sum(total, axis=0, keepdims=True))
            out.append(sides)
        return out

    def coordinate_back_kinds():
        out = []
        for q in range(tiles):
            spot = slice(128 * q, 128 * (q + 1))
            table = monomial_rows(sender_rows[:, spot])
            kinds = sender_rows[0:2, spot]
            rows = [
                jnp.sum(kinds * dkind_products[2 * i : 2 * i + 2, spot], axis=0, keepdims=True)
                for i in range(len(MONOMIALS))
            ]
            out.append([axis_slope(table, axis, lambda i: rows[i]) for axis in range(3)])
        return out

    def radial_pull(block, first, last, spot):
        total = None
        for at in range(first, last):
            term = block[:, 128 * (at - first) : 128 * (at - first + 1)] * slopes[spot, 128 * at : 128 * (at + 1)]
            total = term if total is None else total + term
        return total

    def plane_back():
        for order, first, last in GROUPS:
            end = DEGREE_ROWS[order + 1]
            for spot in strips:
                block = mm(products[0:end, spot], dsums[0:end, 128 * first : 128 * last], TN)
                term = radial_pull(block, first, last, spot)
                if order == 3:
                    pulls[spot, :] = term
                else:
                    pulls[spot, :] += term

    def plane_back_kinds():
        right = stack_right(dkind_sums[...])
        for order, first, last in GROUPS:
            for spot in strips:
                block = once(kind_stack[spot, :], right[:, 128 * first : 128 * last])
                pulls[spot, :] += radial_pull(block, first, last, spot)

    dmixed_one = feature_back(1, get_stats(6, 2), dnormed_one, scale_one)
    moved_one = shell_back([units[0], units[1], units[3]], (blank, blank, blank))
    product_back([GROUPS[1]], 0)
    moved_one = shell_back([units[2], units[4]], moved_one)
    product_back([GROUPS[0]] + GROUPS[2:], DEGREE_ROWS[3])
    dweights_one = weight_back()
    for q in range(tiles):
        top, bottom = dweights_one[q][0:8], dweights_one[q][8:16]
        dmessage_own[2 * q] = jnp.where(low, top, pltpu.roll(bottom, BLOCK, 1))
        dmessage_own[2 * q + 1] = jnp.where(low, pltpu.roll(top, BLOCK, 1), bottom)
    members(
        lambda device, target: push(7, dmessage_own.at[target], dmessage_all.at[col], device)
    )
    dmessage_all[col] = dmessage_own[col]
    kinds_of = sender_rows[...]
    dtable_one = jnp.zeros((PADDED, 8), F32)
    for q in range(tiles):
        dtable_one = dtable_one + mm(dweights_one[q], kinds_of[:, 128 * q : 128 * (q + 1)], NT)
    slopes_one = coordinate_back()
    mix_one = mix_grad(1, dmixed_one)
    scatter_tiles(13, tiles_b, tiles_b_all, base_b)
    await_bytes(dmessage_all, lanes - 1, recv_sem.at[7])
    arrived = dmessage_all[0]
    for k in range(1, lanes):
        arrived = arrived + dmessage_all[k]
    turned = pltpu.roll(arrived, BLOCK, 1)
    dmessage = jnp.concatenate([jnp.where(low, arrived, turned), jnp.where(low, turned, arrived)], axis=0)

    m_low, m_high = halves(dmessage)
    dmessage_both = jnp.concatenate([m_low, m_high], axis=0)
    dnormed_zero = dnormed_head + stacked(message_stack[...], dmessage_both)
    send_stats(8, 3, half_sum, dnormed_zero, dnormed_zero * normed[0], energy_rows)
    dmessage_weight = mm(dmessage_both, normed[0], NT)
    for r in range(4):
        for half in range(2):
            tiles_c[2 * r + half] = dmessage_weight[
                8 * r : 8 * (r + 1), 128 * half : 128 * (half + 1)
            ]
    scatter_tiles(15, tiles_c, tiles_c_all, base_c)
    fold_c = (iota((PADDED, 96), 0) == (iota((PADDED, 96), 1) & 15)).astype(F32)
    d_of = iota((72, 128), 0) - 12 * ((iota((72, 128), 0) * 5462) >> 16)
    seat_mix = [(iota((72, 128), 1) == d_of + 12 * layer).astype(BF16) for layer in range(2)]
    seat_kind = ((lane == row8 + 26) & (row8 < 2)).astype(F32)

    def fold_mix(layer, value):
        wide_value = once(fold_c.astype(BF16), jnp.concatenate(parts(exact(value, seat_mix[layer])), axis=1).astype(BF16))
        return wide_value[:, 0:128] + (wide_value[:, 128:256] + wide_value[:, 256:384])

    final_one = fold_mix(1, mix_one) + mm(dtable_one, seat_kind)
    plane_back()
    share_tiles(13, tiles_b_all, tiles_b_sum, base_b)
    total_zero = get_stats(8, 3)
    share_tiles(15, tiles_c_all, tiles_c_sum, base_c)
    dmixed_zero = feature_back(0, total_zero, dnormed_zero, scale_zero)
    final = fold_mix(0, mix_grad(0, dmixed_zero)) + final_one
    moved_zero, dtables = shell_back_kinds()
    for k in range(2):
        total = jnp.sum(dtables[k], axis=1, keepdims=True)
        final = final + jnp.where(iota((PADDED, 128), 1) == 24 + k, total, 0.0)
    folded = final[0:8] + pltpu.roll(pltpu.roll(final[0:8], 4, 0), 32, 1) + pltpu.roll(final[8:16], 64, 1)
    final_own[...] = folded[0:4]
    everyone(lambda device, _: push(10, final_own, final_all.at[me], device))
    final_all[me] = final_own[...]
    product_back_kinds()
    plane_back_kinds()
    slopes_zero = coordinate_back_kinds()
    pull_of = pulls[...]
    to_own = mm(sender_rows[...], pull_of, NN, lax.Precision.HIGH)
    to_sender = mm(own, pull_of, NT, lax.Precision.HIGH)
    force_own[...] = jnp.zeros_like(force_own)
    for q in range(tiles):
        spot = slice(128 * q, 128 * (q + 1))
        weight_row = to_sender[5:6, spot]
        for axis in range(3):
            value = -2.0 * (to_sender[2 + axis : 3 + axis, spot] + sender_rows[2 + axis : 3 + axis, spot] * weight_row)
            value = value - slopes_zero[q][axis] - slopes_one[q][axis]
            force_own[2 * q, axis : axis + 1, :] = value
            force_own[2 * q + 1, axis : axis + 1, :] = pltpu.roll(value, BLOCK, 1)
    members(lambda device, target: push(9, force_own.at[target], force_all.at[col], device))
    force_all[col] = force_own[col]
    own_force = []
    for axis in range(3):
        pairwise = 2.0 * (to_own[2 + axis : 3 + axis] + own[2 + axis : 3 + axis] * to_own[5:6])
        moved = jnp.sum(moved_zero[axis] + moved_one[axis], axis=0, keepdims=True)
        both = pairwise + moved
        own_force.append(both + pltpu.roll(both, BLOCK, 1))

    group_energy = stat_all[3, row * lanes, 2:3, 96 : 96 + STRUCTS]
    for k in range(1, lanes):
        group_energy = group_energy + stat_all[3, row * lanes + k, 2:3, 96 : 96 + STRUCTS]
    energies_out[...] = group_energy

    gather_tiles(11, tiles_a_sum, base_a)
    gather_tiles(13, tiles_b_sum, base_b)
    pick_ones = ((iota((8, FEATURE_ROWS), 0) == 0) & (iota((8, FEATURE_ROWS), 1) == ONES_ROW)).astype(F32)
    for layer in range(2):
        total = None
        for parity in range(2):
            rows = []
            for r in range(3):
                at = 6 * parity + 2 * r
                summed = (tiles_a_sum, tiles_b_sum)[layer]
                rows.append(jnp.concatenate([summed[at], summed[at + 1]], axis=1))
            block = jnp.concatenate(rows, axis=0)
            if parity == 0:
                hidden_bias_out[layer : layer + 1, :] = mm(pick_ones, block, NT)[0:1]
            part = exact(block, select[parity])
            total = part if total is None else total + part
        hidden_weight_out[layer] = total
    small_sum = jnp.concatenate([tiles_b_sum[12 + r] for r in range(2)], axis=0)
    for layer in range(2):
        inner_weight_out[layer] = small_sum[0:INNER, 32 * layer : 32 * layer + HIDDEN]
        pick = ((row8 == 0) & (lane == 32 * layer + HIDDEN)).astype(F32)
        inner_bias_out[layer : layer + 1, :] = mm(pick, small_sum, NT)[0:1]
        pick = ((row8 == 0) & (lane == 64 + 32 * layer + HIDDEN)).astype(F32)
        energy_weight_out[layer : layer + 1, :] = mm(pick, small_sum, NT)[0:1]
    gather_tiles(15, tiles_c_sum, base_c)
    total = None
    for parity in range(2):
        rows = [
            jnp.concatenate(
                [tiles_c_sum[4 * parity + 2 * r], tiles_c_sum[4 * parity + 2 * r + 1]], axis=1
            )
            for r in range(2)
        ]
        part = exact(jnp.concatenate(rows, axis=0), select[parity])
        total = part if total is None else total + part
    message_weight_out[...] = total[0:CHANNELS]

    await_bytes(final_all, devices - 1, recv_sem.at[10])
    final = final_all[0]
    for k in range(1, devices):
        final = final + final_all[k]
    final = jnp.concatenate([final, jnp.zeros((4, 128), F32)], axis=0)
    upper = jnp.where(row8 < 4, final, pltpu.roll(pltpu.roll(final, 4, 0), 96, 1))
    final = jnp.concatenate([upper, pltpu.roll(final, 64, 1)], axis=0)
    dembedding = None
    for layer in range(2):
        channel_mix_out[:, layer, :] = final[0:CHANNELS, 12 * layer : 12 * (layer + 1)]
        dtable = final[0:CHANNELS, 24 + 2 * layer : 26 + 2 * layer]
        channel_in_out[layer] = lax.dot_general(
            embedding[...],
            dtable,
            (((0,), (1,)), ((), ())),
            precision=lax.Precision.HIGHEST,
            preferred_element_type=F32,
        )
        part = lax.dot_general(
            dtable,
            channel_in[layer],
            (((0,), (1,)), ((), ())),
            precision=lax.Precision.HIGHEST,
            preferred_element_type=F32,
        )
        dembedding = part if dembedding is None else dembedding + part
    embedding_out[...] = dembedding

    await_bytes(force_all, lanes - 1, recv_sem.at[9])
    force = force_all[0]
    for k in range(1, lanes):
        force = force + force_all[k]
    for axis in range(3):
        position_out[axis] = (force[axis : axis + 1] + own_force[axis])[:, 0:BLOCK]

    await_bytes(pack_all, lanes - 1, send_sem.at[0])
    await_bytes(send_all, lanes - 1, send_sem.at[1])
    await_bytes(recv_all, lanes - 1, send_sem.at[2])
    await_bytes(stat_all.at[0], devices - 1, send_sem.at[3])
    await_bytes(message_all, lanes - 1, send_sem.at[4])
    await_bytes(stat_all.at[1], devices - 1, send_sem.at[5])
    await_bytes(stat_all.at[2], devices - 1, send_sem.at[6])
    await_bytes(dmessage_all, lanes - 1, send_sem.at[7])
    await_bytes(stat_all.at[3], devices - 1, send_sem.at[8])
    await_bytes(force_all, lanes - 1, send_sem.at[9])
    await_bytes(final_all, devices - 1, send_sem.at[10])
    drain_tiles(11, tiles_a_all, tiles_a_sum, base_a)
    drain_tiles(13, tiles_b_all, tiles_b_sum, base_b)
    drain_tiles(15, tiles_c_all, tiles_c_sum, base_c)


def hand_over(*refs):
    for source, target in zip(refs[:11], refs[11:]):
        target[...] = source[...]


def solution(mesh):
    lanes = mesh.shape["edge"]
    structs = mesh.shape["struct"]
    devices = lanes * structs

    def step(
        positions,
        species,
        struct_id,
        atom_mask,
        senders,
        receivers,
        edge_mask,
        energy_cot,
        embedding,
        channel_in,
        channel_mix,
        hidden_weight,
        hidden_bias,
        inner_weight,
        inner_bias,
        energy_weight,
        message_weight,
    ):
        owned = positions.shape[2]
        group = owned * lanes
        edges = senders.shape[1]
        inputs = [
            positions,
            species,
            struct_id,
            atom_mask,
            senders,
            receivers,
            edge_mask,
            energy_cot,
            embedding,
            channel_in,
            jnp.transpose(channel_mix, (1, 0, 2)),
            jnp.transpose(hidden_weight, (0, 2, 1)),
            hidden_bias,
            jnp.transpose(inner_weight, (0, 2, 1)),
            inner_bias,
            energy_weight,
            jnp.transpose(message_weight),
        ]
        vmem = pltpu.VMEM
        shapes = [
            (1, STRUCTS),
            (3, 1, owned),
            embedding.shape,
            channel_in.shape,
            (CHANNELS, 2, CHANNELS),
            (2, HIDDEN, FEATURES),
            hidden_bias.shape,
            (2, INNER, HIDDEN),
            inner_bias.shape,
            energy_weight.shape,
            (CHANNELS, FEATURES),
        ]
        scratch = [
            vmem((8, 128), F32),
            vmem((lanes, 8, 128), F32),
            vmem((lanes, 1, edges), I32),
            vmem((1, edges), I32),
            vmem((lanes, 1, edges), I32),
            vmem((2, 128, BLOCK * (group // 256)), F32),
            vmem((group, 128), F32),
            vmem((group, 8), F32),
            vmem((8, group), F32),
            vmem((PAIRS, group, 128), F32),
            vmem((group, 128), F32),
            vmem((group, PLANE_LANES), BF16),
            vmem((group, PLANE_LANES), BF16),
            vmem((PLANE_LANES, group if group <= 512 else 128), BF16),
            vmem((PLANE_LANES, group if group <= 512 else 128), BF16),
            vmem((group, PLANE_LANES), F32),
            vmem((group, 128), F32),
            vmem((PADDED, group), F32),
            vmem((PRODUCT_ROWS, group), F32),
            vmem((752, group), BF16),
            vmem((496, group), BF16),
            vmem((PRODUCT_ROWS, PLANE_LANES), F32),
            vmem((PRODUCT_ROWS, PLANE_LANES), F32),
            vmem((40, group), F32),
            vmem((128, group), BF16),
            vmem((group, 240), BF16),
            vmem((40, PLANE_LANES), F32),
            vmem((SHELLS, 8, 128), F32),
            vmem((20, 8, 128), F32),
            vmem((40, PLANE_LANES), F32),
            vmem((40, group), F32),
            vmem((PRODUCT_ROWS, group), F32),
            vmem((2, 96, 128 * PAIRS), F32),
            vmem((96, 128 * PAIRS), F32),
            vmem((2, FEATURE_ROWS, 128), F32),
            vmem((2, FEATURE_ROWS, 128), F32),
            vmem((2, FEATURE_ROWS, FEATURES), BF16),
            vmem((2, 2 * HEAD_ROWS, FEATURE_ROWS), F32),
            vmem((2, 6 * HEAD_ROWS, FEATURE_ROWS), BF16),
            vmem((2, FEATURE_ROWS, 12 * HEAD_ROWS), BF16),
            vmem((FEATURE_ROWS, 12 * PADDED), BF16),
            vmem((2, INNER, 6 * HIDDEN), BF16),
            vmem((2, HIDDEN, 6 * INNER), BF16),
            vmem((2, 72, 6 * 96), BF16),
            vmem((2, 96, 6 * 72), BF16),
            vmem((4, 8, 128), F32),
            vmem((4, devices, 8, 128), F32),
            vmem((8, 128), F32),
            vmem((lanes, 8, 128), F32),
            vmem((lanes, 8, 128), F32),
            vmem((lanes, 8, 128), F32),
            vmem((lanes, 8, 128), F32),
            vmem((lanes, 8, 128), F32),
            vmem((4, 128), F32),
            vmem((devices, 4, 128), F32),
            vmem((12, 8, 128), F32),
            vmem((devices, 8, 128), F32),
            vmem((12, 8, 128), F32),
            vmem((14, 8, 128), F32),
            vmem((devices, 8, 128), F32),
            vmem((14, 8, 128), F32),
            vmem((8, 8, 128), F32),
            vmem((devices, 8, 128), F32),
            vmem((8, 8, 128), F32),
            pltpu.SemaphoreType.DMA((20,)),
            pltpu.SemaphoreType.DMA((20,)),
            pltpu.SemaphoreType.DMA((17,)),
        ] + [vmem(v.shape, v.dtype) for v in inputs]
        outs = pl.pallas_call(
            functools.partial(body, lanes, structs),
            out_shape=[vmem(s, F32) for s in shapes],
            in_specs=[pl.BlockSpec(memory_space=pl.ANY)] * 17,
            out_specs=[pl.BlockSpec(memory_space=vmem)] * 11,
            scratch_shapes=scratch,
            compiler_params=pltpu.CompilerParams(
                collective_id=0, has_side_effects=True, vmem_limit_bytes=60 * 1024 * 1024
            ),
        )(*inputs)
        outs = pl.pallas_call(
            hand_over,
            out_shape=[jax.ShapeDtypeStruct(s, F32) for s in shapes],
            in_specs=[pl.BlockSpec(memory_space=vmem)] * 11,
            out_specs=[pl.BlockSpec(memory_space=vmem)] * 11,
        )(*(pltpu.with_memory_space_constraint(v, pltpu.VMEM) for v in outs))
        outs = list(outs)
        outs[4] = jnp.transpose(outs[4], (1, 0, 2))
        outs[5] = jnp.transpose(outs[5], (0, 2, 1))
        outs[7] = jnp.transpose(outs[7], (0, 2, 1))
        outs[10] = jnp.transpose(outs[10])
        return tuple(outs)

    tiled = P("struct", "edge")
    return jax.shard_map(
        step,
        mesh=mesh,
        in_specs=(
            P(None, "struct", "edge"),
            tiled,
            tiled,
            tiled,
            tiled,
            tiled,
            tiled,
            P("struct", None),
        )
        + (P(),) * 9,
        out_specs=(P("struct", None), P(None, "struct", "edge")) + (P(),) * 9,
        check_vma=False,
    )
```

```python
import functools
import math

import jax
import jax.numpy as jnp
import numpy as np
from jax import lax
from jax.experimental import pallas as pl
from jax.experimental.pallas import tpu as pltpu
from jax.sharding import PartitionSpec as P

CHANNELS = 12
PADDED = 16
RADIALS = 6
PAIRS = 3
STRUCTS = 8
HIDDEN = 24
INNER = 16
FEATURES = 432
HEAD_ROWS = 40
FEATURE_ROWS = 256
ONES_ROW = 216
BLOCK = 64

cutoff_radius = 6.0
variance_eps = 1e-05
center = 1.5

MESH = pl.DeviceIdType.MESH
F32 = jnp.float32
BF16 = jnp.bfloat16
I32 = jnp.int32
NN = ((1,), (0,))
NT = ((1,), (1,))
TN = ((0,), (0,))

MONOMIALS = sorted(
    [(a, b, c) for a in range(4) for b in range(4) for c in range(4) if a + b + c <= 3],
    key=lambda m: (sum(m), -m[0], -m[1], -m[2]),
)
PLACE = {m: i for i, m in enumerate(MONOMIALS)}
COUNTS = [1, 4, 10, 20]
OFFSETS = [0, 1, 5, 15]
SHELLS = 35
DEGREE_ROWS = [0, 16, 56, 128, 248]
DEGREE_COUNTS = [1, 3, 6, 10]


def row_of(place, tile):
    degree = sum(MONOMIALS[place])
    within = place - sum(DEGREE_COUNTS[:degree])
    return DEGREE_ROWS[degree] + (8 * DEGREE_COUNTS[degree] + 4 * within if tile else 8 * within)


PRODUCT_ROWS = 256
LANE_TILES = [(3, 0), (3, 1), (3, 2), (2, 2), (2, 0), (2, 1), (1, 0), (1, 1), (1, 2), (0, 2), (0, 0), (0, 1)]
GROUPS = [(3, 0, 4), (2, 4, 6), (1, 6, 10), (0, 10, 12)]
PLANE_LANES = 128 * len(LANE_TILES)


def tile_of(order, pair):
    at = LANE_TILES.index((order, pair))
    return slice(128 * at, 128 * (at + 1))


RADIX = 4096.0


def fitted(function, low, high, degree):
    series = np.polynomial.chebyshev.Chebyshev.interpolate(
        lambda w: function(0.5 * (high - low) * w + 0.5 * (high + low)), degree
    )
    return [float(v) for v in series.convert(kind=np.polynomial.Polynomial).coef]


LOW, HIGH = 0.9, 28.1
ANGLE = math.pi / cutoff_radius
SINE = fitted(lambda u: np.sin(ANGLE * np.sqrt(u)) / np.sqrt(u), LOW, HIGH, 6)
COSINE = fitted(lambda u: np.cos(ANGLE * np.sqrt(u)), LOW, HIGH, 6)
NORM = math.sqrt(2.0 / cutoff_radius)


def mm(left, right, kind=NN, precision=lax.Precision.HIGHEST):
    return lax.dot_general(
        left, right, (kind, ((), ())), precision=precision, preferred_element_type=F32
    )


def once(left, right, kind=NN):
    return lax.dot_general(left, right, (kind, ((), ())), preferred_element_type=F32)


def parts(value):
    high = value.astype(BF16).astype(F32)
    rest = value - high
    middle = rest.astype(BF16).astype(F32)
    return high, middle, rest - middle


def stack_left(value):
    high, middle, tail = parts(value)
    stack = jnp.concatenate([high, high, middle, high, tail, middle], axis=0)
    return jnp.transpose(stack).astype(BF16)


def stack_right(value):
    high, middle, tail = parts(value)
    return jnp.concatenate([high, middle, high, tail, high, middle], axis=0).astype(BF16)


def stacked(left, right):
    return once(left, stack_right(right))


def three_rows(value):
    return jnp.concatenate(parts(value), axis=0).astype(BF16)


def exact(left, right, kind=NN):
    rows = left.shape[0]
    out = once(three_rows(left), right, kind)
    return out[0:rows] + (out[rows : 2 * rows] + out[2 * rows :])


def loop(count, action, carry):
    if count <= 8:
        for i in range(count):
            carry = action(i, carry)
        return carry
    return lax.fori_loop(0, count, action, carry)


def aligned(value, size):
    return value if isinstance(value, int) else pl.multiple_of(value, size)


def iota(shape, dim):
    return lax.broadcasted_iota(I32, shape, dim)


def horner(coefficients, w):
    total = jnp.full_like(w, coefficients[-1])
    for value in coefficients[-2::-1]:
        total = total * w + value
    return total


def shifted(terms, order, x, y, z):
    current = terms
    for axis, value in enumerate((x, y, z)):
        two, three = 2.0 * value, 3.0 * value
        square = value * value
        three_square, cube = 3.0 * square, square * value
        factors = [None, [value], [square, two], [cube, three_square, three]]
        fresh = {}
        for m in MONOMIALS[: COUNTS[order]]:
            if axis == 2 and sum(m) != order:
                continue
            power = m[axis]
            total = current[m]
            for lower in range(power):
                source = m[:axis] + (lower,) + m[axis + 1 :]
                total = total + factors[power][lower] * current[source]
            fresh[m] = total
        current = fresh
    return current


def all_shifted(terms, x, y, z):
    out = []
    for order in range(4):
        own = {m: terms[OFFSETS[order] + i] for i, m in enumerate(MONOMIALS[: COUNTS[order]])}
        moved = shifted(own, order, x, y, z) if order else own
        out += [moved[m] for m in MONOMIALS if sum(m) == order]
    return out


def contracted(components):
    by_order = [{}, {}, {}, {}]
    for m, value in zip(MONOMIALS, components):
        by_order[sum(m)][m] = value
    scalar = by_order[0][(0, 0, 0)]
    vx, vy, vz = by_order[1][(1, 0, 0)], by_order[1][(0, 1, 0)], by_order[1][(0, 0, 1)]
    m = by_order[2]
    xx, xy, xz = m[(2, 0, 0)], m[(1, 1, 0)], m[(1, 0, 1)]
    yy, yz, zz = m[(0, 2, 0)], m[(0, 1, 1)], m[(0, 0, 2)]
    q = by_order[3]
    xxx, yyy, zzz = q[(3, 0, 0)], q[(0, 3, 0)], q[(0, 0, 3)]
    xxy, xxz, xyy = q[(2, 1, 0)], q[(2, 0, 1)], q[(1, 2, 0)]
    xyz, xzz, yyz, yzz = q[(1, 1, 1)], q[(1, 0, 2)], q[(0, 2, 1)], q[(0, 1, 2)]
    first = vx * vx + vy * vy + vz * vz
    second = xx * xx + yy * yy + zz * zz + 2.0 * (xy * xy + xz * xz + yz * yz)
    third = (
        xxx * xxx
        + yyy * yyy
        + zzz * zzz
        + 3.0 * (xxy * xxy + xxz * xxz + xyy * xyy + xzz * xzz + yyz * yyz + yzz * yzz)
        + 6.0 * (xyz * xyz)
    )
    fourth = (
        vx * (xx * vx + xy * vy + xz * vz)
        + vy * (xy * vx + yy * vy + yz * vz)
        + vz * (xz * vx + yz * vy + zz * vz)
    )
    xy2, xz2, yz2 = 2.0 * xy, 2.0 * xz, 2.0 * yz
    fifth = (
        vx * (xxx * xx + xyy * yy + xzz * zz + xxy * xy2 + xxz * xz2 + xyz * yz2)
        + vy * (xxy * xx + yyy * yy + yzz * zz + xyy * xy2 + xyz * xz2 + yyz * yz2)
        + vz * (xxz * xx + yyz * yy + zzz * zz + xyz * xy2 + xzz * xz2 + yzz * yz2)
    )
    return (scalar, first, second, third, fourth, fifth)


def invariants(terms, x, y, z):
    return contracted(all_shifted(terms, x, y, z))


def row_sums(values, row8):
    def fold(a, b, size):
        if b is None:
            return a + pltpu.roll(a, 8 - size, 0)
        first = (row8 & size) == 0
        if size == 4:
            return jnp.where(first, a, b) + pltpu.roll(jnp.where(first, b, a), 4, 0)
        return jnp.where(first, a + pltpu.roll(a, 8 - size, 0), b + pltpu.roll(b, size, 0))

    values = list(values) + [None] * (8 - len(values))
    for size in (4, 2, 1):
        values = [fold(values[i], values[i + size], size) for i in range(size)]
    return values[0]


def silu_pair(v):
    gate = 1.0 / (1.0 + jnp.exp(-v))
    return v * gate, gate * (1.0 + v * (1.0 - gate))


class Geometry:
    def __init__(self, columns, own, lane_low):
        dx = own[2:3] + columns[:, 2:3]
        dy = own[3:4] + columns[:, 3:4]
        dz = own[4:5] + columns[:, 4:5]
        self.u = dx * dx + dy * dy + dz * dz + 1.0
        w = (self.u - 0.5 * (LOW + HIGH)) * (2.0 / (HIGH - LOW))
        self.sine = horner(SINE, w)
        self.cosine = horner(COSINE, w)
        self.inverse = lax.rsqrt(self.u)
        self.reach = 1.0 - self.u * (1.0 / (cutoff_radius * cutoff_radius))
        self.lane_low = lane_low

    def sines(self):
        step = 2.0 * (2.0 * self.cosine * self.cosine - 1.0)
        before = jnp.where(self.lane_low, -self.sine, 0.0)
        now = jnp.where(self.lane_low, self.sine, 2.0 * self.cosine * self.sine)
        return self.series(step, before, now)

    def cosines(self):
        double = 2.0 * self.cosine * self.cosine - 1.0
        before = jnp.where(self.lane_low, self.cosine, 1.0)
        now = jnp.where(self.lane_low, self.cosine, double)
        return self.series(2.0 * double, before, now)

    def series(self, step, before, now):
        out = [now]
        for _ in range(PAIRS - 1):
            before, now = now, step * now - before
            out.append(now)
        return out


def body(lanes, structs, *refs):
    sources, held, refs = refs[:17], refs[-17:], refs[17:-17]
    (
        positions,
        species,
        struct_id,
        atom_mask,
        senders,
        receivers,
        edge_mask,
        energy_cot,
        embedding,
        channel_in,
        channel_mix,
        hidden_weight,
        hidden_bias,
        inner_weight,
        inner_bias,
        energy_weight,
        message_weight,
    ) = held
    (
        energies_out,
        position_out,
        embedding_out,
        channel_in_out,
        channel_mix_out,
        hidden_weight_out,
        hidden_bias_out,
        inner_weight_out,
        inner_bias_out,
        energy_weight_out,
        message_weight_out,
        pack,
        pack_all,
        send_all,
        masked_recv,
        recv_all,
        counts,
        pair_weight,
        columns,
        sender_rows,
        radial,
        inverse,
        planes_high,
        planes_low,
        turned_high,
        turned_low,
        slopes,
        pulls,
        weights,
        products,
        product_three,
        product_two,
        sums,
        dsums,
        kind_products,
        kind_three,
        kind_stack,
        kind_sums,
        kind_shells,
        kind_moved,
        dkind_sums,
        dkind_products,
        dproducts,
        invariant,
        dinvariant,
        feats,
        normed,
        select,
        head,
        head_rows,
        message_rows_all,
        head_stack,
        message_stack,
        inner_forward,
        inner_back,
        mix_stack,
        mix_back,
        stat_own,
        stat_all,
        message_own,
        message_all,
        dmessage_own,
        dmessage_all,
        force_own,
        force_all,
        final_own,
        final_all,
        tiles_a,
        tiles_a_all,
        tiles_a_sum,
        tiles_b,
        tiles_b_all,
        tiles_b_sum,
        tiles_c,
        tiles_c_all,
        tiles_c_sum,
        send_sem,
        recv_sem,
        input_sem,
    ) = refs
    devices = lanes * structs
    edge_count = senders.shape[1]
    inputs = [
        pltpu.make_async_copy(source, target, input_sem.at[i])
        for i, (source, target) in enumerate(zip(sources, held))
    ]
    group = pair_weight.shape[0]
    tiles = group // 128
    strips = [slice(k, k + 512) for k in range(0, group, 512)]
    row = lax.axis_index("struct")
    col = lax.axis_index("edge")
    me = row * lanes + col

    def everyone(action):
        def one(k, carry):
            target = lax.rem(me + k, devices)
            action((target // lanes, lax.rem(target, lanes)), target)
            return carry

        if (structs, lanes) == (4, 8):
            for k in range(devices - 1, 0, -1):
                at, there = row ^ (k % structs), col ^ ((k // structs) ^ (2 if k >= 16 else 0))
                action((at, there), at * lanes + there)
        else:
            lax.fori_loop(1, devices, one, 0)

    def members(action):
        def one(k, carry):
            target = lax.rem(col + k, lanes)
            action((row, target), target)
            return carry

        if lanes <= 8:
            for k in range(lanes - 1, 0, -1):
                action((row, col ^ k), col ^ k)
        else:
            lax.fori_loop(1, lanes, one, 0)

    def push(phase, source, target, device):
        pltpu.make_async_remote_copy(
            src_ref=source,
            dst_ref=target,
            send_sem=send_sem.at[phase],
            recv_sem=recv_sem.at[phase],
            device_id=device,
            device_id_type=MESH,
        ).start()

    def await_bytes(buffer, count, sem):
        if count:
            view = buffer.at[pl.ds(0, count)]
            pltpu.make_async_copy(view, view, sem).wait()

    for one_input in inputs[:7]:
        one_input.start()
    barrier = pltpu.get_barrier_semaphore()
    def enter(device, _):
        pl.semaphore_signal(barrier, inc=1, device_id=device, device_id_type=MESH)

    everyone(enter)
    for one_input in inputs[7:]:
        one_input.start()
    for one_input in inputs[:7]:
        one_input.wait()
    pack[...] = jnp.ones_like(pack)
    masked_recv[...] = jnp.where(edge_mask[...] > 0, receivers[...], -1)
    kind = species[...]
    for half in (0, BLOCK):
        spot = pl.ds(half, BLOCK)
        pack[0:1, spot] = (kind == 0).astype(F32)
        pack[1:2, spot] = (kind == 1).astype(F32)
        for axis in range(3):
            pack[2 + axis : 3 + axis, spot] = center - positions[axis]
        pack[6:7, spot] = atom_mask[...].astype(F32)
        pack[7:8, spot] = struct_id[...].astype(F32)
    pl.semaphore_wait(barrier, devices - 1)

    members(lambda device, _: push(0, pack, pack_all.at[col], device))
    members(lambda device, _: push(1, senders, send_all.at[col], device))
    members(lambda device, _: push(2, masked_recv, recv_all.at[col], device))
    pack_all[col] = pack[...]
    send_all[col] = senders[...]
    recv_all[col] = masked_recv[...]

    for one_input in inputs[7:]:
        one_input.wait()
    lane = iota((8, 128), 1)
    low_row = lane[0:1] < BLOCK
    low = lane < BLOCK
    row8 = iota((8, 128), 0)
    own = pack[...] * jnp.where((row8 >= 2) & (row8 <= 4), -1.0, 1.0)
    live = own[6:7]
    first_rows = iota((16, 128), 0)
    lane_half = (iota((16, 128), 1) >= BLOCK).astype(I32)
    half_sum = (first_rows == lane_half).astype(F32)
    wide_lane = iota((8, 512), 1)
    spot_of = 2 * (wide_lane >> 7) + ((wide_lane & 127) >= BLOCK).astype(I32)
    half_pick = (iota((8, 512), 0) == spot_of).astype(F32)
    half_pick = jnp.concatenate([half_pick] * 3 + [jnp.zeros((8, 512), F32)], axis=0).astype(BF16)

    mix_pd = (iota((72, CHANNELS), 0) - 12 * ((iota((72, CHANNELS), 0) * 5462) >> 16)) == iota(
        (72, CHANNELS), 1
    )
    mix_pd = mix_pd.astype(F32)
    mix_pc = ((iota((96, CHANNELS), 0) & 15) == iota((96, CHANNELS), 1)).astype(F32)
    same = ((iota((96, 72), 0) >> 4) == ((iota((96, 72), 1) * 5462) >> 16)).astype(F32)
    same_t = ((iota((72, 96), 1) >> 4) == ((iota((72, 96), 0) * 5462) >> 16)).astype(F32)
    for layer in range(2):
        table = channel_mix[:, layer, :]
        spread_c = mm(mix_pc, table)
        mix_back[layer] = stack_left(mm(mm(mix_pd, table, NT), mix_pc, NT) * same_t)
        mix_stack[layer] = stack_left(mm(spread_c, mix_pd, NT) * same)

    struct_rows = own[7:8].astype(I32)
    member = (struct_rows == iota((STRUCTS, 128), 0)).astype(F32)
    atom_cot = mm(energy_cot[...], member) * live
    counts[...] = jnp.zeros_like(counts)
    chunk = min(2048, edge_count)
    per_slot = edge_count // chunk
    wide = counts.shape[2]

    hot_rows = iota((128, chunk), 0).astype(F32).astype(BF16)
    none = jnp.zeros((), BF16)

    def count_edges(send, recv):
        local = recv - col * BLOCK
        inside = (local >= 0) & (local < BLOCK)
        key = jnp.where(inside, (send >> 8) * BLOCK + local, -1)
        step = jnp.where((send & 128) > 0, RADIX, 1.0).astype(BF16)
        sender_hot = jnp.where(hot_rows == (send & 127).astype(F32).astype(BF16), step, none)
        pair_hot = []
        for first in range(0, wide, 128):
            local_key = jnp.where((key >= first) & (key < first + 128), key - first, -1)
            hit = hot_rows == local_key.astype(F32).astype(BF16)
            pair_hot.append(jnp.where(hit, jnp.ones((), BF16), none))
        pair_hot = jnp.concatenate(pair_hot, axis=0)
        found = once(sender_hot, pair_hot, NT)
        upper = jnp.floor(found * (1.0 / RADIX))
        counts[0] += found - RADIX * upper
        counts[1] += upper

    def count_slot(slot, carry):
        for k in range(per_slot):
            spot = slice(k * chunk, (k + 1) * chunk)
            count_edges(send_all[slot, :, spot], recv_all[slot, :, spot])
        return carry

    count_slot(col, 0)

    for blank_ref in (dkind_sums, dsums, products, invariant.at[1]):
        blank_ref[...] = jnp.zeros(blank_ref.shape, F32)
    await_bytes(pack_all, lanes - 1, recv_sem.at[0])
    for q in range(tiles):
        sender_rows[:, 128 * q : 128 * (q + 1)] = jnp.where(low, pack_all[2 * q], pack_all[2 * q + 1])
    columns[...] = jnp.transpose(sender_rows[...])

    def geometry(start):
        cols = columns[pl.ds(start, BLOCK), :]
        return Geometry(cols, own, low_row)

    def radial_block(i, carry):
        start = aligned(i * BLOCK, BLOCK)
        geo = geometry(start)
        envelope = geo.reach * geo.reach * NORM
        for pair, value in enumerate(geo.sines()):
            radial[pair, pl.ds(start, BLOCK), :] = value * envelope
        inverse[pl.ds(start, BLOCK), :] = geo.inverse
        return carry

    loop(group // BLOCK, radial_block, 0)

    def monomial_rows(rows):
        x, y, z = rows[2:3], rows[3:4], rows[4:5]
        table = {(0, 0, 0): None}
        for m in MONOMIALS[1:]:
            axis = next(i for i in range(3) if m[i])
            lower = m[:axis] + (m[axis] - 1,) + m[axis + 1 :]
            factor = (x, y, z)[axis]
            table[m] = factor if table[lower] is None else table[lower] * factor
        return table

    def spread():
        def one(q, carry):
            spot = pl.ds(aligned(q * 128, 128), 128)
            table = monomial_rows(sender_rows[:, spot])
            h = weights[0:CHANNELS, spot]
            for i, m in enumerate(MONOMIALS):
                value = h if table[m] is None else h * table[m]
                products[row_of(i, 0) : row_of(i, 0) + 8, spot] = value[0:8]
                products[row_of(i, 1) : row_of(i, 1) + 4, spot] = value[8:12]
            return carry

        loop(tiles, one, 0)
        for q in strips:
            split = parts(products[:, q])
            three, two = [], []
            for start, end in zip(DEGREE_ROWS, DEGREE_ROWS[1:]):
                three += [v[start:end] for v in split]
                two += [v[start:end] for v in split[:2]]
            three.append(jnp.zeros((8, three[0].shape[1]), F32))
            product_three[:, q] = jnp.concatenate(three, axis=0).astype(BF16)
            product_two[:, q] = jnp.concatenate(two, axis=0).astype(BF16)


    def kind_spread(q, carry):
        spot = pl.ds(aligned(q * 128, 128), 128)
        table = monomial_rows(sender_rows[:, spot])
        kinds = sender_rows[0:2, spot]
        for i, m in enumerate(MONOMIALS):
            kind_products[2 * i : 2 * i + 2, spot] = kinds if table[m] is None else kinds * table[m]
        return carry

    loop(tiles, kind_spread, 0)
    for q in strips:
        kind_parts = jnp.concatenate(parts(kind_products[:, q]), axis=0)
        blank_rows = jnp.zeros((8, kind_parts.shape[1]), F32)
        kind_three[:, q] = jnp.concatenate([kind_parts, blank_rows], axis=0).astype(BF16)
    columns_of = []
    for kind_of in range(2):
        embedded = mm(embedding[...], (iota((2, 128), 0) == kind_of).astype(F32), TN)
        padded = jnp.concatenate(
            [mm(channel_in[0], embedded, TN), jnp.zeros((PADDED - CHANNELS, 128), F32)], axis=0
        )
        columns_of.append([padded[0:8], padded[8:16]])

    await_bytes(send_all, lanes - 1, recv_sem.at[1])
    await_bytes(recv_all, lanes - 1, recv_sem.at[2])
    if devices <= 32:
        for k in range(1, lanes):
            count_slot(lax.rem(col + k, lanes), 0)
    else:
        lax.fori_loop(1, lanes, lambda k, carry: count_slot(lax.rem(col + k, lanes), carry), 0)
    low_tall = iota((128, 128), 1) < BLOCK
    for block in range(group // 128):
        turn_of = block // 2
        piece = counts[block % 2, :, 128 * (turn_of // 2) : 128 * (turn_of // 2 + 1)]
        turned = pltpu.roll(piece, BLOCK, 1)
        first_half, second_half = (piece, turned) if turn_of % 2 == 0 else (turned, piece)
        pair_weight[128 * block : 128 * (block + 1), :] = jnp.where(
            low_tall, first_half, second_half
        )

    def plane_block(i, carry):
        spot = pl.ds(aligned(i * BLOCK, BLOCK), BLOCK)
        weight = pair_weight[spot, :]
        step = inverse[spot, :]
        for pair in range(PAIRS):
            value = radial[pair, spot, :] * weight
            for order in range(4):
                high = value.astype(BF16)
                planes_high[spot, tile_of(order, pair)] = high
                planes_low[spot, tile_of(order, pair)] = (value - high.astype(F32)).astype(BF16)
                value = value * step
        return carry

    loop(group // BLOCK, plane_block, 0)

    xi, yi, zi = (jnp.broadcast_to(own[r : r + 1], (8, 128)) for r in (2, 3, 4))

    def chunk_spots(i):
        pair, tile = i // 2, i % 2
        return pair, tile, slice(128 * pair, 128 * (pair + 1))

    def kind_component(place, pair):
        return [
            jnp.broadcast_to(kind_moved[place, 2 * pair + k : 2 * pair + k + 1, :], (8, 128))
            for k in range(2)
        ]

    def kind_expand(both, tile):
        return [columns_of[0][tile] * a + columns_of[1][tile] * b for a, b in both]

    units = [(0, pair, None) for pair in range(PAIRS)]
    units += [(1, pair, pair + 1 if pair + 1 < PAIRS else None) for pair in range(0, PAIRS, 2)]

    def joined_rows(ref, start, spot, other):
        value = ref[start : start + 8, spot]
        return value if other is None else jnp.where(row8 < 4, value, ref[start - 4 : start + 4, other])

    def shell_terms(tile, pair, second):
        out = []
        for order in range(4):
            spot = tile_of(order, pair)
            other = None if second is None else tile_of(order, second)
            for m in range(COUNTS[order]):
                out.append(joined_rows(sums, row_of(m, tile), spot, other))
        return out

    def store_rows(ref, start, tile, spot, other, value):
        if tile == 0:
            ref[start : start + 8, spot] = value
        else:
            ref[start : start + 4, spot] = value[0:4]
            if other is not None:
                ref[start : start + 4, other] = value[4:8]

    def pair_lanes(pair):
        return None if pair is None else slice(128 * pair, 128 * (pair + 1))

    def live_rows(value, tile):
        return value if tile == 0 else jnp.where(row8 < CHANNELS - 8, value, 0.0)

    def mix_invariants(layer):
        mixed = stacked(mix_stack[layer], invariant[layer])
        for pair in range(PAIRS):
            feats[layer, 72 * pair : 72 * (pair + 1), :] = mixed[:, 128 * pair : 128 * (pair + 1)]

    def forward_kinds():
        by_high = once(kind_three[...], planes_high[...])
        by_low = once(kind_three[0:80, :], planes_low[...])
        kind_sums[...] = by_high[0:40] + ((by_high[40:80] + by_low[0:40]) + (by_high[80:120] + by_low[40:80]))
        for order in range(4):
            for m in range(COUNTS[order]):
                pieces = [kind_sums[2 * m : 2 * m + 2, tile_of(order, pair)] for pair in range(PAIRS)]
                kind_shells[OFFSETS[order] + m] = jnp.concatenate(
                    pieces + [jnp.zeros((2, 128), F32)], axis=0
                )
        moved = all_shifted([kind_shells[m] for m in range(SHELLS)], xi, yi, zi)
        for place, value in enumerate(moved):
            kind_moved[place] = value
        for pair in range(PAIRS):
            both = [kind_component(place, pair) for place in range(20)]
            for tile in range(2):
                for p, value in enumerate(contracted(kind_expand(both, tile))):
                    start = PADDED * p + 8 * tile
                    invariant[0, start : start + 8, 128 * pair : 128 * (pair + 1)] = value
        mix_invariants(0)

    def forward():
        for order, first, last in GROUPS:
            spot = slice(128 * first, 128 * last)
            end = DEGREE_ROWS[order + 1]
            by_high = once(product_three[0 : -(-3 * end // 16) * 16, :], planes_high[:, spot])
            by_low = once(product_two[0 : 2 * end, :], planes_low[:, spot])
            for start, stop in zip(DEGREE_ROWS[: order + 1], DEGREE_ROWS[1:]):
                size = stop - start
                h, l = 3 * start, 2 * start
                sums[start:stop, spot] = by_high[h : h + size] + (
                    (by_high[h + size : h + 2 * size] + by_low[l : l + size])
                    + (by_high[h + 2 * size : h + 3 * size] + by_low[l + size : l + 2 * size])
                )
        for tile, pair, second in units:
            for p, value in enumerate(invariants(shell_terms(tile, pair, second), xi, yi, zi)):
                store_rows(
                    invariant.at[1], PADDED * p + 8 * tile, tile, pair_lanes(pair), pair_lanes(second), value
                )
        mix_invariants(1)

    def send_stats(phase, index, select_rows, first, second, extra=None):
        values = jnp.concatenate([first, second], axis=0)
        wide_values = jnp.concatenate(parts(values), axis=1).astype(BF16)
        rows = jnp.concatenate([select_rows] * 3, axis=1).astype(BF16)
        both = once(rows, wide_values, NT)
        for k in range(4):
            stat_own[index, 2 * k : 2 * k + 2, :] = both[0:2, 128 * k : 128 * (k + 1)]
        if extra is not None:
            stat_own[index, 2:3, 96 : 96 + STRUCTS] = extra
        everyone(
            lambda device, _: push(phase, stat_own.at[index], stat_all.at[index, me], device)
        )
        stat_all[index, me] = stat_own[index]

    def get_stats(phase, index):
        await_bytes(stat_all.at[index], devices - 1, recv_sem.at[phase])
        sums_of = [stat_all[index, k] for k in range(8)]
        for k in range(8, devices):
            sums_of[k % 8] = sums_of[k % 8] + stat_all[index, k]
        while len(sums_of) > 1:
            sums_of = [a + b for a, b in zip(sums_of[::2], sums_of[1::2])]
        return sums_of[0]

    def widen(rows):
        return once(
            jnp.concatenate([three_rows(rows), jnp.zeros((8, 128), BF16)], axis=0), half_pick, TN
        )

    rest_rows = ONES_ROW - 128

    def tall(wide, start):
        return jnp.concatenate(
            [wide[:, start : start + 128], wide[0:rest_rows, start + 128 : start + 256]], axis=0
        )

    ones_rows = iota((FEATURE_ROWS - ONES_ROW, 128), 0) == 0
    for layer in range(2):
        feats[layer, ONES_ROW:FEATURE_ROWS, :] = ones_rows.astype(F32)
        normed[layer, ONES_ROW:FEATURE_ROWS, :] = ones_rows.astype(F32)

    def send_moments(layer, phase):
        values = feats[layer]
        send_stats(phase, layer, half_sum * live, values, values * values)

    def normalise(layer, phase):
        total = get_stats(phase, layer)
        inverse_count = 1.0 / jnp.maximum(total[2:3, ONES_ROW - 128 : ONES_ROW - 127], 1.0)
        scaled = total * inverse_count
        means = pltpu.roll(scaled, 4, 0)
        scales = lax.rsqrt(scaled - means * means + variance_eps)
        wide = widen(jnp.where(row8 < 4, scaled, scales))
        scale = tall(wide, 256)
        normed[layer, 0:ONES_ROW, :] = (feats[layer, 0:ONES_ROW, :] - tall(wide, 0)) * scale
        split = [v.astype(BF16) for v in parts(normed[layer])]
        return split, scale, inverse_count

    def head_product(left, split):
        rows = left.shape[0] // 3
        by_high = once(left[...], split[0])
        by_middle = once(left[0 : 2 * rows, :], split[1])
        by_tail = once(left[0:rows, :], split[2])
        joined = by_high[0:rows] + (
            (by_high[rows : 2 * rows] + by_middle[0:rows])
            + (by_high[2 * rows :] + by_middle[rows:] + by_tail)
        )
        chosen = jnp.where(low_row, joined[0 : rows // 2], joined[rows // 2 :])
        return chosen + pltpu.roll(chosen, BLOCK, 1)

    def run_head(layer, pre):
        hidden, hidden_slope = silu_pair(pre[0:HIDDEN])
        inner, inner_slope = silu_pair(stacked(inner_forward[layer], hidden) + inner_cols[layer])
        dinner = energy_cols[layer] * atom_cot * inner_slope
        dhidden = stacked(inner_back[layer], dinner) * hidden_slope
        return hidden, inner, dinner, dhidden

    def small_grad(layer, hidden, inner, dinner):
        left = jnp.concatenate([dinner, atom_cot * inner], axis=0)
        blank = jnp.zeros((128 - 32 - 32 * layer, 128), F32)
        right = [hidden, (iota((8, 128), 0) == 0).astype(F32), blank]
        if layer == 1:
            right = [jnp.zeros((32, 128), F32)] + right
        return mm(jnp.where(low_row, left, 0.0), jnp.concatenate(right, axis=0), NT)

    def halves(value):
        return jnp.where(low_row, value, 0.0), jnp.where(low_row, 0.0, value)

    def scatter_tiles(phase, source, target, base):
        for k in range(source.shape[0]):
            t = lax.rem(me + k, source.shape[0])

            @pl.when(me != base + t)
            def _():
                there = base + t
                push(phase, source.at[t], target.at[me], (there // lanes, lax.rem(there, lanes)))

            @pl.when(me == base + t)
            def _():
                target[me] = source[t]

    def mine(base, result):
        return (me >= base) & (me < base + result.shape[0])

    def share_tiles(phase, parts_of, result, base):
        @pl.when(mine(base, result))
        def _():
            await_bytes(parts_of, devices - 1, recv_sem.at[phase])
            total = parts_of[0]
            for k in range(1, devices):
                total = total + parts_of[k]
            result[me - base] = total
            everyone(
                lambda device, _: push(phase + 1, result.at[me - base], result.at[me - base], device)
            )

    def gather_tiles(phase, result, base):
        count_of = result.shape[0]

        @pl.when(mine(base, result))
        def _():
            await_bytes(result, count_of - 1, recv_sem.at[phase + 1])

        @pl.when(jnp.logical_not(mine(base, result)))
        def _():
            await_bytes(result, count_of, recv_sem.at[phase + 1])

    def drain_tiles(phase, parts_of, result, base):
        count_of = result.shape[0]

        @pl.when(mine(base, result))
        def _():
            await_bytes(result, count_of - 1, send_sem.at[phase])
            await_bytes(parts_of, devices - 1, send_sem.at[phase + 1])

        @pl.when(jnp.logical_not(mine(base, result)))
        def _():
            await_bytes(result, count_of, send_sem.at[phase])

    base_a, base_b, base_c = 0, tiles_a.shape[0], devices - tiles_c.shape[0]

    forward_kinds()
    send_moments(0, 3)
    for parity in range(2):
        k = iota((FEATURE_ROWS, FEATURES), 0)
        pair = (k >= 72).astype(I32) + (k >= 144).astype(I32)
        rest = k - 72 * pair
        kind_of = (rest * 5462) >> 16
        channel = rest - 12 * kind_of
        place = channel * 36 + (2 * pair + parity) * 6 + kind_of
        hit = (place == iota((FEATURE_ROWS, FEATURES), 1)) & (k < ONES_ROW)
        select[parity] = hit.astype(F32).astype(BF16)
    inner_cols, energy_cols = [], []
    head[...] = jnp.zeros_like(head)
    for layer in range(2):
        for parity in range(2):
            base = HEAD_ROWS * parity
            block = exact(hidden_weight[layer], select[parity], NT)
            if parity == 0:
                spot = (iota((2, FEATURE_ROWS), 1) == ONES_ROW) & (
                    iota((2, FEATURE_ROWS), 0) == layer
                )
                block = block + mm(hidden_bias[...], spot.astype(F32), TN)
            head[layer, base : base + HIDDEN, :] = block
            if layer == 0:
                message_rows = jnp.concatenate(
                    [message_weight[...], jnp.zeros((PADDED - CHANNELS, FEATURES), F32)], axis=0
                )
                head[0, base + HIDDEN : base + HEAD_ROWS, :] = exact(message_rows, select[parity], NT)
        whole = head[layer]
        head_rows[layer] = three_rows(
            jnp.concatenate([whole[0:HIDDEN], whole[HEAD_ROWS : HEAD_ROWS + HIDDEN]], axis=0)
        )
        head_stack[layer] = stack_left(whole)
        if layer == 0:
            through_rows = jnp.concatenate([whole[HIDDEN:HEAD_ROWS], whole[HEAD_ROWS + HIDDEN :]], axis=0)
            message_rows_all[...] = three_rows(through_rows)
            message_stack[...] = stack_left(through_rows)
        inner_back[layer] = stack_left(inner_weight[layer])
        inner_forward[layer] = stack_left(jnp.transpose(inner_weight[layer]))
        pick = (iota((2, 128), 0) == layer).astype(F32)
        inner_cols.append(mm(inner_bias[...], pick, TN))
        energy_cols.append(mm(energy_weight[...], pick, TN))

    if group <= 512:
        turned_high[...] = jnp.transpose(planes_high[...])
        turned_low[...] = jnp.transpose(planes_low[...])

    def against(left, lane_spot, spot, low_part):
        if group <= 512:
            return once(left, (turned_low if low_part else turned_high)[lane_spot, spot])
        return once(left, (planes_low if low_part else planes_high)[spot, lane_spot], NT)

    split_zero, scale_zero, inverse_count = normalise(0, 3)
    message = head_product(message_rows_all, split_zero)
    message_own[...] = jnp.where(low, message[0:8], message[8:16])
    members(lambda device, _: push(4, message_own, message_all.at[col], device))
    message_all[col] = message_own[...]
    hidden_zero, inner_zero, dinner_zero, dhidden_zero = run_head(0, head_product(head_rows.at[0], split_zero))
    d_low, d_high = halves(dhidden_zero)
    gap = jnp.zeros((HEAD_ROWS - HIDDEN, 128), F32)
    dnormed_head = stacked(head_stack[0], jnp.concatenate([d_low, gap, d_high, gap], axis=0))

    def pack_head(target, layer, d_low, d_high):
        block = mm(jnp.concatenate([d_low, d_high], axis=0), normed[layer], NT)
        for r in range(6):
            for half in range(2):
                target[2 * r + half] = block[8 * r : 8 * (r + 1), 128 * half : 128 * (half + 1)]

    pack_head(tiles_a, 0, d_low, d_high)
    scatter_tiles(11, tiles_a, tiles_a_all, 0)
    weights[...] = jnp.zeros_like(weights)
    embedded = mm(embedding[...], sender_rows[0:2, :], TN)
    weights[0:CHANNELS, :] = mm(channel_in[1], embedded, TN)
    await_bytes(message_all, lanes - 1, recv_sem.at[4])
    for q in range(tiles):
        even, odd = message_all[2 * q], message_all[2 * q + 1]
        spot = slice(128 * q, 128 * (q + 1))
        weights[0:8, spot] += jnp.where(low, even, pltpu.roll(odd, BLOCK, 1))
        weights[8:16, spot] += jnp.where(low, pltpu.roll(even, BLOCK, 1), odd)

    spread()
    forward()
    send_moments(1, 5)
    turn = ANGLE * (1.0 + (iota((1, 128), 1) >= BLOCK).astype(F32))

    def slope_block(i, carry):
        start = aligned(i * BLOCK, BLOCK)
        spot = pl.ds(start, BLOCK)
        geo = geometry(start)
        step = geo.inverse
        square = step * step
        envelope = geo.reach * geo.reach * NORM
        slope = geo.reach * (-2.0 * NORM / (cutoff_radius * cutoff_radius))
        weight = pair_weight[spot, :]
        for pair, (sine, cosine) in enumerate(zip(geo.sines(), geo.cosines())):
            rate = (turn + 2.0 * ANGLE * pair) * cosine - sine
            value = weight * ((0.5 * square) * rate * envelope + sine * slope)
            plane = weight * (sine * envelope)
            slopes[spot, tile_of(0, pair)] = value
            for order in range(1, 4):
                plane = plane * step
                value = value * step - (0.5 * square) * plane
                slopes[spot, tile_of(order, pair)] = value
        return carry

    loop(group // BLOCK, slope_block, 0)
    for q in strips:
        kind_stack[q, :] = stack_left(kind_products[:, q])

    share_tiles(11, tiles_a_all, tiles_a_sum, base_a)
    split_one, scale_one, _ = normalise(1, 5)
    hidden_one, inner_one, dinner_one, dhidden_one = run_head(1, head_product(head_rows.at[1], split_one))
    d_low, d_high = halves(dhidden_one)
    dnormed_one = stacked(head_stack[1], jnp.concatenate([d_low, gap, d_high, gap], axis=0))
    send_stats(6, 2, half_sum, dnormed_one, dnormed_one * normed[1])

    pack_head(tiles_b, 1, d_low, d_high)
    small = small_grad(0, hidden_zero, inner_zero, dinner_zero)
    small = small + small_grad(1, hidden_one, inner_one, dinner_one)
    for r in range(2):
        tiles_b[12 + r] = small[8 * r : 8 * (r + 1)] + pltpu.roll(small[16 + 8 * r : 24 + 8 * r], 64, 1)
    atom_energy = jnp.sum(energy_cols[0] * inner_zero + energy_cols[1] * inner_one, axis=0, keepdims=True)
    atom_energy = jnp.where(low_row, live * atom_energy, 0.0)
    energy_rows = mm(jnp.broadcast_to(atom_energy, (8, 128)), member, NT)[0:1]
    def feature_back(layer, total, dnormed, scale):
        wide = widen(total * inverse_count)
        dfeats = scale * (
            dnormed[0:ONES_ROW] - live * (tall(wide, 0) + tall(wide, 256) * normed[layer, 0:ONES_ROW, :])
        )
        dmixed = jnp.concatenate([dfeats[72 * pair : 72 * (pair + 1)] for pair in range(PAIRS)], axis=1)
        dinvariant[...] = stacked(mix_back[layer], dmixed)
        return dmixed

    def mix_grad(layer, dmixed):
        return mm(invariant[layer], dmixed, NT, lax.Precision.HIGH) * same

    blank = jnp.zeros((8, 128), F32)

    def shell_back(some_units, moved):
        for tile, pair, second in some_units:
            cots = tuple(
                joined_rows(dinvariant, PADDED * p + 8 * tile, pair_lanes(pair), pair_lanes(second))
                for p in range(6)
            )
            _, pull = jax.vjp(invariants, shell_terms(tile, pair, second), xi, yi, zi)
            dterms, *shift = pull(cots)
            for order in range(4):
                spot = tile_of(order, pair)
                other = None if second is None else tile_of(order, second)
                for m in range(COUNTS[order]):
                    store_rows(dsums, row_of(m, tile), tile, spot, other, dterms[OFFSETS[order] + m])
            if tile == 1 and second is None:
                shift = [jnp.where(row8 < 4, v, 0.0) for v in shift]
            moved = tuple(a + b for a, b in zip(moved, shift))
        return moved

    def shell_back_kinds():
        dtable = [[blank, blank], [blank, blank]]
        folded = [[] for _ in range(20)]
        for pair in range(PAIRS):
            both = [kind_component(place, pair) for place in range(20)]
            sides = []
            for tile in range(2):
                cots = tuple(dinvariant[PADDED * p + 8 * tile : PADDED * p + 8 * tile + 8, 128 * pair : 128 * (pair + 1)] for p in range(6))
                _, pull = jax.vjp(contracted, kind_expand(both, tile))
                sides.append(pull(cots)[0])
                for k in range(2):
                    for place in range(20):
                        dtable[k][tile] = dtable[k][tile] + sides[tile][place] * both[place][k]
            for place in range(20):
                for k in range(2):
                    folded[place].append(
                        columns_of[k][0] * sides[0][place] + columns_of[k][1] * sides[1][place]
                    )
        dmoved = [jnp.where(row8 < 2 * PAIRS, row_sums(v, row8), 0.0) for v in folded]
        _, pull = jax.vjp(all_shifted, [kind_shells[m] for m in range(SHELLS)], xi, yi, zi)
        dterms, *moved = pull(dmoved)
        for order in range(4):
            for m in range(COUNTS[order]):
                value = dterms[OFFSETS[order] + m]
                for pair in range(PAIRS):
                    dkind_sums[2 * m : 2 * m + 2, tile_of(order, pair)] = value[2 * pair : 2 * pair + 2]
        return tuple(moved), [jnp.concatenate(halves_of, axis=0) for halves_of in dtable]

    def product_back(groups, done):
        for order, first, last in groups:
            lane_spot = slice(128 * first, 128 * last)
            end = DEGREE_ROWS[order + 1]
            high, low_part, _ = parts(dsums[0:end, lane_spot])
            left = jnp.concatenate([high, low_part], axis=0).astype(BF16)
            for spot in strips:
                by_high = against(left, lane_spot, spot, False)
                block = by_high[0:end] + (by_high[end:] + against(left[0:end], lane_spot, spot, True))
                shared = min(done, end)
                if shared:
                    dproducts[0:shared, spot] += block[0:shared]
                if end > done:
                    dproducts[done:end, spot] = block[done:end]
            done = max(done, end)

    def product_back_kinds():
        high, low_part, _ = parts(dkind_sums[...])
        left = jnp.concatenate([high, low_part], axis=0).astype(BF16)
        for spot in strips:
            whole = slice(0, PLANE_LANES)
            by_high = against(left, whole, spot, False)
            dkind_products[:, spot] = by_high[0:40] + (by_high[40:] + against(left[0:48], whole, spot, True)[0:40])

    def weight_back():
        out = []
        for q in range(tiles):
            spot = slice(128 * q, 128 * (q + 1))
            table = monomial_rows(sender_rows[:, spot])
            both = []
            for tile in range(2):
                total = None
                for i, m in enumerate(MONOMIALS):
                    term = dproducts[row_of(i, tile) : row_of(i, tile) + 8, spot]
                    term = term if table[m] is None else term * table[m]
                    total = term if total is None else total + term
                both.append(live_rows(total, tile))
            out.append(jnp.concatenate(both, axis=0))
        return out

    def axis_slope(table, axis, value_of):
        total = None
        for i, m in enumerate(MONOMIALS):
            if not m[axis]:
                continue
            lower = table[m[:axis] + (m[axis] - 1,) + m[axis + 1 :]]
            term = value_of(i)
            if lower is not None:
                term = (float(m[axis]) * lower) * term
            total = term if total is None else total + term
        return total

    def coordinate_back():
        out = []
        for q in range(tiles):
            spot = slice(128 * q, 128 * (q + 1))
            table = monomial_rows(sender_rows[:, spot])
            sides = []
            for axis in range(3):
                total = None
                for tile in range(2):
                    slope = axis_slope(
                        table, axis, lambda i: dproducts[row_of(i, tile) : row_of(i, tile) + 8, spot]
                    )
                    term = weights[8 * tile : 8 * tile + 8, spot] * live_rows(slope, tile)
                    total = term if total is None else total + term
                sides.append(jnp.sum(total, axis=0, keepdims=True))
            out.append(sides)
        return out

    def coordinate_back_kinds():
        out = []
        for q in range(tiles):
            spot = slice(128 * q, 128 * (q + 1))
            table = monomial_rows(sender_rows[:, spot])
            kinds = sender_rows[0:2, spot]
            rows = [
                jnp.sum(kinds * dkind_products[2 * i : 2 * i + 2, spot], axis=0, keepdims=True)
                for i in range(len(MONOMIALS))
            ]
            out.append([axis_slope(table, axis, lambda i: rows[i]) for axis in range(3)])
        return out

    def radial_pull(block, first, last, spot):
        total = None
        for at in range(first, last):
            term = block[:, 128 * (at - first) : 128 * (at - first + 1)] * slopes[spot, 128 * at : 128 * (at + 1)]
            total = term if total is None else total + term
        return total

    def plane_back():
        for order, first, last in GROUPS:
            end = DEGREE_ROWS[order + 1]
            for spot in strips:
                block = mm(products[0:end, spot], dsums[0:end, 128 * first : 128 * last], TN)
                term = radial_pull(block, first, last, spot)
                if order == 3:
                    pulls[spot, :] = term
                else:
                    pulls[spot, :] += term

    def plane_back_kinds():
        right = stack_right(dkind_sums[...])
        for order, first, last in GROUPS:
            for spot in strips:
                block = once(kind_stack[spot, :], right[:, 128 * first : 128 * last])
                pulls[spot, :] += radial_pull(block, first, last, spot)

    dmixed_one = feature_back(1, get_stats(6, 2), dnormed_one, scale_one)
    moved_one = shell_back([units[0], units[1], units[3]], (blank, blank, blank))
    product_back([GROUPS[1]], 0)
    moved_one = shell_back([units[2], units[4]], moved_one)
    product_back([GROUPS[0]] + GROUPS[2:], DEGREE_ROWS[3])
    dweights_one = weight_back()
    for q in range(tiles):
        top, bottom = dweights_one[q][0:8], dweights_one[q][8:16]
        dmessage_own[2 * q] = jnp.where(low, top, pltpu.roll(bottom, BLOCK, 1))
        dmessage_own[2 * q + 1] = jnp.where(low, pltpu.roll(top, BLOCK, 1), bottom)
    members(
        lambda device, target: push(7, dmessage_own.at[target], dmessage_all.at[col], device)
    )
    dmessage_all[col] = dmessage_own[col]
    kinds_of = sender_rows[...]
    dtable_one = jnp.zeros((PADDED, 8), F32)
    for q in range(tiles):
        dtable_one = dtable_one + mm(dweights_one[q], kinds_of[:, 128 * q : 128 * (q + 1)], NT)
    slopes_one = coordinate_back()
    mix_one = mix_grad(1, dmixed_one)
    scatter_tiles(13, tiles_b, tiles_b_all, base_b)
    await_bytes(dmessage_all, lanes - 1, recv_sem.at[7])
    arrived = dmessage_all[0]
    for k in range(1, lanes):
        arrived = arrived + dmessage_all[k]
    turned = pltpu.roll(arrived, BLOCK, 1)
    dmessage = jnp.concatenate([jnp.where(low, arrived, turned), jnp.where(low, turned, arrived)], axis=0)

    m_low, m_high = halves(dmessage)
    dmessage_both = jnp.concatenate([m_low, m_high], axis=0)
    dnormed_zero = dnormed_head + stacked(message_stack[...], dmessage_both)
    send_stats(8, 3, half_sum, dnormed_zero, dnormed_zero * normed[0], energy_rows)
    dmessage_weight = mm(dmessage_both, normed[0], NT)
    for r in range(4):
        for half in range(2):
            tiles_c[2 * r + half] = dmessage_weight[
                8 * r : 8 * (r + 1), 128 * half : 128 * (half + 1)
            ]
    scatter_tiles(15, tiles_c, tiles_c_all, base_c)
    fold_c = (iota((PADDED, 96), 0) == (iota((PADDED, 96), 1) & 15)).astype(F32)
    d_of = iota((72, 128), 0) - 12 * ((iota((72, 128), 0) * 5462) >> 16)
    seat_mix = [(iota((72, 128), 1) == d_of + 12 * layer).astype(BF16) for layer in range(2)]
    seat_kind = ((lane == row8 + 26) & (row8 < 2)).astype(F32)

    def fold_mix(layer, value):
        wide_value = once(fold_c.astype(BF16), jnp.concatenate(parts(exact(value, seat_mix[layer])), axis=1).astype(BF16))
        return wide_value[:, 0:128] + (wide_value[:, 128:256] + wide_value[:, 256:384])

    final_one = fold_mix(1, mix_one) + mm(dtable_one, seat_kind)
    plane_back()
    share_tiles(13, tiles_b_all, tiles_b_sum, base_b)
    total_zero = get_stats(8, 3)
    share_tiles(15, tiles_c_all, tiles_c_sum, base_c)
    dmixed_zero = feature_back(0, total_zero, dnormed_zero, scale_zero)
    final = fold_mix(0, mix_grad(0, dmixed_zero)) + final_one
    moved_zero, dtables = shell_back_kinds()
    for k in range(2):
        total = jnp.sum(dtables[k], axis=1, keepdims=True)
        final = final + jnp.where(iota((PADDED, 128), 1) == 24 + k, total, 0.0)
    folded = final[0:8] + pltpu.roll(pltpu.roll(final[0:8], 4, 0), 32, 1) + pltpu.roll(final[8:16], 64, 1)
    final_own[...] = folded[0:4]
    everyone(lambda device, _: push(10, final_own, final_all.at[me], device))
    final_all[me] = final_own[...]
    product_back_kinds()
    plane_back_kinds()
    slopes_zero = coordinate_back_kinds()
    pull_of = pulls[...]
    to_own = mm(sender_rows[...], pull_of, NN, lax.Precision.HIGH)
    to_sender = mm(own, pull_of, NT, lax.Precision.HIGH)
    force_own[...] = jnp.zeros_like(force_own)
    for q in range(tiles):
        spot = slice(128 * q, 128 * (q + 1))
        weight_row = to_sender[5:6, spot]
        for axis in range(3):
            value = -2.0 * (to_sender[2 + axis : 3 + axis, spot] + sender_rows[2 + axis : 3 + axis, spot] * weight_row)
            value = value - slopes_zero[q][axis] - slopes_one[q][axis]
            force_own[2 * q, axis : axis + 1, :] = value
            force_own[2 * q + 1, axis : axis + 1, :] = pltpu.roll(value, BLOCK, 1)
    members(lambda device, target: push(9, force_own.at[target], force_all.at[col], device))
    force_all[col] = force_own[col]
    own_force = []
    for axis in range(3):
        pairwise = 2.0 * (to_own[2 + axis : 3 + axis] + own[2 + axis : 3 + axis] * to_own[5:6])
        moved = jnp.sum(moved_zero[axis] + moved_one[axis], axis=0, keepdims=True)
        both = pairwise + moved
        own_force.append(both + pltpu.roll(both, BLOCK, 1))

    group_energy = stat_all[3, row * lanes, 2:3, 96 : 96 + STRUCTS]
    for k in range(1, lanes):
        group_energy = group_energy + stat_all[3, row * lanes + k, 2:3, 96 : 96 + STRUCTS]
    energies_out[...] = group_energy

    gather_tiles(11, tiles_a_sum, base_a)
    gather_tiles(13, tiles_b_sum, base_b)
    pick_ones = ((iota((8, FEATURE_ROWS), 0) == 0) & (iota((8, FEATURE_ROWS), 1) == ONES_ROW)).astype(F32)
    for layer in range(2):
        total = None
        for parity in range(2):
            rows = []
            for r in range(3):
                at = 6 * parity + 2 * r
                summed = (tiles_a_sum, tiles_b_sum)[layer]
                rows.append(jnp.concatenate([summed[at], summed[at + 1]], axis=1))
            block = jnp.concatenate(rows, axis=0)
            if parity == 0:
                hidden_bias_out[layer : layer + 1, :] = mm(pick_ones, block, NT)[0:1]
            part = exact(block, select[parity])
            total = part if total is None else total + part
        hidden_weight_out[layer] = total
    small_sum = jnp.concatenate([tiles_b_sum[12 + r] for r in range(2)], axis=0)
    for layer in range(2):
        inner_weight_out[layer] = small_sum[0:INNER, 32 * layer : 32 * layer + HIDDEN]
        pick = ((row8 == 0) & (lane == 32 * layer + HIDDEN)).astype(F32)
        inner_bias_out[layer : layer + 1, :] = mm(pick, small_sum, NT)[0:1]
        pick = ((row8 == 0) & (lane == 64 + 32 * layer + HIDDEN)).astype(F32)
        energy_weight_out[layer : layer + 1, :] = mm(pick, small_sum, NT)[0:1]
    gather_tiles(15, tiles_c_sum, base_c)
    total = None
    for parity in range(2):
        rows = [
            jnp.concatenate(
                [tiles_c_sum[4 * parity + 2 * r], tiles_c_sum[4 * parity + 2 * r + 1]], axis=1
            )
            for r in range(2)
        ]
        part = exact(jnp.concatenate(rows, axis=0), select[parity])
        total = part if total is None else total + part
    message_weight_out[...] = total[0:CHANNELS]

    await_bytes(final_all, devices - 1, recv_sem.at[10])
    final = final_all[0]
    for k in range(1, devices):
        final = final + final_all[k]
    final = jnp.concatenate([final, jnp.zeros((4, 128), F32)], axis=0)
    upper = jnp.where(row8 < 4, final, pltpu.roll(pltpu.roll(final, 4, 0), 96, 1))
    final = jnp.concatenate([upper, pltpu.roll(final, 64, 1)], axis=0)
    dembedding = None
    for layer in range(2):
        channel_mix_out[:, layer, :] = final[0:CHANNELS, 12 * layer : 12 * (layer + 1)]
        dtable = final[0:CHANNELS, 24 + 2 * layer : 26 + 2 * layer]
        channel_in_out[layer] = lax.dot_general(
            embedding[...],
            dtable,
            (((0,), (1,)), ((), ())),
            precision=lax.Precision.HIGHEST,
            preferred_element_type=F32,
        )
        part = lax.dot_general(
            dtable,
            channel_in[layer],
            (((0,), (1,)), ((), ())),
            precision=lax.Precision.HIGHEST,
            preferred_element_type=F32,
        )
        dembedding = part if dembedding is None else dembedding + part
    embedding_out[...] = dembedding

    await_bytes(force_all, lanes - 1, recv_sem.at[9])
    force = force_all[0]
    for k in range(1, lanes):
        force = force + force_all[k]
    for axis in range(3):
        position_out[axis] = (force[axis : axis + 1] + own_force[axis])[:, 0:BLOCK]

    await_bytes(pack_all, lanes - 1, send_sem.at[0])
    await_bytes(send_all, lanes - 1, send_sem.at[1])
    await_bytes(recv_all, lanes - 1, send_sem.at[2])
    await_bytes(stat_all.at[0], devices - 1, send_sem.at[3])
    await_bytes(message_all, lanes - 1, send_sem.at[4])
    await_bytes(stat_all.at[1], devices - 1, send_sem.at[5])
    await_bytes(stat_all.at[2], devices - 1, send_sem.at[6])
    await_bytes(dmessage_all, lanes - 1, send_sem.at[7])
    await_bytes(stat_all.at[3], devices - 1, send_sem.at[8])
    await_bytes(force_all, lanes - 1, send_sem.at[9])
    await_bytes(final_all, devices - 1, send_sem.at[10])
    drain_tiles(11, tiles_a_all, tiles_a_sum, base_a)
    drain_tiles(13, tiles_b_all, tiles_b_sum, base_b)
    drain_tiles(15, tiles_c_all, tiles_c_sum, base_c)


def hand_over(*refs):
    for source, target in zip(refs[:11], refs[11:]):
        target[...] = source[...]


def solution(mesh):
    lanes = mesh.shape["edge"]
    structs = mesh.shape["struct"]
    devices = lanes * structs

    def step(
        positions,
        species,
        struct_id,
        atom_mask,
        senders,
        receivers,
        edge_mask,
        energy_cot,
        embedding,
        channel_in,
        channel_mix,
        hidden_weight,
        hidden_bias,
        inner_weight,
        inner_bias,
        energy_weight,
        message_weight,
    ):
        owned = positions.shape[2]
        group = owned * lanes
        edges = senders.shape[1]
        inputs = [
            positions,
            species,
            struct_id,
            atom_mask,
            senders,
            receivers,
            edge_mask,
            energy_cot,
            embedding,
            channel_in,
            jnp.transpose(channel_mix, (1, 0, 2)),
            jnp.transpose(hidden_weight, (0, 2, 1)),
            hidden_bias,
            jnp.transpose(inner_weight, (0, 2, 1)),
            inner_bias,
            energy_weight,
            jnp.transpose(message_weight),
        ]
        vmem = pltpu.VMEM
        shapes = [
            (1, STRUCTS),
            (3, 1, owned),
            embedding.shape,
            channel_in.shape,
            (CHANNELS, 2, CHANNELS),
            (2, HIDDEN, FEATURES),
            hidden_bias.shape,
            (2, INNER, HIDDEN),
            inner_bias.shape,
            energy_weight.shape,
            (CHANNELS, FEATURES),
        ]
        scratch = [
            vmem((8, 128), F32),
            vmem((lanes, 8, 128), F32),
            vmem((lanes, 1, edges), I32),
            vmem((1, edges), I32),
            vmem((lanes, 1, edges), I32),
            vmem((2, 128, BLOCK * (group // 256)), F32),
            vmem((group, 128), F32),
            vmem((group, 8), F32),
            vmem((8, group), F32),
            vmem((PAIRS, group, 128), F32),
            vmem((group, 128), F32),
            vmem((group, PLANE_LANES), BF16),
            vmem((group, PLANE_LANES), BF16),
            vmem((PLANE_LANES, group if group <= 512 else 128), BF16),
            vmem((PLANE_LANES, group if group <= 512 else 128), BF16),
            vmem((group, PLANE_LANES), F32),
            vmem((group, 128), F32),
            vmem((PADDED, group), F32),
            vmem((PRODUCT_ROWS, group), F32),
            vmem((752, group), BF16),
            vmem((496, group), BF16),
            vmem((PRODUCT_ROWS, PLANE_LANES), F32),
            vmem((PRODUCT_ROWS, PLANE_LANES), F32),
            vmem((40, group), F32),
            vmem((128, group), BF16),
            vmem((group, 240), BF16),
            vmem((40, PLANE_LANES), F32),
            vmem((SHELLS, 8, 128), F32),
            vmem((20, 8, 128), F32),
            vmem((40, PLANE_LANES), F32),
            vmem((40, group), F32),
            vmem((PRODUCT_ROWS, group), F32),
            vmem((2, 96, 128 * PAIRS), F32),
            vmem((96, 128 * PAIRS), F32),
            vmem((2, FEATURE_ROWS, 128), F32),
            vmem((2, FEATURE_ROWS, 128), F32),
            vmem((2, FEATURE_ROWS, FEATURES), BF16),
            vmem((2, 2 * HEAD_ROWS, FEATURE_ROWS), F32),
            vmem((2, 6 * HIDDEN, FEATURE_ROWS), BF16),
            vmem((6 * PADDED, FEATURE_ROWS), BF16),
            vmem((2, FEATURE_ROWS, 12 * HEAD_ROWS), BF16),
            vmem((FEATURE_ROWS, 12 * PADDED), BF16),
            vmem((2, INNER, 6 * HIDDEN), BF16),
            vmem((2, HIDDEN, 6 * INNER), BF16),
            vmem((2, 72, 6 * 96), BF16),
            vmem((2, 96, 6 * 72), BF16),
            vmem((4, 8, 128), F32),
            vmem((4, devices, 8, 128), F32),
            vmem((8, 128), F32),
            vmem((lanes, 8, 128), F32),
            vmem((lanes, 8, 128), F32),
            vmem((lanes, 8, 128), F32),
            vmem((lanes, 8, 128), F32),
            vmem((lanes, 8, 128), F32),
            vmem((4, 128), F32),
            vmem((devices, 4, 128), F32),
            vmem((12, 8, 128), F32),
            vmem((devices, 8, 128), F32),
            vmem((12, 8, 128), F32),
            vmem((14, 8, 128), F32),
            vmem((devices, 8, 128), F32),
            vmem((14, 8, 128), F32),
            vmem((8, 8, 128), F32),
            vmem((devices, 8, 128), F32),
            vmem((8, 8, 128), F32),
            pltpu.SemaphoreType.DMA((20,)),
            pltpu.SemaphoreType.DMA((20,)),
            pltpu.SemaphoreType.DMA((17,)),
        ] + [vmem(v.shape, v.dtype) for v in inputs]
        outs = pl.pallas_call(
            functools.partial(body, lanes, structs),
            out_shape=[vmem(s, F32) for s in shapes],
            in_specs=[pl.BlockSpec(memory_space=pl.ANY)] * 17,
            out_specs=[pl.BlockSpec(memory_space=vmem)] * 11,
            scratch_shapes=scratch,
            compiler_params=pltpu.CompilerParams(
                collective_id=0, has_side_effects=True, vmem_limit_bytes=60 * 1024 * 1024
            ),
        )(*inputs)
        outs = pl.pallas_call(
            hand_over,
            out_shape=[jax.ShapeDtypeStruct(s, F32) for s in shapes],
            in_specs=[pl.BlockSpec(memory_space=vmem)] * 11,
            out_specs=[pl.BlockSpec(memory_space=vmem)] * 11,
        )(*(pltpu.with_memory_space_constraint(v, pltpu.VMEM) for v in outs))
        outs = list(outs)
        outs[4] = jnp.transpose(outs[4], (1, 0, 2))
        outs[5] = jnp.transpose(outs[5], (0, 2, 1))
        outs[7] = jnp.transpose(outs[7], (0, 2, 1))
        outs[10] = jnp.transpose(outs[10])
        return tuple(outs)

    tiled = P("struct", "edge")
    return jax.shard_map(
        step,
        mesh=mesh,
        in_specs=(
            P(None, "struct", "edge"),
            tiled,
            tiled,
            tiled,
            tiled,
            tiled,
            tiled,
            P("struct", None),
        )
        + (P(),) * 9,
        out_specs=(P("struct", None), P(None, "struct", "edge")) + (P(),) * 9,
        check_vma=False,
    )
```
